32 devices in a mesh: gx: 4 (over z), gy: 8 (over y, x, core).
Axes of the slice: x: 2, y: 2, z: 4, core: 2. Of those that a mesh axis runs over, the one named last changes fastest.
Arguments:
- particles: float32 [384, 6, 128], P(('gx', 'gy')), may hold values from -6 to 6
- occupancy: int32 [384], P(('gx', 'gy')), may hold values from 32 to 128, as said below
- neighbours: int32 [384, 16], P(('gx', 'gy')), may hold values from 0 to 383, as said below
- curve_cuts: int32 [2, 32], replicated, may hold values from 0 to 378, as said below
Outputs:
- after_first: float32 [768, 6, 128], P(('gx', 'gy'))
- after_second: float32 [768, 6, 128], P(('gx', 'gy'))
The draws below stay inside these ranges and needn't reach their ends.
Inputs may be any that keep to these rules, and one draw needn't show every extreme that they name: `occupancy`: each tile holds at least 32 live particles, and some tile in every draw holds 128. `neighbours`: tile t lists 16 different tiles among the curve positions t + 1 to t + 24, counted modulo 384. `curve_cuts`: entry d of each row is d * 12 + e with e between -6 and 6, and e is 0 for device 0; so each device owns 0 to 24 tiles, and in every step some device owns exactly 24.
All inputs are finite; a program needn't handle non-finite values.
Results may differ from the reference program's by a relative error of at most 0.0001.
Values sent between devices are 32-bit elements; how exact they have to be, the bound alone decides.
No kernel may reach another device: no remote copies, remote signals or barrier semaphores. Data moves between devices by JAX's collectives and lax.ppermute only.
A program may use at most 64 MiB of HBM per device.

```python
import jax
import jax.numpy as jnp
from jax import lax

TILE_P = 128
NBR = 16
STEPS = 2
TILE_DEV = 12
HALF = 6
CAP = 24
WIN = 24
NT = 384
DEVICES = 32


def draw_occupancy(key, part):
    count_key, pick_key = jax.random.split(key)
    filled = jax.random.randint(count_key, (NT,), TILE_P // 4, TILE_P + 1, dtype=jnp.int32)
    chosen = jax.random.randint(pick_key, (), 0, NT, dtype=jnp.int32)
    return filled.at[chosen].set(TILE_P)


def draw_neighbours(key, part):
    scores = jax.random.randint(key, (NT, WIN), 0, 2 ** 20, dtype=jnp.int32) * WIN + jnp.arange(WIN, dtype=jnp.int32)[None, :]
    ranked = jnp.argsort(scores, axis=1, stable=True)[:, :NBR].astype(jnp.int32)
    return ((jnp.arange(NT, dtype=jnp.int32)[:, None] + ranked + 1) % NT).astype(jnp.int32)


def draw_curve_cuts(key, part):
    shift_key, pick_key = jax.random.split(key)
    departure = jax.random.randint(shift_key, (STEPS, DEVICES), -HALF, HALF + 1, dtype=jnp.int32)
    departure = departure.at[:, 0].set(0)
    chosen = jax.random.randint(pick_key, (STEPS,), 1, DEVICES - 1, dtype=jnp.int32)
    step_rows = jnp.arange(STEPS, dtype=jnp.int32)
    departure = departure.at[step_rows, chosen].set(-HALF)
    departure = departure.at[step_rows, chosen + 1].set(HALF)
    return (jnp.arange(DEVICES, dtype=jnp.int32)[None, :] * TILE_DEV + departure).astype(jnp.int32)


def shard_levels(own_key, dims, shards, least, top_value):
    def one(dim, parts):
        steps = jax.random.uniform(jax.random.fold_in(jax.random.fold_in(own_key, 6), dim), (parts,), jnp.float32, least / len(shards), top_value / len(shards))
        return jnp.repeat(jnp.exp(steps), dims[dim] // parts).reshape((-1,) + (1,) * (len(dims) - dim - 1))

    factor_of = one(*shards[0])
    for cut in shards[1:]:
        factor_of = factor_of * one(*cut)
    return factor_of


def noise(own_key, extent, spread, most, shards=(), held_as=jnp.bfloat16):
    values = jax.random.normal(own_key, extent, jnp.float32) * spread
    if len(shards) > 0:
        values = shard_levels(own_key, extent, shards, -0.22, 0.18) * values
    return jnp.clip(values, min=-most, max=most).astype(held_as)


def setup_inputs(seed: int = 0) -> dict:
    streams_of = jax.random.split(jax.random.key(seed), 5)
    particles = noise(streams_of[0], (NT, 6, TILE_P), 1.0, 6.0, ((0, 32),), jnp.float32)
    occupancy = draw_occupancy(jax.random.fold_in(streams_of[4], 71), 0)
    neighbours = draw_neighbours(jax.random.fold_in(streams_of[4], 71), 0)
    curve_cuts = draw_curve_cuts(jax.random.fold_in(streams_of[4], 71), 0)
    return dict(particles=particles, occupancy=occupancy, neighbours=neighbours, curve_cuts=curve_cuts)


soften = 0.05
time_step = 0.5
block_tiles = 4


def pair_terms(targets, sources):
    target_pos = targets[:, None, :3, :, None]
    source_pos = sources[:, :, :3, None, :]
    separation = source_pos - target_pos
    distance_sq = jnp.sum(separation * separation, axis=2) + soften
    kernel = distance_sq ** -1.5
    action = jnp.sum(kernel[:, :, None] * sources[:, :, 3][:, :, None, None, :] * separation, axis=(1, 4))
    reaction = -jnp.sum(kernel[:, :, None] * targets[:, 3][:, None, None, :, None] * separation, axis=3)
    return action, reaction


def forces(pos_weight, neighbours):
    block_count = NT // block_tiles

    def block_pass(react_pool, inputs):
        targets, source_ids = inputs
        sources = jnp.concatenate([targets[:, None], pos_weight[source_ids]], axis=1)
        action, reaction = pair_terms(targets, sources)
        react_pool = react_pool.at[source_ids.reshape(-1)].add(reaction[:, 1:].reshape(-1, 3, TILE_P))
        return react_pool, action

    start_pool = jnp.zeros((NT, 3, TILE_P), jnp.float32)
    react_pool, actions = lax.scan(block_pass, start_pool, (pos_weight.reshape(block_count, block_tiles, 4, TILE_P), neighbours.reshape(block_count, block_tiles, NBR)))
    return react_pool + actions.reshape(NT, 3, TILE_P)


def reference(particles, occupancy, neighbours, curve_cuts):
    weight = (jnp.arange(TILE_P, dtype=jnp.int32)[None, :] < occupancy[:, None]).astype(jnp.float32)
    position = particles[:, :3]
    velocity = particles[:, 3:]
    snapshots = []
    for step_index in range(STEPS):
        pos_weight = jnp.concatenate([position, weight[:, None]], axis=1)
        acceleration = forces(pos_weight, neighbours)
        velocity = weight[:, None] * (velocity + time_step * acceleration / TILE_P)
        position = weight[:, None] * (position + time_step * velocity)
        starts = curve_cuts[step_index]
        segment_end = jnp.concatenate([starts[1:], jnp.array([NT], jnp.int32)])
        slot_tiles = starts[:, None] + jnp.arange(CAP, dtype=jnp.int32)[None, :]
        occupied = (slot_tiles < segment_end[:, None]).reshape(-1).astype(jnp.float32)
        merged = jnp.concatenate([position, velocity], axis=1)
        picked = merged[jnp.clip(slot_tiles, 0, NT - 1).reshape(-1)]
        snapshots.append(picked * occupied[:, None, None])
    return (snapshots[0], snapshots[1])
```

```python
import functools

import jax
import jax.numpy as jnp
from jax import lax
from jax.experimental import pallas as pl
from jax.experimental.pallas import tpu as pltpu
from jax.sharding import PartitionSpec as P

AXES = ("gx", "gy")
STEPS = 2

soften = 0.05
time_step = 0.5
reach = 2
chunk = 4
feature_rows = 32
moment_rows = 16
lanes = 128


def shifted(value, steps):
    count = lax.axis_size(AXES)
    pairs = [(source, (source + steps) % count) for source in range(count)]
    return lax.ppermute(value, AXES, pairs)


def shifted_open(value, steps):
    count = lax.axis_size(AXES)
    first, last = (max(0, -steps), min(count, count - steps))
    return lax.ppermute(value, AXES, [(source, source + steps) for source in range(first, last)])


def round_up(value, step):
    return -(-value // step) * step


def device_index():
    return lax.axis_index("gx") * lax.axis_size("gy") + lax.axis_index("gy")


def pieces(value, count):
    parts = []
    rest = value
    for _ in range(count - 1):
        part = rest.astype(jnp.bfloat16).astype(jnp.float32)
        parts.append(part)
        rest = rest - part
    parts.append(rest.astype(jnp.bfloat16).astype(jnp.float32))
    return parts


def pack_kernel(total_tiles, particles_ref, occupancy_ref, neighbours_ref, packed_ref):
    tiles, slots = packed_ref.shape[1:]
    listed = neighbours_ref.shape[1]
    for row in range(3):
        packed_ref[row] = particles_ref[:, row, :]
    tile_ids = lax.broadcasted_iota(jnp.int32, (tiles, listed), 0)
    offsets = neighbours_ref[...] - (device_index() * tiles + tile_ids)
    offsets = jnp.where(offsets < 0, offsets + total_tiles, offsets)
    packed_ref[3] = jnp.zeros((tiles, slots), jnp.float32)
    packed_ref[3, :, :listed] = offsets.astype(jnp.float32)
    for tile in range(tiles):
        live = occupancy_ref[tile].astype(jnp.float32)
        packed_ref[3, tile : tile + 1, listed : listed + 1] = jnp.full((1, 1), live)


def build_lists(aux, window, tiles, listed, rows):
    center = reach * tiles
    place = lax.broadcasted_iota(jnp.int32, (rows, lanes), 0).astype(jnp.float32)
    lane = lax.broadcasted_iota(jnp.int32, (rows, lanes), 1).astype(jnp.float32)
    mask = place == lane + center
    for entry in range(listed):
        mask = mask | (place + aux[:, entry : entry + 1] == lane + center)
    own_rows = round_up(tiles, 8)
    own = aux[center : center + own_rows]
    own_place = lax.broadcasted_iota(jnp.int32, (own_rows, lanes), 0).astype(jnp.float32) + center
    own_lane = lax.broadcasted_iota(jnp.int32, (own_rows, lanes), 1).astype(jnp.float32)
    listing = own_place + own[:, 0:1] == own_lane
    for entry in range(1, listed):
        listing = listing | (own_place + own[:, entry : entry + 1] == own_lane)
    listing = jnp.where(listing, 1.0, 0.0)
    listing = jnp.concatenate([listing, jnp.zeros((lanes - own_rows, lanes), jnp.float32)], axis=0)
    listing = jnp.transpose(listing)[:rows]
    mask = jnp.where(lane < tiles, jnp.maximum(jnp.where(mask, 1.0, 0.0), listing), 0.0)
    earlier = lax.broadcasted_iota(jnp.int32, (rows, rows), 1) < lax.broadcasted_iota(jnp.int32, (rows, rows), 0)
    rank = jnp.dot(
        jnp.where(earlier, 1.0, 0.0).astype(jnp.bfloat16),
        mask.astype(jnp.bfloat16),
        preferred_element_type=jnp.float32,
    )
    key = jnp.where(mask > 0.5, rank, -1.0)
    counts = jnp.sum(mask, axis=0, keepdims=True)
    lists = []
    for tile in range(tiles):
        hit = key[:, tile : tile + 1] == lane
        lists.append(jnp.sum(jnp.where(hit, place - window, 0.0), axis=0, keepdims=True) + window)
    lists.append(jnp.full((1, lanes), float(window)))
    lists.append(counts)
    return [row.astype(jnp.int32) for row in lists]


def build_features(place_of, weight, tiles, rows, refs):
    feature_ref, moment_ref, source_ref, target_ref, moments_ref = refs
    center = reach * tiles
    middle = [jnp.mean(axis[center : center + 8], keepdims=True) for axis in place_of]
    centred = [axis - mid for axis, mid in zip(place_of, middle)]
    norm = centred[0] * centred[0] + centred[1] * centred[1] + centred[2] * centred[2]
    ones = jnp.ones_like(norm)
    source_rows = []
    target_rows = []
    moments = []
    for axis in centred:
        near, mid, far = pieces(axis, 3)
        near_2, mid_2, far_2 = (-2.0 * near, -2.0 * mid, -2.0 * far)
        source_rows += [near, near, mid, mid, near, far]
        target_rows += [near_2, mid_2, near_2, mid_2, far_2, near_2]
        moments += [weight * near, weight * mid, weight * far]
    source_rows += pieces(norm, 3) + [ones] * 3
    target_rows += [ones] * 3 + pieces(norm + soften, 3)
    moments.append(weight)
    zeros = jnp.zeros_like(norm)
    source_rows += [zeros] * (feature_rows - len(source_rows))
    moments += [zeros] * (moment_rows - len(moments))
    for row, value in enumerate(source_rows):
        feature_ref[:, row, :] = value
    for row, value in enumerate(moments):
        moment_ref[:, row, :] = value
    per_group = lanes // feature_rows
    for group in range(rows // per_group):
        block = feature_ref[group * per_group : (group + 1) * per_group].reshape(lanes, lanes)
        source_ref[group] = jnp.transpose(block).astype(jnp.bfloat16)
    for tile in range(rows):
        moment = moment_ref[tile].astype(jnp.bfloat16)
        moments_ref[tile] = jnp.concatenate([moment, moment], axis=1)
    target_rows += [zeros] * (feature_rows - len(target_rows))
    own_rows = round_up(tiles, 8)
    for row, value in enumerate(target_rows):
        feature_ref[:own_rows, row, :] = value[center : center + own_rows]
    blank = jnp.zeros((feature_rows, lanes), jnp.bfloat16)
    for tile in range(tiles + 1):
        target = feature_ref[tile].astype(jnp.bfloat16)
        for variant in range(per_group):
            for part in range(per_group):
                target_ref[tile, variant, part * feature_rows : (part + 1) * feature_rows, :] = (
                    target if part == variant else blank
                )
    return centred


def accumulate(tiles, lists_ref, source_ref, target_ref, moments_ref, distance_ref, kernel_ref, total_ref):
    per_group = lanes // feature_rows
    total_ref[...] = jnp.zeros(total_ref.shape, jnp.float32)
    chunk_counts = [(lists_ref[tiles + 1, tile] + chunk - 1) // chunk for tile in range(tiles)]
    chunk_total = functools.reduce(lambda left, right: left + right, chunk_counts)

    def step(_, carry):
        tile, part, tile_1, part_1, tile_2, part_2 = carry
        moment = jnp.concatenate(
            [moments_ref[lists_ref[tile_2, part_2 * chunk + entry]] for entry in range(chunk)], axis=1
        )
        total_ref[tile_2] += jnp.dot(moment, kernel_ref[...], preferred_element_type=jnp.float32)
        for entry in range(chunk):
            inverse = lax.rsqrt(distance_ref[entry])
            kernel = inverse * inverse * inverse
            high = kernel.astype(jnp.bfloat16)
            low = (kernel - high.astype(jnp.float32)).astype(jnp.bfloat16)
            kernel_ref[entry * 2 * lanes : entry * 2 * lanes + lanes, :] = high
            kernel_ref[entry * 2 * lanes + lanes : (entry + 1) * 2 * lanes, :] = low
        for entry in range(chunk):
            source = lists_ref[tile, part * chunk + entry]
            distance_ref[entry] = jnp.dot(
                source_ref[source // per_group],
                target_ref[tile, source % per_group],
                preferred_element_type=jnp.float32,
            )
        filled = lists_ref[tiles + 1, tile]
        more = (part + 1) * chunk < filled
        next_tile = jnp.where(more, tile, jnp.minimum(tile + 1, tiles))
        next_part = jnp.where(more, part + 1, 0)
        return (next_tile, next_part, tile, part, tile_1, part_1)

    zero = jnp.int32(0)
    spare = jnp.int32(tiles)
    lax.fori_loop(0, chunk_total + 2, step, (zero, zero, spare, zero, spare, zero))


def advance(tiles, centred, place_own, speed_own, weight_own, total_ref, state_ref):
    center = reach * tiles
    zeroth = total_ref[:tiles, 9, :]
    for axis in range(3):
        first = total_ref[:tiles, 3 * axis, :] + total_ref[:tiles, 3 * axis + 1, :] + total_ref[:tiles, 3 * axis + 2, :]
        force = first - centred[axis][center : center + tiles] * zeroth
        speed = weight_own * (speed_own[axis] + time_step * force / lanes)
        state_ref[axis] = weight_own * (place_own[axis] + time_step * speed)
        state_ref[3 + axis] = speed


def first_kernel(
    listed, before_2, before_1, own_ref, after_1, after_2, particles_ref, state_ref, weight_ref, lists_ref, *scratch
):
    planes, scalars, copy_sem, feature_ref, moment_ref, source_ref, target_ref, moments_ref, *loop_refs = scratch
    tiles, slots = own_ref.shape[1:]
    rows = planes.shape[1]
    window = (2 * reach + 1) * tiles
    planes[:, window:, :] = jnp.zeros((4, rows - window, slots), jnp.float32)
    for block, ref in enumerate((before_2, before_1, own_ref, after_1, after_2)):
        planes[:, block * tiles : (block + 1) * tiles, :] = ref[...]
    aux = planes[3]
    for row, value in enumerate(build_lists(aux, window, tiles, listed, rows)):
        lists_ref[row : row + 1, :] = value
    copy = pltpu.make_async_copy(lists_ref, scalars, copy_sem)
    copy.start()
    slot = lax.broadcasted_iota(jnp.int32, (rows, slots), 1).astype(jnp.float32)
    weight = jnp.where(slot < aux[:, listed : listed + 1], 1.0, 0.0)
    weight_ref[...] = weight
    refs = (feature_ref, moment_ref, source_ref, target_ref, moments_ref)
    centred = build_features([planes[axis] for axis in range(3)], weight, tiles, rows, refs)
    copy.wait()
    accumulate(tiles, scalars, source_ref, target_ref, moments_ref, *loop_refs)
    center = reach * tiles
    advance(
        tiles,
        centred,
        [own_ref[axis] for axis in range(3)],
        [particles_ref[:, 3 + axis, :] for axis in range(3)],
        weight[center : center + tiles],
        loop_refs[-1],
        state_ref,
    )


def place_rows(step, total_tiles, cuts_ref, lower, own, upper, pool_ref, out_ref):
    tiles = own[0].shape[0]
    half = tiles // 2
    capacity = out_ref.shape[0]
    device = device_index()
    last = cuts_ref.shape[1] - 1
    first_tile = cuts_ref[step, device]
    next_tile = jnp.where(device == last, total_tiles, cuts_ref[step, jnp.minimum(device + 1, last)])
    owned = next_tile - first_tile
    start = first_tile - (device * tiles - half)
    for row in range(6):
        pool_ref[:half, row, :] = lower[row]
        pool_ref[half : half + tiles, row, :] = own[row]
        pool_ref[half + tiles : 2 * tiles, row, :] = upper[row]
    for slot in range(capacity):
        source = jnp.minimum(start + slot, 2 * tiles - 1)
        out_ref[slot] = jnp.where(slot < owned, pool_ref[source], 0.0)


def second_kernel(
    total_tiles, lists_ref, cuts_ref, before_2, before_1, own_ref, after_1, after_2, weight_ref, state_ref, out_ref, *scratch
):
    planes, pool_ref, feature_ref, moment_ref, source_ref, target_ref, moments_ref, *loop_refs = scratch
    tiles, slots = own_ref.shape[1:]
    half = tiles // 2
    rows = planes.shape[1]
    window = (2 * reach + 1) * tiles
    planes[:, window:, :] = jnp.zeros((3, rows - window, slots), jnp.float32)
    for block, ref in enumerate((before_2, before_1, own_ref, after_1, after_2)):
        planes[:, block * tiles : (block + 1) * tiles, :] = ref[:3]
    weight = weight_ref[...]
    refs = (feature_ref, moment_ref, source_ref, target_ref, moments_ref)
    centred = build_features([planes[axis] for axis in range(3)], weight, tiles, rows, refs)
    accumulate(tiles, lists_ref, source_ref, target_ref, moments_ref, *loop_refs)
    center = reach * tiles
    advance(
        tiles,
        centred,
        [own_ref[axis] for axis in range(3)],
        [own_ref[3 + axis] for axis in range(3)],
        weight[center : center + tiles],
        loop_refs[-1],
        state_ref,
    )
    place_rows(
        0,
        total_tiles,
        cuts_ref,
        [before_1[row, tiles - half :, :] for row in range(6)],
        [own_ref[row] for row in range(6)],
        [after_1[row, :half, :] for row in range(6)],
        pool_ref,
        out_ref,
    )


def third_kernel(total_tiles, cuts_ref, lower_ref, own_ref, upper_ref, out_ref, pool_ref):
    place_rows(
        1,
        total_tiles,
        cuts_ref,
        [lower_ref[row] for row in range(6)],
        [own_ref[row] for row in range(6)],
        [upper_ref[row] for row in range(6)],
        pool_ref,
        out_ref,
    )


def body(particles, occupancy, neighbours, curve_cuts):
    tiles, _, slots = particles.shape
    listed = neighbours.shape[1]
    total_tiles = tiles * lax.axis_size(AXES)
    half = tiles // 2
    rows = round_up((2 * reach + 1) * tiles + 1, 8)
    vmem = pl.BlockSpec(memory_space=pltpu.VMEM)
    smem = pl.BlockSpec(memory_space=pltpu.SMEM)

    def shape(*sizes, dtype=jnp.float32):
        return jax.ShapeDtypeStruct(sizes, dtype)

    packed = pl.pallas_call(
        functools.partial(pack_kernel, total_tiles),
        out_shape=shape(4, tiles, slots),
        in_specs=[vmem, smem, vmem],
        out_specs=vmem,
        name="pack",
    )(particles, occupancy, neighbours)
    feature_scratch = [
        pltpu.VMEM((rows, feature_rows, lanes), jnp.float32),
        pltpu.VMEM((rows, moment_rows, lanes), jnp.float32),
        pltpu.VMEM((rows * feature_rows // lanes, lanes, lanes), jnp.bfloat16),
        pltpu.VMEM((tiles + 1, lanes // feature_rows, lanes, lanes), jnp.bfloat16),
        pltpu.VMEM((rows, moment_rows, 2 * lanes), jnp.bfloat16),
        pltpu.VMEM((chunk, lanes, lanes), jnp.float32),
        pltpu.VMEM((chunk * 2 * lanes, lanes), jnp.bfloat16),
        pltpu.VMEM((round_up(tiles + 1, 8), moment_rows, lanes), jnp.float32),
    ]
    pool_scratch = pltpu.VMEM((2 * tiles, 6, slots), jnp.float32)
    list_rows = round_up(tiles + 2, 8)
    state, weight, lists = pl.pallas_call(
        functools.partial(first_kernel, listed),
        out_shape=(shape(6, tiles, slots), shape(rows, slots), shape(list_rows, lanes, dtype=jnp.int32)),
        in_specs=[vmem] * 6,
        out_specs=(vmem, vmem, vmem),
        scratch_shapes=[
            pltpu.VMEM((4, rows, slots), jnp.float32),
            pltpu.SMEM((list_rows, lanes), jnp.int32),
            pltpu.SemaphoreType.DMA,
        ]
        + feature_scratch,
        name="first_step",
    )(shifted(packed, 2), shifted(packed, 1), packed, shifted(packed, -1), shifted(packed, -2), particles)
    state_2, after_first = pl.pallas_call(
        functools.partial(second_kernel, total_tiles),
        out_shape=(shape(6, tiles, slots), shape(2 * tiles, 6, slots)),
        in_specs=[smem, smem] + [vmem] * 6,
        out_specs=(vmem, vmem),
        scratch_shapes=[pltpu.VMEM((3, rows, slots), jnp.float32), pool_scratch] + feature_scratch,
        name="second_step",
    )(
        lists,
        curve_cuts,
        shifted(state, 2),
        shifted(state, 1),
        state,
        shifted(state, -1),
        shifted(state, -2),
        weight,
    )
    lower = shifted_open(state_2[:, tiles - half :, :], 1)
    upper = shifted_open(state_2[:, :half, :], -1)
    after_second = pl.pallas_call(
        functools.partial(third_kernel, total_tiles),
        out_shape=shape(2 * tiles, 6, slots),
        in_specs=[smem, vmem, vmem, vmem],
        out_specs=vmem,
        scratch_shapes=[pool_scratch],
        name="place",
    )(curve_cuts, lower, state_2, upper)
    return (after_first, after_second)


def solution(mesh):
    in_specs = (P(AXES, None, None), P(AXES), P(AXES, None), P())
    out_specs = (P(AXES, None, None), P(AXES, None, None))
    return jax.shard_map(body, mesh=mesh, in_specs=in_specs, out_specs=out_specs, check_vma=False)
```

```python
import functools

import jax
import jax.numpy as jnp
from jax import lax
from jax.experimental import pallas as pl
from jax.experimental.pallas import tpu as pltpu
from jax.sharding import PartitionSpec as P

AXES = ("gx", "gy")
STEPS = 2

soften = 0.05
time_step = 0.5
reach = 2
chunk = 4
feature_rows = 32
far_norm = 1e36
lanes = 128


def shifted(value, steps):
    count = lax.axis_size(AXES)
    pairs = [(source, (source + steps) % count) for source in range(count)]
    return lax.ppermute(value, AXES, pairs)


def shifted_open(value, steps):
    count = lax.axis_size(AXES)
    first, last = (max(0, -steps), min(count, count - steps))
    return lax.ppermute(value, AXES, [(source, source + steps) for source in range(first, last)])


def round_up(value, step):
    return -(-value // step) * step


def device_index():
    return lax.axis_index("gx") * lax.axis_size("gy") + lax.axis_index("gy")


def pieces(value, count):
    parts = []
    rest = value
    for _ in range(count - 1):
        part = rest.astype(jnp.bfloat16).astype(jnp.float32)
        parts.append(part)
        rest = rest - part
    parts.append(rest.astype(jnp.bfloat16).astype(jnp.float32))
    return parts


def pack_kernel(total_tiles, particles_ref, occupancy_ref, neighbours_ref, packed_ref, speed_ref):
    tiles, slots = packed_ref.shape[1:]
    listed = neighbours_ref.shape[1]
    for row in range(3):
        packed_ref[row] = particles_ref[:, row, :]
        speed_ref[row] = particles_ref[:, 3 + row, :]
    tile_ids = lax.broadcasted_iota(jnp.int32, (tiles, listed), 0)
    offsets = neighbours_ref[...] - (device_index() * tiles + tile_ids)
    offsets = jnp.where(offsets < 0, offsets + total_tiles, offsets)
    packed_ref[3] = jnp.zeros((tiles, slots), jnp.float32)
    packed_ref[3, :, :listed] = offsets.astype(jnp.float32)
    for tile in range(tiles):
        live = occupancy_ref[tile].astype(jnp.float32)
        packed_ref[3, tile : tile + 1, listed : listed + 1] = jnp.full((1, 1), live)


def build_lists(aux, window, tiles, listed, rows):
    center = reach * tiles
    place = lax.broadcasted_iota(jnp.int32, (rows, lanes), 0).astype(jnp.float32)
    lane = lax.broadcasted_iota(jnp.int32, (rows, lanes), 1).astype(jnp.float32)
    mask = place == lane + center
    for entry in range(listed):
        mask = mask | (place + aux[:, entry : entry + 1] == lane + center)
    own_rows = round_up(tiles, 8)
    own = aux[center : center + own_rows]
    own_place = lax.broadcasted_iota(jnp.int32, (own_rows, lanes), 0).astype(jnp.float32) + center
    own_lane = lax.broadcasted_iota(jnp.int32, (own_rows, lanes), 1).astype(jnp.float32)
    listing = own_place + own[:, 0:1] == own_lane
    for entry in range(1, listed):
        listing = listing | (own_place + own[:, entry : entry + 1] == own_lane)
    listing = jnp.where(listing, 1.0, 0.0)
    listing = jnp.concatenate([listing, jnp.zeros((lanes - own_rows, lanes), jnp.float32)], axis=0)
    listing = jnp.transpose(listing)[:rows]
    mask = jnp.where(lane < tiles, jnp.maximum(jnp.where(mask, 1.0, 0.0), listing), 0.0)
    earlier = lax.broadcasted_iota(jnp.int32, (rows, rows), 1) < lax.broadcasted_iota(jnp.int32, (rows, rows), 0)
    rank = jnp.dot(
        jnp.where(earlier, 1.0, 0.0).astype(jnp.bfloat16),
        mask.astype(jnp.bfloat16),
        preferred_element_type=jnp.float32,
    )
    key = jnp.where(mask > 0.5, rank, -1.0)
    counts = jnp.sum(mask, axis=0, keepdims=True)
    lists = []
    for tile in range(tiles):
        hit = key[:, tile : tile + 1] == lane
        lists.append(jnp.sum(jnp.where(hit, place - window, 0.0), axis=0, keepdims=True) + window)
    lists.append(jnp.full((1, lanes), float(window)))
    lists.append(counts)
    return [row.astype(jnp.int32) for row in lists]


def build_features(place_of, weight, tiles, refs):
    feature_ref, moment_ref, source_ref, target_ref = refs
    rows = feature_ref.shape[0]
    center = reach * tiles
    middle = [jnp.mean(axis[center : center + 8], keepdims=True) for axis in place_of]
    centred = [axis - mid for axis, mid in zip(place_of, middle)]
    ones = jnp.ones_like(weight)
    zeros = jnp.zeros_like(weight)
    source_rows = []
    target_rows = []
    norm = zeros
    for axis, value in enumerate(centred):
        norm = norm + value * value
        live = weight * value
        moment_ref[:, axis, :] = live
        near, mid, far = pieces(live, 3)
        source_rows += [near, near, mid, mid, near, far]
        near, mid, far = [-2.0 * part for part in pieces(value, 3)]
        target_rows += [near, mid, near, mid, far, near]
    source_rows += pieces(jnp.where(weight > 0.5, norm, far_norm), 3) + [ones] * 3
    target_rows += [ones] * 3 + pieces(norm + soften, 3)
    source_rows += [zeros] * (feature_rows - len(source_rows))
    target_rows += [zeros] * (feature_rows - len(target_rows))
    for row, value in enumerate(source_rows):
        feature_ref[:, row, :] = value
    for tile in range(rows):
        source_ref[tile] = feature_ref[tile].astype(jnp.bfloat16)
    own_rows = round_up(tiles, 8)
    for row, value in enumerate(target_rows):
        feature_ref[:own_rows, row, :] = value[center : center + own_rows]
    blank = jnp.zeros((lanes - feature_rows, lanes), jnp.float32)
    for tile in range(tiles + 1):
        block = jnp.concatenate([feature_ref[tile], blank], axis=0)
        target_ref[tile] = jnp.transpose(block)[:, :feature_rows].astype(jnp.bfloat16)
    return centred


def accumulate(tiles, lists_ref, source_ref, target_ref, moment_ref, distance_ref, total_ref, sums_ref):
    total_ref[...] = jnp.zeros(total_ref.shape, jnp.float32)
    chunk_counts = [(lists_ref[tiles + 1, tile] + chunk - 1) // chunk for tile in range(tiles)]
    chunk_total = functools.reduce(lambda left, right: left + right, chunk_counts)

    def step(_, carry):
        tile, part, tile_1, part_1 = carry
        places = []
        for entry in range(chunk):
            source = lists_ref[tile_1, part_1 * chunk + entry]
            places.append([jnp.broadcast_to(moment_ref[source, axis : axis + 1, :], (8, lanes)) for axis in range(3)])
        for first in range(0, lanes, 8):
            strip = slice(first, first + 8)
            sums = [total_ref[tile_1, row, strip, :] for row in range(4)]
            for entry in range(chunk):
                column = (entry % 2) * lanes
                inverse = lax.rsqrt(distance_ref[entry // 2, strip, column : column + lanes])
                kernel = inverse * inverse * inverse
                for axis in range(3):
                    sums[axis] = sums[axis] + kernel * places[entry][axis]
                sums[3] = sums[3] + kernel
            for row in range(4):
                total_ref[tile_1, row, strip, :] = sums[row]
        for pair in range(chunk // 2):
            sources = [lists_ref[tile, part * chunk + 2 * pair + entry] for entry in range(2)]
            distance_ref[pair] = jnp.dot(
                target_ref[tile],
                jnp.concatenate([source_ref[source] for source in sources], axis=1),
                preferred_element_type=jnp.float32,
            )
        more = (part + 1) * chunk < lists_ref[tiles + 1, tile]
        next_tile = jnp.where(more, tile, jnp.minimum(tile + 1, tiles))
        next_part = jnp.where(more, part + 1, 0)
        return (next_tile, next_part, tile, part)

    zero = jnp.int32(0)
    spare = jnp.int32(tiles)
    lax.fori_loop(0, chunk_total + 1, step, (zero, zero, spare, zero))
    for tile in range(tiles):
        for row in range(4):
            sums_ref[row, tile : tile + 1, :] = jnp.sum(jnp.transpose(total_ref[tile, row]), axis=0, keepdims=True)


def advance(centred, place_own, speed_own, weight_own, sums_ref, state_ref):
    tiles = weight_own.shape[0]
    center = reach * tiles
    zeroth = sums_ref[3, :tiles, :]
    for axis in range(3):
        force = sums_ref[axis, :tiles, :] - centred[axis][center : center + tiles] * zeroth
        speed = weight_own * (speed_own[axis] + time_step * force / lanes)
        state_ref[axis] = weight_own * (place_own[axis] + time_step * speed)
        state_ref[3 + axis] = speed


def first_kernel(
    listed, before_2, before_1, own_ref, after_1, after_2, speed_ref, state_ref, weight_ref, lists_ref, *scratch
):
    planes, scalars, copy_sem, feature_ref, moment_ref, source_ref, target_ref, *loop_refs = scratch
    tiles, slots = own_ref.shape[1:]
    rows = planes.shape[1]
    window = (2 * reach + 1) * tiles
    planes[:, window:, :] = jnp.zeros((4, rows - window, slots), jnp.float32)
    for block, ref in enumerate((before_2, before_1, own_ref, after_1, after_2)):
        planes[:, block * tiles : (block + 1) * tiles, :] = ref[...]
    aux = planes[3]
    for row, value in enumerate(build_lists(aux, window, tiles, listed, rows)):
        lists_ref[row : row + 1, :] = value
    copy = pltpu.make_async_copy(lists_ref, scalars, copy_sem)
    copy.start()
    slot = lax.broadcasted_iota(jnp.int32, (rows, slots), 1).astype(jnp.float32)
    weight = jnp.where(slot < aux[:, listed : listed + 1], 1.0, 0.0)
    weight_ref[...] = weight
    refs = (feature_ref, moment_ref, source_ref, target_ref)
    centred = build_features([planes[axis] for axis in range(3)], weight, tiles, refs)
    copy.wait()
    accumulate(tiles, scalars, source_ref, target_ref, moment_ref, *loop_refs)
    center = reach * tiles
    advance(
        centred,
        [own_ref[axis] for axis in range(3)],
        [speed_ref[axis] for axis in range(3)],
        weight[center : center + tiles],
        loop_refs[-1],
        state_ref,
    )


def place_rows(step, total_tiles, cuts_ref, lower, own, upper, pool_ref, out_ref):
    tiles, slots = own[0].shape
    half = tiles // 2
    capacity = out_ref.shape[1]
    device = device_index()
    last = cuts_ref.shape[1] - 1
    first_tile = cuts_ref[step, device]
    next_tile = jnp.where(device == last, total_tiles, cuts_ref[step, jnp.minimum(device + 1, last)])
    owned = next_tile - first_tile
    start = first_tile - (device * tiles - half)
    filled = lax.broadcasted_iota(jnp.int32, (capacity, slots), 0) < owned
    for row in range(6):
        pool_ref[row, :half, :] = lower[row]
        pool_ref[row, half : half + tiles, :] = own[row]
        pool_ref[row, half + tiles : 2 * tiles, :] = upper[row]
    for row in range(6):
        out_ref[row] = jnp.where(filled, pool_ref[row, pl.ds(start, capacity), :], 0.0)


def second_kernel(
    total_tiles,
    cuts_ref,
    lists_ref,
    before_2,
    before_1,
    own_ref,
    after_1,
    after_2,
    weight_ref,
    state_ref,
    down_ref,
    up_ref,
    out_ref,
    *scratch
):
    planes, scalars, copy_sem, pool_ref, feature_ref, moment_ref, source_ref, target_ref, *loop_refs = scratch
    tiles, slots = own_ref.shape[1:]
    half = tiles // 2
    rows = planes.shape[1]
    window = (2 * reach + 1) * tiles
    copy = pltpu.make_async_copy(lists_ref, scalars, copy_sem)
    copy.start()
    planes[:, window:, :] = jnp.zeros((3, rows - window, slots), jnp.float32)
    for block, ref in enumerate((before_2, before_1, own_ref, after_1, after_2)):
        planes[:, block * tiles : (block + 1) * tiles, :] = ref[:3]
    weight = weight_ref[...]
    refs = (feature_ref, moment_ref, source_ref, target_ref)
    centred = build_features([planes[axis] for axis in range(3)], weight, tiles, refs)
    copy.wait()
    accumulate(tiles, scalars, source_ref, target_ref, moment_ref, *loop_refs)
    center = reach * tiles
    advance(
        centred,
        [own_ref[axis] for axis in range(3)],
        [own_ref[3 + axis] for axis in range(3)],
        weight[center : center + tiles],
        loop_refs[-1],
        state_ref,
    )
    down_ref[...] = state_ref[:, :half, :]
    up_ref[...] = state_ref[:, tiles - half :, :]
    place_rows(
        0,
        total_tiles,
        cuts_ref,
        [before_1[row, tiles - half :, :] for row in range(6)],
        [own_ref[row] for row in range(6)],
        [after_1[row, :half, :] for row in range(6)],
        pool_ref,
        out_ref,
    )


def third_kernel(total_tiles, cuts_ref, lower_ref, own_ref, upper_ref, out_ref, pool_ref):
    place_rows(
        1,
        total_tiles,
        cuts_ref,
        [lower_ref[row] for row in range(6)],
        [own_ref[row] for row in range(6)],
        [upper_ref[row] for row in range(6)],
        pool_ref,
        out_ref,
    )


def near(value):
    return pltpu.with_memory_space_constraint(value, pltpu.VMEM)


def body(particles, occupancy, neighbours, curve_cuts):
    tiles, _, slots = particles.shape
    listed = neighbours.shape[1]
    total_tiles = tiles * lax.axis_size(AXES)
    half = tiles // 2
    capacity = 2 * tiles
    rows = round_up((2 * reach + 1) * tiles + 1, 8)
    list_rows = round_up(tiles + 2, 8)
    vmem = pl.BlockSpec(memory_space=pltpu.VMEM)
    smem = pl.BlockSpec(memory_space=pltpu.SMEM)

    def held(*sizes, dtype=jnp.float32):
        return pltpu.VMEM(sizes, dtype)

    packed, speed = pl.pallas_call(
        functools.partial(pack_kernel, total_tiles),
        out_shape=(held(4, tiles, slots), held(3, tiles, slots)),
        in_specs=[vmem, smem, vmem],
        out_specs=(vmem, vmem),
        name="pack",
    )(particles, occupancy, neighbours)
    list_scratch = [pltpu.SMEM((list_rows, lanes), jnp.int32), pltpu.SemaphoreType.DMA]
    feature_scratch = [
        pltpu.VMEM((rows, feature_rows, lanes), jnp.float32),
        pltpu.VMEM((rows, 8, lanes), jnp.float32),
        pltpu.VMEM((rows, feature_rows, lanes), jnp.bfloat16),
        pltpu.VMEM((tiles + 1, lanes, feature_rows), jnp.bfloat16),
        pltpu.VMEM((chunk // 2, lanes, 2 * lanes), jnp.float32),
        pltpu.VMEM((tiles + 1, 4, lanes, lanes), jnp.float32),
        pltpu.VMEM((4, round_up(tiles, 8), lanes), jnp.float32),
    ]
    pool_scratch = pltpu.VMEM((6, round_up(capacity + tiles, 8), slots), jnp.float32)
    blocks = [near(value) for value in (shifted(packed, 2), shifted(packed, 1), packed, shifted(packed, -1), shifted(packed, -2))]
    state, weight, lists = pl.pallas_call(
        functools.partial(first_kernel, listed),
        out_shape=(held(6, tiles, slots), held(rows, slots), held(list_rows, lanes, dtype=jnp.int32)),
        in_specs=[vmem] * 6,
        out_specs=(vmem, vmem, vmem),
        scratch_shapes=[pltpu.VMEM((4, rows, slots), jnp.float32)] + list_scratch + feature_scratch,
        name="first_step",
    )(*blocks, near(speed))
    blocks = [near(value) for value in (shifted(state, 2), shifted(state, 1), state, shifted(state, -1), shifted(state, -2))]
    state_2, down, up, after_first = pl.pallas_call(
        functools.partial(second_kernel, total_tiles),
        out_shape=(
            held(6, tiles, slots),
            held(6, half, slots),
            held(6, half, slots),
            jax.ShapeDtypeStruct((6, capacity, slots), jnp.float32),
        ),
        in_specs=[smem] + [vmem] * 7,
        out_specs=(vmem, vmem, vmem, vmem),
        scratch_shapes=[pltpu.VMEM((3, rows, slots), jnp.float32)] + list_scratch + [pool_scratch] + feature_scratch,
        name="second_step",
    )(curve_cuts, near(lists), *blocks, near(weight))
    lower = shifted_open(up, 1)
    upper = shifted_open(down, -1)
    after_second = pl.pallas_call(
        functools.partial(third_kernel, total_tiles),
        out_shape=jax.ShapeDtypeStruct((6, capacity, slots), jnp.float32),
        in_specs=[smem, vmem, vmem, vmem],
        out_specs=vmem,
        scratch_shapes=[pool_scratch],
        name="place",
    )(curve_cuts, near(lower), near(state_2), near(upper))
    return (jnp.transpose(after_first, (1, 0, 2)), jnp.transpose(after_second, (1, 0, 2)))


def solution(mesh):
    in_specs = (P(AXES, None, None), P(AXES), P(AXES, None), P())
    out_specs = (P(AXES, None, None), P(AXES, None, None))
    return jax.shard_map(body, mesh=mesh, in_specs=in_specs, out_specs=out_specs, check_vma=False)
```

```python
import functools

import jax
import jax.numpy as jnp
from jax import lax
from jax.experimental import pallas as pl
from jax.experimental.pallas import tpu as pltpu
from jax.sharding import PartitionSpec as P

AXES = ("gx", "gy")
STEPS = 2

soften = 0.05
time_step = 0.5
reach = 2
chunk = 8
feature_rows = 32
far_norm = 1e36
lanes = 128


def shifted(value, steps):
    count = lax.axis_size(AXES)
    pairs = [(source, (source + steps) % count) for source in range(count)]
    return lax.ppermute(value, AXES, pairs)


def shifted_open(value, steps):
    count = lax.axis_size(AXES)
    first, last = (max(0, -steps), min(count, count - steps))
    return lax.ppermute(value, AXES, [(source, source + steps) for source in range(first, last)])


def round_up(value, step):
    return -(-value // step) * step


def device_index():
    return lax.axis_index("gx") * lax.axis_size("gy") + lax.axis_index("gy")


def pieces(value, count):
    parts = []
    rest = value
    for _ in range(count - 1):
        part = rest.astype(jnp.bfloat16).astype(jnp.float32)
        parts.append(part)
        rest = rest - part
    parts.append(rest.astype(jnp.bfloat16).astype(jnp.float32))
    return parts


def pack_kernel(total_tiles, particles_ref, occupancy_ref, neighbours_ref, packed_ref, speed_ref):
    tiles, slots = (particles_ref.shape[0], particles_ref.shape[2])
    listed = neighbours_ref.shape[1]
    for row in range(3):
        packed_ref[row * tiles : (row + 1) * tiles, :] = particles_ref[:, row, :]
        speed_ref[row * tiles : (row + 1) * tiles, :] = particles_ref[:, 3 + row, :]
    tile_ids = lax.broadcasted_iota(jnp.int32, (tiles, listed), 0)
    offsets = neighbours_ref[...] - (device_index() * tiles + tile_ids)
    offsets = jnp.where(offsets < 0, offsets + total_tiles, offsets)
    packed_ref[3 * tiles :, :] = jnp.zeros((tiles, slots), jnp.float32)
    packed_ref[3 * tiles :, :listed] = offsets.astype(jnp.float32)
    for tile in range(tiles):
        live = occupancy_ref[tile].astype(jnp.float32)
        packed_ref[3 * tiles + tile : 3 * tiles + tile + 1, listed : listed + 1] = jnp.full((1, 1), live)


def build_lists(aux, window, tiles, listed, rows):
    center = reach * tiles
    place = lax.broadcasted_iota(jnp.int32, (rows, lanes), 0).astype(jnp.float32)
    lane = lax.broadcasted_iota(jnp.int32, (rows, lanes), 1).astype(jnp.float32)
    mask = place == lane + center
    for entry in range(listed):
        mask = mask | (place + aux[:, entry : entry + 1] == lane + center)
    own_rows = round_up(tiles, 8)
    own = aux[center : center + own_rows]
    own_place = lax.broadcasted_iota(jnp.int32, (own_rows, lanes), 0).astype(jnp.float32) + center
    own_lane = lax.broadcasted_iota(jnp.int32, (own_rows, lanes), 1).astype(jnp.float32)
    listing = own_place + own[:, 0:1] == own_lane
    for entry in range(1, listed):
        listing = listing | (own_place + own[:, entry : entry + 1] == own_lane)
    listing = jnp.where(listing, 1.0, 0.0)
    listing = jnp.concatenate([listing, jnp.zeros((lanes - own_rows, lanes), jnp.float32)], axis=0)
    listing = jnp.transpose(listing)[:rows]
    mask = jnp.where(lane < tiles, jnp.maximum(jnp.where(mask, 1.0, 0.0), listing), 0.0)
    earlier = lax.broadcasted_iota(jnp.int32, (rows, rows), 1) < lax.broadcasted_iota(jnp.int32, (rows, rows), 0)
    rank = jnp.dot(
        jnp.where(earlier, 1.0, 0.0).astype(jnp.bfloat16),
        mask.astype(jnp.bfloat16),
        preferred_element_type=jnp.float32,
    )
    key = jnp.where(mask > 0.5, rank, -1.0)
    counts = jnp.sum(mask, axis=0, keepdims=True)
    lists = []
    for tile in range(tiles):
        hit = key[:, tile : tile + 1] == lane
        lists.append(jnp.sum(jnp.where(hit, place - window, 0.0), axis=0, keepdims=True) + window)
    lists.append(jnp.full((1, lanes), float(window)))
    lists.append(counts)
    return [row.astype(jnp.int32) for row in lists]


def build_features(place_of, weight, tiles, refs):
    feature_ref, moment_ref, source_ref, target_ref = refs
    rows = feature_ref.shape[0]
    center = reach * tiles
    middle = [jnp.mean(axis[center : center + 8], keepdims=True) for axis in place_of]
    centred = [axis - mid for axis, mid in zip(place_of, middle)]
    ones = jnp.ones_like(weight)
    zeros = jnp.zeros_like(weight)
    source_rows = []
    target_rows = []
    norm = zeros
    for axis, value in enumerate(centred):
        norm = norm + value * value
        live = weight * value
        moment_ref[:, axis, :] = live
        near, mid, far = pieces(live, 3)
        source_rows += [near, near, mid, mid, near, far]
        near, mid, far = [-2.0 * part for part in pieces(value, 3)]
        target_rows += [near, mid, near, mid, far, near]
    source_rows += pieces(jnp.where(weight > 0.5, norm, far_norm), 3) + [ones] * 3
    target_rows += [ones] * 3 + pieces(norm + soften, 3)
    source_rows += [zeros] * (feature_rows - len(source_rows))
    target_rows += [zeros] * (feature_rows - len(target_rows))
    for row, value in enumerate(source_rows):
        feature_ref[:, row, :] = value
    for tile in range(rows):
        source_ref[tile] = feature_ref[tile].astype(jnp.bfloat16)
    own_rows = round_up(tiles, 8)
    for row, value in enumerate(target_rows):
        feature_ref[:own_rows, row, :] = value[center : center + own_rows]
    blank = jnp.zeros((lanes - feature_rows, lanes), jnp.float32)
    for tile in range(tiles + 1):
        block = jnp.concatenate([feature_ref[tile], blank], axis=0)
        target_ref[tile] = jnp.transpose(block)[:, :feature_rows].astype(jnp.bfloat16)
    return centred


def accumulate(tiles, lists_ref, source_ref, target_ref, moment_ref, distance_ref, total_ref, sums_ref):
    total_ref[...] = jnp.zeros(total_ref.shape, jnp.float32)
    chunk_counts = [(lists_ref[tiles + 1, tile] + chunk - 1) // chunk for tile in range(tiles)]
    chunk_total = functools.reduce(lambda left, right: left + right, chunk_counts)

    def step(_, carry):
        tile, part, tile_1, part_1 = carry
        places = []
        for entry in range(chunk):
            source = lists_ref[tile_1, part_1 * chunk + entry]
            places.append([jnp.broadcast_to(moment_ref[source, axis : axis + 1, :], (8, lanes)) for axis in range(3)])
        for first in range(0, lanes, 8):
            strip = slice(first, first + 8)
            sums = [total_ref[tile_1, row, strip, :] for row in range(4)]
            for entry in range(chunk):
                column = (entry % 2) * lanes
                inverse = lax.rsqrt(distance_ref[entry // 2, strip, column : column + lanes])
                kernel = inverse * inverse * inverse
                for axis in range(3):
                    sums[axis] = sums[axis] + kernel * places[entry][axis]
                sums[3] = sums[3] + kernel
            for row in range(4):
                total_ref[tile_1, row, strip, :] = sums[row]
        for pair in range(chunk // 2):
            sources = [lists_ref[tile, part * chunk + 2 * pair + entry] for entry in range(2)]
            distance_ref[pair] = jnp.dot(
                target_ref[tile],
                jnp.concatenate([source_ref[source] for source in sources], axis=1),
                preferred_element_type=jnp.float32,
            )
        more = (part + 1) * chunk < lists_ref[tiles + 1, tile]
        next_tile = jnp.where(more, tile, jnp.minimum(tile + 1, tiles))
        next_part = jnp.where(more, part + 1, 0)
        return (next_tile, next_part, tile, part)

    zero = jnp.int32(0)
    spare = jnp.int32(tiles)
    lax.fori_loop(0, chunk_total + 1, step, (zero, zero, spare, zero))
    for tile in range(tiles):
        for row in range(4):
            sums_ref[row, tile : tile + 1, :] = jnp.sum(jnp.transpose(total_ref[tile, row]), axis=0, keepdims=True)


def advance(centred, place_own, speed_own, weight_own, sums_ref):
    tiles = weight_own.shape[0]
    center = reach * tiles
    zeroth = sums_ref[3, :tiles, :]
    places, speeds = ([], [])
    for axis in range(3):
        force = sums_ref[axis, :tiles, :] - centred[axis][center : center + tiles] * zeroth
        speeds.append(weight_own * (speed_own[axis] + time_step * force / lanes))
        places.append(weight_own * (place_own[axis] + time_step * speeds[axis]))
    return places, speeds


def part_of(ref, tiles, row):
    return ref[row * tiles : (row + 1) * tiles, :]


def fill_planes(planes, tiles, blocks):
    kinds, rows, slots = planes.shape
    window = (2 * reach + 1) * tiles
    planes[:, window:, :] = jnp.zeros((kinds, rows - window, slots), jnp.float32)
    for block, ref in enumerate(blocks):
        for kind in range(kinds):
            planes[kind, block * tiles : (block + 1) * tiles, :] = part_of(ref, tiles, kind)


def first_kernel(
    listed,
    before_2,
    before_1,
    own_ref,
    after_1,
    after_2,
    speed_ref,
    place_out,
    speed_out,
    down_out,
    up_out,
    weight_ref,
    lists_ref,
    *scratch
):
    planes, scalars, copy_sem, feature_ref, moment_ref, source_ref, target_ref, *loop_refs = scratch
    rows, slots = planes.shape[1:]
    tiles = own_ref.shape[0] // 4
    half = tiles // 2
    window = (2 * reach + 1) * tiles
    fill_planes(planes, tiles, (before_2, before_1, own_ref, after_1, after_2))
    aux = planes[3]
    for row, value in enumerate(build_lists(aux, window, tiles, listed, rows)):
        lists_ref[row : row + 1, :] = value
    copy = pltpu.make_async_copy(lists_ref, scalars, copy_sem)
    copy.start()
    slot = lax.broadcasted_iota(jnp.int32, (rows, slots), 1).astype(jnp.float32)
    weight = jnp.where(slot < aux[:, listed : listed + 1], 1.0, 0.0)
    weight_ref[...] = weight
    refs = (feature_ref, moment_ref, source_ref, target_ref)
    centred = build_features([planes[axis] for axis in range(3)], weight, tiles, refs)
    copy.wait()
    accumulate(tiles, scalars, source_ref, target_ref, moment_ref, *loop_refs)
    center = reach * tiles
    places, speeds = advance(
        centred,
        [part_of(own_ref, tiles, axis) for axis in range(3)],
        [part_of(speed_ref, tiles, axis) for axis in range(3)],
        weight[center : center + tiles],
        loop_refs[-1],
    )
    for axis in range(3):
        strip = slice(axis * tiles, (axis + 1) * tiles)
        place_out[strip, :] = places[axis]
        speed_out[strip, :] = speeds[axis]
        down_out[strip, :] = places[axis]
        up_out[strip, :] = places[axis]
        strip = slice(3 * tiles + axis * half, 3 * tiles + (axis + 1) * half)
        down_out[strip, :] = speeds[axis][:half]
        up_out[strip, :] = speeds[axis][tiles - half :]


def place_rows(step, total_tiles, cuts_ref, lower, own, upper, pool_ref, out_ref):
    tiles, slots = own[0].shape
    half = tiles // 2
    capacity = out_ref.shape[1]
    device = device_index()
    last = cuts_ref.shape[1] - 1
    first_tile = cuts_ref[step, device]
    next_tile = jnp.where(device == last, total_tiles, cuts_ref[step, jnp.minimum(device + 1, last)])
    owned = next_tile - first_tile
    start = first_tile - (device * tiles - half)
    filled = lax.broadcasted_iota(jnp.int32, (capacity, slots), 0) < owned
    for row in range(6):
        pool_ref[row, :half, :] = lower[row]
        pool_ref[row, half : half + tiles, :] = own[row]
        pool_ref[row, half + tiles : 2 * tiles, :] = upper[row]
    for row in range(6):
        out_ref[row] = jnp.where(filled, pool_ref[row, pl.ds(start, capacity), :], 0.0)


def second_kernel(
    total_tiles,
    cuts_ref,
    lists_ref,
    before_2,
    before_1,
    own_ref,
    after_1,
    after_2,
    speed_ref,
    weight_ref,
    state_ref,
    down_ref,
    up_ref,
    out_ref,
    *scratch
):
    planes, scalars, copy_sem, pool_ref, feature_ref, moment_ref, source_ref, target_ref, *loop_refs = scratch
    tiles = own_ref.shape[0] // 3
    half = tiles // 2
    copy = pltpu.make_async_copy(lists_ref, scalars, copy_sem)
    copy.start()
    fill_planes(planes, tiles, (before_2, before_1, own_ref, after_1, after_2))
    weight = weight_ref[...]
    refs = (feature_ref, moment_ref, source_ref, target_ref)
    centred = build_features([planes[axis] for axis in range(3)], weight, tiles, refs)
    copy.wait()
    accumulate(tiles, scalars, source_ref, target_ref, moment_ref, *loop_refs)
    center = reach * tiles
    place_own = [part_of(own_ref, tiles, axis) for axis in range(3)]
    speed_own = [part_of(speed_ref, tiles, axis) for axis in range(3)]
    places, speeds = advance(centred, place_own, speed_own, weight[center : center + tiles], loop_refs[-1])
    for row, value in enumerate(places + speeds):
        state_ref[row] = value
        down_ref[row * half : (row + 1) * half, :] = value[:half]
        up_ref[row * half : (row + 1) * half, :] = value[tiles - half :]
    speed_rows = [slice(3 * tiles + axis * half, 3 * tiles + (axis + 1) * half) for axis in range(3)]
    place_rows(
        0,
        total_tiles,
        cuts_ref,
        [part_of(before_1, tiles, axis)[tiles - half :] for axis in range(3)] + [before_1[strip, :] for strip in speed_rows],
        place_own + speed_own,
        [part_of(after_1, tiles, axis)[:half] for axis in range(3)] + [after_1[strip, :] for strip in speed_rows],
        pool_ref,
        out_ref,
    )


def third_kernel(total_tiles, cuts_ref, lower_ref, own_ref, upper_ref, out_ref, pool_ref):
    half = own_ref.shape[1] // 2
    place_rows(
        1,
        total_tiles,
        cuts_ref,
        [part_of(lower_ref, half, row) for row in range(6)],
        [own_ref[row] for row in range(6)],
        [part_of(upper_ref, half, row) for row in range(6)],
        pool_ref,
        out_ref,
    )


def near(value):
    return pltpu.with_memory_space_constraint(value, pltpu.VMEM)


def body(particles, occupancy, neighbours, curve_cuts):
    tiles, _, slots = particles.shape
    listed = neighbours.shape[1]
    total_tiles = tiles * lax.axis_size(AXES)
    half = tiles // 2
    capacity = 2 * tiles
    rows = round_up((2 * reach + 1) * tiles + 1, 8)
    list_rows = round_up(tiles + 2, 8)
    vmem = pl.BlockSpec(memory_space=pltpu.VMEM)
    smem = pl.BlockSpec(memory_space=pltpu.SMEM)

    def held(*sizes, dtype=jnp.float32):
        return pltpu.VMEM(sizes, dtype)

    packed, speed = pl.pallas_call(
        functools.partial(pack_kernel, total_tiles),
        out_shape=(held(4 * tiles, slots), held(3 * tiles, slots)),
        in_specs=[vmem, smem, vmem],
        out_specs=(vmem, vmem),
        name="pack",
    )(particles, occupancy, neighbours)
    list_scratch = [pltpu.SMEM((list_rows, lanes), jnp.int32), pltpu.SemaphoreType.DMA]
    feature_scratch = [
        pltpu.VMEM((rows, feature_rows, lanes), jnp.float32),
        pltpu.VMEM((rows, 8, lanes), jnp.float32),
        pltpu.VMEM((rows, feature_rows, lanes), jnp.bfloat16),
        pltpu.VMEM((tiles + 1, lanes, feature_rows), jnp.bfloat16),
        pltpu.VMEM((chunk // 2, lanes, 2 * lanes), jnp.float32),
        pltpu.VMEM((tiles + 1, 4, lanes, lanes), jnp.float32),
        pltpu.VMEM((4, round_up(tiles, 8), lanes), jnp.float32),
    ]
    pool_scratch = pltpu.VMEM((6, round_up(capacity + tiles, 8), slots), jnp.float32)
    blocks = [shifted(packed, 2), shifted(packed, 1), packed, shifted(packed, -1), shifted(packed, -2)]
    edge = 3 * tiles + 3 * half
    place, speed, down, up, weight, lists = pl.pallas_call(
        functools.partial(first_kernel, listed),
        out_shape=(
            held(3 * tiles, slots),
            held(3 * tiles, slots),
            held(edge, slots),
            held(edge, slots),
            held(rows, slots),
            held(list_rows, lanes, dtype=jnp.int32),
        ),
        in_specs=[vmem] * 6,
        out_specs=[vmem] * 6,
        scratch_shapes=[pltpu.VMEM((4, rows, slots), jnp.float32)] + list_scratch + feature_scratch,
        name="first_step",
    )(*[near(value) for value in blocks], near(speed))
    blocks = [shifted(place, 2), shifted(up, 1), place, shifted(down, -1), shifted(place, -2)]
    state_2, down, up, after_first = pl.pallas_call(
        functools.partial(second_kernel, total_tiles),
        out_shape=(
            held(6, tiles, slots),
            held(6 * half, slots),
            held(6 * half, slots),
            jax.ShapeDtypeStruct((6, capacity, slots), jnp.float32),
        ),
        in_specs=[smem] + [vmem] * 8,
        out_specs=[vmem] * 4,
        scratch_shapes=[pltpu.VMEM((3, rows, slots), jnp.float32)] + list_scratch + [pool_scratch] + feature_scratch,
        name="second_step",
    )(curve_cuts, near(lists), *[near(value) for value in blocks], near(speed), near(weight))
    lower = shifted_open(up, 1)
    upper = shifted_open(down, -1)
    after_second = pl.pallas_call(
        functools.partial(third_kernel, total_tiles),
        out_shape=jax.ShapeDtypeStruct((6, capacity, slots), jnp.float32),
        in_specs=[smem, vmem, vmem, vmem],
        out_specs=vmem,
        scratch_shapes=[pool_scratch],
        name="place",
    )(curve_cuts, near(lower), near(state_2), near(upper))
    return (jnp.transpose(after_first, (1, 0, 2)), jnp.transpose(after_second, (1, 0, 2)))


def solution(mesh):
    in_specs = (P(AXES, None, None), P(AXES), P(AXES, None), P())
    out_specs = (P(AXES, None, None), P(AXES, None, None))
    return jax.shard_map(body, mesh=mesh, in_specs=in_specs, out_specs=out_specs, check_vma=False)
```

```python
import functools

import jax
import jax.numpy as jnp
from jax import lax
from jax.experimental import pallas as pl
from jax.experimental.pallas import tpu as pltpu
from jax.sharding import PartitionSpec as P

AXES = ("gx", "gy")
STEPS = 2

soften = 0.05
time_step = 0.5
reach = 2
chunk = 8
feature_rows = 32
far_norm = 1e36
lanes = 128


def shifted(value, steps):
    count = lax.axis_size(AXES)
    pairs = [(source, (source + steps) % count) for source in range(count)]
    return lax.ppermute(value, AXES, pairs)


def shifted_open(value, steps):
    count = lax.axis_size(AXES)
    first, last = (max(0, -steps), min(count, count - steps))
    return lax.ppermute(value, AXES, [(source, source + steps) for source in range(first, last)])


def round_up(value, step):
    return -(-value // step) * step


def device_index():
    return lax.axis_index("gx") * lax.axis_size("gy") + lax.axis_index("gy")


def pieces(value, count):
    parts = []
    rest = value
    for _ in range(count - 1):
        part = rest.astype(jnp.bfloat16).astype(jnp.float32)
        parts.append(part)
        rest = rest - part
    parts.append(rest.astype(jnp.bfloat16).astype(jnp.float32))
    return parts


def pack_kernel(total_tiles, particles_ref, occupancy_ref, neighbours_ref, packed_ref, speed_ref):
    tiles, slots = (particles_ref.shape[0], particles_ref.shape[2])
    listed = neighbours_ref.shape[1]
    for row in range(3):
        packed_ref[row * tiles : (row + 1) * tiles, :] = particles_ref[:, row, :]
        speed_ref[row * tiles : (row + 1) * tiles, :] = particles_ref[:, 3 + row, :]
    tile_ids = lax.broadcasted_iota(jnp.int32, (tiles, listed), 0)
    offsets = neighbours_ref[...] - (device_index() * tiles + tile_ids)
    offsets = jnp.where(offsets < 0, offsets + total_tiles, offsets)
    packed_ref[3 * tiles :, :] = jnp.zeros((tiles, slots), jnp.float32)
    packed_ref[3 * tiles :, :listed] = offsets.astype(jnp.float32)
    for tile in range(tiles):
        live = occupancy_ref[tile].astype(jnp.float32)
        packed_ref[3 * tiles + tile : 3 * tiles + tile + 1, listed : listed + 1] = jnp.full((1, 1), live)


def build_lists(aux, window, tiles, listed, rows):
    center = reach * tiles
    place = lax.broadcasted_iota(jnp.int32, (rows, lanes), 0).astype(jnp.float32)
    lane = lax.broadcasted_iota(jnp.int32, (rows, lanes), 1).astype(jnp.float32)
    mask = place == lane + center
    for entry in range(listed):
        mask = mask | (place + aux[:, entry : entry + 1] == lane + center)
    own_rows = round_up(tiles, 8)
    own = aux[center : center + own_rows]
    own_place = lax.broadcasted_iota(jnp.int32, (own_rows, lanes), 0).astype(jnp.float32) + center
    own_lane = lax.broadcasted_iota(jnp.int32, (own_rows, lanes), 1).astype(jnp.float32)
    listing = own_place + own[:, 0:1] == own_lane
    for entry in range(1, listed):
        listing = listing | (own_place + own[:, entry : entry + 1] == own_lane)
    listing = jnp.where(listing, 1.0, 0.0)
    listing = jnp.concatenate([listing, jnp.zeros((lanes - own_rows, lanes), jnp.float32)], axis=0)
    listing = jnp.transpose(listing)[:rows]
    mask = jnp.where(lane < tiles, jnp.maximum(jnp.where(mask, 1.0, 0.0), listing), 0.0)
    earlier = lax.broadcasted_iota(jnp.int32, (rows, rows), 1) < lax.broadcasted_iota(jnp.int32, (rows, rows), 0)
    rank = jnp.dot(
        jnp.where(earlier, 1.0, 0.0).astype(jnp.bfloat16),
        mask.astype(jnp.bfloat16),
        preferred_element_type=jnp.float32,
    )
    key = jnp.where(mask > 0.5, rank, -1.0)
    counts = jnp.sum(mask, axis=0, keepdims=True)
    lists = []
    for tile in range(tiles):
        hit = key[:, tile : tile + 1] == lane
        lists.append(jnp.sum(jnp.where(hit, place - window, 0.0), axis=0, keepdims=True) + window)
    lists.append(jnp.full((1, lanes), float(window)))
    lists.append(counts)
    return [row.astype(jnp.int32) for row in lists]


def build_features(place_of, weight, tiles, refs):
    feature_ref, moment_ref, source_ref, target_ref = refs
    rows = feature_ref.shape[0]
    center = reach * tiles
    middle = [jnp.mean(axis[center : center + 8], keepdims=True) for axis in place_of]
    centred = [axis - mid for axis, mid in zip(place_of, middle)]
    ones = jnp.ones_like(weight)
    zeros = jnp.zeros_like(weight)
    source_rows = []
    target_rows = []
    norm = zeros
    for axis, value in enumerate(centred):
        norm = norm + value * value
        live = weight * value
        moment_ref[:, axis, :] = live
        near, mid, far = pieces(live, 3)
        source_rows += [near, near, mid, mid, near, far]
        near, mid, far = [-2.0 * part for part in pieces(value, 3)]
        target_rows += [near, mid, near, mid, far, near]
    source_rows += pieces(jnp.where(weight > 0.5, norm, far_norm), 3) + [ones] * 3
    target_rows += [ones] * 3 + pieces(norm + soften, 3)
    source_rows += [zeros] * (feature_rows - len(source_rows))
    target_rows += [zeros] * (feature_rows - len(target_rows))
    for row, value in enumerate(source_rows):
        feature_ref[:, row, :] = value
    for tile in range(rows):
        source_ref[tile] = feature_ref[tile].astype(jnp.bfloat16)
    own_rows = round_up(tiles, 8)
    for row, value in enumerate(target_rows):
        feature_ref[:own_rows, row, :] = value[center : center + own_rows]
    blank = jnp.zeros((lanes - feature_rows, lanes), jnp.float32)
    for tile in range(tiles + 1):
        block = jnp.concatenate([feature_ref[tile], blank], axis=0)
        target_ref[tile] = jnp.transpose(block)[:, :feature_rows].astype(jnp.bfloat16)
    return centred


def accumulate(tiles, lists_ref, source_ref, target_ref, moment_ref, distance_ref, total_ref, sums_ref):
    total_ref[...] = jnp.zeros(total_ref.shape, jnp.float32)
    chunk_counts = [(lists_ref[tiles + 1, tile] + chunk - 1) // chunk for tile in range(tiles)]
    chunk_total = functools.reduce(lambda left, right: left + right, chunk_counts)

    def step(_, carry):
        tile, part, tile_1, part_1 = carry
        places = []
        for entry in range(chunk):
            source = lists_ref[tile_1, part_1 * chunk + entry]
            places.append([jnp.broadcast_to(moment_ref[source, axis : axis + 1, :], (8, lanes)) for axis in range(3)])
        for first in range(0, lanes, 8):
            strip = slice(first, first + 8)
            sums = [total_ref[tile_1, row, strip, :] for row in range(4)]
            for entry in range(chunk):
                column = (entry % 2) * lanes
                kernel = jnp.exp(-1.5 * jnp.log(distance_ref[entry // 2, strip, column : column + lanes]))
                for axis in range(3):
                    sums[axis] = sums[axis] + kernel * places[entry][axis]
                sums[3] = sums[3] + kernel
            for row in range(4):
                total_ref[tile_1, row, strip, :] = sums[row]
        for pair in range(chunk // 2):
            sources = [lists_ref[tile, part * chunk + 2 * pair + entry] for entry in range(2)]
            distance_ref[pair] = jnp.dot(
                target_ref[tile],
                jnp.concatenate([source_ref[source] for source in sources], axis=1),
                preferred_element_type=jnp.float32,
            )
        more = (part + 1) * chunk < lists_ref[tiles + 1, tile]
        next_tile = jnp.where(more, tile, jnp.minimum(tile + 1, tiles))
        next_part = jnp.where(more, part + 1, 0)
        return (next_tile, next_part, tile, part)

    zero = jnp.int32(0)
    spare = jnp.int32(tiles)
    lax.fori_loop(0, chunk_total + 1, step, (zero, zero, spare, zero))
    for tile in range(tiles):
        for row in range(4):
            sums_ref[row, tile : tile + 1, :] = jnp.sum(jnp.transpose(total_ref[tile, row]), axis=0, keepdims=True)


def advance(centred, place_own, speed_own, weight_own, sums_ref):
    tiles = weight_own.shape[0]
    center = reach * tiles
    zeroth = sums_ref[3, :tiles, :]
    places, speeds = ([], [])
    for axis in range(3):
        force = sums_ref[axis, :tiles, :] - centred[axis][center : center + tiles] * zeroth
        speeds.append(weight_own * (speed_own[axis] + time_step * force / lanes))
        places.append(weight_own * (place_own[axis] + time_step * speeds[axis]))
    return places, speeds


def part_of(ref, tiles, row):
    return ref[row * tiles : (row + 1) * tiles, :]


def fill_planes(planes, tiles, blocks):
    kinds, rows, slots = planes.shape
    window = (2 * reach + 1) * tiles
    planes[:, window:, :] = jnp.zeros((kinds, rows - window, slots), jnp.float32)
    for block, ref in enumerate(blocks):
        for kind in range(kinds):
            planes[kind, block * tiles : (block + 1) * tiles, :] = part_of(ref, tiles, kind)


def first_kernel(
    listed,
    before_2,
    before_1,
    own_ref,
    after_1,
    after_2,
    speed_ref,
    place_out,
    speed_out,
    down_out,
    up_out,
    weight_ref,
    lists_ref,
    *scratch
):
    planes, scalars, copy_sem, feature_ref, moment_ref, source_ref, target_ref, *loop_refs = scratch
    rows, slots = planes.shape[1:]
    tiles = own_ref.shape[0] // 4
    half = tiles // 2
    window = (2 * reach + 1) * tiles
    fill_planes(planes, tiles, (before_2, before_1, own_ref, after_1, after_2))
    aux = planes[3]
    for row, value in enumerate(build_lists(aux, window, tiles, listed, rows)):
        lists_ref[row : row + 1, :] = value
    copy = pltpu.make_async_copy(lists_ref, scalars, copy_sem)
    copy.start()
    slot = lax.broadcasted_iota(jnp.int32, (rows, slots), 1).astype(jnp.float32)
    weight = jnp.where(slot < aux[:, listed : listed + 1], 1.0, 0.0)
    weight_ref[...] = weight
    refs = (feature_ref, moment_ref, source_ref, target_ref)
    centred = build_features([planes[axis] for axis in range(3)], weight, tiles, refs)
    copy.wait()
    accumulate(tiles, scalars, source_ref, target_ref, moment_ref, *loop_refs)
    center = reach * tiles
    places, speeds = advance(
        centred,
        [part_of(own_ref, tiles, axis) for axis in range(3)],
        [part_of(speed_ref, tiles, axis) for axis in range(3)],
        weight[center : center + tiles],
        loop_refs[-1],
    )
    for axis in range(3):
        strip = slice(axis * tiles, (axis + 1) * tiles)
        place_out[strip, :] = places[axis]
        speed_out[strip, :] = speeds[axis]
        down_out[strip, :] = places[axis]
        up_out[strip, :] = places[axis]
        strip = slice(3 * tiles + axis * half, 3 * tiles + (axis + 1) * half)
        down_out[strip, :] = speeds[axis][:half]
        up_out[strip, :] = speeds[axis][tiles - half :]


def place_rows(step, total_tiles, cuts_ref, lower, own, upper, pool_ref, out_ref):
    tiles, slots = own[0].shape
    half = tiles // 2
    capacity = out_ref.shape[1]
    device = device_index()
    last = cuts_ref.shape[1] - 1
    first_tile = cuts_ref[step, device]
    next_tile = jnp.where(device == last, total_tiles, cuts_ref[step, jnp.minimum(device + 1, last)])
    owned = next_tile - first_tile
    start = first_tile - (device * tiles - half)
    filled = lax.broadcasted_iota(jnp.int32, (capacity, slots), 0) < owned
    for row in range(6):
        pool_ref[row, :half, :] = lower[row]
        pool_ref[row, half : half + tiles, :] = own[row]
        pool_ref[row, half + tiles : 2 * tiles, :] = upper[row]
    for row in range(6):
        out_ref[row] = jnp.where(filled, pool_ref[row, pl.ds(start, capacity), :], 0.0)


def second_kernel(
    total_tiles,
    cuts_ref,
    lists_ref,
    before_2,
    before_1,
    own_ref,
    after_1,
    after_2,
    speed_ref,
    weight_ref,
    state_ref,
    down_ref,
    up_ref,
    out_ref,
    *scratch
):
    planes, scalars, copy_sem, pool_ref, feature_ref, moment_ref, source_ref, target_ref, *loop_refs = scratch
    tiles = own_ref.shape[0] // 3
    half = tiles // 2
    copy = pltpu.make_async_copy(lists_ref, scalars, copy_sem)
    copy.start()
    fill_planes(planes, tiles, (before_2, before_1, own_ref, after_1, after_2))
    weight = weight_ref[...]
    refs = (feature_ref, moment_ref, source_ref, target_ref)
    centred = build_features([planes[axis] for axis in range(3)], weight, tiles, refs)
    copy.wait()
    accumulate(tiles, scalars, source_ref, target_ref, moment_ref, *loop_refs)
    center = reach * tiles
    place_own = [part_of(own_ref, tiles, axis) for axis in range(3)]
    speed_own = [part_of(speed_ref, tiles, axis) for axis in range(3)]
    places, speeds = advance(centred, place_own, speed_own, weight[center : center + tiles], loop_refs[-1])
    for row, value in enumerate(places + speeds):
        state_ref[row] = value
        down_ref[row * half : (row + 1) * half, :] = value[:half]
        up_ref[row * half : (row + 1) * half, :] = value[tiles - half :]
    speed_rows = [slice(3 * tiles + axis * half, 3 * tiles + (axis + 1) * half) for axis in range(3)]
    place_rows(
        0,
        total_tiles,
        cuts_ref,
        [part_of(before_1, tiles, axis)[tiles - half :] for axis in range(3)] + [before_1[strip, :] for strip in speed_rows],
        place_own + speed_own,
        [part_of(after_1, tiles, axis)[:half] for axis in range(3)] + [after_1[strip, :] for strip in speed_rows],
        pool_ref,
        out_ref,
    )


def third_kernel(total_tiles, cuts_ref, lower_ref, own_ref, upper_ref, out_ref, pool_ref):
    half = own_ref.shape[1] // 2
    place_rows(
        1,
        total_tiles,
        cuts_ref,
        [part_of(lower_ref, half, row) for row in range(6)],
        [own_ref[row] for row in range(6)],
        [part_of(upper_ref, half, row) for row in range(6)],
        pool_ref,
        out_ref,
    )


def near(value):
    return pltpu.with_memory_space_constraint(value, pltpu.VMEM)


def body(particles, occupancy, neighbours, curve_cuts):
    tiles, _, slots = particles.shape
    listed = neighbours.shape[1]
    total_tiles = tiles * lax.axis_size(AXES)
    half = tiles // 2
    capacity = 2 * tiles
    rows = round_up((2 * reach + 1) * tiles + 1, 8)
    list_rows = round_up(tiles + 2, 8)
    vmem = pl.BlockSpec(memory_space=pltpu.VMEM)
    smem = pl.BlockSpec(memory_space=pltpu.SMEM)

    def held(*sizes, dtype=jnp.float32):
        return pltpu.VMEM(sizes, dtype)

    packed, speed = pl.pallas_call(
        functools.partial(pack_kernel, total_tiles),
        out_shape=(held(4 * tiles, slots), held(3 * tiles, slots)),
        in_specs=[vmem, smem, vmem],
        out_specs=(vmem, vmem),
        name="pack",
    )(particles, occupancy, neighbours)
    list_scratch = [pltpu.SMEM((list_rows, lanes), jnp.int32), pltpu.SemaphoreType.DMA]
    feature_scratch = [
        pltpu.VMEM((rows, feature_rows, lanes), jnp.float32),
        pltpu.VMEM((rows, 8, lanes), jnp.float32),
        pltpu.VMEM((rows, feature_rows, lanes), jnp.bfloat16),
        pltpu.VMEM((tiles + 1, lanes, feature_rows), jnp.bfloat16),
        pltpu.VMEM((chunk // 2, lanes, 2 * lanes), jnp.float32),
        pltpu.VMEM((tiles + 1, 4, lanes, lanes), jnp.float32),
        pltpu.VMEM((4, round_up(tiles, 8), lanes), jnp.float32),
    ]
    pool_scratch = pltpu.VMEM((6, round_up(capacity + tiles, 8), slots), jnp.float32)
    blocks = [shifted(packed, 2), shifted(packed, 1), packed, shifted(packed, -1), shifted(packed, -2)]
    edge = 3 * tiles + 3 * half
    place, speed, down, up, weight, lists = pl.pallas_call(
        functools.partial(first_kernel, listed),
        out_shape=(
            held(3 * tiles, slots),
            held(3 * tiles, slots),
            held(edge, slots),
            held(edge, slots),
            held(rows, slots),
            held(list_rows, lanes, dtype=jnp.int32),
        ),
        in_specs=[vmem] * 6,
        out_specs=[vmem] * 6,
        scratch_shapes=[pltpu.VMEM((4, rows, slots), jnp.float32)] + list_scratch + feature_scratch,
        name="first_step",
    )(*[near(value) for value in blocks], near(speed))
    blocks = [shifted(place, 2), shifted(up, 1), place, shifted(down, -1), shifted(place, -2)]
    state_2, down, up, after_first = pl.pallas_call(
        functools.partial(second_kernel, total_tiles),
        out_shape=(
            held(6, tiles, slots),
            held(6 * half, slots),
            held(6 * half, slots),
            jax.ShapeDtypeStruct((6, capacity, slots), jnp.float32),
        ),
        in_specs=[smem] + [vmem] * 8,
        out_specs=[vmem] * 4,
        scratch_shapes=[pltpu.VMEM((3, rows, slots), jnp.float32)] + list_scratch + [pool_scratch] + feature_scratch,
        name="second_step",
    )(curve_cuts, near(lists), *[near(value) for value in blocks], near(speed), near(weight))
    lower = shifted_open(up, 1)
    upper = shifted_open(down, -1)
    after_second = pl.pallas_call(
        functools.partial(third_kernel, total_tiles),
        out_shape=jax.ShapeDtypeStruct((6, capacity, slots), jnp.float32),
        in_specs=[smem, vmem, vmem, vmem],
        out_specs=vmem,
        scratch_shapes=[pool_scratch],
        name="place",
    )(curve_cuts, near(lower), near(state_2), near(upper))
    return (jnp.transpose(after_first, (1, 0, 2)), jnp.transpose(after_second, (1, 0, 2)))


def solution(mesh):
    in_specs = (P(AXES, None, None), P(AXES), P(AXES, None), P())
    out_specs = (P(AXES, None, None), P(AXES, None, None))
    return jax.shard_map(body, mesh=mesh, in_specs=in_specs, out_specs=out_specs, check_vma=False)
```

```python
import functools

import jax
import jax.numpy as jnp
from jax import lax
from jax.experimental import pallas as pl
from jax.experimental.pallas import tpu as pltpu
from jax.sharding import PartitionSpec as P

AXES = ("gx", "gy")
STEPS = 2

soften = 0.05
time_step = 0.5
reach = 2
chunk = 4
feature_rows = 32
far_norm = 1e36
lanes = 128
vmem_limit = 16 << 20


def shifted(value, steps):
    count = lax.axis_size(AXES)
    pairs = [(source, (source + steps) % count) for source in range(count)]
    return lax.ppermute(value, AXES, pairs)


def swapped(value, first, wrap=True):
    count = lax.axis_size(AXES)
    pairs = []
    for lower in range(first, count, 2):
        if wrap or lower + 1 < count:
            upper = (lower + 1) % count
            pairs += [(lower, upper), (upper, lower)]
    return lax.ppermute(value, AXES, pairs)


def round_up(value, step):
    return -(-value // step) * step


def device_index():
    return lax.axis_index("gx") * lax.axis_size("gy") + lax.axis_index("gy")


def pieces(value, count):
    parts = []
    rest = value
    for _ in range(count - 1):
        part = rest.astype(jnp.bfloat16).astype(jnp.float32)
        parts.append(part)
        rest = rest - part
    parts.append(rest.astype(jnp.bfloat16).astype(jnp.float32))
    return parts


def pack_kernel(total_tiles, particles_ref, occupancy_ref, neighbours_ref, packed_ref, speed_ref):
    tiles, slots = (particles_ref.shape[0], particles_ref.shape[2])
    listed = neighbours_ref.shape[1]
    for row in range(3):
        packed_ref[row * tiles : (row + 1) * tiles, :] = particles_ref[:, row, :]
        speed_ref[row * tiles : (row + 1) * tiles, :] = particles_ref[:, 3 + row, :]
    tile_ids = lax.broadcasted_iota(jnp.int32, (tiles, listed), 0)
    offsets = neighbours_ref[...] - (device_index() * tiles + tile_ids)
    offsets = jnp.where(offsets < 0, offsets + total_tiles, offsets)
    packed_ref[3 * tiles :, :] = jnp.zeros((tiles, slots), jnp.float32)
    packed_ref[3 * tiles :, :listed] = offsets.astype(jnp.float32)
    for tile in range(tiles):
        live = occupancy_ref[tile].astype(jnp.float32)
        packed_ref[3 * tiles + tile : 3 * tiles + tile + 1, listed : listed + 1] = jnp.full((1, 1), live)


def places_of(index, tiles, offsets):
    place = index + offsets[0]
    for block in range(1, len(offsets)):
        place = jnp.where(index >= block * tiles, index - block * tiles + offsets[block], place)
    return jnp.where(index >= len(offsets) * tiles, -1000.0, place)


def build_lists(aux, own, tiles, listed, offsets):
    rows = aux.shape[0]
    dummy = len(offsets) * tiles
    index = lax.broadcasted_iota(jnp.int32, (rows, lanes), 0).astype(jnp.float32)
    lane = lax.broadcasted_iota(jnp.int32, (rows, lanes), 1).astype(jnp.float32)
    place = places_of(index, tiles, offsets)
    mask = place == lane
    for entry in range(listed):
        mask = mask | (place + aux[:, entry : entry + 1] == lane)
    own_rows = own.shape[0]
    own_index = lax.broadcasted_iota(jnp.int32, (own_rows, lanes), 0).astype(jnp.float32)
    own_lane = lax.broadcasted_iota(jnp.int32, (own_rows, lanes), 1).astype(jnp.float32)
    own_place = places_of(own_lane, tiles, offsets)
    listing = own_index + own[:, 0:1] == own_place
    for entry in range(1, listed):
        listing = listing | (own_index + own[:, entry : entry + 1] == own_place)
    listing = jnp.where(listing, 1.0, 0.0)
    listing = jnp.concatenate([listing, jnp.zeros((lanes - own_rows, lanes), jnp.float32)], axis=0)
    listing = jnp.transpose(listing)[:rows]
    mask = jnp.maximum(jnp.where(mask, 1.0, 0.0), listing)
    mask = jnp.where((lane < tiles) & (index < dummy), mask, 0.0)
    earlier = lax.broadcasted_iota(jnp.int32, (rows, rows), 1) < lax.broadcasted_iota(jnp.int32, (rows, rows), 0)
    rank = jnp.dot(
        jnp.where(earlier, 1.0, 0.0).astype(jnp.bfloat16),
        mask.astype(jnp.bfloat16),
        preferred_element_type=jnp.float32,
    )
    key = jnp.where(mask > 0.5, rank, -1.0)
    counts = jnp.sum(mask, axis=0, keepdims=True)
    lists = []
    for tile in range(tiles):
        hit = key[:, tile : tile + 1] == lane
        lists.append(jnp.sum(jnp.where(hit, index - dummy, 0.0), axis=0, keepdims=True) + dummy)
    lists.append(jnp.full((1, lanes), float(dummy)))
    lists.append(counts)
    return [row.astype(jnp.int32) for row in lists]


def middles(own_place):
    return [jnp.mean(axis[:8], keepdims=True) for axis in own_place]


def build_sources(places, middle, weight, feature_ref, moment_ref, source_ref):
    rows = weight.shape[0]
    ones = jnp.ones_like(weight)
    zeros = jnp.zeros_like(weight)
    features = []
    norm = zeros
    for axis in range(3):
        value = weight * (places[axis] - middle[axis])
        norm = norm + value * value
        moment_ref[:rows, axis, :] = value
        high, mid, low = pieces(value, 3)
        features += [high, high, mid, mid, high, low]
    features += pieces(jnp.where(weight > 0.5, norm, far_norm), 3) + [ones] * 3
    features += [zeros] * (feature_rows - len(features))
    for row, value in enumerate(features):
        feature_ref[:rows, row, :] = value
    for tile in range(rows):
        source_ref[tile] = feature_ref[tile].astype(jnp.bfloat16)


def build_targets(own_place, middle, feature_ref, target_ref):
    tiles = own_place[0].shape[0]
    ones = jnp.ones_like(own_place[0])
    zeros = jnp.zeros_like(own_place[0])
    features = []
    norm = zeros
    for axis in range(3):
        value = own_place[axis] - middle[axis]
        norm = norm + value * value
        high, mid, low = [-2.0 * part for part in pieces(value, 3)]
        features += [high, mid, high, mid, low, high]
    features += [ones] * 3 + pieces(norm + soften, 3)
    features += [zeros] * (feature_rows - len(features))
    for row, value in enumerate(features):
        feature_ref[:tiles, row, :] = value
    blank = jnp.zeros((lanes - feature_rows, lanes), jnp.float32)
    for tile in range(tiles):
        block = jnp.concatenate([feature_ref[tile], blank], axis=0)
        target_ref[tile] = jnp.transpose(block)[:, :feature_rows].astype(jnp.bfloat16)
    target_ref[tiles] = target_ref[0]


def accumulate(tiles, lists_ref, source_ref, target_ref, moment_ref, buffers, total_ref):
    chunk_counts = [(lists_ref[tiles + 1, tile] + chunk - 1) // chunk for tile in range(tiles)]
    chunk_total = functools.reduce(lambda left, right: left + right, [jnp.maximum(count, 1) for count in chunk_counts])

    def following(tile, part):
        more = (part + 1) * chunk < lists_ref[tiles + 1, tile]
        return (jnp.where(more, tile, jnp.minimum(tile + 1, tiles)), jnp.where(more, part + 1, 0))

    def distances(tile, part, distance_ref):
        for pair in range(chunk // 2):
            sources = [lists_ref[tile, part * chunk + 2 * pair + entry] for entry in range(2)]
            distance_ref[pair] = jnp.dot(
                target_ref[tile],
                jnp.concatenate([source_ref[source] for source in sources], axis=1),
                preferred_element_type=jnp.float32,
            )

    def kernels(tile, part, distance_ref):
        places = []
        for entry in range(chunk):
            source = lists_ref[tile, part * chunk + entry]
            places.append([jnp.broadcast_to(moment_ref[source, axis : axis + 1, :], (8, lanes)) for axis in range(3)])
        for first in range(0, lanes, 8):
            strip = slice(first, first + 8)
            sums = [total_ref[tile, row, strip, :] for row in range(4)]
            for entry in range(chunk):
                column = (entry % 2) * lanes
                inverse = lax.rsqrt(distance_ref[entry // 2, strip, column : column + lanes])
                kernel = inverse * inverse * inverse
                for axis in range(3):
                    sums[axis] = sums[axis] + kernel * places[entry][axis]
                sums[3] = sums[3] + kernel
            for row in range(4):
                total_ref[tile, row, strip, :] = sums[row]

    def step(_, carry):
        tile, part = carry
        tile_1, part_1 = following(tile, part)
        tile_2, part_2 = following(tile_1, part_1)
        kernels(tile, part, buffers[0])
        distances(tile_1, part_1, buffers[1])
        kernels(tile_1, part_1, buffers[1])
        distances(tile_2, part_2, buffers[0])
        return (tile_2, part_2)

    zero = jnp.int32(0)
    distances(zero, zero, buffers[0])
    lax.fori_loop(0, (chunk_total + 1) // 2, step, (zero, zero))


def advance(middle, place_own, speed_own, weight_own, total_ref, sums_ref):
    tiles = weight_own.shape[0]
    for tile in range(tiles):
        for row in range(4):
            sums_ref[row, tile : tile + 1, :] = jnp.sum(jnp.transpose(total_ref[tile, row]), axis=0, keepdims=True)
    zeroth = sums_ref[3, :tiles, :]
    places, speeds = ([], [])
    for axis in range(3):
        force = sums_ref[axis, :tiles, :] - (place_own[axis] - middle[axis]) * zeroth
        speeds.append(weight_own * (speed_own[axis] + time_step * force / lanes))
        places.append(weight_own * (place_own[axis] + time_step * speeds[axis]))
    return places, speeds


def part_of(ref, tiles, row):
    return ref[row * tiles : (row + 1) * tiles, :]


def fill_planes(planes, tiles, blocks):
    kinds, rows, slots = planes.shape
    filled = len(blocks) * tiles
    planes[:, filled:, :] = jnp.zeros((kinds, rows - filled, slots), jnp.float32)
    for block, ref in enumerate(blocks):
        for kind in range(kinds):
            planes[kind, block * tiles : (block + 1) * tiles, :] = part_of(ref, tiles, kind)


def weights_of(aux, listed):
    slot = lax.broadcasted_iota(jnp.int32, aux.shape, 1).astype(jnp.float32)
    return jnp.where(slot < aux[:, listed : listed + 1], 1.0, 0.0)


def offsets_of(tiles, near_pair):
    toward = jnp.where(device_index() % 2 == 0, 1.0, -1.0) * float(tiles)
    if near_pair:
        return [0.0, toward]
    return [-float(reach * tiles), -toward, float(reach * tiles)]


def prepare(first, near_pair, listed, own_ref, blocks, lists_ref, weight_ref, tools):
    planes, scalars, copy_sem, feature_ref, moment_ref, source_ref = tools
    tiles = own_ref.shape[0] // planes.shape[0]
    if not first:
        copy = pltpu.make_async_copy(lists_ref, scalars, copy_sem)
        copy.start()
    fill_planes(planes, tiles, blocks)
    if first:
        aux = planes[3]
        own_aux = jnp.concatenate(
            [part_of(own_ref, tiles, 3), jnp.zeros((round_up(tiles, 8) - tiles, lanes), jnp.float32)], axis=0
        )
        for row, value in enumerate(build_lists(aux, own_aux, tiles, listed, offsets_of(tiles, near_pair))):
            lists_ref[row : row + 1, :] = value
        copy = pltpu.make_async_copy(lists_ref, scalars, copy_sem)
        copy.start()
        weight_ref[...] = weights_of(aux, listed)
    middle = middles([part_of(own_ref, tiles, axis) for axis in range(3)])
    build_sources([planes[axis] for axis in range(3)], middle, weight_ref[...], feature_ref, moment_ref, source_ref)
    return middle, copy


def begin(listed, first, *refs):
    if first:
        own_ref, sibling_ref, total_ref, target_ref, lists_ref, weight_ref, *scratch = refs
    else:
        own_ref, sibling_ref, lists_ref, weight_ref, total_ref, target_ref, *scratch = refs
    *tools, buffer_0, buffer_1 = scratch
    tiles = own_ref.shape[0] // tools[0].shape[0]
    middle, copy = prepare(first, True, listed, own_ref, (own_ref, sibling_ref), lists_ref, weight_ref, tools)
    build_targets([part_of(own_ref, tiles, axis) for axis in range(3)], middle, tools[3], target_ref)
    total_ref[...] = jnp.zeros(total_ref.shape, jnp.float32)
    copy.wait()
    accumulate(tiles, tools[1], tools[5], target_ref, tools[4], (buffer_0, buffer_1), total_ref)


def halves(speed, even, half):
    first, last = (speed[:half], speed[half:])
    return jnp.where(even, last, first), jnp.where(even, first, last)


def first_finish(
    listed, own_ref, below, beside, above, total_in, target_ref, weight_own_ref, speed_ref, *refs
):
    total_ref, lists_ref, weight_ref, place_out, speed_out, sibling_out, beside_out, *scratch = refs
    *tools, buffer_0, buffer_1, sums_ref = scratch
    tiles = own_ref.shape[0] // tools[0].shape[0]
    half = tiles // 2
    middle, copy = prepare(True, False, listed, own_ref, (below, beside, above), lists_ref, weight_ref, tools)
    copy.wait()
    accumulate(tiles, tools[1], tools[5], target_ref, tools[4], (buffer_0, buffer_1), total_ref)
    places, speeds = advance(
        middle,
        [part_of(own_ref, tiles, axis) for axis in range(3)],
        [part_of(speed_ref, tiles, axis) for axis in range(3)],
        weight_own_ref[:tiles, :],
        total_ref,
        sums_ref,
    )
    even = device_index() % 2 == 0
    for axis in range(3):
        strip = slice(axis * tiles, (axis + 1) * tiles)
        place_out[strip, :] = places[axis]
        speed_out[strip, :] = speeds[axis]
        sibling_out[strip, :] = places[axis]
        beside_out[strip, :] = places[axis]
        strip = slice(3 * tiles + axis * half, 3 * tiles + (axis + 1) * half)
        sibling_out[strip, :], beside_out[strip, :] = halves(speeds[axis], even, half)


def second_finish(
    total_tiles,
    cuts_ref,
    own_ref,
    below,
    beside,
    above,
    total_in,
    target_ref,
    weight_own_ref,
    speed_ref,
    sibling_ref,
    lists_ref,
    weight_ref,
    total_ref,
    state_ref,
    sibling_out,
    beside_out,
    out_ref,
    *scratch
):
    *tools, buffer_0, buffer_1, sums_ref, pool_ref = scratch
    tiles = own_ref.shape[0] // 3
    half = tiles // 2
    middle, copy = prepare(False, False, None, own_ref, (below, beside, above), lists_ref, weight_ref, tools)
    copy.wait()
    accumulate(tiles, tools[1], tools[5], target_ref, tools[4], (buffer_0, buffer_1), total_ref)
    place_own = [part_of(own_ref, tiles, axis) for axis in range(3)]
    speed_own = [part_of(speed_ref, tiles, axis) for axis in range(3)]
    places, speeds = advance(middle, place_own, speed_own, weight_own_ref[:tiles, :], total_ref, sums_ref)
    even = device_index() % 2 == 0
    for row, value in enumerate(places + speeds):
        state_ref[row] = value
        strip = slice(row * half, (row + 1) * half)
        sibling_out[strip, :], beside_out[strip, :] = halves(value, even, half)
    lower, upper = ([], [])
    for row in range(6):
        if row < 3:
            sides = [part_of(ref, tiles, row) for ref in (sibling_ref, beside)]
            low_sides, high_sides = ([side[tiles - half :] for side in sides], [side[:half] for side in sides])
        else:
            strip = slice(3 * tiles + (row - 3) * half, 3 * tiles + (row - 2) * half)
            low_sides = high_sides = [ref[strip, :] for ref in (sibling_ref, beside)]
        lower.append(jnp.where(even, low_sides[1], low_sides[0]))
        upper.append(jnp.where(even, high_sides[0], high_sides[1]))
    place_rows(0, total_tiles, cuts_ref, lower, place_own + speed_own, upper, pool_ref, out_ref)


def place_rows(step, total_tiles, cuts_ref, lower, own, upper, pool_ref, out_ref):
    tiles, slots = own[0].shape
    half = tiles // 2
    capacity = out_ref.shape[1]
    device = device_index()
    last = cuts_ref.shape[1] - 1
    first_tile = cuts_ref[step, device]
    next_tile = jnp.where(device == last, total_tiles, cuts_ref[step, jnp.minimum(device + 1, last)])
    owned = next_tile - first_tile
    start = first_tile - (device * tiles - half)
    filled = lax.broadcasted_iota(jnp.int32, (capacity, slots), 0) < owned
    for row in range(6):
        pool_ref[row, :half, :] = lower[row]
        pool_ref[row, half : half + tiles, :] = own[row]
        pool_ref[row, half + tiles : 2 * tiles, :] = upper[row]
    for row in range(6):
        out_ref[row] = jnp.where(filled, pool_ref[row, pl.ds(start, capacity), :], 0.0)


def third_kernel(total_tiles, cuts_ref, sibling_ref, own_ref, beside_ref, out_ref, pool_ref):
    half = own_ref.shape[1] // 2
    even = device_index() % 2 == 0
    lower, upper = ([], [])
    for row in range(6):
        sibling, beside = (part_of(sibling_ref, half, row), part_of(beside_ref, half, row))
        lower.append(jnp.where(even, beside, sibling))
        upper.append(jnp.where(even, sibling, beside))
    place_rows(1, total_tiles, cuts_ref, lower, [own_ref[row] for row in range(6)], upper, pool_ref, out_ref)


def near(value):
    return pltpu.with_memory_space_constraint(value, pltpu.VMEM)


def body(particles, occupancy, neighbours, curve_cuts):
    tiles, _, slots = particles.shape
    listed = neighbours.shape[1]
    total_tiles = tiles * lax.axis_size(AXES)
    half = tiles // 2
    capacity = 2 * tiles
    near_rows = round_up(2 * tiles + 1, 8)
    far_rows = round_up((reach + 1) * tiles + 1, 8)
    list_rows = round_up(tiles + 2, 8)
    vmem = pl.BlockSpec(memory_space=pltpu.VMEM)
    smem = pl.BlockSpec(memory_space=pltpu.SMEM)

    def held(*sizes, dtype=jnp.float32):
        return pltpu.VMEM(sizes, dtype)

    def call(kernel, name, outs, ins, scratch, flops=0, aliases=None):
        held_ins = [value if kind is smem else near(value) for kind, value in ins]
        return pl.pallas_call(
            kernel,
            out_shape=outs,
            in_specs=[kind for kind, _ in ins],
            out_specs=[vmem] * len(outs),
            scratch_shapes=scratch,
            input_output_aliases=aliases or {},
            compiler_params=pltpu.CompilerParams(vmem_limit_bytes=vmem_limit),
            cost_estimate=pl.CostEstimate(flops=flops, bytes_accessed=1 << 20, transcendentals=0),
            name=name,
        )(*held_ins)

    def tools(rows, kinds):
        return [
            pltpu.VMEM((kinds, rows, slots), jnp.float32),
            pltpu.SMEM((list_rows, lanes), jnp.int32),
            pltpu.SemaphoreType.DMA,
            pltpu.VMEM((rows, feature_rows, lanes), jnp.float32),
            pltpu.VMEM((rows, 8, lanes), jnp.float32),
            pltpu.VMEM((rows, feature_rows, lanes), jnp.bfloat16),
            pltpu.VMEM((chunk // 2, lanes, 2 * lanes), jnp.float32),
            pltpu.VMEM((chunk // 2, lanes, 2 * lanes), jnp.float32),
        ]

    packed, speed = pl.pallas_call(
        functools.partial(pack_kernel, total_tiles),
        out_shape=(held(4 * tiles, slots), held(3 * tiles, slots)),
        in_specs=[vmem, smem, vmem],
        out_specs=(vmem, vmem),
        compiler_params=pltpu.CompilerParams(vmem_limit_bytes=vmem_limit),
        name="pack",
    )(particles, occupancy, neighbours)
    pool_scratch = pltpu.VMEM((6, round_up(capacity + tiles, 8), slots), jnp.float32)
    sums_scratch = pltpu.VMEM((4, round_up(tiles, 8), lanes), jnp.float32)
    totals = held(tiles + 1, 4, lanes, lanes)
    targets = held(tiles + 1, lanes, feature_rows, dtype=jnp.bfloat16)
    lists = held(list_rows, lanes, dtype=jnp.int32)
    edge = 3 * tiles + 3 * half
    work = 1 << 32

    sibling = swapped(packed, 0)
    beside, below, above = (swapped(packed, 1), shifted(packed, reach), shifted(packed, -reach))
    total, target, near_lists, near_weight = call(
        functools.partial(begin, listed, True),
        "first_near",
        [totals, targets, lists, held(near_rows, slots)],
        [(vmem, packed), (vmem, sibling)],
        tools(near_rows, 4),
        work,
    )
    total, far_lists, far_weight, place, speed, sibling, beside = call(
        functools.partial(first_finish, listed),
        "first_far",
        [totals, lists, held(far_rows, slots), held(3 * tiles, slots), held(3 * tiles, slots), held(edge, slots), held(edge, slots)],
        [(vmem, value) for value in (packed, below, beside, above, total, target, near_weight, speed)],
        tools(far_rows, 4) + [sums_scratch],
        work,
        {4: 0},
    )
    sibling = swapped(sibling, 0)
    beside, below, above = (swapped(beside, 1), shifted(place, reach), shifted(place, -reach))
    total, target = call(
        functools.partial(begin, listed, False),
        "second_near",
        [totals, targets],
        [(vmem, value) for value in (place, sibling, near_lists, near_weight)],
        tools(near_rows, 3),
        work,
    )
    _, state, sibling, beside, after_first = call(
        functools.partial(second_finish, total_tiles),
        "second_far",
        [
            totals,
            held(6, tiles, slots),
            held(6 * half, slots),
            held(6 * half, slots),
            jax.ShapeDtypeStruct((6, capacity, slots), jnp.float32),
        ],
        [(smem, curve_cuts)]
        + [
            (vmem, value)
            for value in (place, below, beside, above, total, target, near_weight, speed, sibling, far_lists, far_weight)
        ],
        tools(far_rows, 3) + [sums_scratch, pool_scratch],
        work,
        {5: 0},
    )
    (after_second,) = call(
        functools.partial(third_kernel, total_tiles),
        "place",
        [jax.ShapeDtypeStruct((6, capacity, slots), jnp.float32)],
        [(smem, curve_cuts), (vmem, swapped(sibling, 0)), (vmem, state), (vmem, swapped(beside, 1, wrap=False))],
        [pool_scratch],
    )
    return (jnp.transpose(after_first, (1, 0, 2)), jnp.transpose(after_second, (1, 0, 2)))


def solution(mesh):
    in_specs = (P(AXES, None, None), P(AXES), P(AXES, None), P())
    out_specs = (P(AXES, None, None), P(AXES, None, None))
    return jax.shard_map(body, mesh=mesh, in_specs=in_specs, out_specs=out_specs, check_vma=False)
```

```python
import functools

import jax
import jax.numpy as jnp
from jax import lax
from jax.experimental import pallas as pl
from jax.experimental.pallas import tpu as pltpu
from jax.sharding import PartitionSpec as P

AXES = ("gx", "gy")
STEPS = 2

soften = 0.05
time_step = 0.5
reach = 2
chunk = 4
feature_rows = 32
moment_rows = 16
far_norm = 1e36
lanes = 128
vmem_limit = 16 << 20


def shifted(value, steps):
    count = lax.axis_size(AXES)
    pairs = [(source, (source + steps) % count) for source in range(count)]
    return lax.ppermute(value, AXES, pairs)


def swapped(value, first, wrap=True):
    count = lax.axis_size(AXES)
    pairs = []
    for lower in range(first, count, 2):
        if wrap or lower + 1 < count:
            upper = (lower + 1) % count
            pairs += [(lower, upper), (upper, lower)]
    return lax.ppermute(value, AXES, pairs)


def round_up(value, step):
    return -(-value // step) * step


def device_index():
    return lax.axis_index("gx") * lax.axis_size("gy") + lax.axis_index("gy")


def pieces(value, count):
    parts = []
    rest = value
    for _ in range(count - 1):
        part = rest.astype(jnp.bfloat16).astype(jnp.float32)
        parts.append(part)
        rest = rest - part
    parts.append(rest.astype(jnp.bfloat16).astype(jnp.float32))
    return parts


def pack_kernel(total_tiles, particles_ref, occupancy_ref, neighbours_ref, packed_ref, speed_ref):
    tiles, slots = (particles_ref.shape[0], particles_ref.shape[2])
    listed = neighbours_ref.shape[1]
    for row in range(3):
        packed_ref[row * tiles : (row + 1) * tiles, :] = particles_ref[:, row, :]
        speed_ref[row * tiles : (row + 1) * tiles, :] = particles_ref[:, 3 + row, :]
    tile_ids = lax.broadcasted_iota(jnp.int32, (tiles, listed), 0)
    offsets = neighbours_ref[...] - (device_index() * tiles + tile_ids)
    offsets = jnp.where(offsets < 0, offsets + total_tiles, offsets)
    packed_ref[3 * tiles :, :] = jnp.zeros((tiles, slots), jnp.float32)
    packed_ref[3 * tiles :, :listed] = offsets.astype(jnp.float32)
    for tile in range(tiles):
        live = occupancy_ref[tile].astype(jnp.float32)
        packed_ref[3 * tiles + tile : 3 * tiles + tile + 1, listed : listed + 1] = jnp.full((1, 1), live)


def places_of(index, tiles, offsets):
    place = index + offsets[0]
    for block in range(1, len(offsets)):
        place = jnp.where(index >= block * tiles, index - block * tiles + offsets[block], place)
    return jnp.where(index >= len(offsets) * tiles, -1000.0, place)


def build_lists(aux, own, tiles, listed, offsets):
    rows = aux.shape[0]
    dummy = len(offsets) * tiles
    index = lax.broadcasted_iota(jnp.int32, (rows, lanes), 0).astype(jnp.float32)
    lane = lax.broadcasted_iota(jnp.int32, (rows, lanes), 1).astype(jnp.float32)
    place = places_of(index, tiles, offsets)
    mask = place == lane
    for entry in range(listed):
        mask = mask | (place + aux[:, entry : entry + 1] == lane)
    own_rows = own.shape[0]
    own_index = lax.broadcasted_iota(jnp.int32, (own_rows, lanes), 0).astype(jnp.float32)
    own_lane = lax.broadcasted_iota(jnp.int32, (own_rows, lanes), 1).astype(jnp.float32)
    own_place = places_of(own_lane, tiles, offsets)
    listing = own_index + own[:, 0:1] == own_place
    for entry in range(1, listed):
        listing = listing | (own_index + own[:, entry : entry + 1] == own_place)
    listing = jnp.where(listing, 1.0, 0.0)
    listing = jnp.concatenate([listing, jnp.zeros((lanes - own_rows, lanes), jnp.float32)], axis=0)
    listing = jnp.transpose(listing)[:rows]
    mask = jnp.maximum(jnp.where(mask, 1.0, 0.0), listing)
    mask = jnp.where((lane < tiles) & (index < dummy), mask, 0.0)
    earlier = lax.broadcasted_iota(jnp.int32, (rows, rows), 1) < lax.broadcasted_iota(jnp.int32, (rows, rows), 0)
    rank = jnp.dot(
        jnp.where(earlier, 1.0, 0.0).astype(jnp.bfloat16),
        mask.astype(jnp.bfloat16),
        preferred_element_type=jnp.float32,
    )
    key = jnp.where(mask > 0.5, rank, -1.0)
    counts = jnp.sum(mask, axis=0, keepdims=True)
    lists = []
    for tile in range(tiles):
        hit = key[:, tile : tile + 1] == lane
        lists.append(jnp.sum(jnp.where(hit, index - dummy, 0.0), axis=0, keepdims=True) + dummy)
    lists.append(jnp.full((1, lanes), float(dummy)))
    lists.append(counts)
    return [row.astype(jnp.int32) for row in lists]


def middles(own_place):
    return [jnp.mean(axis[:8], keepdims=True) for axis in own_place]


def build_sources(places, middle, weight, feature_ref, moment_ref, source_ref, moments_ref):
    rows = weight.shape[0]
    ones = jnp.ones_like(weight)
    zeros = jnp.zeros_like(weight)
    features = []
    moments = []
    norm = zeros
    for axis in range(3):
        value = weight * (places[axis] - middle[axis])
        norm = norm + value * value
        high, mid, low = pieces(value, 3)
        features += [high, high, mid, mid, high, low]
        moments += [high, mid, low]
    features += pieces(jnp.where(weight > 0.5, norm, far_norm), 3) + [ones] * 3
    features += [zeros] * (feature_rows - len(features))
    moments.append(weight)
    moments += [zeros] * (moment_rows - len(moments))
    for row, value in enumerate(features):
        feature_ref[:rows, row, :] = value
    for row, value in enumerate(moments):
        moment_ref[:, row, :] = value
    for tile in range(rows):
        source_ref[tile] = feature_ref[tile].astype(jnp.bfloat16)
    group = lanes // moment_rows
    lane_group = lax.broadcasted_iota(jnp.int32, (lanes, lanes), 1) // moment_rows
    for first in range(0, rows, group):
        block = jnp.transpose(moment_ref[first : first + group].reshape(lanes, lanes))
        for entry in range(group):
            moments_ref[first + entry] = jnp.where(lane_group == entry, block, 0.0).astype(jnp.bfloat16)


def build_targets(own_place, middle, feature_ref, target_ref):
    tiles = own_place[0].shape[0]
    ones = jnp.ones_like(own_place[0])
    zeros = jnp.zeros_like(own_place[0])
    features = []
    norm = zeros
    for axis in range(3):
        value = own_place[axis] - middle[axis]
        norm = norm + value * value
        high, mid, low = [-2.0 * part for part in pieces(value, 3)]
        features += [high, mid, high, mid, low, high]
    features += [ones] * 3 + pieces(norm + soften, 3)
    features += [zeros] * (feature_rows - len(features))
    for row, value in enumerate(features):
        feature_ref[:tiles, row, :] = value
    lane_group = lax.broadcasted_iota(jnp.int32, (lanes, lanes), 1) // feature_rows
    pairs = chunk // 2
    for tile in range(tiles):
        feature = feature_ref[tile]
        block = jnp.transpose(jnp.concatenate([feature] * (lanes // feature_rows), axis=0))
        for pair in range(pairs):
            part = jnp.where(lane_group == pair, block, 0.0)[:, : pairs * feature_rows]
            target_ref[tile, pair * lanes : (pair + 1) * lanes, :] = part.astype(jnp.bfloat16)
    target_ref[tiles] = target_ref[0]


def accumulate(tiles, lists_ref, source_ref, target_ref, moments_ref, buffers, total_ref):
    chunk_counts = [(lists_ref[tiles + 1, tile] + chunk - 1) // chunk for tile in range(tiles)]
    chunk_total = functools.reduce(lambda left, right: left + right, [jnp.maximum(count, 1) for count in chunk_counts])
    distance_refs, kernel_refs = (buffers[:2], buffers[2:])

    def following(tile, part):
        more = (part + 1) * chunk < lists_ref[tiles + 1, tile]
        return (jnp.where(more, tile, jnp.minimum(tile + 1, tiles)), jnp.where(more, part + 1, 0))

    def sources_of(tile, part):
        return [lists_ref[tile, part * chunk + entry] for entry in range(chunk)]

    def distances(tile, part, distance_ref):
        features = [source_ref[source] for source in sources_of(tile, part)]
        pairs = [jnp.concatenate(features[first : first + 2], axis=1) for first in range(0, chunk, 2)]
        distance_ref[...] = jnp.dot(target_ref[tile], jnp.concatenate(pairs, axis=0), preferred_element_type=jnp.float32)

    def kernels(distance_ref, kernel_ref):
        for pair in range(chunk // 2):
            columns = slice(pair * 2 * lanes, (pair + 1) * 2 * lanes)
            for first in range(0, lanes, 16):
                inverse = lax.rsqrt(distance_ref[pair * lanes + first : pair * lanes + first + 16, :])
                kernel = inverse * inverse * inverse
                high = kernel.astype(jnp.bfloat16)
                kernel_ref[first : first + 16, columns] = high
                kernel_ref[lanes + first : lanes + first + 16, columns] = (kernel - high.astype(jnp.float32)).astype(
                    jnp.bfloat16
                )

    def sums(tile, part, kernel_ref):
        moments = jnp.concatenate([moments_ref[source] for source in sources_of(tile, part)], axis=0)
        both = jnp.dot(kernel_ref[...], moments, preferred_element_type=jnp.float32)
        total_ref[tile] += both[:lanes] + both[lanes:]

    def step(_, carry):
        (tile_0, part_0), (tile_1, part_1) = carry
        tile_2, part_2 = following(tile_1, part_1)
        tile_3, part_3 = following(tile_2, part_2)
        sums(tile_0, part_0, kernel_refs[1])
        kernels(distance_refs[0], kernel_refs[0])
        distances(tile_2, part_2, distance_refs[1])
        sums(tile_1, part_1, kernel_refs[0])
        kernels(distance_refs[1], kernel_refs[1])
        distances(tile_3, part_3, distance_refs[0])
        return ((tile_2, part_2), (tile_3, part_3))

    zero = jnp.int32(0)
    spare = jnp.int32(tiles)
    distances(zero, zero, distance_refs[0])
    lax.fori_loop(0, (chunk_total + 2) // 2, step, ((spare, zero), (zero, zero)))


def advance(middle, place_own, speed_own, weight_own, total_ref, sums_ref):
    tiles = weight_own.shape[0]
    for tile in range(tiles):
        folded = jnp.sum(jnp.transpose(total_ref[tile]).reshape(lanes // moment_rows, moment_rows, lanes), axis=0)
        for axis in range(3):
            sums_ref[axis, tile : tile + 1, :] = (
                folded[3 * axis : 3 * axis + 1] + folded[3 * axis + 1 : 3 * axis + 2] + folded[3 * axis + 2 : 3 * axis + 3]
            )
        sums_ref[3, tile : tile + 1, :] = folded[9:10]
    zeroth = sums_ref[3, :tiles, :]
    places, speeds = ([], [])
    for axis in range(3):
        force = sums_ref[axis, :tiles, :] - (place_own[axis] - middle[axis]) * zeroth
        speeds.append(weight_own * (speed_own[axis] + time_step * force / lanes))
        places.append(weight_own * (place_own[axis] + time_step * speeds[axis]))
    return places, speeds


def part_of(ref, tiles, row):
    return ref[row * tiles : (row + 1) * tiles, :]


def fill_planes(planes, tiles, blocks):
    kinds, rows, slots = planes.shape
    filled = len(blocks) * tiles
    planes[:, filled:, :] = jnp.zeros((kinds, rows - filled, slots), jnp.float32)
    for block, ref in enumerate(blocks):
        for kind in range(kinds):
            planes[kind, block * tiles : (block + 1) * tiles, :] = part_of(ref, tiles, kind)


def weights_of(aux, listed):
    slot = lax.broadcasted_iota(jnp.int32, aux.shape, 1).astype(jnp.float32)
    return jnp.where(slot < aux[:, listed : listed + 1], 1.0, 0.0)


def offsets_of(tiles, near_pair):
    toward = jnp.where(device_index() % 2 == 0, 1.0, -1.0) * float(tiles)
    if near_pair:
        return [0.0, toward]
    return [-float(reach * tiles), -toward, float(reach * tiles)]


def prepare(first, near_pair, listed, own_ref, blocks, lists_ref, weight_ref, tools):
    planes, scalars, copy_sem, feature_ref, moment_ref, source_ref, moments_ref = tools
    tiles = own_ref.shape[0] // planes.shape[0]
    if not first:
        copy = pltpu.make_async_copy(lists_ref, scalars, copy_sem)
        copy.start()
    fill_planes(planes, tiles, blocks)
    if first:
        aux = planes[3]
        own_aux = jnp.concatenate(
            [part_of(own_ref, tiles, 3), jnp.zeros((round_up(tiles, 8) - tiles, lanes), jnp.float32)], axis=0
        )
        for row, value in enumerate(build_lists(aux, own_aux, tiles, listed, offsets_of(tiles, near_pair))):
            lists_ref[row : row + 1, :] = value
        copy = pltpu.make_async_copy(lists_ref, scalars, copy_sem)
        copy.start()
        weight_ref[...] = weights_of(aux, listed)
    middle = middles([part_of(own_ref, tiles, axis) for axis in range(3)])
    build_sources([planes[axis] for axis in range(3)], middle, weight_ref[...], feature_ref, moment_ref, source_ref, moments_ref)
    return middle, copy


def begin(listed, first, *refs):
    if first:
        own_ref, sibling_ref, total_ref, target_ref, lists_ref, weight_ref, *scratch = refs
    else:
        own_ref, sibling_ref, lists_ref, weight_ref, total_ref, target_ref, *scratch = refs
    tools, buffers = (scratch[:7], scratch[7:])
    tiles = own_ref.shape[0] // tools[0].shape[0]
    middle, copy = prepare(first, True, listed, own_ref, (own_ref, sibling_ref), lists_ref, weight_ref, tools)
    build_targets([part_of(own_ref, tiles, axis) for axis in range(3)], middle, tools[3], target_ref)
    total_ref[...] = jnp.zeros(total_ref.shape, jnp.float32)
    copy.wait()
    accumulate(tiles, tools[1], tools[5], target_ref, tools[6], buffers, total_ref)


def halves(speed, even, half):
    first, last = (speed[:half], speed[half:])
    return jnp.where(even, last, first), jnp.where(even, first, last)


def first_finish(
    listed, own_ref, below, beside, above, total_in, target_ref, weight_own_ref, speed_ref, *refs
):
    total_ref, lists_ref, weight_ref, place_out, speed_out, sibling_out, beside_out, *scratch = refs
    *rest, sums_ref = scratch
    tools, buffers = (rest[:7], rest[7:])
    tiles = own_ref.shape[0] // tools[0].shape[0]
    half = tiles // 2
    middle, copy = prepare(True, False, listed, own_ref, (below, beside, above), lists_ref, weight_ref, tools)
    copy.wait()
    accumulate(tiles, tools[1], tools[5], target_ref, tools[6], buffers, total_ref)
    places, speeds = advance(
        middle,
        [part_of(own_ref, tiles, axis) for axis in range(3)],
        [part_of(speed_ref, tiles, axis) for axis in range(3)],
        weight_own_ref[:tiles, :],
        total_ref,
        sums_ref,
    )
    even = device_index() % 2 == 0
    for axis in range(3):
        strip = slice(axis * tiles, (axis + 1) * tiles)
        place_out[strip, :] = places[axis]
        speed_out[strip, :] = speeds[axis]
        sibling_out[strip, :] = places[axis]
        beside_out[strip, :] = places[axis]
        strip = slice(3 * tiles + axis * half, 3 * tiles + (axis + 1) * half)
        sibling_out[strip, :], beside_out[strip, :] = halves(speeds[axis], even, half)


def second_finish(
    total_tiles,
    cuts_ref,
    own_ref,
    below,
    beside,
    above,
    total_in,
    target_ref,
    weight_own_ref,
    speed_ref,
    sibling_ref,
    lists_ref,
    weight_ref,
    total_ref,
    state_ref,
    sibling_out,
    beside_out,
    out_ref,
    *scratch
):
    *rest, sums_ref, pool_ref = scratch
    tools, buffers = (rest[:7], rest[7:])
    tiles = own_ref.shape[0] // 3
    half = tiles // 2
    middle, copy = prepare(False, False, None, own_ref, (below, beside, above), lists_ref, weight_ref, tools)
    copy.wait()
    accumulate(tiles, tools[1], tools[5], target_ref, tools[6], buffers, total_ref)
    place_own = [part_of(own_ref, tiles, axis) for axis in range(3)]
    speed_own = [part_of(speed_ref, tiles, axis) for axis in range(3)]
    places, speeds = advance(middle, place_own, speed_own, weight_own_ref[:tiles, :], total_ref, sums_ref)
    even = device_index() % 2 == 0
    for row, value in enumerate(places + speeds):
        state_ref[row] = value
        strip = slice(row * half, (row + 1) * half)
        sibling_out[strip, :], beside_out[strip, :] = halves(value, even, half)
    lower, upper = ([], [])
    for row in range(6):
        if row < 3:
            sides = [part_of(ref, tiles, row) for ref in (sibling_ref, beside)]
            low_sides, high_sides = ([side[tiles - half :] for side in sides], [side[:half] for side in sides])
        else:
            strip = slice(3 * tiles + (row - 3) * half, 3 * tiles + (row - 2) * half)
            low_sides = high_sides = [ref[strip, :] for ref in (sibling_ref, beside)]
        lower.append(jnp.where(even, low_sides[1], low_sides[0]))
        upper.append(jnp.where(even, high_sides[0], high_sides[1]))
    place_rows(0, total_tiles, cuts_ref, lower, place_own + speed_own, upper, pool_ref, out_ref)


def place_rows(step, total_tiles, cuts_ref, lower, own, upper, pool_ref, out_ref):
    tiles, slots = own[0].shape
    half = tiles // 2
    capacity = out_ref.shape[1]
    device = device_index()
    last = cuts_ref.shape[1] - 1
    first_tile = cuts_ref[step, device]
    next_tile = jnp.where(device == last, total_tiles, cuts_ref[step, jnp.minimum(device + 1, last)])
    owned = next_tile - first_tile
    start = first_tile - (device * tiles - half)
    filled = lax.broadcasted_iota(jnp.int32, (capacity, slots), 0) < owned
    for row in range(6):
        pool_ref[row, :half, :] = lower[row]
        pool_ref[row, half : half + tiles, :] = own[row]
        pool_ref[row, half + tiles : 2 * tiles, :] = upper[row]
    for row in range(6):
        out_ref[row] = jnp.where(filled, pool_ref[row, pl.ds(start, capacity), :], 0.0)


def third_kernel(total_tiles, cuts_ref, sibling_ref, own_ref, beside_ref, out_ref, pool_ref):
    half = own_ref.shape[1] // 2
    even = device_index() % 2 == 0
    lower, upper = ([], [])
    for row in range(6):
        sibling, beside = (part_of(sibling_ref, half, row), part_of(beside_ref, half, row))
        lower.append(jnp.where(even, beside, sibling))
        upper.append(jnp.where(even, sibling, beside))
    place_rows(1, total_tiles, cuts_ref, lower, [own_ref[row] for row in range(6)], upper, pool_ref, out_ref)


def near(value):
    return pltpu.with_memory_space_constraint(value, pltpu.VMEM)


def body(particles, occupancy, neighbours, curve_cuts):
    tiles, _, slots = particles.shape
    listed = neighbours.shape[1]
    total_tiles = tiles * lax.axis_size(AXES)
    half = tiles // 2
    capacity = 2 * tiles
    near_rows = round_up(2 * tiles + 1, 8)
    far_rows = round_up((reach + 1) * tiles + 1, 8)
    list_rows = round_up(tiles + 2, 8)
    vmem = pl.BlockSpec(memory_space=pltpu.VMEM)
    smem = pl.BlockSpec(memory_space=pltpu.SMEM)

    def held(*sizes, dtype=jnp.float32):
        return pltpu.VMEM(sizes, dtype)

    def call(kernel, name, outs, ins, scratch, flops=0, aliases=None):
        held_ins = [value if kind is smem else near(value) for kind, value in ins]
        return pl.pallas_call(
            kernel,
            out_shape=outs,
            in_specs=[kind for kind, _ in ins],
            out_specs=[vmem] * len(outs),
            scratch_shapes=scratch,
            input_output_aliases=aliases or {},
            compiler_params=pltpu.CompilerParams(vmem_limit_bytes=vmem_limit),
            cost_estimate=pl.CostEstimate(flops=flops, bytes_accessed=1 << 20, transcendentals=0),
            name=name,
        )(*held_ins)

    def tools(rows, kinds):
        return [
            pltpu.VMEM((kinds, rows, slots), jnp.float32),
            pltpu.SMEM((list_rows, lanes), jnp.int32),
            pltpu.SemaphoreType.DMA,
            pltpu.VMEM((rows, feature_rows, lanes), jnp.float32),
            pltpu.VMEM((rows, moment_rows, lanes), jnp.float32),
            pltpu.VMEM((rows, feature_rows, lanes), jnp.bfloat16),
            pltpu.VMEM((rows, lanes, lanes), jnp.bfloat16),
            pltpu.VMEM((chunk // 2 * lanes, 2 * lanes), jnp.float32),
            pltpu.VMEM((chunk // 2 * lanes, 2 * lanes), jnp.float32),
            pltpu.VMEM((2 * lanes, chunk * lanes), jnp.bfloat16),
            pltpu.VMEM((2 * lanes, chunk * lanes), jnp.bfloat16),
        ]

    packed, speed = pl.pallas_call(
        functools.partial(pack_kernel, total_tiles),
        out_shape=(held(4 * tiles, slots), held(3 * tiles, slots)),
        in_specs=[vmem, smem, vmem],
        out_specs=(vmem, vmem),
        compiler_params=pltpu.CompilerParams(vmem_limit_bytes=vmem_limit),
        name="pack",
    )(particles, occupancy, neighbours)
    pool_scratch = pltpu.VMEM((6, round_up(capacity + tiles, 8), slots), jnp.float32)
    sums_scratch = pltpu.VMEM((4, round_up(tiles, 8), lanes), jnp.float32)
    totals = held(tiles + 1, lanes, lanes)
    targets = held(tiles + 1, chunk // 2 * lanes, chunk // 2 * feature_rows, dtype=jnp.bfloat16)
    lists = held(list_rows, lanes, dtype=jnp.int32)
    edge = 3 * tiles + 3 * half
    work = 1 << 32

    sibling = swapped(packed, 0)
    beside, below, above = (swapped(packed, 1), shifted(packed, reach), shifted(packed, -reach))
    total, target, near_lists, near_weight = call(
        functools.partial(begin, listed, True),
        "first_near",
        [totals, targets, lists, held(near_rows, slots)],
        [(vmem, packed), (vmem, sibling)],
        tools(near_rows, 4),
        work,
    )
    total, far_lists, far_weight, place, speed, sibling, beside = call(
        functools.partial(first_finish, listed),
        "first_far",
        [totals, lists, held(far_rows, slots), held(3 * tiles, slots), held(3 * tiles, slots), held(edge, slots), held(edge, slots)],
        [(vmem, value) for value in (packed, below, beside, above, total, target, near_weight, speed)],
        tools(far_rows, 4) + [sums_scratch],
        work,
        {4: 0},
    )
    sibling = swapped(sibling, 0)
    beside, below, above = (swapped(beside, 1), shifted(place, reach), shifted(place, -reach))
    total, target = call(
        functools.partial(begin, listed, False),
        "second_near",
        [totals, targets],
        [(vmem, value) for value in (place, sibling, near_lists, near_weight)],
        tools(near_rows, 3),
        work,
    )
    _, state, sibling, beside, after_first = call(
        functools.partial(second_finish, total_tiles),
        "second_far",
        [
            totals,
            held(6, tiles, slots),
            held(6 * half, slots),
            held(6 * half, slots),
            jax.ShapeDtypeStruct((6, capacity, slots), jnp.float32),
        ],
        [(smem, curve_cuts)]
        + [
            (vmem, value)
            for value in (place, below, beside, above, total, target, near_weight, speed, sibling, far_lists, far_weight)
        ],
        tools(far_rows, 3) + [sums_scratch, pool_scratch],
        work,
        {5: 0},
    )
    (after_second,) = call(
        functools.partial(third_kernel, total_tiles),
        "place",
        [jax.ShapeDtypeStruct((6, capacity, slots), jnp.float32)],
        [(smem, curve_cuts), (vmem, swapped(sibling, 0)), (vmem, state), (vmem, swapped(beside, 1, wrap=False))],
        [pool_scratch],
    )
    return (jnp.transpose(after_first, (1, 0, 2)), jnp.transpose(after_second, (1, 0, 2)))


def solution(mesh):
    in_specs = (P(AXES, None, None), P(AXES), P(AXES, None), P())
    out_specs = (P(AXES, None, None), P(AXES, None, None))
    return jax.shard_map(body, mesh=mesh, in_specs=in_specs, out_specs=out_specs, check_vma=False)
```

```python
import functools

import jax
import jax.numpy as jnp
from jax import lax
from jax.experimental import pallas as pl
from jax.experimental.pallas import tpu as pltpu
from jax.sharding import PartitionSpec as P

AXES = ("gx", "gy")
STEPS = 2

soften = 0.05
time_step = 0.5
reach = 2
chunk = 4
feature_rows = 32
moment_rows = 16
far_norm = 1e36
lanes = 128
vmem_limit = 16 << 20


def shifted(value, steps):
    count = lax.axis_size(AXES)
    pairs = [(source, (source + steps) % count) for source in range(count)]
    return lax.ppermute(value, AXES, pairs)


def swapped(value, first, wrap=True):
    count = lax.axis_size(AXES)
    pairs = []
    for lower in range(first, count, 2):
        if wrap or lower + 1 < count:
            upper = (lower + 1) % count
            pairs += [(lower, upper), (upper, lower)]
    return lax.ppermute(value, AXES, pairs)


def round_up(value, step):
    return -(-value // step) * step


def device_index():
    return lax.axis_index("gx") * lax.axis_size("gy") + lax.axis_index("gy")


def pieces(value, count):
    parts = []
    rest = value
    for _ in range(count - 1):
        part = rest.astype(jnp.bfloat16).astype(jnp.float32)
        parts.append(part)
        rest = rest - part
    parts.append(rest.astype(jnp.bfloat16).astype(jnp.float32))
    return parts


def pack_kernel(total_tiles, particles_ref, occupancy_ref, neighbours_ref, packed_ref, speed_ref):
    tiles, slots = (particles_ref.shape[0], particles_ref.shape[2])
    listed = neighbours_ref.shape[1]
    for row in range(3):
        packed_ref[row * tiles : (row + 1) * tiles, :] = particles_ref[:, row, :]
        speed_ref[row * tiles : (row + 1) * tiles, :] = particles_ref[:, 3 + row, :]
    tile_ids = lax.broadcasted_iota(jnp.int32, (tiles, listed), 0)
    offsets = neighbours_ref[...] - (device_index() * tiles + tile_ids)
    offsets = jnp.where(offsets < 0, offsets + total_tiles, offsets)
    packed_ref[3 * tiles :, :] = jnp.zeros((tiles, slots), jnp.float32)
    packed_ref[3 * tiles :, :listed] = offsets.astype(jnp.float32)
    for tile in range(tiles):
        live = occupancy_ref[tile].astype(jnp.float32)
        packed_ref[3 * tiles + tile : 3 * tiles + tile + 1, listed : listed + 1] = jnp.full((1, 1), live)


def places_of(index, tiles, offsets):
    place = index + offsets[0]
    for block in range(1, len(offsets)):
        place = jnp.where(index >= block * tiles, index - block * tiles + offsets[block], place)
    return jnp.where(index >= len(offsets) * tiles, -1000.0, place)


def build_lists(aux, own, tiles, listed, offsets):
    rows = aux.shape[0]
    dummy = len(offsets) * tiles
    index = lax.broadcasted_iota(jnp.int32, (rows, lanes), 0).astype(jnp.float32)
    lane = lax.broadcasted_iota(jnp.int32, (rows, lanes), 1).astype(jnp.float32)
    place = places_of(index, tiles, offsets)
    mask = place == lane
    for entry in range(listed):
        mask = mask | (place + aux[:, entry : entry + 1] == lane)
    own_rows = own.shape[0]
    own_index = lax.broadcasted_iota(jnp.int32, (own_rows, lanes), 0).astype(jnp.float32)
    own_lane = lax.broadcasted_iota(jnp.int32, (own_rows, lanes), 1).astype(jnp.float32)
    own_place = places_of(own_lane, tiles, offsets)
    listing = own_index + own[:, 0:1] == own_place
    for entry in range(1, listed):
        listing = listing | (own_index + own[:, entry : entry + 1] == own_place)
    listing = jnp.where(listing, 1.0, 0.0)
    listing = jnp.concatenate([listing, jnp.zeros((lanes - own_rows, lanes), jnp.float32)], axis=0)
    listing = jnp.transpose(listing)[:rows]
    mask = jnp.maximum(jnp.where(mask, 1.0, 0.0), listing)
    mask = jnp.where((lane < tiles) & (index < dummy), mask, 0.0)
    earlier = lax.broadcasted_iota(jnp.int32, (rows, rows), 1) < lax.broadcasted_iota(jnp.int32, (rows, rows), 0)
    rank = jnp.dot(
        jnp.where(earlier, 1.0, 0.0).astype(jnp.bfloat16),
        mask.astype(jnp.bfloat16),
        preferred_element_type=jnp.float32,
    )
    key = jnp.where(mask > 0.5, rank, -1.0)
    counts = jnp.sum(mask, axis=0, keepdims=True)
    lists = []
    for tile in range(tiles):
        hit = key[:, tile : tile + 1] == lane
        lists.append(jnp.sum(jnp.where(hit, index - dummy, 0.0), axis=0, keepdims=True) + dummy)
    lists.append(jnp.full((1, lanes), float(dummy)))
    lists.append(counts)
    return [row.astype(jnp.int32) for row in lists]


def middles(own_place):
    return [jnp.mean(axis[:8], keepdims=True) for axis in own_place]


def build_sources(places, middle, weight, feature_ref, moment_ref, source_ref, moments_ref):
    rows = weight.shape[0]
    ones = jnp.ones_like(weight)
    zeros = jnp.zeros_like(weight)
    features = []
    moments = []
    norm = zeros
    for axis in range(3):
        value = weight * (places[axis] - middle[axis])
        norm = norm + value * value
        high, mid, low = pieces(value, 3)
        features += [high, high, mid, mid, high, low]
        moments += [high, mid, low]
    features += pieces(jnp.where(weight > 0.5, norm, far_norm), 3) + [ones] * 3
    features += [zeros] * (feature_rows - len(features))
    moments.append(weight)
    moments += [zeros] * (moment_rows - len(moments))
    for row, value in enumerate(features):
        feature_ref[:rows, row, :] = value
    for row, value in enumerate(moments):
        moment_ref[:, row, :] = value
    for tile in range(rows):
        source_ref[tile] = feature_ref[tile].astype(jnp.bfloat16)
    group = lanes // moment_rows
    lane_group = lax.broadcasted_iota(jnp.int32, (lanes, lanes), 1) // moment_rows
    for first in range(0, rows, group):
        block = jnp.transpose(moment_ref[first : first + group].reshape(lanes, lanes))
        for entry in range(group):
            moments_ref[first + entry] = jnp.where(lane_group == entry, block, 0.0).astype(jnp.bfloat16)


def build_targets(own_place, middle, feature_ref, target_ref):
    tiles = own_place[0].shape[0]
    ones = jnp.ones_like(own_place[0])
    zeros = jnp.zeros_like(own_place[0])
    features = []
    norm = zeros
    for axis in range(3):
        value = own_place[axis] - middle[axis]
        norm = norm + value * value
        high, mid, low = [-2.0 * part for part in pieces(value, 3)]
        features += [high, mid, high, mid, low, high]
    features += [ones] * 3 + pieces(norm + soften, 3)
    features += [zeros] * (feature_rows - len(features))
    for row, value in enumerate(features):
        feature_ref[:tiles, row, :] = value
    blank = jnp.zeros((lanes - feature_rows, lanes), jnp.float32)
    for tile in range(tiles):
        block = jnp.concatenate([feature_ref[tile], blank], axis=0)
        target_ref[tile] = jnp.transpose(block)[:, :feature_rows].astype(jnp.bfloat16)
    target_ref[tiles] = target_ref[0]


def accumulate(tiles, lists_ref, source_ref, target_ref, moments_ref, buffers, total_ref):
    chunk_counts = [(lists_ref[tiles + 1, tile] + chunk - 1) // chunk for tile in range(tiles)]
    chunk_total = functools.reduce(lambda left, right: left + right, [jnp.maximum(count, 1) for count in chunk_counts])
    distance_refs, kernel_refs = (buffers[:2], buffers[2:])

    def following(tile, part):
        more = (part + 1) * chunk < lists_ref[tiles + 1, tile]
        return (jnp.where(more, tile, jnp.minimum(tile + 1, tiles)), jnp.where(more, part + 1, 0))

    def sources_of(tile, part):
        return [lists_ref[tile, part * chunk + entry] for entry in range(chunk)]

    def distances(tile, part, distance_ref):
        features = [source_ref[source] for source in sources_of(tile, part)]
        for pair in range(chunk // 2):
            distance_ref[pair * lanes : (pair + 1) * lanes, :] = jnp.dot(
                target_ref[tile],
                jnp.concatenate(features[2 * pair : 2 * pair + 2], axis=1),
                preferred_element_type=jnp.float32,
            )

    def kernels(distance_ref, kernel_ref):
        for pair in range(chunk // 2):
            columns = slice(pair * 2 * lanes, (pair + 1) * 2 * lanes)
            for first in range(0, lanes, 16):
                inverse = lax.rsqrt(distance_ref[pair * lanes + first : pair * lanes + first + 16, :])
                kernel = inverse * inverse * inverse
                high = kernel.astype(jnp.bfloat16)
                kernel_ref[first : first + 16, columns] = high
                kernel_ref[lanes + first : lanes + first + 16, columns] = (kernel - high.astype(jnp.float32)).astype(
                    jnp.bfloat16
                )

    def sums(tile, part, kernel_ref):
        moments = [moments_ref[source] for source in sources_of(tile, part)]
        total = total_ref[tile]
        for pair in range(chunk // 2):
            both = jnp.dot(
                kernel_ref[:, pair * 2 * lanes : (pair + 1) * 2 * lanes],
                jnp.concatenate(moments[2 * pair : 2 * pair + 2], axis=0),
                preferred_element_type=jnp.float32,
            )
            total = total + (both[:lanes] + both[lanes:])
        total_ref[tile] = total

    def step(_, carry):
        (tile_0, part_0), (tile_1, part_1) = carry
        tile_2, part_2 = following(tile_1, part_1)
        tile_3, part_3 = following(tile_2, part_2)
        sums(tile_0, part_0, kernel_refs[1])
        kernels(distance_refs[0], kernel_refs[0])
        distances(tile_2, part_2, distance_refs[1])
        sums(tile_1, part_1, kernel_refs[0])
        kernels(distance_refs[1], kernel_refs[1])
        distances(tile_3, part_3, distance_refs[0])
        return ((tile_2, part_2), (tile_3, part_3))

    zero = jnp.int32(0)
    spare = jnp.int32(tiles)
    distances(zero, zero, distance_refs[0])
    lax.fori_loop(0, (chunk_total + 2) // 2, step, ((spare, zero), (zero, zero)))


def advance(middle, place_own, speed_own, weight_own, total_ref, sums_ref):
    tiles = weight_own.shape[0]
    for tile in range(tiles):
        folded = jnp.sum(jnp.transpose(total_ref[tile]).reshape(lanes // moment_rows, moment_rows, lanes), axis=0)
        for axis in range(3):
            sums_ref[axis, tile : tile + 1, :] = (
                folded[3 * axis : 3 * axis + 1] + folded[3 * axis + 1 : 3 * axis + 2] + folded[3 * axis + 2 : 3 * axis + 3]
            )
        sums_ref[3, tile : tile + 1, :] = folded[9:10]
    zeroth = sums_ref[3, :tiles, :]
    places, speeds = ([], [])
    for axis in range(3):
        force = sums_ref[axis, :tiles, :] - (place_own[axis] - middle[axis]) * zeroth
        speeds.append(weight_own * (speed_own[axis] + time_step * force / lanes))
        places.append(weight_own * (place_own[axis] + time_step * speeds[axis]))
    return places, speeds


def part_of(ref, tiles, row):
    return ref[row * tiles : (row + 1) * tiles, :]


def fill_planes(planes, tiles, blocks):
    kinds, rows, slots = planes.shape
    filled = len(blocks) * tiles
    planes[:, filled:, :] = jnp.zeros((kinds, rows - filled, slots), jnp.float32)
    for block, ref in enumerate(blocks):
        for kind in range(kinds):
            planes[kind, block * tiles : (block + 1) * tiles, :] = part_of(ref, tiles, kind)


def weights_of(aux, listed):
    slot = lax.broadcasted_iota(jnp.int32, aux.shape, 1).astype(jnp.float32)
    return jnp.where(slot < aux[:, listed : listed + 1], 1.0, 0.0)


def offsets_of(tiles, near_pair):
    toward = jnp.where(device_index() % 2 == 0, 1.0, -1.0) * float(tiles)
    if near_pair:
        return [0.0, toward]
    return [-float(reach * tiles), -toward, float(reach * tiles)]


def prepare(first, near_pair, listed, own_ref, blocks, lists_ref, weight_ref, tools):
    planes, scalars, copy_sem, feature_ref, moment_ref, source_ref, moments_ref = tools
    tiles = own_ref.shape[0] // planes.shape[0]
    if not first:
        copy = pltpu.make_async_copy(lists_ref, scalars, copy_sem)
        copy.start()
    fill_planes(planes, tiles, blocks)
    if first:
        aux = planes[3]
        own_aux = jnp.concatenate(
            [part_of(own_ref, tiles, 3), jnp.zeros((round_up(tiles, 8) - tiles, lanes), jnp.float32)], axis=0
        )
        for row, value in enumerate(build_lists(aux, own_aux, tiles, listed, offsets_of(tiles, near_pair))):
            lists_ref[row : row + 1, :] = value
        copy = pltpu.make_async_copy(lists_ref, scalars, copy_sem)
        copy.start()
        weight_ref[...] = weights_of(aux, listed)
    middle = middles([part_of(own_ref, tiles, axis) for axis in range(3)])
    build_sources([planes[axis] for axis in range(3)], middle, weight_ref[...], feature_ref, moment_ref, source_ref, moments_ref)
    return middle, copy


def begin(listed, first, *refs):
    if first:
        own_ref, sibling_ref, total_ref, target_ref, lists_ref, weight_ref, *scratch = refs
    else:
        own_ref, sibling_ref, lists_ref, weight_ref, total_ref, target_ref, *scratch = refs
    tools, buffers = (scratch[:7], scratch[7:])
    tiles = own_ref.shape[0] // tools[0].shape[0]
    middle, copy = prepare(first, True, listed, own_ref, (own_ref, sibling_ref), lists_ref, weight_ref, tools)
    build_targets([part_of(own_ref, tiles, axis) for axis in range(3)], middle, tools[3], target_ref)
    total_ref[...] = jnp.zeros(total_ref.shape, jnp.float32)
    copy.wait()
    accumulate(tiles, tools[1], tools[5], target_ref, tools[6], buffers, total_ref)


def halves(speed, even, half):
    first, last = (speed[:half], speed[half:])
    return jnp.where(even, last, first), jnp.where(even, first, last)


def first_finish(
    listed, own_ref, below, beside, above, total_in, target_ref, weight_own_ref, speed_ref, *refs
):
    total_ref, lists_ref, weight_ref, place_out, speed_out, sibling_out, beside_out, *scratch = refs
    *rest, sums_ref = scratch
    tools, buffers = (rest[:7], rest[7:])
    tiles = own_ref.shape[0] // tools[0].shape[0]
    half = tiles // 2
    middle, copy = prepare(True, False, listed, own_ref, (below, beside, above), lists_ref, weight_ref, tools)
    copy.wait()
    accumulate(tiles, tools[1], tools[5], target_ref, tools[6], buffers, total_ref)
    places, speeds = advance(
        middle,
        [part_of(own_ref, tiles, axis) for axis in range(3)],
        [part_of(speed_ref, tiles, axis) for axis in range(3)],
        weight_own_ref[:tiles, :],
        total_ref,
        sums_ref,
    )
    even = device_index() % 2 == 0
    for axis in range(3):
        strip = slice(axis * tiles, (axis + 1) * tiles)
        place_out[strip, :] = places[axis]
        speed_out[strip, :] = speeds[axis]
        sibling_out[strip, :] = places[axis]
        beside_out[strip, :] = places[axis]
        strip = slice(3 * tiles + axis * half, 3 * tiles + (axis + 1) * half)
        sibling_out[strip, :], beside_out[strip, :] = halves(speeds[axis], even, half)


def second_finish(
    total_tiles,
    cuts_ref,
    own_ref,
    below,
    beside,
    above,
    total_in,
    target_ref,
    weight_own_ref,
    speed_ref,
    sibling_ref,
    lists_ref,
    weight_ref,
    total_ref,
    state_ref,
    sibling_out,
    beside_out,
    out_ref,
    *scratch
):
    *rest, sums_ref, pool_ref = scratch
    tools, buffers = (rest[:7], rest[7:])
    tiles = own_ref.shape[0] // 3
    half = tiles // 2
    middle, copy = prepare(False, False, None, own_ref, (below, beside, above), lists_ref, weight_ref, tools)
    copy.wait()
    accumulate(tiles, tools[1], tools[5], target_ref, tools[6], buffers, total_ref)
    place_own = [part_of(own_ref, tiles, axis) for axis in range(3)]
    speed_own = [part_of(speed_ref, tiles, axis) for axis in range(3)]
    places, speeds = advance(middle, place_own, speed_own, weight_own_ref[:tiles, :], total_ref, sums_ref)
    even = device_index() % 2 == 0
    for row, value in enumerate(places + speeds):
        state_ref[row] = value
        strip = slice(row * half, (row + 1) * half)
        sibling_out[strip, :], beside_out[strip, :] = halves(value, even, half)
    lower, upper = ([], [])
    for row in range(6):
        if row < 3:
            sides = [part_of(ref, tiles, row) for ref in (sibling_ref, beside)]
            low_sides, high_sides = ([side[tiles - half :] for side in sides], [side[:half] for side in sides])
        else:
            strip = slice(3 * tiles + (row - 3) * half, 3 * tiles + (row - 2) * half)
            low_sides = high_sides = [ref[strip, :] for ref in (sibling_ref, beside)]
        lower.append(jnp.where(even, low_sides[1], low_sides[0]))
        upper.append(jnp.where(even, high_sides[0], high_sides[1]))
    place_rows(0, total_tiles, cuts_ref, lower, place_own + speed_own, upper, pool_ref, out_ref)


def place_rows(step, total_tiles, cuts_ref, lower, own, upper, pool_ref, out_ref):
    tiles, slots = own[0].shape
    half = tiles // 2
    capacity = out_ref.shape[1]
    device = device_index()
    last = cuts_ref.shape[1] - 1
    first_tile = cuts_ref[step, device]
    next_tile = jnp.where(device == last, total_tiles, cuts_ref[step, jnp.minimum(device + 1, last)])
    owned = next_tile - first_tile
    start = first_tile - (device * tiles - half)
    filled = lax.broadcasted_iota(jnp.int32, (capacity, slots), 0) < owned
    for row in range(6):
        pool_ref[row, :half, :] = lower[row]
        pool_ref[row, half : half + tiles, :] = own[row]
        pool_ref[row, half + tiles : 2 * tiles, :] = upper[row]
    for row in range(6):
        out_ref[row] = jnp.where(filled, pool_ref[row, pl.ds(start, capacity), :], 0.0)


def third_kernel(total_tiles, cuts_ref, sibling_ref, own_ref, beside_ref, out_ref, pool_ref):
    half = own_ref.shape[1] // 2
    even = device_index() % 2 == 0
    lower, upper = ([], [])
    for row in range(6):
        sibling, beside = (part_of(sibling_ref, half, row), part_of(beside_ref, half, row))
        lower.append(jnp.where(even, beside, sibling))
        upper.append(jnp.where(even, sibling, beside))
    place_rows(1, total_tiles, cuts_ref, lower, [own_ref[row] for row in range(6)], upper, pool_ref, out_ref)


def near(value):
    return pltpu.with_memory_space_constraint(value, pltpu.VMEM)


def body(particles, occupancy, neighbours, curve_cuts):
    tiles, _, slots = particles.shape
    listed = neighbours.shape[1]
    total_tiles = tiles * lax.axis_size(AXES)
    half = tiles // 2
    capacity = 2 * tiles
    near_rows = round_up(2 * tiles + 1, 8)
    far_rows = round_up((reach + 1) * tiles + 1, 8)
    list_rows = round_up(tiles + 2, 8)
    vmem = pl.BlockSpec(memory_space=pltpu.VMEM)
    smem = pl.BlockSpec(memory_space=pltpu.SMEM)

    def held(*sizes, dtype=jnp.float32):
        return pltpu.VMEM(sizes, dtype)

    def call(kernel, name, outs, ins, scratch, flops=0, aliases=None):
        held_ins = [value if kind is smem else near(value) for kind, value in ins]
        return pl.pallas_call(
            kernel,
            out_shape=outs,
            in_specs=[kind for kind, _ in ins],
            out_specs=[vmem] * len(outs),
            scratch_shapes=scratch,
            input_output_aliases=aliases or {},
            compiler_params=pltpu.CompilerParams(vmem_limit_bytes=vmem_limit),
            cost_estimate=pl.CostEstimate(flops=flops, bytes_accessed=1 << 20, transcendentals=0),
            name=name,
        )(*held_ins)

    def tools(rows, kinds):
        return [
            pltpu.VMEM((kinds, rows, slots), jnp.float32),
            pltpu.SMEM((list_rows, lanes), jnp.int32),
            pltpu.SemaphoreType.DMA,
            pltpu.VMEM((rows, feature_rows, lanes), jnp.float32),
            pltpu.VMEM((rows, moment_rows, lanes), jnp.float32),
            pltpu.VMEM((rows, feature_rows, lanes), jnp.bfloat16),
            pltpu.VMEM((rows, lanes, lanes), jnp.bfloat16),
            pltpu.VMEM((chunk // 2 * lanes, 2 * lanes), jnp.float32),
            pltpu.VMEM((chunk // 2 * lanes, 2 * lanes), jnp.float32),
            pltpu.VMEM((2 * lanes, chunk * lanes), jnp.bfloat16),
            pltpu.VMEM((2 * lanes, chunk * lanes), jnp.bfloat16),
        ]

    packed, speed = pl.pallas_call(
        functools.partial(pack_kernel, total_tiles),
        out_shape=(held(4 * tiles, slots), held(3 * tiles, slots)),
        in_specs=[vmem, smem, vmem],
        out_specs=(vmem, vmem),
        compiler_params=pltpu.CompilerParams(vmem_limit_bytes=vmem_limit),
        name="pack",
    )(particles, occupancy, neighbours)
    pool_scratch = pltpu.VMEM((6, round_up(capacity + tiles, 8), slots), jnp.float32)
    sums_scratch = pltpu.VMEM((4, round_up(tiles, 8), lanes), jnp.float32)
    totals = held(tiles + 1, lanes, lanes)
    targets = held(tiles + 1, lanes, feature_rows, dtype=jnp.bfloat16)
    lists = held(list_rows, lanes, dtype=jnp.int32)
    edge = 3 * tiles + 3 * half
    work = 1 << 32

    sibling = swapped(packed, 0)
    beside, below, above = (swapped(packed, 1), shifted(packed, reach), shifted(packed, -reach))
    total, target, near_lists, near_weight = call(
        functools.partial(begin, listed, True),
        "first_near",
        [totals, targets, lists, held(near_rows, slots)],
        [(vmem, packed), (vmem, sibling)],
        tools(near_rows, 4),
        work,
    )
    total, far_lists, far_weight, place, speed, sibling, beside = call(
        functools.partial(first_finish, listed),
        "first_far",
        [totals, lists, held(far_rows, slots), held(3 * tiles, slots), held(3 * tiles, slots), held(edge, slots), held(edge, slots)],
        [(vmem, value) for value in (packed, below, beside, above, total, target, near_weight, speed)],
        tools(far_rows, 4) + [sums_scratch],
        work,
        {4: 0},
    )
    sibling = swapped(sibling, 0)
    beside, below, above = (swapped(beside, 1), shifted(place, reach), shifted(place, -reach))
    total, target = call(
        functools.partial(begin, listed, False),
        "second_near",
        [totals, targets],
        [(vmem, value) for value in (place, sibling, near_lists, near_weight)],
        tools(near_rows, 3),
        work,
    )
    _, state, sibling, beside, after_first = call(
        functools.partial(second_finish, total_tiles),
        "second_far",
        [
            totals,
            held(6, tiles, slots),
            held(6 * half, slots),
            held(6 * half, slots),
            jax.ShapeDtypeStruct((6, capacity, slots), jnp.float32),
        ],
        [(smem, curve_cuts)]
        + [
            (vmem, value)
            for value in (place, below, beside, above, total, target, near_weight, speed, sibling, far_lists, far_weight)
        ],
        tools(far_rows, 3) + [sums_scratch, pool_scratch],
        work,
        {5: 0},
    )
    (after_second,) = call(
        functools.partial(third_kernel, total_tiles),
        "place",
        [jax.ShapeDtypeStruct((6, capacity, slots), jnp.float32)],
        [(smem, curve_cuts), (vmem, swapped(sibling, 0)), (vmem, state), (vmem, swapped(beside, 1, wrap=False))],
        [pool_scratch],
    )
    return (jnp.transpose(after_first, (1, 0, 2)), jnp.transpose(after_second, (1, 0, 2)))


def solution(mesh):
    in_specs = (P(AXES, None, None), P(AXES), P(AXES, None), P())
    out_specs = (P(AXES, None, None), P(AXES, None, None))
    return jax.shard_map(body, mesh=mesh, in_specs=in_specs, out_specs=out_specs, check_vma=False)
```

```python
import functools

import jax
import jax.numpy as jnp
from jax import lax
from jax.experimental import pallas as pl
from jax.experimental.pallas import tpu as pltpu
from jax.sharding import PartitionSpec as P

AXES = ("gx", "gy")
STEPS = 2

soften = 0.05
time_step = 0.5
reach = 2
chunk = 4
units = 4
feature_rows = 32
far_norm = 1e36
lanes = 128
vmem_limit = 16 << 20


def shifted(value, steps):
    count = lax.axis_size(AXES)
    pairs = [(source, (source + steps) % count) for source in range(count)]
    return lax.ppermute(value, AXES, pairs)


def swapped(value, first, wrap=True):
    count = lax.axis_size(AXES)
    pairs = []
    for lower in range(first, count, 2):
        if wrap or lower + 1 < count:
            upper = (lower + 1) % count
            pairs += [(lower, upper), (upper, lower)]
    return lax.ppermute(value, AXES, pairs)


def round_up(value, step):
    return -(-value // step) * step


def device_index():
    return lax.axis_index("gx") * lax.axis_size("gy") + lax.axis_index("gy")


def pieces(value, count):
    parts = []
    rest = value
    for _ in range(count - 1):
        part = rest.astype(jnp.bfloat16).astype(jnp.float32)
        parts.append(part)
        rest = rest - part
    parts.append(rest.astype(jnp.bfloat16).astype(jnp.float32))
    return parts


def pack_kernel(total_tiles, particles_ref, occupancy_ref, neighbours_ref, packed_ref, speed_ref):
    tiles, slots = (particles_ref.shape[0], particles_ref.shape[2])
    listed = neighbours_ref.shape[1]
    for row in range(3):
        packed_ref[row * tiles : (row + 1) * tiles, :] = particles_ref[:, row, :]
        speed_ref[row * tiles : (row + 1) * tiles, :] = particles_ref[:, 3 + row, :]
    tile_ids = lax.broadcasted_iota(jnp.int32, (tiles, listed), 0)
    offsets = neighbours_ref[...] - (device_index() * tiles + tile_ids)
    offsets = jnp.where(offsets < 0, offsets + total_tiles, offsets)
    packed_ref[3 * tiles :, :] = jnp.zeros((tiles, slots), jnp.float32)
    packed_ref[3 * tiles :, :listed] = offsets.astype(jnp.float32)
    for tile in range(tiles):
        live = occupancy_ref[tile].astype(jnp.float32)
        packed_ref[3 * tiles + tile : 3 * tiles + tile + 1, listed : listed + 1] = jnp.full((1, 1), live)


def places_of(index, tiles, offsets):
    place = index + offsets[0]
    for block in range(1, len(offsets)):
        place = jnp.where(index >= block * tiles, index - block * tiles + offsets[block], place)
    return jnp.where(index >= len(offsets) * tiles, -1000.0, place)


def build_lists(aux, own, tiles, listed, offsets):
    rows = aux.shape[0]
    dummy = len(offsets) * tiles
    index = lax.broadcasted_iota(jnp.int32, (rows, lanes), 0).astype(jnp.float32)
    lane = lax.broadcasted_iota(jnp.int32, (rows, lanes), 1).astype(jnp.float32)
    place = places_of(index, tiles, offsets)
    mask = place == lane
    for entry in range(listed):
        mask = mask | (place + aux[:, entry : entry + 1] == lane)
    own_rows = own.shape[0]
    own_index = lax.broadcasted_iota(jnp.int32, (own_rows, lanes), 0).astype(jnp.float32)
    own_lane = lax.broadcasted_iota(jnp.int32, (own_rows, lanes), 1).astype(jnp.float32)
    own_place = places_of(own_lane, tiles, offsets)
    listing = own_index + own[:, 0:1] == own_place
    for entry in range(1, listed):
        listing = listing | (own_index + own[:, entry : entry + 1] == own_place)
    listing = jnp.where(listing, 1.0, 0.0)
    listing = jnp.concatenate([listing, jnp.zeros((lanes - own_rows, lanes), jnp.float32)], axis=0)
    listing = jnp.transpose(listing)[:rows]
    mask = jnp.maximum(jnp.where(mask, 1.0, 0.0), listing)
    mask = jnp.where((lane < tiles) & (index < dummy), mask, 0.0)
    earlier = lax.broadcasted_iota(jnp.int32, (rows, rows), 1) < lax.broadcasted_iota(jnp.int32, (rows, rows), 0)
    rank = jnp.dot(
        jnp.where(earlier, 1.0, 0.0).astype(jnp.bfloat16),
        mask.astype(jnp.bfloat16),
        preferred_element_type=jnp.float32,
    )
    key = jnp.where(mask > 0.5, rank, -1.0)
    counts = jnp.sum(mask, axis=0, keepdims=True)
    lists = []
    for tile in range(tiles):
        hit = key[:, tile : tile + 1] == lane
        lists.append(jnp.sum(jnp.where(hit, index - dummy, 0.0), axis=0, keepdims=True) + dummy)
    lists.append(jnp.full((1, lanes), float(dummy)))
    lists.append(counts)
    return [row.astype(jnp.int32) for row in lists]


def middles(own_place):
    return [jnp.mean(axis[:8], keepdims=True) for axis in own_place]


def build_sources(places, middle, weight, feature_ref, moment_ref, source_ref):
    rows = weight.shape[0]
    ones = jnp.ones_like(weight)
    zeros = jnp.zeros_like(weight)
    features = []
    norm = zeros
    for axis in range(3):
        value = weight * (places[axis] - middle[axis])
        norm = norm + value * value
        moment_ref[:rows, axis, :] = value
        high, mid, low = pieces(value, 3)
        features += [high, high, mid, mid, high, low]
    features += pieces(jnp.where(weight > 0.5, norm, far_norm), 3) + [ones] * 3
    features += [zeros] * (feature_rows - len(features))
    for row, value in enumerate(features):
        feature_ref[:rows, row, :] = value
    for tile in range(rows):
        source_ref[tile] = feature_ref[tile].astype(jnp.bfloat16)


def build_targets(own_place, middle, feature_ref, target_ref):
    tiles = own_place[0].shape[0]
    ones = jnp.ones_like(own_place[0])
    zeros = jnp.zeros_like(own_place[0])
    features = []
    norm = zeros
    for axis in range(3):
        value = own_place[axis] - middle[axis]
        norm = norm + value * value
        high, mid, low = [-2.0 * part for part in pieces(value, 3)]
        features += [high, mid, high, mid, low, high]
    features += [ones] * 3 + pieces(norm + soften, 3)
    features += [zeros] * (feature_rows - len(features))
    for row, value in enumerate(features):
        feature_ref[:tiles, row, :] = value
    blank = jnp.zeros((lanes - feature_rows, lanes), jnp.float32)
    for tile in range(tiles):
        block = jnp.concatenate([feature_ref[tile], blank], axis=0)
        target_ref[tile] = jnp.transpose(block)[:, :feature_rows].astype(jnp.bfloat16)
    target_ref[tiles] = target_ref[0]


def accumulate(tiles, lists_ref, source_ref, target_ref, moment_ref, total_ref):
    chunk_counts = [(lists_ref[tiles + 1, tile] + chunk - 1) // chunk for tile in range(tiles)]
    chunk_total = functools.reduce(lambda left, right: left + right, [jnp.maximum(count, 1) for count in chunk_counts])

    def following(tile, part):
        more = (part + 1) * chunk < lists_ref[tiles + 1, tile]
        return (jnp.where(more, tile, jnp.minimum(tile + 1, tiles)), jnp.where(more, part + 1, 0))

    def sources_of(tile, part):
        return [lists_ref[tile, part * chunk + entry] for entry in range(chunk)]

    def distances(tile, sources):
        target = target_ref[tile]
        features = [source_ref[source] for source in sources]
        return [
            jnp.dot(target, jnp.concatenate(features[first : first + 2], axis=1), preferred_element_type=jnp.float32)
            for first in range(0, chunk, 2)
        ]

    def kernels(tile, places, squares):
        for first in range(0, lanes, 8):
            strip = slice(first, first + 8)
            sums = [total_ref[tile, row, strip, :] for row in range(4)]
            for entry in range(chunk):
                column = (entry % 2) * lanes
                inverse = lax.rsqrt(squares[entry // 2][strip, column : column + lanes])
                kernel = inverse * inverse * inverse
                for axis in range(3):
                    sums[axis] = sums[axis] + kernel * places[entry][axis]
                sums[3] = sums[3] + kernel
            for row in range(4):
                total_ref[tile, row, strip, :] = sums[row]

    def step(_, carry):
        tile, part = carry
        work = []
        for _ in range(units):
            sources = sources_of(tile, part)
            places = [
                [jnp.broadcast_to(moment_ref[source, axis : axis + 1, :], (8, lanes)) for axis in range(3)]
                for source in sources
            ]
            work.append((tile, places, distances(tile, sources)))
            tile, part = following(tile, part)
        for item in work:
            kernels(*item)
        return (tile, part)

    zero = jnp.int32(0)
    lax.fori_loop(0, (chunk_total + units - 1) // units, step, (zero, zero))


def advance(middle, place_own, speed_own, weight_own, total_ref, sums_ref):
    tiles = weight_own.shape[0]
    for tile in range(tiles):
        for row in range(4):
            sums_ref[row, tile : tile + 1, :] = jnp.sum(jnp.transpose(total_ref[tile, row]), axis=0, keepdims=True)
    zeroth = sums_ref[3, :tiles, :]
    places, speeds = ([], [])
    for axis in range(3):
        force = sums_ref[axis, :tiles, :] - (place_own[axis] - middle[axis]) * zeroth
        speeds.append(weight_own * (speed_own[axis] + time_step * force / lanes))
        places.append(weight_own * (place_own[axis] + time_step * speeds[axis]))
    return places, speeds


def part_of(ref, tiles, row):
    return ref[row * tiles : (row + 1) * tiles, :]


def fill_planes(planes, tiles, blocks):
    kinds, rows, slots = planes.shape
    filled = len(blocks) * tiles
    planes[:, filled:, :] = jnp.zeros((kinds, rows - filled, slots), jnp.float32)
    for block, ref in enumerate(blocks):
        for kind in range(kinds):
            planes[kind, block * tiles : (block + 1) * tiles, :] = part_of(ref, tiles, kind)


def weights_of(aux, listed):
    slot = lax.broadcasted_iota(jnp.int32, aux.shape, 1).astype(jnp.float32)
    return jnp.where(slot < aux[:, listed : listed + 1], 1.0, 0.0)


def offsets_of(tiles, near_pair):
    toward = jnp.where(device_index() % 2 == 0, 1.0, -1.0) * float(tiles)
    if near_pair:
        return [0.0, toward]
    return [-float(reach * tiles), -toward, float(reach * tiles)]


def prepare(first, near_pair, listed, own_ref, blocks, lists_ref, weight_ref, tools):
    planes, scalars, copy_sem, feature_ref, moment_ref, source_ref = tools
    tiles = own_ref.shape[0] // planes.shape[0]
    if not first:
        copy = pltpu.make_async_copy(lists_ref, scalars, copy_sem)
        copy.start()
    fill_planes(planes, tiles, blocks)
    if first:
        aux = planes[3]
        own_aux = jnp.concatenate(
            [part_of(own_ref, tiles, 3), jnp.zeros((round_up(tiles, 8) - tiles, lanes), jnp.float32)], axis=0
        )
        for row, value in enumerate(build_lists(aux, own_aux, tiles, listed, offsets_of(tiles, near_pair))):
            lists_ref[row : row + 1, :] = value
        copy = pltpu.make_async_copy(lists_ref, scalars, copy_sem)
        copy.start()
        weight_ref[...] = weights_of(aux, listed)
    middle = middles([part_of(own_ref, tiles, axis) for axis in range(3)])
    build_sources([planes[axis] for axis in range(3)], middle, weight_ref[...], feature_ref, moment_ref, source_ref)
    return middle, copy


def begin(listed, first, *refs):
    if first:
        own_ref, sibling_ref, total_ref, target_ref, lists_ref, weight_ref, *scratch = refs
    else:
        own_ref, sibling_ref, lists_ref, weight_ref, total_ref, target_ref, *scratch = refs
    tools = scratch
    tiles = own_ref.shape[0] // tools[0].shape[0]
    middle, copy = prepare(first, True, listed, own_ref, (own_ref, sibling_ref), lists_ref, weight_ref, tools)
    build_targets([part_of(own_ref, tiles, axis) for axis in range(3)], middle, tools[3], target_ref)
    total_ref[...] = jnp.zeros(total_ref.shape, jnp.float32)
    copy.wait()
    accumulate(tiles, tools[1], tools[5], target_ref, tools[4], total_ref)


def halves(speed, even, half):
    first, last = (speed[:half], speed[half:])
    return jnp.where(even, last, first), jnp.where(even, first, last)


def first_finish(
    listed, own_ref, below, beside, above, total_in, target_ref, weight_own_ref, speed_ref, *refs
):
    total_ref, lists_ref, weight_ref, place_out, speed_out, sibling_out, beside_out, *scratch = refs
    *tools, sums_ref = scratch
    tiles = own_ref.shape[0] // tools[0].shape[0]
    half = tiles // 2
    middle, copy = prepare(True, False, listed, own_ref, (below, beside, above), lists_ref, weight_ref, tools)
    copy.wait()
    accumulate(tiles, tools[1], tools[5], target_ref, tools[4], total_ref)
    places, speeds = advance(
        middle,
        [part_of(own_ref, tiles, axis) for axis in range(3)],
        [part_of(speed_ref, tiles, axis) for axis in range(3)],
        weight_own_ref[:tiles, :],
        total_ref,
        sums_ref,
    )
    even = device_index() % 2 == 0
    for axis in range(3):
        strip = slice(axis * tiles, (axis + 1) * tiles)
        place_out[strip, :] = places[axis]
        speed_out[strip, :] = speeds[axis]
        sibling_out[strip, :] = places[axis]
        beside_out[strip, :] = places[axis]
        strip = slice(3 * tiles + axis * half, 3 * tiles + (axis + 1) * half)
        sibling_out[strip, :], beside_out[strip, :] = halves(speeds[axis], even, half)


def second_finish(
    total_tiles,
    cuts_ref,
    own_ref,
    below,
    beside,
    above,
    total_in,
    target_ref,
    weight_own_ref,
    speed_ref,
    sibling_ref,
    lists_ref,
    weight_ref,
    total_ref,
    state_ref,
    sibling_out,
    beside_out,
    out_ref,
    *scratch
):
    *tools, sums_ref, pool_ref = scratch
    tiles = own_ref.shape[0] // 3
    half = tiles // 2
    middle, copy = prepare(False, False, None, own_ref, (below, beside, above), lists_ref, weight_ref, tools)
    copy.wait()
    accumulate(tiles, tools[1], tools[5], target_ref, tools[4], total_ref)
    place_own = [part_of(own_ref, tiles, axis) for axis in range(3)]
    speed_own = [part_of(speed_ref, tiles, axis) for axis in range(3)]
    places, speeds = advance(middle, place_own, speed_own, weight_own_ref[:tiles, :], total_ref, sums_ref)
    even = device_index() % 2 == 0
    for row, value in enumerate(places + speeds):
        state_ref[row] = value
        strip = slice(row * half, (row + 1) * half)
        sibling_out[strip, :], beside_out[strip, :] = halves(value, even, half)
    lower, upper = ([], [])
    for row in range(6):
        if row < 3:
            sides = [part_of(ref, tiles, row) for ref in (sibling_ref, beside)]
            low_sides, high_sides = ([side[tiles - half :] for side in sides], [side[:half] for side in sides])
        else:
            strip = slice(3 * tiles + (row - 3) * half, 3 * tiles + (row - 2) * half)
            low_sides = high_sides = [ref[strip, :] for ref in (sibling_ref, beside)]
        lower.append(jnp.where(even, low_sides[1], low_sides[0]))
        upper.append(jnp.where(even, high_sides[0], high_sides[1]))
    place_rows(0, total_tiles, cuts_ref, lower, place_own + speed_own, upper, pool_ref, out_ref)


def place_rows(step, total_tiles, cuts_ref, lower, own, upper, pool_ref, out_ref):
    tiles, slots = own[0].shape
    half = tiles // 2
    capacity = out_ref.shape[1]
    device = device_index()
    last = cuts_ref.shape[1] - 1
    first_tile = cuts_ref[step, device]
    next_tile = jnp.where(device == last, total_tiles, cuts_ref[step, jnp.minimum(device + 1, last)])
    owned = next_tile - first_tile
    start = first_tile - (device * tiles - half)
    filled = lax.broadcasted_iota(jnp.int32, (capacity, slots), 0) < owned
    for row in range(6):
        pool_ref[row, :half, :] = lower[row]
        pool_ref[row, half : half + tiles, :] = own[row]
        pool_ref[row, half + tiles : 2 * tiles, :] = upper[row]
    for row in range(6):
        out_ref[row] = jnp.where(filled, pool_ref[row, pl.ds(start, capacity), :], 0.0)


def third_kernel(total_tiles, cuts_ref, sibling_ref, own_ref, beside_ref, out_ref, pool_ref):
    half = own_ref.shape[1] // 2
    even = device_index() % 2 == 0
    lower, upper = ([], [])
    for row in range(6):
        sibling, beside = (part_of(sibling_ref, half, row), part_of(beside_ref, half, row))
        lower.append(jnp.where(even, beside, sibling))
        upper.append(jnp.where(even, sibling, beside))
    place_rows(1, total_tiles, cuts_ref, lower, [own_ref[row] for row in range(6)], upper, pool_ref, out_ref)


def near(value):
    return pltpu.with_memory_space_constraint(value, pltpu.VMEM)


def body(particles, occupancy, neighbours, curve_cuts):
    tiles, _, slots = particles.shape
    listed = neighbours.shape[1]
    total_tiles = tiles * lax.axis_size(AXES)
    half = tiles // 2
    capacity = 2 * tiles
    near_rows = round_up(2 * tiles + 1, 8)
    far_rows = round_up((reach + 1) * tiles + 1, 8)
    list_rows = round_up(tiles + 2, 8)
    vmem = pl.BlockSpec(memory_space=pltpu.VMEM)
    smem = pl.BlockSpec(memory_space=pltpu.SMEM)

    def held(*sizes, dtype=jnp.float32):
        return pltpu.VMEM(sizes, dtype)

    def call(kernel, name, outs, ins, scratch, flops=0, aliases=None):
        held_ins = [value if kind is smem else near(value) for kind, value in ins]
        return pl.pallas_call(
            kernel,
            out_shape=outs,
            in_specs=[kind for kind, _ in ins],
            out_specs=[vmem] * len(outs),
            scratch_shapes=scratch,
            input_output_aliases=aliases or {},
            compiler_params=pltpu.CompilerParams(vmem_limit_bytes=vmem_limit),
            cost_estimate=pl.CostEstimate(flops=flops, bytes_accessed=1 << 20, transcendentals=0),
            name=name,
        )(*held_ins)

    def tools(rows, kinds):
        return [
            pltpu.VMEM((kinds, rows, slots), jnp.float32),
            pltpu.SMEM((list_rows, lanes), jnp.int32),
            pltpu.SemaphoreType.DMA,
            pltpu.VMEM((rows, feature_rows, lanes), jnp.float32),
            pltpu.VMEM((rows, 8, lanes), jnp.float32),
            pltpu.VMEM((rows, feature_rows, lanes), jnp.bfloat16),
        ]

    packed, speed = pl.pallas_call(
        functools.partial(pack_kernel, total_tiles),
        out_shape=(held(4 * tiles, slots), held(3 * tiles, slots)),
        in_specs=[vmem, smem, vmem],
        out_specs=(vmem, vmem),
        compiler_params=pltpu.CompilerParams(vmem_limit_bytes=vmem_limit),
        name="pack",
    )(particles, occupancy, neighbours)
    pool_scratch = pltpu.VMEM((6, round_up(capacity + tiles, 8), slots), jnp.float32)
    sums_scratch = pltpu.VMEM((4, round_up(tiles, 8), lanes), jnp.float32)
    totals = held(tiles + 1, 4, lanes, lanes)
    targets = held(tiles + 1, lanes, feature_rows, dtype=jnp.bfloat16)
    lists = held(list_rows, lanes, dtype=jnp.int32)
    edge = 3 * tiles + 3 * half
    work = 1 << 32

    sibling = swapped(packed, 0)
    beside, below, above = (swapped(packed, 1), shifted(packed, reach), shifted(packed, -reach))
    total, target, near_lists, near_weight = call(
        functools.partial(begin, listed, True),
        "first_near",
        [totals, targets, lists, held(near_rows, slots)],
        [(vmem, packed), (vmem, sibling)],
        tools(near_rows, 4),
        work,
    )
    total, far_lists, far_weight, place, speed, sibling, beside = call(
        functools.partial(first_finish, listed),
        "first_far",
        [totals, lists, held(far_rows, slots), held(3 * tiles, slots), held(3 * tiles, slots), held(edge, slots), held(edge, slots)],
        [(vmem, value) for value in (packed, below, beside, above, total, target, near_weight, speed)],
        tools(far_rows, 4) + [sums_scratch],
        work,
        {4: 0},
    )
    sibling = swapped(sibling, 0)
    beside, below, above = (swapped(beside, 1), shifted(place, reach), shifted(place, -reach))
    total, target = call(
        functools.partial(begin, listed, False),
        "second_near",
        [totals, targets],
        [(vmem, value) for value in (place, sibling, near_lists, near_weight)],
        tools(near_rows, 3),
        work,
    )
    _, state, sibling, beside, after_first = call(
        functools.partial(second_finish, total_tiles),
        "second_far",
        [
            totals,
            held(6, tiles, slots),
            held(6 * half, slots),
            held(6 * half, slots),
            jax.ShapeDtypeStruct((6, capacity, slots), jnp.float32),
        ],
        [(smem, curve_cuts)]
        + [
            (vmem, value)
            for value in (place, below, beside, above, total, target, near_weight, speed, sibling, far_lists, far_weight)
        ],
        tools(far_rows, 3) + [sums_scratch, pool_scratch],
        work,
        {5: 0},
    )
    (after_second,) = call(
        functools.partial(third_kernel, total_tiles),
        "place",
        [jax.ShapeDtypeStruct((6, capacity, slots), jnp.float32)],
        [(smem, curve_cuts), (vmem, swapped(sibling, 0)), (vmem, state), (vmem, swapped(beside, 1, wrap=False))],
        [pool_scratch],
    )
    return (jnp.transpose(after_first, (1, 0, 2)), jnp.transpose(after_second, (1, 0, 2)))


def solution(mesh):
    in_specs = (P(AXES, None, None), P(AXES), P(AXES, None), P())
    out_specs = (P(AXES, None, None), P(AXES, None, None))
    return jax.shard_map(body, mesh=mesh, in_specs=in_specs, out_specs=out_specs, check_vma=False)
```

```python
import functools

import jax
import jax.numpy as jnp
from jax import lax
from jax.experimental import pallas as pl
from jax.experimental.pallas import tpu as pltpu
from jax.sharding import PartitionSpec as P

AXES = ("gx", "gy")
STEPS = 2

soften = 0.05
time_step = 0.5
reach = 2
chunk = 4
units = 4
feature_rows = 32
moment_rows = 16
far_norm = 1e36
lanes = 128
vmem_limit = 16 << 20


def shifted(value, steps):
    count = lax.axis_size(AXES)
    pairs = [(source, (source + steps) % count) for source in range(count)]
    return lax.ppermute(value, AXES, pairs)


def swapped(value, first, wrap=True):
    count = lax.axis_size(AXES)
    pairs = []
    for lower in range(first, count, 2):
        if wrap or lower + 1 < count:
            upper = (lower + 1) % count
            pairs += [(lower, upper), (upper, lower)]
    return lax.ppermute(value, AXES, pairs)


def round_up(value, step):
    return -(-value // step) * step


def device_index():
    return lax.axis_index("gx") * lax.axis_size("gy") + lax.axis_index("gy")


def pieces(value, count):
    parts = []
    rest = value
    for _ in range(count - 1):
        part = rest.astype(jnp.bfloat16).astype(jnp.float32)
        parts.append(part)
        rest = rest - part
    parts.append(rest.astype(jnp.bfloat16).astype(jnp.float32))
    return parts


def pack_kernel(total_tiles, particles_ref, occupancy_ref, neighbours_ref, packed_ref, speed_ref):
    tiles, slots = (particles_ref.shape[0], particles_ref.shape[2])
    listed = neighbours_ref.shape[1]
    for row in range(3):
        packed_ref[row * tiles : (row + 1) * tiles, :] = particles_ref[:, row, :]
        speed_ref[row * tiles : (row + 1) * tiles, :] = particles_ref[:, 3 + row, :]
    tile_ids = lax.broadcasted_iota(jnp.int32, (tiles, listed), 0)
    offsets = neighbours_ref[...] - (device_index() * tiles + tile_ids)
    offsets = jnp.where(offsets < 0, offsets + total_tiles, offsets)
    packed_ref[3 * tiles :, :] = jnp.zeros((tiles, slots), jnp.float32)
    packed_ref[3 * tiles :, :listed] = offsets.astype(jnp.float32)
    for tile in range(tiles):
        live = occupancy_ref[tile].astype(jnp.float32)
        packed_ref[3 * tiles + tile : 3 * tiles + tile + 1, listed : listed + 1] = jnp.full((1, 1), live)


def places_of(index, tiles, offsets):
    place = index + offsets[0]
    for block in range(1, len(offsets)):
        place = jnp.where(index >= block * tiles, index - block * tiles + offsets[block], place)
    return jnp.where(index >= len(offsets) * tiles, -1000.0, place)


def build_lists(aux, own, tiles, listed, offsets):
    rows = aux.shape[0]
    dummy = len(offsets) * tiles
    index = lax.broadcasted_iota(jnp.int32, (rows, lanes), 0).astype(jnp.float32)
    lane = lax.broadcasted_iota(jnp.int32, (rows, lanes), 1).astype(jnp.float32)
    place = places_of(index, tiles, offsets)
    mask = place == lane
    for entry in range(listed):
        mask = mask | (place + aux[:, entry : entry + 1] == lane)
    own_rows = own.shape[0]
    own_index = lax.broadcasted_iota(jnp.int32, (own_rows, lanes), 0).astype(jnp.float32)
    own_lane = lax.broadcasted_iota(jnp.int32, (own_rows, lanes), 1).astype(jnp.float32)
    own_place = places_of(own_lane, tiles, offsets)
    listing = own_index + own[:, 0:1] == own_place
    for entry in range(1, listed):
        listing = listing | (own_index + own[:, entry : entry + 1] == own_place)
    listing = jnp.where(listing, 1.0, 0.0)
    listing = jnp.concatenate([listing, jnp.zeros((lanes - own_rows, lanes), jnp.float32)], axis=0)
    listing = jnp.transpose(listing)[:rows]
    mask = jnp.maximum(jnp.where(mask, 1.0, 0.0), listing)
    mask = jnp.where((lane < tiles) & (index < dummy), mask, 0.0)
    earlier = lax.broadcasted_iota(jnp.int32, (rows, rows), 1) < lax.broadcasted_iota(jnp.int32, (rows, rows), 0)
    rank = jnp.dot(
        jnp.where(earlier, 1.0, 0.0).astype(jnp.bfloat16),
        mask.astype(jnp.bfloat16),
        preferred_element_type=jnp.float32,
    )
    key = jnp.where(mask > 0.5, rank, -1.0)
    counts = jnp.sum(mask, axis=0, keepdims=True)
    lists = []
    for tile in range(tiles):
        hit = key[:, tile : tile + 1] == lane
        lists.append(jnp.sum(jnp.where(hit, index - dummy, 0.0), axis=0, keepdims=True) + dummy)
    lists.append(jnp.full((1, lanes), float(dummy)))
    lists.append(counts)
    return [row.astype(jnp.int32) for row in lists]


def middles(own_place):
    return [jnp.mean(axis[:8], keepdims=True) for axis in own_place]


def build_sources(places, middle, weight, feature_ref, moment_ref, source_ref, moments_ref):
    rows = weight.shape[0]
    ones = jnp.ones_like(weight)
    zeros = jnp.zeros_like(weight)
    features = []
    moments = []
    norm = zeros
    for axis in range(3):
        value = weight * (places[axis] - middle[axis])
        norm = norm + value * value
        high, mid, low = pieces(value, 3)
        features += [high, high, mid, mid, high, low]
        moments += [high, mid, low]
    features += pieces(jnp.where(weight > 0.5, norm, far_norm), 3) + [ones] * 3
    features += [zeros] * (feature_rows - len(features))
    moments.append(weight)
    moments += [zeros] * (moment_rows - len(moments))
    for row, value in enumerate(features):
        feature_ref[:rows, row, :] = value
    for row, value in enumerate(moments):
        moment_ref[:, row, :] = value
    for tile in range(rows):
        source_ref[tile] = feature_ref[tile].astype(jnp.bfloat16)
    group = lanes // moment_rows
    lane_group = lax.broadcasted_iota(jnp.int32, (lanes, lanes), 1) // moment_rows
    for first in range(0, rows, group):
        block = jnp.transpose(moment_ref[first : first + group].reshape(lanes, lanes))
        for entry in range(group):
            moments_ref[first + entry] = jnp.where(lane_group == entry, block, 0.0).astype(jnp.bfloat16)


def build_targets(own_place, middle, feature_ref, target_ref):
    tiles = own_place[0].shape[0]
    ones = jnp.ones_like(own_place[0])
    zeros = jnp.zeros_like(own_place[0])
    features = []
    norm = zeros
    for axis in range(3):
        value = own_place[axis] - middle[axis]
        norm = norm + value * value
        high, mid, low = [-2.0 * part for part in pieces(value, 3)]
        features += [high, mid, high, mid, low, high]
    features += [ones] * 3 + pieces(norm + soften, 3)
    features += [zeros] * (feature_rows - len(features))
    for row, value in enumerate(features):
        feature_ref[:tiles, row, :] = value
    lane_group = lax.broadcasted_iota(jnp.int32, (lanes, lanes), 1) // feature_rows
    pairs = chunk // 2
    for tile in range(tiles):
        feature = feature_ref[tile]
        block = jnp.transpose(jnp.concatenate([feature] * (lanes // feature_rows), axis=0))
        for pair in range(pairs):
            part = jnp.where(lane_group == pair, block, 0.0)[:, : pairs * feature_rows]
            target_ref[tile, pair * lanes : (pair + 1) * lanes, :] = part.astype(jnp.bfloat16)
    target_ref[tiles] = target_ref[0]


def accumulate(tiles, lists_ref, source_ref, target_ref, moments_ref, total_ref):
    chunk_counts = [(lists_ref[tiles + 1, tile] + chunk - 1) // chunk for tile in range(tiles)]
    chunk_total = functools.reduce(lambda left, right: left + right, [jnp.maximum(count, 1) for count in chunk_counts])

    def following(tile, part):
        more = (part + 1) * chunk < lists_ref[tiles + 1, tile]
        return (jnp.where(more, tile, jnp.minimum(tile + 1, tiles)), jnp.where(more, part + 1, 0))

    def distances(tile, sources):
        features = [source_ref[source] for source in sources]
        pairs = [jnp.concatenate(features[first : first + 2], axis=1) for first in range(0, chunk, 2)]
        return jnp.dot(target_ref[tile], jnp.concatenate(pairs, axis=0), preferred_element_type=jnp.float32)

    def sums(squares, moments):
        total = None
        for pair in range(chunk // 2):
            inverse = lax.rsqrt(squares[pair * lanes : (pair + 1) * lanes])
            kernel = inverse * inverse * inverse
            high = kernel.astype(jnp.bfloat16)
            low = (kernel - high.astype(jnp.float32)).astype(jnp.bfloat16)
            both = jnp.dot(
                jnp.concatenate([high, low], axis=0),
                jnp.concatenate(moments[2 * pair : 2 * pair + 2], axis=0),
                preferred_element_type=jnp.float32,
            )
            part = both[:lanes] + both[lanes:]
            total = part if total is None else total + part
        return total

    def step(_, carry):
        tile, part = carry
        work = []
        for _ in range(units):
            sources = [lists_ref[tile, part * chunk + entry] for entry in range(chunk)]
            work.append((tile, distances(tile, sources), [moments_ref[source] for source in sources]))
            tile, part = following(tile, part)
        for item, total in [(item, sums(squares, moments)) for item, squares, moments in work]:
            total_ref[item] += total
        return (tile, part)

    zero = jnp.int32(0)
    lax.fori_loop(0, (chunk_total + units - 1) // units, step, (zero, zero))


def advance(middle, place_own, speed_own, weight_own, total_ref, sums_ref):
    tiles = weight_own.shape[0]
    for tile in range(tiles):
        folded = jnp.sum(jnp.transpose(total_ref[tile]).reshape(lanes // moment_rows, moment_rows, lanes), axis=0)
        for axis in range(3):
            sums_ref[axis, tile : tile + 1, :] = (
                folded[3 * axis : 3 * axis + 1] + folded[3 * axis + 1 : 3 * axis + 2] + folded[3 * axis + 2 : 3 * axis + 3]
            )
        sums_ref[3, tile : tile + 1, :] = folded[9:10]
    zeroth = sums_ref[3, :tiles, :]
    places, speeds = ([], [])
    for axis in range(3):
        force = sums_ref[axis, :tiles, :] - (place_own[axis] - middle[axis]) * zeroth
        speeds.append(weight_own * (speed_own[axis] + time_step * force / lanes))
        places.append(weight_own * (place_own[axis] + time_step * speeds[axis]))
    return places, speeds


def part_of(ref, tiles, row):
    return ref[row * tiles : (row + 1) * tiles, :]


def fill_planes(planes, tiles, blocks):
    kinds, rows, slots = planes.shape
    filled = len(blocks) * tiles
    planes[:, filled:, :] = jnp.zeros((kinds, rows - filled, slots), jnp.float32)
    for block, ref in enumerate(blocks):
        for kind in range(kinds):
            planes[kind, block * tiles : (block + 1) * tiles, :] = part_of(ref, tiles, kind)


def weights_of(aux, listed):
    slot = lax.broadcasted_iota(jnp.int32, aux.shape, 1).astype(jnp.float32)
    return jnp.where(slot < aux[:, listed : listed + 1], 1.0, 0.0)


def offsets_of(tiles, near_pair):
    toward = jnp.where(device_index() % 2 == 0, 1.0, -1.0) * float(tiles)
    if near_pair:
        return [0.0, toward]
    return [-float(reach * tiles), -toward, float(reach * tiles)]


def prepare(first, near_pair, listed, own_ref, blocks, lists_ref, weight_ref, tools):
    planes, scalars, copy_sem, feature_ref, moment_ref, source_ref, moments_ref = tools
    tiles = own_ref.shape[0] // planes.shape[0]
    if not first:
        copy = pltpu.make_async_copy(lists_ref, scalars, copy_sem)
        copy.start()
    fill_planes(planes, tiles, blocks)
    if first:
        aux = planes[3]
        own_aux = jnp.concatenate(
            [part_of(own_ref, tiles, 3), jnp.zeros((round_up(tiles, 8) - tiles, lanes), jnp.float32)], axis=0
        )
        for row, value in enumerate(build_lists(aux, own_aux, tiles, listed, offsets_of(tiles, near_pair))):
            lists_ref[row : row + 1, :] = value
        copy = pltpu.make_async_copy(lists_ref, scalars, copy_sem)
        copy.start()
        weight_ref[...] = weights_of(aux, listed)
    middle = middles([part_of(own_ref, tiles, axis) for axis in range(3)])
    build_sources([planes[axis] for axis in range(3)], middle, weight_ref[...], feature_ref, moment_ref, source_ref, moments_ref)
    return middle, copy


def begin(listed, first, *refs):
    if first:
        own_ref, sibling_ref, total_ref, target_ref, lists_ref, weight_ref, *scratch = refs
    else:
        own_ref, sibling_ref, lists_ref, weight_ref, total_ref, target_ref, *scratch = refs
    tools = scratch
    tiles = own_ref.shape[0] // tools[0].shape[0]
    middle, copy = prepare(first, True, listed, own_ref, (own_ref, sibling_ref), lists_ref, weight_ref, tools)
    build_targets([part_of(own_ref, tiles, axis) for axis in range(3)], middle, tools[3], target_ref)
    total_ref[...] = jnp.zeros(total_ref.shape, jnp.float32)
    copy.wait()
    accumulate(tiles, tools[1], tools[5], target_ref, tools[6], total_ref)


def halves(speed, even, half):
    first, last = (speed[:half], speed[half:])
    return jnp.where(even, last, first), jnp.where(even, first, last)


def first_finish(
    listed, own_ref, below, beside, above, total_in, target_ref, weight_own_ref, speed_ref, *refs
):
    total_ref, lists_ref, weight_ref, place_out, speed_out, sibling_out, beside_out, *scratch = refs
    *tools, sums_ref = scratch
    tiles = own_ref.shape[0] // tools[0].shape[0]
    half = tiles // 2
    middle, copy = prepare(True, False, listed, own_ref, (below, beside, above), lists_ref, weight_ref, tools)
    copy.wait()
    accumulate(tiles, tools[1], tools[5], target_ref, tools[6], total_ref)
    places, speeds = advance(
        middle,
        [part_of(own_ref, tiles, axis) for axis in range(3)],
        [part_of(speed_ref, tiles, axis) for axis in range(3)],
        weight_own_ref[:tiles, :],
        total_ref,
        sums_ref,
    )
    even = device_index() % 2 == 0
    for axis in range(3):
        strip = slice(axis * tiles, (axis + 1) * tiles)
        place_out[strip, :] = places[axis]
        speed_out[strip, :] = speeds[axis]
        sibling_out[strip, :] = places[axis]
        beside_out[strip, :] = places[axis]
        strip = slice(3 * tiles + axis * half, 3 * tiles + (axis + 1) * half)
        sibling_out[strip, :], beside_out[strip, :] = halves(speeds[axis], even, half)


def second_finish(
    total_tiles,
    cuts_ref,
    own_ref,
    below,
    beside,
    above,
    total_in,
    target_ref,
    weight_own_ref,
    speed_ref,
    sibling_ref,
    lists_ref,
    weight_ref,
    total_ref,
    state_ref,
    sibling_out,
    beside_out,
    out_ref,
    *scratch
):
    *tools, sums_ref, pool_ref = scratch
    tiles = own_ref.shape[0] // 3
    half = tiles // 2
    middle, copy = prepare(False, False, None, own_ref, (below, beside, above), lists_ref, weight_ref, tools)
    copy.wait()
    accumulate(tiles, tools[1], tools[5], target_ref, tools[6], total_ref)
    place_own = [part_of(own_ref, tiles, axis) for axis in range(3)]
    speed_own = [part_of(speed_ref, tiles, axis) for axis in range(3)]
    places, speeds = advance(middle, place_own, speed_own, weight_own_ref[:tiles, :], total_ref, sums_ref)
    even = device_index() % 2 == 0
    for row, value in enumerate(places + speeds):
        state_ref[row] = value
        strip = slice(row * half, (row + 1) * half)
        sibling_out[strip, :], beside_out[strip, :] = halves(value, even, half)
    lower, upper = ([], [])
    for row in range(6):
        if row < 3:
            sides = [part_of(ref, tiles, row) for ref in (sibling_ref, beside)]
            low_sides, high_sides = ([side[tiles - half :] for side in sides], [side[:half] for side in sides])
        else:
            strip = slice(3 * tiles + (row - 3) * half, 3 * tiles + (row - 2) * half)
            low_sides = high_sides = [ref[strip, :] for ref in (sibling_ref, beside)]
        lower.append(jnp.where(even, low_sides[1], low_sides[0]))
        upper.append(jnp.where(even, high_sides[0], high_sides[1]))
    place_rows(0, total_tiles, cuts_ref, lower, place_own + speed_own, upper, pool_ref, out_ref)


def place_rows(step, total_tiles, cuts_ref, lower, own, upper, pool_ref, out_ref):
    tiles, slots = own[0].shape
    half = tiles // 2
    capacity = out_ref.shape[1]
    device = device_index()
    last = cuts_ref.shape[1] - 1
    first_tile = cuts_ref[step, device]
    next_tile = jnp.where(device == last, total_tiles, cuts_ref[step, jnp.minimum(device + 1, last)])
    owned = next_tile - first_tile
    start = first_tile - (device * tiles - half)
    filled = lax.broadcasted_iota(jnp.int32, (capacity, slots), 0) < owned
    for row in range(6):
        pool_ref[row, :half, :] = lower[row]
        pool_ref[row, half : half + tiles, :] = own[row]
        pool_ref[row, half + tiles : 2 * tiles, :] = upper[row]
    for row in range(6):
        out_ref[row] = jnp.where(filled, pool_ref[row, pl.ds(start, capacity), :], 0.0)


def third_kernel(total_tiles, cuts_ref, sibling_ref, own_ref, beside_ref, out_ref, pool_ref):
    half = own_ref.shape[1] // 2
    even = device_index() % 2 == 0
    lower, upper = ([], [])
    for row in range(6):
        sibling, beside = (part_of(sibling_ref, half, row), part_of(beside_ref, half, row))
        lower.append(jnp.where(even, beside, sibling))
        upper.append(jnp.where(even, sibling, beside))
    place_rows(1, total_tiles, cuts_ref, lower, [own_ref[row] for row in range(6)], upper, pool_ref, out_ref)


def near(value):
    return pltpu.with_memory_space_constraint(value, pltpu.VMEM)


def body(particles, occupancy, neighbours, curve_cuts):
    tiles, _, slots = particles.shape
    listed = neighbours.shape[1]
    total_tiles = tiles * lax.axis_size(AXES)
    half = tiles // 2
    capacity = 2 * tiles
    near_rows = round_up(2 * tiles + 1, 8)
    far_rows = round_up((reach + 1) * tiles + 1, 8)
    list_rows = round_up(tiles + 2, 8)
    vmem = pl.BlockSpec(memory_space=pltpu.VMEM)
    smem = pl.BlockSpec(memory_space=pltpu.SMEM)

    def held(*sizes, dtype=jnp.float32):
        return pltpu.VMEM(sizes, dtype)

    def call(kernel, name, outs, ins, scratch, flops=0, aliases=None):
        held_ins = [value if kind is smem else near(value) for kind, value in ins]
        return pl.pallas_call(
            kernel,
            out_shape=outs,
            in_specs=[kind for kind, _ in ins],
            out_specs=[vmem] * len(outs),
            scratch_shapes=scratch,
            input_output_aliases=aliases or {},
            compiler_params=pltpu.CompilerParams(vmem_limit_bytes=vmem_limit),
            cost_estimate=pl.CostEstimate(flops=flops, bytes_accessed=1 << 20, transcendentals=0),
            name=name,
        )(*held_ins)

    def tools(rows, kinds):
        return [
            pltpu.VMEM((kinds, rows, slots), jnp.float32),
            pltpu.SMEM((list_rows, lanes), jnp.int32),
            pltpu.SemaphoreType.DMA,
            pltpu.VMEM((rows, feature_rows, lanes), jnp.float32),
            pltpu.VMEM((rows, moment_rows, lanes), jnp.float32),
            pltpu.VMEM((rows, feature_rows, lanes), jnp.bfloat16),
            pltpu.VMEM((rows, lanes, lanes), jnp.bfloat16),
        ]

    packed, speed = pl.pallas_call(
        functools.partial(pack_kernel, total_tiles),
        out_shape=(held(4 * tiles, slots), held(3 * tiles, slots)),
        in_specs=[vmem, smem, vmem],
        out_specs=(vmem, vmem),
        compiler_params=pltpu.CompilerParams(vmem_limit_bytes=vmem_limit),
        name="pack",
    )(particles, occupancy, neighbours)
    pool_scratch = pltpu.VMEM((6, round_up(capacity + tiles, 8), slots), jnp.float32)
    sums_scratch = pltpu.VMEM((4, round_up(tiles, 8), lanes), jnp.float32)
    totals = held(tiles + 1, lanes, lanes)
    targets = held(tiles + 1, chunk // 2 * lanes, chunk // 2 * feature_rows, dtype=jnp.bfloat16)
    lists = held(list_rows, lanes, dtype=jnp.int32)
    edge = 3 * tiles + 3 * half
    work = 1 << 32

    sibling = swapped(packed, 0)
    beside, below, above = (swapped(packed, 1), shifted(packed, reach), shifted(packed, -reach))
    total, target, near_lists, near_weight = call(
        functools.partial(begin, listed, True),
        "first_near",
        [totals, targets, lists, held(near_rows, slots)],
        [(vmem, packed), (vmem, sibling)],
        tools(near_rows, 4),
        work,
    )
    total, far_lists, far_weight, place, speed, sibling, beside = call(
        functools.partial(first_finish, listed),
        "first_far",
        [totals, lists, held(far_rows, slots), held(3 * tiles, slots), held(3 * tiles, slots), held(edge, slots), held(edge, slots)],
        [(vmem, value) for value in (packed, below, beside, above, total, target, near_weight, speed)],
        tools(far_rows, 4) + [sums_scratch],
        work,
        {4: 0},
    )
    sibling = swapped(sibling, 0)
    beside, below, above = (swapped(beside, 1), shifted(place, reach), shifted(place, -reach))
    total, target = call(
        functools.partial(begin, listed, False),
        "second_near",
        [totals, targets],
        [(vmem, value) for value in (place, sibling, near_lists, near_weight)],
        tools(near_rows, 3),
        work,
    )
    _, state, sibling, beside, after_first = call(
        functools.partial(second_finish, total_tiles),
        "second_far",
        [
            totals,
            held(6, tiles, slots),
            held(6 * half, slots),
            held(6 * half, slots),
            jax.ShapeDtypeStruct((6, capacity, slots), jnp.float32),
        ],
        [(smem, curve_cuts)]
        + [
            (vmem, value)
            for value in (place, below, beside, above, total, target, near_weight, speed, sibling, far_lists, far_weight)
        ],
        tools(far_rows, 3) + [sums_scratch, pool_scratch],
        work,
        {5: 0},
    )
    (after_second,) = call(
        functools.partial(third_kernel, total_tiles),
        "place",
        [jax.ShapeDtypeStruct((6, capacity, slots), jnp.float32)],
        [(smem, curve_cuts), (vmem, swapped(sibling, 0)), (vmem, state), (vmem, swapped(beside, 1, wrap=False))],
        [pool_scratch],
    )
    return (jnp.transpose(after_first, (1, 0, 2)), jnp.transpose(after_second, (1, 0, 2)))


def solution(mesh):
    in_specs = (P(AXES, None, None), P(AXES), P(AXES, None), P())
    out_specs = (P(AXES, None, None), P(AXES, None, None))
    return jax.shard_map(body, mesh=mesh, in_specs=in_specs, out_specs=out_specs, check_vma=False)
```

```python
import functools

import jax
import jax.numpy as jnp
from jax import lax
from jax.experimental import pallas as pl
from jax.experimental.pallas import tpu as pltpu
from jax.sharding import PartitionSpec as P

AXES = ("gx", "gy")
STEPS = 2

soften = 0.05
time_step = 0.5
reach = 2
chunk = 4
units = 4
feature_rows = 32
far_norm = 1e36
lanes = 128
vmem_limit = 16 << 20


def gathered(value):
    count = lax.axis_size(AXES)
    groups = [[(first + step) % count for step in range(4)] for first in range(0, count, 2)]
    return [lax.all_gather(value, AXES, axis_index_groups=groups[half::2]) for half in range(2)]


def far_blocks(aligned, offset):
    spot = device_index() % 4
    low = spot < 2
    side = spot % 2
    below = jnp.where(low, offset[side], aligned[side])
    above = jnp.where(low, aligned[side + 2], offset[side + 2])
    inner = (spot == 1) | (spot == 2)
    beside = jnp.where(inner, aligned[jnp.where(spot == 1, 2, 1)], offset[jnp.where(spot == 0, 1, 2)])
    return (below, beside, above)


def swapped(value, first, wrap=True):
    count = lax.axis_size(AXES)
    pairs = []
    for lower in range(first, count, 2):
        if wrap or lower + 1 < count:
            upper = (lower + 1) % count
            pairs += [(lower, upper), (upper, lower)]
    return lax.ppermute(value, AXES, pairs)


def round_up(value, step):
    return -(-value // step) * step


def device_index():
    return lax.axis_index("gx") * lax.axis_size("gy") + lax.axis_index("gy")


def pieces(value, count):
    parts = []
    rest = value
    for _ in range(count - 1):
        part = rest.astype(jnp.bfloat16).astype(jnp.float32)
        parts.append(part)
        rest = rest - part
    parts.append(rest.astype(jnp.bfloat16).astype(jnp.float32))
    return parts


def pack_kernel(total_tiles, particles_ref, occupancy_ref, neighbours_ref, packed_ref, speed_ref):
    tiles, slots = (particles_ref.shape[0], particles_ref.shape[2])
    listed = neighbours_ref.shape[1]
    for row in range(3):
        packed_ref[row * tiles : (row + 1) * tiles, :] = particles_ref[:, row, :]
        speed_ref[row * tiles : (row + 1) * tiles, :] = particles_ref[:, 3 + row, :]
    tile_ids = lax.broadcasted_iota(jnp.int32, (tiles, listed), 0)
    offsets = neighbours_ref[...] - (device_index() * tiles + tile_ids)
    offsets = jnp.where(offsets < 0, offsets + total_tiles, offsets)
    packed_ref[3 * tiles :, :] = jnp.zeros((tiles, slots), jnp.float32)
    packed_ref[3 * tiles :, :listed] = offsets.astype(jnp.float32)
    for tile in range(tiles):
        live = occupancy_ref[tile].astype(jnp.float32)
        packed_ref[3 * tiles + tile : 3 * tiles + tile + 1, listed : listed + 1] = jnp.full((1, 1), live)


def places_of(index, tiles, offsets):
    place = index + offsets[0]
    for block in range(1, len(offsets)):
        place = jnp.where(index >= block * tiles, index - block * tiles + offsets[block], place)
    return jnp.where(index >= len(offsets) * tiles, -1000.0, place)


def build_lists(aux, own, tiles, listed, offsets):
    rows = aux.shape[0]
    dummy = len(offsets) * tiles
    index = lax.broadcasted_iota(jnp.int32, (rows, lanes), 0).astype(jnp.float32)
    lane = lax.broadcasted_iota(jnp.int32, (rows, lanes), 1).astype(jnp.float32)
    place = places_of(index, tiles, offsets)
    mask = place == lane
    for entry in range(listed):
        mask = mask | (place + aux[:, entry : entry + 1] == lane)
    own_rows = own.shape[0]
    own_index = lax.broadcasted_iota(jnp.int32, (own_rows, lanes), 0).astype(jnp.float32)
    own_lane = lax.broadcasted_iota(jnp.int32, (own_rows, lanes), 1).astype(jnp.float32)
    own_place = places_of(own_lane, tiles, offsets)
    listing = own_index + own[:, 0:1] == own_place
    for entry in range(1, listed):
        listing = listing | (own_index + own[:, entry : entry + 1] == own_place)
    listing = jnp.where(listing, 1.0, 0.0)
    listing = jnp.concatenate([listing, jnp.zeros((lanes - own_rows, lanes), jnp.float32)], axis=0)
    listing = jnp.transpose(listing)[:rows]
    mask = jnp.maximum(jnp.where(mask, 1.0, 0.0), listing)
    mask = jnp.where((lane < tiles) & (index < dummy), mask, 0.0)
    earlier = lax.broadcasted_iota(jnp.int32, (rows, rows), 1) < lax.broadcasted_iota(jnp.int32, (rows, rows), 0)
    rank = jnp.dot(
        jnp.where(earlier, 1.0, 0.0).astype(jnp.bfloat16),
        mask.astype(jnp.bfloat16),
        preferred_element_type=jnp.float32,
    )
    key = jnp.where(mask > 0.5, rank, -1.0)
    counts = jnp.sum(mask, axis=0, keepdims=True)
    lists = []
    for tile in range(tiles):
        hit = key[:, tile : tile + 1] == lane
        lists.append(jnp.sum(jnp.where(hit, index - dummy, 0.0), axis=0, keepdims=True) + dummy)
    lists.append(jnp.full((1, lanes), float(dummy)))
    lists.append(counts)
    return [row.astype(jnp.int32) for row in lists]


def middles(own_place):
    return [jnp.mean(axis[:8], keepdims=True) for axis in own_place]


def build_sources(places, middle, weight, feature_ref, moment_ref, source_ref):
    rows = weight.shape[0]
    ones = jnp.ones_like(weight)
    zeros = jnp.zeros_like(weight)
    features = []
    norm = zeros
    for axis in range(3):
        value = weight * (places[axis] - middle[axis])
        norm = norm + value * value
        moment_ref[:rows, axis, :] = value
        high, mid, low = pieces(value, 3)
        features += [high, high, mid, mid, high, low]
    features += pieces(jnp.where(weight > 0.5, norm, far_norm), 3) + [ones] * 3
    features += [zeros] * (feature_rows - len(features))
    for row, value in enumerate(features):
        feature_ref[:rows, row, :] = value
    for tile in range(rows):
        source_ref[tile] = feature_ref[tile].astype(jnp.bfloat16)


def build_targets(own_place, middle, feature_ref, target_ref):
    tiles = own_place[0].shape[0]
    ones = jnp.ones_like(own_place[0])
    zeros = jnp.zeros_like(own_place[0])
    features = []
    norm = zeros
    for axis in range(3):
        value = own_place[axis] - middle[axis]
        norm = norm + value * value
        high, mid, low = [-2.0 * part for part in pieces(value, 3)]
        features += [high, mid, high, mid, low, high]
    features += [ones] * 3 + pieces(norm + soften, 3)
    features += [zeros] * (feature_rows - len(features))
    for row, value in enumerate(features):
        feature_ref[:tiles, row, :] = value
    lane_group = lax.broadcasted_iota(jnp.int32, (lanes, lanes), 1) // feature_rows
    pairs = chunk // 2
    for tile in range(tiles):
        feature = feature_ref[tile]
        block = jnp.transpose(jnp.concatenate([feature] * (lanes // feature_rows), axis=0))
        for pair in range(pairs):
            part = jnp.where(lane_group == pair, block, 0.0)[:, : pairs * feature_rows]
            target_ref[tile, pair * lanes : (pair + 1) * lanes, :] = part.astype(jnp.bfloat16)
    target_ref[tiles] = target_ref[0]


def accumulate(tiles, lists_ref, source_ref, target_ref, moment_ref, total_ref):
    chunk_counts = [(lists_ref[tiles + 1, tile] + chunk - 1) // chunk for tile in range(tiles)]
    chunk_total = functools.reduce(lambda left, right: left + right, [jnp.maximum(count, 1) for count in chunk_counts])

    def following(tile, part):
        more = (part + 1) * chunk < lists_ref[tiles + 1, tile]
        return (jnp.where(more, tile, jnp.minimum(tile + 1, tiles)), jnp.where(more, part + 1, 0))

    def sources_of(tile, part):
        return [lists_ref[tile, part * chunk + entry] for entry in range(chunk)]

    def distances(tile, sources):
        features = [source_ref[source] for source in sources]
        pairs = [jnp.concatenate(features[first : first + 2], axis=1) for first in range(0, chunk, 2)]
        return jnp.dot(target_ref[tile], jnp.concatenate(pairs, axis=0), preferred_element_type=jnp.float32)

    def kernels(tile, places, squares):
        for first in range(0, lanes, 8):
            strip = slice(first, first + 8)
            sums = [total_ref[tile, row, strip, :] for row in range(4)]
            for entry in range(chunk):
                row, column = (entry // 2 * lanes + first, entry % 2 * lanes)
                inverse = lax.rsqrt(squares[row : row + 8, column : column + lanes])
                kernel = inverse * inverse * inverse
                for axis in range(3):
                    sums[axis] = sums[axis] + kernel * places[entry][axis]
                sums[3] = sums[3] + kernel
            for row in range(4):
                total_ref[tile, row, strip, :] = sums[row]

    def step(_, carry):
        tile, part = carry
        work = []
        for _ in range(units):
            sources = sources_of(tile, part)
            places = [
                [jnp.broadcast_to(moment_ref[source, axis : axis + 1, :], (8, lanes)) for axis in range(3)]
                for source in sources
            ]
            work.append((tile, places, distances(tile, sources)))
            tile, part = following(tile, part)
        for item in work:
            kernels(*item)
        return (tile, part)

    zero = jnp.int32(0)
    lax.fori_loop(0, (chunk_total + units - 1) // units, step, (zero, zero))


def advance(middle, place_own, speed_own, weight_own, total_ref, sums_ref):
    tiles = weight_own.shape[0]
    for tile in range(tiles):
        for row in range(4):
            sums_ref[row, tile : tile + 1, :] = jnp.sum(jnp.transpose(total_ref[tile, row]), axis=0, keepdims=True)
    zeroth = sums_ref[3, :tiles, :]
    places, speeds = ([], [])
    for axis in range(3):
        force = sums_ref[axis, :tiles, :] - (place_own[axis] - middle[axis]) * zeroth
        speeds.append(weight_own * (speed_own[axis] + time_step * force / lanes))
        places.append(weight_own * (place_own[axis] + time_step * speeds[axis]))
    return places, speeds


def part_of(ref, tiles, row):
    return ref[row * tiles : (row + 1) * tiles, :]


def fill_planes(planes, tiles, blocks):
    kinds, rows, slots = planes.shape
    filled = len(blocks) * tiles
    planes[:, filled:, :] = jnp.zeros((kinds, rows - filled, slots), jnp.float32)
    for block, ref in enumerate(blocks):
        for kind in range(kinds):
            planes[kind, block * tiles : (block + 1) * tiles, :] = part_of(ref, tiles, kind)


def weights_of(aux, listed):
    slot = lax.broadcasted_iota(jnp.int32, aux.shape, 1).astype(jnp.float32)
    return jnp.where(slot < aux[:, listed : listed + 1], 1.0, 0.0)


def offsets_of(tiles, near_pair):
    toward = jnp.where(device_index() % 2 == 0, 1.0, -1.0) * float(tiles)
    if near_pair:
        return [0.0, toward]
    return [-float(reach * tiles), -toward, float(reach * tiles)]


def prepare(first, near_pair, listed, own_ref, blocks, lists_ref, weight_ref, tools):
    planes, scalars, copy_sem, feature_ref, moment_ref, source_ref = tools
    tiles = own_ref.shape[0] // planes.shape[0]
    if not first:
        copy = pltpu.make_async_copy(lists_ref, scalars, copy_sem)
        copy.start()
    fill_planes(planes, tiles, blocks)
    if first:
        aux = planes[3]
        own_aux = jnp.concatenate(
            [part_of(own_ref, tiles, 3), jnp.zeros((round_up(tiles, 8) - tiles, lanes), jnp.float32)], axis=0
        )
        for row, value in enumerate(build_lists(aux, own_aux, tiles, listed, offsets_of(tiles, near_pair))):
            lists_ref[row : row + 1, :] = value
        copy = pltpu.make_async_copy(lists_ref, scalars, copy_sem)
        copy.start()
        weight_ref[...] = weights_of(aux, listed)
    middle = middles([part_of(own_ref, tiles, axis) for axis in range(3)])
    build_sources([planes[axis] for axis in range(3)], middle, weight_ref[...], feature_ref, moment_ref, source_ref)
    return middle, copy


def begin(listed, first, *refs):
    if first:
        own_ref, sibling_ref, total_ref, target_ref, lists_ref, weight_ref, *scratch = refs
    else:
        own_ref, sibling_ref, lists_ref, weight_ref, total_ref, target_ref, *scratch = refs
    tools = scratch
    tiles = own_ref.shape[0] // tools[0].shape[0]
    middle, copy = prepare(first, True, listed, own_ref, (own_ref, sibling_ref), lists_ref, weight_ref, tools)
    build_targets([part_of(own_ref, tiles, axis) for axis in range(3)], middle, tools[3], target_ref)
    total_ref[...] = jnp.zeros(total_ref.shape, jnp.float32)
    copy.wait()
    accumulate(tiles, tools[1], tools[5], target_ref, tools[4], total_ref)


def halves(speed, even, half):
    first, last = (speed[:half], speed[half:])
    return jnp.where(even, last, first), jnp.where(even, first, last)


def first_finish(
    listed, own_ref, aligned, offset, total_in, target_ref, weight_own_ref, speed_ref, *refs
):
    total_ref, lists_ref, weight_ref, place_out, speed_out, sibling_out, beside_out, *scratch = refs
    *tools, sums_ref = scratch
    tiles = own_ref.shape[0] // tools[0].shape[0]
    half = tiles // 2
    middle, copy = prepare(True, False, listed, own_ref, far_blocks(aligned, offset), lists_ref, weight_ref, tools)
    copy.wait()
    accumulate(tiles, tools[1], tools[5], target_ref, tools[4], total_ref)
    places, speeds = advance(
        middle,
        [part_of(own_ref, tiles, axis) for axis in range(3)],
        [part_of(speed_ref, tiles, axis) for axis in range(3)],
        weight_own_ref[:tiles, :],
        total_ref,
        sums_ref,
    )
    even = device_index() % 2 == 0
    for axis in range(3):
        strip = slice(axis * tiles, (axis + 1) * tiles)
        place_out[strip, :] = places[axis]
        speed_out[strip, :] = speeds[axis]
        sibling_out[strip, :] = places[axis]
        beside_out[strip, :] = places[axis]
        strip = slice(3 * tiles + axis * half, 3 * tiles + (axis + 1) * half)
        sibling_out[strip, :], beside_out[strip, :] = halves(speeds[axis], even, half)


def second_finish(
    total_tiles,
    cuts_ref,
    own_ref,
    aligned,
    offset,
    total_in,
    target_ref,
    weight_own_ref,
    speed_ref,
    sibling_ref,
    lists_ref,
    weight_ref,
    total_ref,
    state_ref,
    sibling_out,
    beside_out,
    out_ref,
    *scratch
):
    *tools, sums_ref, pool_ref = scratch
    tiles = own_ref.shape[0] // 3
    half = tiles // 2
    below, beside, above = far_blocks(aligned, offset)
    middle, copy = prepare(False, False, None, own_ref, (below, beside, above), lists_ref, weight_ref, tools)
    copy.wait()
    accumulate(tiles, tools[1], tools[5], target_ref, tools[4], total_ref)
    place_own = [part_of(own_ref, tiles, axis) for axis in range(3)]
    speed_own = [part_of(speed_ref, tiles, axis) for axis in range(3)]
    places, speeds = advance(middle, place_own, speed_own, weight_own_ref[:tiles, :], total_ref, sums_ref)
    even = device_index() % 2 == 0
    for row, value in enumerate(places + speeds):
        state_ref[row] = value
        strip = slice(row * half, (row + 1) * half)
        sibling_out[strip, :], beside_out[strip, :] = halves(value, even, half)
    lower, upper = ([], [])
    for row in range(6):
        if row < 3:
            sides = [part_of(ref, tiles, row) for ref in (sibling_ref, beside)]
            low_sides, high_sides = ([side[tiles - half :] for side in sides], [side[:half] for side in sides])
        else:
            strip = slice(3 * tiles + (row - 3) * half, 3 * tiles + (row - 2) * half)
            low_sides = high_sides = [ref[strip, :] for ref in (sibling_ref, beside)]
        lower.append(jnp.where(even, low_sides[1], low_sides[0]))
        upper.append(jnp.where(even, high_sides[0], high_sides[1]))
    place_rows(0, total_tiles, cuts_ref, lower, place_own + speed_own, upper, pool_ref, out_ref)


def place_rows(step, total_tiles, cuts_ref, lower, own, upper, pool_ref, out_ref):
    tiles, slots = own[0].shape
    half = tiles // 2
    capacity = out_ref.shape[1]
    device = device_index()
    last = cuts_ref.shape[1] - 1
    first_tile = cuts_ref[step, device]
    next_tile = jnp.where(device == last, total_tiles, cuts_ref[step, jnp.minimum(device + 1, last)])
    owned = next_tile - first_tile
    start = first_tile - (device * tiles - half)
    filled = lax.broadcasted_iota(jnp.int32, (capacity, slots), 0) < owned
    for row in range(6):
        pool_ref[row, :half, :] = lower[row]
        pool_ref[row, half : half + tiles, :] = own[row]
        pool_ref[row, half + tiles : 2 * tiles, :] = upper[row]
    for row in range(6):
        out_ref[row] = jnp.where(filled, pool_ref[row, pl.ds(start, capacity), :], 0.0)


def third_kernel(total_tiles, cuts_ref, sibling_ref, own_ref, beside_ref, out_ref, pool_ref):
    half = own_ref.shape[1] // 2
    even = device_index() % 2 == 0
    lower, upper = ([], [])
    for row in range(6):
        sibling, beside = (part_of(sibling_ref, half, row), part_of(beside_ref, half, row))
        lower.append(jnp.where(even, beside, sibling))
        upper.append(jnp.where(even, sibling, beside))
    place_rows(1, total_tiles, cuts_ref, lower, [own_ref[row] for row in range(6)], upper, pool_ref, out_ref)


def far(value):
    return pltpu.with_memory_space_constraint(value, pltpu.HBM)


def near(value):
    return pltpu.with_memory_space_constraint(value, pltpu.VMEM)


def body(particles, occupancy, neighbours, curve_cuts):
    tiles, _, slots = particles.shape
    listed = neighbours.shape[1]
    total_tiles = tiles * lax.axis_size(AXES)
    half = tiles // 2
    capacity = 2 * tiles
    near_rows = round_up(2 * tiles + 1, 8)
    far_rows = round_up((reach + 1) * tiles + 1, 8)
    list_rows = round_up(tiles + 2, 8)
    vmem = pl.BlockSpec(memory_space=pltpu.VMEM)
    smem = pl.BlockSpec(memory_space=pltpu.SMEM)
    fetched = "fetched"

    def held(*sizes, dtype=jnp.float32):
        return pltpu.VMEM(sizes, dtype)

    def call(kernel, name, outs, ins, scratch, flops=0, aliases=None):
        held_ins = [far(value) if kind in (smem, fetched) else near(value) for kind, value in ins]
        return pl.pallas_call(
            kernel,
            out_shape=outs,
            in_specs=[vmem if kind is fetched else kind for kind, _ in ins],
            out_specs=[vmem] * len(outs),
            scratch_shapes=scratch,
            input_output_aliases=aliases or {},
            compiler_params=pltpu.CompilerParams(vmem_limit_bytes=vmem_limit),
            cost_estimate=pl.CostEstimate(flops=flops, bytes_accessed=1 << 20, transcendentals=0),
            name=name,
        )(*held_ins)

    def tools(rows, kinds):
        return [
            pltpu.VMEM((kinds, rows, slots), jnp.float32),
            pltpu.SMEM((list_rows, lanes), jnp.int32),
            pltpu.SemaphoreType.DMA,
            pltpu.VMEM((rows, feature_rows, lanes), jnp.float32),
            pltpu.VMEM((rows, 8, lanes), jnp.float32),
            pltpu.VMEM((rows, feature_rows, lanes), jnp.bfloat16),
        ]

    packed, speed = pl.pallas_call(
        functools.partial(pack_kernel, total_tiles),
        out_shape=(held(4 * tiles, slots), held(3 * tiles, slots)),
        in_specs=[vmem, smem, vmem],
        out_specs=(vmem, vmem),
        compiler_params=pltpu.CompilerParams(vmem_limit_bytes=vmem_limit),
        name="pack",
    )(far(particles), far(occupancy), far(neighbours))
    pool_scratch = pltpu.VMEM((6, round_up(capacity + tiles, 8), slots), jnp.float32)
    sums_scratch = pltpu.VMEM((4, round_up(tiles, 8), lanes), jnp.float32)
    totals = held(tiles + 1, 4, lanes, lanes)
    targets = held(tiles + 1, chunk // 2 * lanes, chunk // 2 * feature_rows, dtype=jnp.bfloat16)
    lists = held(list_rows, lanes, dtype=jnp.int32)
    edge = 3 * tiles + 3 * half
    work = 1 << 32

    sibling = swapped(packed, 0)
    aligned, offset = gathered(packed)
    total, target, near_lists, near_weight = call(
        functools.partial(begin, listed, True),
        "first_near",
        [totals, targets, lists, held(near_rows, slots)],
        [(vmem, packed), (vmem, sibling)],
        tools(near_rows, 4),
        work,
    )
    total, far_lists, far_weight, place, speed, sibling, beside = call(
        functools.partial(first_finish, listed),
        "first_far",
        [totals, lists, held(far_rows, slots), held(3 * tiles, slots), held(3 * tiles, slots), held(edge, slots), held(edge, slots)],
        [(vmem, packed), (fetched, aligned), (fetched, offset)]
        + [(vmem, value) for value in (total, target, near_weight, speed)],
        tools(far_rows, 4) + [sums_scratch],
        work,
        {3: 0},
    )
    sibling = swapped(sibling, 0)
    aligned, offset = gathered(beside)
    total, target = call(
        functools.partial(begin, listed, False),
        "second_near",
        [totals, targets],
        [(vmem, value) for value in (place, sibling, near_lists, near_weight)],
        tools(near_rows, 3),
        work,
    )
    _, state, sibling, beside, after_first = call(
        functools.partial(second_finish, total_tiles),
        "second_far",
        [
            totals,
            held(6, tiles, slots),
            held(6 * half, slots),
            held(6 * half, slots),
            jax.ShapeDtypeStruct((6, capacity, slots), jnp.float32),
        ],
        [(smem, curve_cuts), (vmem, place), (fetched, aligned), (fetched, offset)]
        + [(vmem, value) for value in (total, target, near_weight, speed, sibling, far_lists, far_weight)],
        tools(far_rows, 3) + [sums_scratch, pool_scratch],
        work,
        {4: 0},
    )
    (after_second,) = call(
        functools.partial(third_kernel, total_tiles),
        "place",
        [jax.ShapeDtypeStruct((6, capacity, slots), jnp.float32)],
        [(smem, curve_cuts), (vmem, swapped(sibling, 0)), (vmem, state), (vmem, swapped(beside, 1, wrap=False))],
        [pool_scratch],
    )
    return (jnp.transpose(after_first, (1, 0, 2)), jnp.transpose(after_second, (1, 0, 2)))


def solution(mesh):
    in_specs = (P(AXES, None, None), P(AXES), P(AXES, None), P())
    out_specs = (P(AXES, None, None), P(AXES, None, None))
    return jax.shard_map(body, mesh=mesh, in_specs=in_specs, out_specs=out_specs, check_vma=False)
```

```python
import functools

import jax
import jax.numpy as jnp
from jax import lax
from jax.experimental import pallas as pl
from jax.experimental.pallas import tpu as pltpu
from jax.sharding import PartitionSpec as P

AXES = ("gx", "gy")
STEPS = 2

soften = 0.05
time_step = 0.5
reach = 2
chunk = 4
units = 4
feature_rows = 32
far_norm = 1e36
lanes = 128
vmem_limit = 16 << 20


def swapped(value, first, stride=1, wrap=True):
    count = lax.axis_size(AXES)
    pairs = []
    for start in range(first, count, 2 * stride):
        for lower in range(start, start + stride):
            if wrap or lower + stride < count:
                upper = (lower + stride) % count
                pairs += [(lower, upper), (upper, lower)]
    return lax.ppermute(value, AXES, pairs)


def round_up(value, step):
    return -(-value // step) * step


def device_index():
    return lax.axis_index("gx") * lax.axis_size("gy") + lax.axis_index("gy")


def pieces(value, count):
    parts = []
    rest = value
    for _ in range(count - 1):
        part = rest.astype(jnp.bfloat16).astype(jnp.float32)
        parts.append(part)
        rest = rest - part
    parts.append(rest.astype(jnp.bfloat16).astype(jnp.float32))
    return parts


def pack_kernel(total_tiles, particles_ref, occupancy_ref, neighbours_ref, packed_ref, speed_ref):
    tiles, slots = (particles_ref.shape[0], particles_ref.shape[2])
    listed = neighbours_ref.shape[1]
    for row in range(3):
        packed_ref[row * tiles : (row + 1) * tiles, :] = particles_ref[:, row, :]
        speed_ref[row * tiles : (row + 1) * tiles, :] = particles_ref[:, 3 + row, :]
    tile_ids = lax.broadcasted_iota(jnp.int32, (tiles, listed), 0)
    offsets = neighbours_ref[...] - (device_index() * tiles + tile_ids)
    offsets = jnp.where(offsets < 0, offsets + total_tiles, offsets)
    packed_ref[3 * tiles :, :] = jnp.zeros((tiles, slots), jnp.float32)
    packed_ref[3 * tiles :, :listed] = offsets.astype(jnp.float32)
    for tile in range(tiles):
        live = occupancy_ref[tile].astype(jnp.float32)
        packed_ref[3 * tiles + tile : 3 * tiles + tile + 1, listed : listed + 1] = jnp.full((1, 1), live)


def places_of(index, tiles, offsets):
    place = index + offsets[0]
    for block in range(1, len(offsets)):
        place = jnp.where(index >= block * tiles, index - block * tiles + offsets[block], place)
    return jnp.where(index >= len(offsets) * tiles, -1000.0, place)


def build_lists(aux, own, tiles, listed, offsets):
    rows = aux.shape[0]
    dummy = len(offsets) * tiles
    index = lax.broadcasted_iota(jnp.int32, (rows, lanes), 0).astype(jnp.float32)
    lane = lax.broadcasted_iota(jnp.int32, (rows, lanes), 1).astype(jnp.float32)
    place = places_of(index, tiles, offsets)
    mask = place == lane
    for entry in range(listed):
        mask = mask | (place + aux[:, entry : entry + 1] == lane)
    own_rows = own.shape[0]
    own_index = lax.broadcasted_iota(jnp.int32, (own_rows, lanes), 0).astype(jnp.float32)
    own_lane = lax.broadcasted_iota(jnp.int32, (own_rows, lanes), 1).astype(jnp.float32)
    own_place = places_of(own_lane, tiles, offsets)
    listing = own_index + own[:, 0:1] == own_place
    for entry in range(1, listed):
        listing = listing | (own_index + own[:, entry : entry + 1] == own_place)
    listing = jnp.where(listing, 1.0, 0.0)
    listing = jnp.concatenate([listing, jnp.zeros((lanes - own_rows, lanes), jnp.float32)], axis=0)
    listing = jnp.transpose(listing)[:rows]
    mask = jnp.maximum(jnp.where(mask, 1.0, 0.0), listing)
    mask = jnp.where((lane < tiles) & (index < dummy), mask, 0.0)
    earlier = lax.broadcasted_iota(jnp.int32, (rows, rows), 1) < lax.broadcasted_iota(jnp.int32, (rows, rows), 0)
    rank = jnp.dot(
        jnp.where(earlier, 1.0, 0.0).astype(jnp.bfloat16),
        mask.astype(jnp.bfloat16),
        preferred_element_type=jnp.float32,
    )
    key = jnp.where(mask > 0.5, rank, -1.0)
    counts = jnp.sum(mask, axis=0, keepdims=True)
    lists = []
    for tile in range(tiles):
        hit = key[:, tile : tile + 1] == lane
        lists.append(jnp.sum(jnp.where(hit, index - dummy, 0.0), axis=0, keepdims=True) + dummy)
    lists.append(jnp.full((1, lanes), float(dummy)))
    lists.append(counts)
    return [row.astype(jnp.int32) for row in lists]


def middles(own_place):
    return [jnp.mean(axis[:8], keepdims=True) for axis in own_place]


def build_sources(places, middle, weight, feature_ref, moment_ref, source_ref):
    rows = weight.shape[0]
    ones = jnp.ones_like(weight)
    zeros = jnp.zeros_like(weight)
    features = []
    norm = zeros
    for axis in range(3):
        value = weight * (places[axis] - middle[axis])
        norm = norm + value * value
        moment_ref[:rows, axis, :] = value
        high, mid, low = pieces(value, 3)
        features += [high, high, mid, mid, high, low]
    features += pieces(jnp.where(weight > 0.5, norm, far_norm), 3) + [ones] * 3
    features += [zeros] * (feature_rows - len(features))
    for row, value in enumerate(features):
        feature_ref[:rows, row, :] = value
    for tile in range(rows):
        source_ref[tile] = feature_ref[tile].astype(jnp.bfloat16)


def build_targets(own_place, middle, feature_ref, target_ref):
    tiles = own_place[0].shape[0]
    ones = jnp.ones_like(own_place[0])
    zeros = jnp.zeros_like(own_place[0])
    features = []
    norm = zeros
    for axis in range(3):
        value = own_place[axis] - middle[axis]
        norm = norm + value * value
        high, mid, low = [-2.0 * part for part in pieces(value, 3)]
        features += [high, mid, high, mid, low, high]
    features += [ones] * 3 + pieces(norm + soften, 3)
    features += [zeros] * (feature_rows - len(features))
    for row, value in enumerate(features):
        feature_ref[:tiles, row, :] = value
    blank = jnp.zeros((lanes - feature_rows, lanes), jnp.float32)
    for tile in range(tiles):
        block = jnp.concatenate([feature_ref[tile], blank], axis=0)
        target_ref[tile] = jnp.transpose(block)[:, :feature_rows].astype(jnp.bfloat16)
    target_ref[tiles] = target_ref[0]


def accumulate(tiles, lists_ref, source_ref, target_ref, moment_ref, total_ref):
    chunk_counts = [(lists_ref[tiles + 1, tile] + chunk - 1) // chunk for tile in range(tiles)]
    chunk_total = functools.reduce(lambda left, right: left + right, [jnp.maximum(count, 1) for count in chunk_counts])

    def following(tile, part):
        more = (part + 1) * chunk < lists_ref[tiles + 1, tile]
        return (jnp.where(more, tile, jnp.minimum(tile + 1, tiles)), jnp.where(more, part + 1, 0))

    def sources_of(tile, part):
        return [lists_ref[tile, part * chunk + entry] for entry in range(chunk)]

    def distances(tile, sources):
        target = target_ref[tile]
        features = [source_ref[source] for source in sources]
        return [
            jnp.dot(target, jnp.concatenate(features[first : first + 2], axis=1), preferred_element_type=jnp.float32)
            for first in range(0, chunk, 2)
        ]

    def kernels(tile, places, squares):
        for first in range(0, lanes, 8):
            strip = slice(first, first + 8)
            sums = [total_ref[tile, row, strip, :] for row in range(4)]
            for entry in range(chunk):
                column = (entry % 2) * lanes
                inverse = lax.rsqrt(squares[entry // 2][strip, column : column + lanes])
                kernel = inverse * inverse * inverse
                for axis in range(3):
                    sums[axis] = sums[axis] + kernel * places[entry][axis]
                sums[3] = sums[3] + kernel
            for row in range(4):
                total_ref[tile, row, strip, :] = sums[row]

    def step(_, carry):
        tile, part = carry
        waiting = None
        for _ in range(units):
            sources = sources_of(tile, part)
            places = [
                [jnp.broadcast_to(moment_ref[source, axis : axis + 1, :], (8, lanes)) for axis in range(3)]
                for source in sources
            ]
            item = (tile, places, distances(tile, sources))
            if waiting is not None:
                kernels(*waiting)
            waiting = item
            tile, part = following(tile, part)
        kernels(*waiting)
        return (tile, part)

    zero = jnp.int32(0)
    lax.fori_loop(0, (chunk_total + units - 1) // units, step, (zero, zero))


def advance(middle, place_own, speed_own, weight_own, total_ref, sums_ref):
    tiles = weight_own.shape[0]
    for tile in range(tiles):
        for row in range(4):
            sums_ref[row, tile : tile + 1, :] = jnp.sum(jnp.transpose(total_ref[tile, row]), axis=0, keepdims=True)
    zeroth = sums_ref[3, :tiles, :]
    places, speeds = ([], [])
    for axis in range(3):
        force = sums_ref[axis, :tiles, :] - (place_own[axis] - middle[axis]) * zeroth
        speeds.append(weight_own * (speed_own[axis] + time_step * force / lanes))
        places.append(weight_own * (place_own[axis] + time_step * speeds[axis]))
    return places, speeds


def part_of(ref, tiles, row):
    return ref[row * tiles : (row + 1) * tiles, :]


def fill_planes(planes, tiles, blocks):
    kinds, rows, slots = planes.shape
    filled = len(blocks) * tiles
    planes[:, filled:, :] = jnp.zeros((kinds, rows - filled, slots), jnp.float32)
    for block, ref in enumerate(blocks):
        for kind in range(kinds):
            planes[kind, block * tiles : (block + 1) * tiles, :] = part_of(ref, tiles, kind)


def weights_of(aux, listed):
    slot = lax.broadcasted_iota(jnp.int32, aux.shape, 1).astype(jnp.float32)
    return jnp.where(slot < aux[:, listed : listed + 1], 1.0, 0.0)


def offsets_of(tiles, near_pair):
    device = device_index()
    toward = jnp.where(device % 2 == 0, 1.0, -1.0) * float(tiles)
    if near_pair:
        return [0.0, toward]
    across = jnp.where(device % (2 * reach) < reach, 1.0, -1.0) * float(reach * tiles)
    return [across, -toward, -across]


def prepare(first, near_pair, listed, own_ref, blocks, lists_ref, weight_ref, tools):
    planes, scalars, copy_sem, feature_ref, moment_ref, source_ref = tools
    tiles = own_ref.shape[0] // planes.shape[0]
    if not first:
        copy = pltpu.make_async_copy(lists_ref, scalars, copy_sem)
        copy.start()
    fill_planes(planes, tiles, blocks)
    if first:
        aux = planes[3]
        own_aux = jnp.concatenate(
            [part_of(own_ref, tiles, 3), jnp.zeros((round_up(tiles, 8) - tiles, lanes), jnp.float32)], axis=0
        )
        for row, value in enumerate(build_lists(aux, own_aux, tiles, listed, offsets_of(tiles, near_pair))):
            lists_ref[row : row + 1, :] = value
        copy = pltpu.make_async_copy(lists_ref, scalars, copy_sem)
        copy.start()
        weight_ref[...] = weights_of(aux, listed)
    middle = middles([part_of(own_ref, tiles, axis) for axis in range(3)])
    build_sources([planes[axis] for axis in range(3)], middle, weight_ref[...], feature_ref, moment_ref, source_ref)
    return middle, copy


def begin(listed, first, *refs):
    if first:
        own_ref, sibling_ref, total_ref, target_ref, lists_ref, weight_ref, *scratch = refs
    else:
        own_ref, sibling_ref, lists_ref, weight_ref, total_ref, target_ref, *scratch = refs
    tools = scratch
    tiles = own_ref.shape[0] // tools[0].shape[0]
    middle, copy = prepare(first, True, listed, own_ref, (own_ref, sibling_ref), lists_ref, weight_ref, tools)
    build_targets([part_of(own_ref, tiles, axis) for axis in range(3)], middle, tools[3], target_ref)
    total_ref[...] = jnp.zeros(total_ref.shape, jnp.float32)
    copy.wait()
    accumulate(tiles, tools[1], tools[5], target_ref, tools[4], total_ref)


def halves(speed, even, half):
    first, last = (speed[:half], speed[half:])
    return jnp.where(even, last, first), jnp.where(even, first, last)


def first_finish(
    listed, own_ref, aligned, beside, offset, total_in, target_ref, weight_own_ref, speed_ref, *refs
):
    total_ref, lists_ref, weight_ref, place_out, speed_out, sibling_out, beside_out, *scratch = refs
    *tools, sums_ref = scratch
    tiles = own_ref.shape[0] // tools[0].shape[0]
    half = tiles // 2
    middle, copy = prepare(True, False, listed, own_ref, (aligned, beside, offset), lists_ref, weight_ref, tools)
    copy.wait()
    accumulate(tiles, tools[1], tools[5], target_ref, tools[4], total_ref)
    places, speeds = advance(
        middle,
        [part_of(own_ref, tiles, axis) for axis in range(3)],
        [part_of(speed_ref, tiles, axis) for axis in range(3)],
        weight_own_ref[:tiles, :],
        total_ref,
        sums_ref,
    )
    even = device_index() % 2 == 0
    for axis in range(3):
        strip = slice(axis * tiles, (axis + 1) * tiles)
        place_out[strip, :] = places[axis]
        speed_out[strip, :] = speeds[axis]
        sibling_out[strip, :] = places[axis]
        beside_out[strip, :] = places[axis]
        strip = slice(3 * tiles + axis * half, 3 * tiles + (axis + 1) * half)
        sibling_out[strip, :], beside_out[strip, :] = halves(speeds[axis], even, half)


def second_finish(
    total_tiles,
    cuts_ref,
    own_ref,
    aligned,
    beside,
    offset,
    total_in,
    target_ref,
    weight_own_ref,
    speed_ref,
    sibling_ref,
    lists_ref,
    weight_ref,
    total_ref,
    state_ref,
    sibling_out,
    beside_out,
    out_ref,
    *scratch
):
    *tools, sums_ref, pool_ref = scratch
    tiles = own_ref.shape[0] // 3
    half = tiles // 2
    middle, copy = prepare(False, False, None, own_ref, (aligned, beside, offset), lists_ref, weight_ref, tools)
    copy.wait()
    accumulate(tiles, tools[1], tools[5], target_ref, tools[4], total_ref)
    place_own = [part_of(own_ref, tiles, axis) for axis in range(3)]
    speed_own = [part_of(speed_ref, tiles, axis) for axis in range(3)]
    places, speeds = advance(middle, place_own, speed_own, weight_own_ref[:tiles, :], total_ref, sums_ref)
    even = device_index() % 2 == 0
    for row, value in enumerate(places + speeds):
        state_ref[row] = value
        strip = slice(row * half, (row + 1) * half)
        sibling_out[strip, :], beside_out[strip, :] = halves(value, even, half)
    lower, upper = ([], [])
    for row in range(6):
        if row < 3:
            sides = [part_of(ref, tiles, row) for ref in (sibling_ref, beside)]
            low_sides, high_sides = ([side[tiles - half :] for side in sides], [side[:half] for side in sides])
        else:
            strip = slice(3 * tiles + (row - 3) * half, 3 * tiles + (row - 2) * half)
            low_sides = high_sides = [ref[strip, :] for ref in (sibling_ref, beside)]
        lower.append(jnp.where(even, low_sides[1], low_sides[0]))
        upper.append(jnp.where(even, high_sides[0], high_sides[1]))
    place_rows(0, total_tiles, cuts_ref, lower, place_own + speed_own, upper, pool_ref, out_ref)


def place_rows(step, total_tiles, cuts_ref, lower, own, upper, pool_ref, out_ref):
    tiles, slots = own[0].shape
    half = tiles // 2
    capacity = out_ref.shape[1]
    device = device_index()
    last = cuts_ref.shape[1] - 1
    first_tile = cuts_ref[step, device]
    next_tile = jnp.where(device == last, total_tiles, cuts_ref[step, jnp.minimum(device + 1, last)])
    owned = next_tile - first_tile
    start = first_tile - (device * tiles - half)
    filled = lax.broadcasted_iota(jnp.int32, (capacity, slots), 0) < owned
    for row in range(6):
        pool_ref[row, :half, :] = lower[row]
        pool_ref[row, half : half + tiles, :] = own[row]
        pool_ref[row, half + tiles : 2 * tiles, :] = upper[row]
    for row in range(6):
        out_ref[row] = jnp.where(filled, pool_ref[row, pl.ds(start, capacity), :], 0.0)


def third_kernel(total_tiles, cuts_ref, sibling_ref, own_ref, beside_ref, out_ref, pool_ref):
    half = own_ref.shape[1] // 2
    even = device_index() % 2 == 0
    lower, upper = ([], [])
    for row in range(6):
        sibling, beside = (part_of(sibling_ref, half, row), part_of(beside_ref, half, row))
        lower.append(jnp.where(even, beside, sibling))
        upper.append(jnp.where(even, sibling, beside))
    place_rows(1, total_tiles, cuts_ref, lower, [own_ref[row] for row in range(6)], upper, pool_ref, out_ref)


def far(value):
    return pltpu.with_memory_space_constraint(value, pltpu.HBM)


def near(value):
    return pltpu.with_memory_space_constraint(value, pltpu.VMEM)


def body(particles, occupancy, neighbours, curve_cuts):
    tiles, _, slots = particles.shape
    listed = neighbours.shape[1]
    total_tiles = tiles * lax.axis_size(AXES)
    half = tiles // 2
    capacity = 2 * tiles
    near_rows = round_up(2 * tiles + 1, 8)
    far_rows = round_up((reach + 1) * tiles + 1, 8)
    list_rows = round_up(tiles + 2, 8)
    vmem = pl.BlockSpec(memory_space=pltpu.VMEM)
    smem = pl.BlockSpec(memory_space=pltpu.SMEM)

    def held(*sizes, dtype=jnp.float32):
        return pltpu.VMEM(sizes, dtype)

    def call(kernel, name, outs, ins, scratch, flops=0, aliases=None):
        held_ins = [far(value) if kind is smem else near(value) for kind, value in ins]
        return pl.pallas_call(
            kernel,
            out_shape=outs,
            in_specs=[kind for kind, _ in ins],
            out_specs=[vmem] * len(outs),
            scratch_shapes=scratch,
            input_output_aliases=aliases or {},
            compiler_params=pltpu.CompilerParams(vmem_limit_bytes=vmem_limit),
            cost_estimate=pl.CostEstimate(flops=flops, bytes_accessed=1 << 20, transcendentals=0),
            name=name,
        )(*held_ins)

    def tools(rows, kinds):
        return [
            pltpu.VMEM((kinds, rows, slots), jnp.float32),
            pltpu.SMEM((list_rows, lanes), jnp.int32),
            pltpu.SemaphoreType.DMA,
            pltpu.VMEM((rows, feature_rows, lanes), jnp.float32),
            pltpu.VMEM((rows, 8, lanes), jnp.float32),
            pltpu.VMEM((rows, feature_rows, lanes), jnp.bfloat16),
        ]

    packed, speed = pl.pallas_call(
        functools.partial(pack_kernel, total_tiles),
        out_shape=(held(4 * tiles, slots), held(3 * tiles, slots)),
        in_specs=[vmem, smem, vmem],
        out_specs=(vmem, vmem),
        compiler_params=pltpu.CompilerParams(vmem_limit_bytes=vmem_limit),
        name="pack",
    )(far(particles), far(occupancy), far(neighbours))
    pool_scratch = pltpu.VMEM((6, round_up(capacity + tiles, 8), slots), jnp.float32)
    sums_scratch = pltpu.VMEM((4, round_up(tiles, 8), lanes), jnp.float32)
    totals = held(tiles + 1, 4, lanes, lanes)
    targets = held(tiles + 1, lanes, feature_rows, dtype=jnp.bfloat16)
    lists = held(list_rows, lanes, dtype=jnp.int32)
    edge = 3 * tiles + 3 * half
    work = 1 << 32

    sibling = swapped(packed, 0)
    beside, aligned, offset = (swapped(packed, 1), swapped(packed, 0, reach), swapped(packed, reach, reach))
    total, target, near_lists, near_weight = call(
        functools.partial(begin, listed, True),
        "first_near",
        [totals, targets, lists, held(near_rows, slots)],
        [(vmem, packed), (vmem, sibling)],
        tools(near_rows, 4),
        work,
    )
    total, far_lists, far_weight, place, speed, sibling, beside = call(
        functools.partial(first_finish, listed),
        "first_far",
        [totals, lists, held(far_rows, slots), held(3 * tiles, slots), held(3 * tiles, slots), held(edge, slots), held(edge, slots)],
        [(vmem, value) for value in (packed, aligned, beside, offset, total, target, near_weight, speed)],
        tools(far_rows, 4) + [sums_scratch],
        work,
        {4: 0},
    )
    sibling = swapped(sibling, 0)
    beside, aligned, offset = (swapped(beside, 1), swapped(place, 0, reach), swapped(place, reach, reach))
    total, target = call(
        functools.partial(begin, listed, False),
        "second_near",
        [totals, targets],
        [(vmem, value) for value in (place, sibling, near_lists, near_weight)],
        tools(near_rows, 3),
        work,
    )
    _, state, sibling, beside, after_first = call(
        functools.partial(second_finish, total_tiles),
        "second_far",
        [
            totals,
            held(6, tiles, slots),
            held(6 * half, slots),
            held(6 * half, slots),
            jax.ShapeDtypeStruct((6, capacity, slots), jnp.float32),
        ],
        [(smem, curve_cuts)]
        + [
            (vmem, value)
            for value in (place, aligned, beside, offset, total, target, near_weight, speed, sibling, far_lists, far_weight)
        ],
        tools(far_rows, 3) + [sums_scratch, pool_scratch],
        work,
        {5: 0},
    )
    (after_second,) = call(
        functools.partial(third_kernel, total_tiles),
        "place",
        [jax.ShapeDtypeStruct((6, capacity, slots), jnp.float32)],
        [(smem, curve_cuts), (vmem, swapped(sibling, 0)), (vmem, state), (vmem, swapped(beside, 1, wrap=False))],
        [pool_scratch],
    )
    return (jnp.transpose(after_first, (1, 0, 2)), jnp.transpose(after_second, (1, 0, 2)))


def solution(mesh):
    in_specs = (P(AXES, None, None), P(AXES), P(AXES, None), P())
    out_specs = (P(AXES, None, None), P(AXES, None, None))
    return jax.shard_map(body, mesh=mesh, in_specs=in_specs, out_specs=out_specs, check_vma=False)
```

```python
import functools

import jax
import jax.numpy as jnp
from jax import lax
from jax.experimental import pallas as pl
from jax.experimental.pallas import tpu as pltpu
from jax.sharding import PartitionSpec as P

AXES = ("gx", "gy")
STEPS = 2

soften = 0.05
time_step = 0.5
reach = 2
chunk = 4
units = 8
feature_rows = 32
far_norm = 1e36
lanes = 128
block_rows = 64
vmem_limit = 16 << 20


def swapped(value, first, stride=1, wrap=True):
    count = lax.axis_size(AXES)
    pairs = []
    for start in range(first, count, 2 * stride):
        for lower in range(start, start + stride):
            if wrap or lower + stride < count:
                upper = (lower + stride) % count
                pairs += [(lower, upper), (upper, lower)]
    return lax.ppermute(value, AXES, pairs)


def round_up(value, step):
    return -(-value // step) * step


def device_index():
    return lax.axis_index("gx") * lax.axis_size("gy") + lax.axis_index("gy")


def pieces(value, count):
    parts = []
    rest = value
    for _ in range(count - 1):
        part = rest.astype(jnp.bfloat16).astype(jnp.float32)
        parts.append(part)
        rest = rest - part
    parts.append(rest.astype(jnp.bfloat16).astype(jnp.float32))
    return parts


def pack_kernel(total_tiles, particles_ref, occupancy_ref, neighbours_ref, packed_ref, speed_ref):
    tiles, slots = (particles_ref.shape[0], particles_ref.shape[2])
    listed = neighbours_ref.shape[1]
    for row in range(3):
        packed_ref[row * tiles : (row + 1) * tiles, :] = particles_ref[:, row, :]
        speed_ref[row * tiles : (row + 1) * tiles, :] = particles_ref[:, 3 + row, :]
    tile_ids = lax.broadcasted_iota(jnp.int32, (tiles, listed), 0)
    offsets = neighbours_ref[...] - (device_index() * tiles + tile_ids)
    offsets = jnp.where(offsets < 0, offsets + total_tiles, offsets)
    packed_ref[3 * tiles :, :] = jnp.zeros((tiles, slots), jnp.float32)
    packed_ref[3 * tiles :, :listed] = offsets.astype(jnp.float32)
    for tile in range(tiles):
        live = occupancy_ref[tile].astype(jnp.float32)
        packed_ref[3 * tiles + tile : 3 * tiles + tile + 1, listed : listed + 1] = jnp.full((1, 1), live)


def places_of(index, tiles, offsets):
    place = index + offsets[0]
    for block in range(1, len(offsets)):
        place = jnp.where(index >= block * tiles, index - block * tiles + offsets[block], place)
    return jnp.where(index >= len(offsets) * tiles, -1000.0, place)


def build_lists(aux, own, tiles, listed, offsets):
    rows = aux.shape[0]
    dummy = len(offsets) * tiles
    index = lax.broadcasted_iota(jnp.int32, (rows, lanes), 0).astype(jnp.float32)
    lane = lax.broadcasted_iota(jnp.int32, (rows, lanes), 1).astype(jnp.float32)
    place = places_of(index, tiles, offsets)
    mask = place == lane
    for entry in range(listed):
        mask = mask | (place + aux[:, entry : entry + 1] == lane)
    own_rows = own.shape[0]
    own_index = lax.broadcasted_iota(jnp.int32, (own_rows, lanes), 0).astype(jnp.float32)
    own_lane = lax.broadcasted_iota(jnp.int32, (own_rows, lanes), 1).astype(jnp.float32)
    own_place = places_of(own_lane, tiles, offsets)
    listing = own_index + own[:, 0:1] == own_place
    for entry in range(1, listed):
        listing = listing | (own_index + own[:, entry : entry + 1] == own_place)
    listing = jnp.where(listing, 1.0, 0.0)
    listing = jnp.concatenate([listing, jnp.zeros((lanes - own_rows, lanes), jnp.float32)], axis=0)
    listing = jnp.transpose(listing)[:rows]
    mask = jnp.maximum(jnp.where(mask, 1.0, 0.0), listing)
    mask = jnp.where((lane < tiles) & (index < dummy), mask, 0.0)
    earlier = lax.broadcasted_iota(jnp.int32, (rows, rows), 1) < lax.broadcasted_iota(jnp.int32, (rows, rows), 0)
    rank = jnp.dot(
        jnp.where(earlier, 1.0, 0.0).astype(jnp.bfloat16),
        mask.astype(jnp.bfloat16),
        preferred_element_type=jnp.float32,
    )
    key = jnp.where(mask > 0.5, rank, -1.0)
    counts = jnp.sum(mask, axis=0, keepdims=True)
    lists = []
    for tile in range(tiles):
        hit = key[:, tile : tile + 1] == lane
        row = jnp.sum(jnp.where(hit, index - dummy, 0.0), axis=0, keepdims=True) + dummy
        live = own[tile : tile + 1, listed : listed + 1]
        blocks = jnp.full((1, 1), 1.0)
        for filled in range(block_rows, lanes, block_rows):
            blocks = blocks + jnp.where(live > filled, 1.0, 0.0)
        lists.append(jnp.where(lane[:1] == lanes - 1, blocks, row))
    lists.append(jnp.where(lane[:1] == lanes - 1, 1.0, float(dummy)))
    lists.append(counts)
    return [row.astype(jnp.int32) for row in lists]


def middles(own_place):
    return [jnp.mean(axis[:8], keepdims=True) for axis in own_place]


def feature_of(feature_ref, tile):
    return feature_ref[tile * feature_rows : (tile + 1) * feature_rows, :]


def build_sources(places, middle, weight, feature_ref, moment_ref, source_ref):
    rows = weight.shape[0]
    ones = jnp.ones_like(weight)
    zeros = jnp.zeros_like(weight)
    features = []
    norm = zeros
    for axis in range(3):
        value = weight * (places[axis] - middle[axis])
        norm = norm + value * value
        moment_ref.reshape(rows * 8, lanes)[pl.ds(axis, rows, 8), :] = value
        high, mid, low = pieces(value, 3)
        features += [high, high, mid, mid, high, low]
    features += pieces(jnp.where(weight > 0.5, norm, far_norm), 3) + [ones] * 3
    features += [zeros] * (feature_rows - len(features))
    for row, value in enumerate(features):
        feature_ref[pl.ds(row, rows, feature_rows), :] = value
    for tile in range(rows):
        source_ref[tile] = feature_of(feature_ref, tile).astype(jnp.bfloat16)


def build_targets(own_place, middle, feature_ref, target_ref):
    tiles = own_place[0].shape[0]
    ones = jnp.ones_like(own_place[0])
    zeros = jnp.zeros_like(own_place[0])
    features = []
    norm = zeros
    for axis in range(3):
        value = own_place[axis] - middle[axis]
        norm = norm + value * value
        high, mid, low = [-2.0 * part for part in pieces(value, 3)]
        features += [high, mid, high, mid, low, high]
    features += [ones] * 3 + pieces(norm + soften, 3)
    features += [zeros] * (feature_rows - len(features))
    for row, value in enumerate(features):
        feature_ref[pl.ds(row, tiles, feature_rows), :] = value
    blank = jnp.zeros((lanes - feature_rows, lanes), jnp.float32)
    blocks = lanes // block_rows
    for tile in range(tiles):
        turned = jnp.transpose(jnp.concatenate([feature_of(feature_ref, tile), blank], axis=0))
        turned = turned[:, :feature_rows].astype(jnp.bfloat16)
        for block in range(blocks):
            target_ref[tile * blocks + block] = turned[block * block_rows : (block + 1) * block_rows]
    target_ref[tiles * blocks] = target_ref[0]


def accumulate(tiles, lists_ref, source_ref, target_ref, moment_ref, total_ref):
    blocks = lanes // block_rows
    item_counts = [
        jnp.maximum((lists_ref[tiles + 1, tile] + chunk - 1) // chunk, 1) * lists_ref[tile, lanes - 1] for tile in range(tiles)
    ]
    item_total = functools.reduce(lambda left, right: left + right, item_counts)

    def following(tile, block, part):
        more = (part + 1) * chunk < lists_ref[tiles + 1, tile]
        again = block + 1 < lists_ref[tile, lanes - 1]
        return (
            jnp.where(more | again, tile, jnp.minimum(tile + 1, tiles)),
            jnp.where(more, block, jnp.where(again, block + 1, 0)),
            jnp.where(more, part + 1, 0),
        )

    def sources_of(tile, part):
        return [lists_ref[tile, part * chunk + entry] for entry in range(chunk)]

    def distances(spot, sources):
        target = target_ref[spot]
        features = [source_ref[source] for source in sources]
        return [
            jnp.dot(target, jnp.concatenate(features[first : first + 2], axis=1), preferred_element_type=jnp.float32)
            for first in range(0, chunk, 2)
        ]

    def kernels(spot, places, squares):
        for first in range(0, block_rows, 8):
            strip = slice(first, first + 8)
            sums = [total_ref[spot, row, strip, :] for row in range(4)]
            for entry in range(chunk):
                column = (entry % 2) * lanes
                inverse = lax.rsqrt(squares[entry // 2][strip, column : column + lanes])
                kernel = inverse * inverse * inverse
                for axis in range(3):
                    sums[axis] = sums[axis] + kernel * places[entry][axis]
                sums[3] = sums[3] + kernel
            for row in range(4):
                total_ref[spot, row, strip, :] = sums[row]

    def step(_, carry):
        tile, block, part = carry
        waiting = None
        for _ in range(units):
            sources = sources_of(tile, part)
            places = [
                [jnp.broadcast_to(moment_ref[source, axis : axis + 1, :], (8, lanes)) for axis in range(3)]
                for source in sources
            ]
            spot = tile * blocks + block
            item = (spot, places, distances(spot, sources))
            if waiting is not None:
                kernels(*waiting)
            waiting = item
            tile, block, part = following(tile, block, part)
        kernels(*waiting)
        return (tile, block, part)

    zero = jnp.int32(0)
    lax.fori_loop(0, (item_total + units - 1) // units, step, (zero, zero, zero))


def advance(middle, place_own, speed_own, weight_own, total_ref, sums_ref):
    tiles = weight_own.shape[0]
    blocks = lanes // block_rows
    for tile in range(tiles):
        for row in range(4):
            parts = [total_ref[tile * blocks + block, row] for block in range(blocks)]
            total = jnp.sum(jnp.transpose(jnp.concatenate(parts, axis=0)), axis=0, keepdims=True)
            sums_ref[row, tile : tile + 1, :] = total
    zeroth = sums_ref[3, :tiles, :]
    places, speeds = ([], [])
    for axis in range(3):
        force = sums_ref[axis, :tiles, :] - (place_own[axis] - middle[axis]) * zeroth
        speeds.append(weight_own * (speed_own[axis] + time_step * force / lanes))
        places.append(weight_own * (place_own[axis] + time_step * speeds[axis]))
    return places, speeds


def part_of(ref, tiles, row):
    return ref[row * tiles : (row + 1) * tiles, :]


def fill_planes(planes, tiles, blocks):
    kinds, rows, slots = planes.shape
    filled = len(blocks) * tiles
    planes[:, filled:, :] = jnp.zeros((kinds, rows - filled, slots), jnp.float32)
    for block, ref in enumerate(blocks):
        for kind in range(kinds):
            planes[kind, block * tiles : (block + 1) * tiles, :] = part_of(ref, tiles, kind)


def weights_of(aux, listed):
    slot = lax.broadcasted_iota(jnp.int32, aux.shape, 1).astype(jnp.float32)
    return jnp.where(slot < aux[:, listed : listed + 1], 1.0, 0.0)


def offsets_of(tiles, near_pair):
    device = device_index()
    toward = jnp.where(device % 2 == 0, 1.0, -1.0) * float(tiles)
    if near_pair:
        return [0.0, toward]
    across = jnp.where(device % (2 * reach) < reach, 1.0, -1.0) * float(reach * tiles)
    return [across, -toward, -across]


def prepare(first, near_pair, listed, own_ref, blocks, lists_ref, weight_ref, tools):
    planes, scalars, copy_sem, feature_ref, moment_ref, source_ref = tools
    tiles = own_ref.shape[0] // planes.shape[0]
    if not first:
        copy = pltpu.make_async_copy(lists_ref, scalars, copy_sem)
        copy.start()
    fill_planes(planes, tiles, blocks)
    if first:
        aux = planes[3]
        own_aux = jnp.concatenate(
            [part_of(own_ref, tiles, 3), jnp.zeros((round_up(tiles, 8) - tiles, lanes), jnp.float32)], axis=0
        )
        for row, value in enumerate(build_lists(aux, own_aux, tiles, listed, offsets_of(tiles, near_pair))):
            lists_ref[row : row + 1, :] = value
        copy = pltpu.make_async_copy(lists_ref, scalars, copy_sem)
        copy.start()
        weight_ref[...] = weights_of(aux, listed)
    middle = middles([part_of(own_ref, tiles, axis) for axis in range(3)])
    build_sources([planes[axis] for axis in range(3)], middle, weight_ref[...], feature_ref, moment_ref, source_ref)
    return middle, copy


def begin(listed, first, *refs):
    if first:
        own_ref, sibling_ref, total_ref, target_ref, lists_ref, weight_ref, *scratch = refs
    else:
        own_ref, sibling_ref, lists_ref, weight_ref, total_ref, target_ref, *scratch = refs
    tools = scratch
    tiles = own_ref.shape[0] // tools[0].shape[0]
    middle, copy = prepare(first, True, listed, own_ref, (own_ref, sibling_ref), lists_ref, weight_ref, tools)
    build_targets([part_of(own_ref, tiles, axis) for axis in range(3)], middle, tools[3], target_ref)
    total_ref[...] = jnp.zeros(total_ref.shape, jnp.float32)
    copy.wait()
    accumulate(tiles, tools[1], tools[5], target_ref, tools[4], total_ref)


def halves(speed, even, half):
    first, last = (speed[:half], speed[half:])
    return jnp.where(even, last, first), jnp.where(even, first, last)


def first_finish(
    listed, own_ref, aligned, beside, offset, total_in, target_ref, weight_own_ref, speed_ref, *refs
):
    total_ref, lists_ref, weight_ref, place_out, speed_out, sibling_out, beside_out, *scratch = refs
    *tools, sums_ref = scratch
    tiles = own_ref.shape[0] // tools[0].shape[0]
    half = tiles // 2
    middle, copy = prepare(True, False, listed, own_ref, (aligned, beside, offset), lists_ref, weight_ref, tools)
    copy.wait()
    accumulate(tiles, tools[1], tools[5], target_ref, tools[4], total_ref)
    places, speeds = advance(
        middle,
        [part_of(own_ref, tiles, axis) for axis in range(3)],
        [part_of(speed_ref, tiles, axis) for axis in range(3)],
        weight_own_ref[:tiles, :],
        total_ref,
        sums_ref,
    )
    even = device_index() % 2 == 0
    for axis in range(3):
        strip = slice(axis * tiles, (axis + 1) * tiles)
        place_out[strip, :] = places[axis]
        speed_out[strip, :] = speeds[axis]
        sibling_out[strip, :] = places[axis]
        beside_out[strip, :] = places[axis]
        strip = slice(3 * tiles + axis * half, 3 * tiles + (axis + 1) * half)
        sibling_out[strip, :], beside_out[strip, :] = halves(speeds[axis], even, half)


def second_finish(
    total_tiles,
    cuts_ref,
    own_ref,
    aligned,
    beside,
    offset,
    total_in,
    target_ref,
    weight_own_ref,
    speed_ref,
    sibling_ref,
    lists_ref,
    weight_ref,
    total_ref,
    state_ref,
    sibling_out,
    beside_out,
    out_ref,
    *scratch
):
    *tools, sums_ref, pool_ref = scratch
    tiles = own_ref.shape[0] // 3
    half = tiles // 2
    middle, copy = prepare(False, False, None, own_ref, (aligned, beside, offset), lists_ref, weight_ref, tools)
    copy.wait()
    accumulate(tiles, tools[1], tools[5], target_ref, tools[4], total_ref)
    place_own = [part_of(own_ref, tiles, axis) for axis in range(3)]
    speed_own = [part_of(speed_ref, tiles, axis) for axis in range(3)]
    places, speeds = advance(middle, place_own, speed_own, weight_own_ref[:tiles, :], total_ref, sums_ref)
    even = device_index() % 2 == 0
    for row, value in enumerate(places + speeds):
        state_ref[row] = value
        strip = slice(row * half, (row + 1) * half)
        sibling_out[strip, :], beside_out[strip, :] = halves(value, even, half)
    lower, upper = ([], [])
    for row in range(6):
        if row < 3:
            sides = [part_of(ref, tiles, row) for ref in (sibling_ref, beside)]
            low_sides, high_sides = ([side[tiles - half :] for side in sides], [side[:half] for side in sides])
        else:
            strip = slice(3 * tiles + (row - 3) * half, 3 * tiles + (row - 2) * half)
            low_sides = high_sides = [ref[strip, :] for ref in (sibling_ref, beside)]
        lower.append(jnp.where(even, low_sides[1], low_sides[0]))
        upper.append(jnp.where(even, high_sides[0], high_sides[1]))
    place_rows(0, total_tiles, cuts_ref, lower, place_own + speed_own, upper, pool_ref, out_ref)


def place_rows(step, total_tiles, cuts_ref, lower, own, upper, pool_ref, out_ref):
    tiles, slots = own[0].shape
    half = tiles // 2
    capacity = out_ref.shape[1]
    device = device_index()
    last = cuts_ref.shape[1] - 1
    first_tile = cuts_ref[step, device]
    next_tile = jnp.where(device == last, total_tiles, cuts_ref[step, jnp.minimum(device + 1, last)])
    owned = next_tile - first_tile
    start = first_tile - (device * tiles - half)
    filled = lax.broadcasted_iota(jnp.int32, (capacity, slots), 0) < owned
    for row in range(6):
        pool_ref[row, :half, :] = lower[row]
        pool_ref[row, half : half + tiles, :] = own[row]
        pool_ref[row, half + tiles : 2 * tiles, :] = upper[row]
    for row in range(6):
        out_ref[row] = jnp.where(filled, pool_ref[row, pl.ds(start, capacity), :], 0.0)


def third_kernel(total_tiles, cuts_ref, sibling_ref, own_ref, beside_ref, out_ref, pool_ref):
    half = own_ref.shape[1] // 2
    even = device_index() % 2 == 0
    lower, upper = ([], [])
    for row in range(6):
        sibling, beside = (part_of(sibling_ref, half, row), part_of(beside_ref, half, row))
        lower.append(jnp.where(even, beside, sibling))
        upper.append(jnp.where(even, sibling, beside))
    place_rows(1, total_tiles, cuts_ref, lower, [own_ref[row] for row in range(6)], upper, pool_ref, out_ref)


def far(value):
    return pltpu.with_memory_space_constraint(value, pltpu.HBM)


def near(value):
    return pltpu.with_memory_space_constraint(value, pltpu.VMEM)


def body(particles, occupancy, neighbours, curve_cuts):
    tiles, _, slots = particles.shape
    listed = neighbours.shape[1]
    total_tiles = tiles * lax.axis_size(AXES)
    half = tiles // 2
    capacity = 2 * tiles
    near_rows = round_up(2 * tiles + 1, 8)
    far_rows = round_up((reach + 1) * tiles + 1, 8)
    list_rows = round_up(tiles + 2, 8)
    vmem = pl.BlockSpec(memory_space=pltpu.VMEM)
    smem = pl.BlockSpec(memory_space=pltpu.SMEM)

    def held(*sizes, dtype=jnp.float32):
        return pltpu.VMEM(sizes, dtype)

    def call(kernel, name, outs, ins, scratch, flops=0, aliases=None):
        held_ins = [far(value) if kind is smem else near(value) for kind, value in ins]
        return pl.pallas_call(
            kernel,
            out_shape=outs,
            in_specs=[kind for kind, _ in ins],
            out_specs=[vmem] * len(outs),
            scratch_shapes=scratch,
            input_output_aliases=aliases or {},
            compiler_params=pltpu.CompilerParams(vmem_limit_bytes=vmem_limit),
            cost_estimate=pl.CostEstimate(flops=flops, bytes_accessed=1 << 20, transcendentals=0),
            name=name,
        )(*held_ins)

    def tools(rows, kinds):
        return [
            pltpu.VMEM((kinds, rows, slots), jnp.float32),
            pltpu.SMEM((list_rows, lanes), jnp.int32),
            pltpu.SemaphoreType.DMA,
            pltpu.VMEM((rows * feature_rows, lanes), jnp.float32),
            pltpu.VMEM((rows, 8, lanes), jnp.float32),
            pltpu.VMEM((rows, feature_rows, lanes), jnp.bfloat16),
        ]

    packed, speed = pl.pallas_call(
        functools.partial(pack_kernel, total_tiles),
        out_shape=(held(4 * tiles, slots), held(3 * tiles, slots)),
        in_specs=[vmem, smem, vmem],
        out_specs=(vmem, vmem),
        compiler_params=pltpu.CompilerParams(vmem_limit_bytes=vmem_limit),
        name="pack",
    )(far(particles), far(occupancy), far(neighbours))
    pool_scratch = pltpu.VMEM((6, round_up(capacity + tiles, 8), slots), jnp.float32)
    sums_scratch = pltpu.VMEM((4, round_up(tiles, 8), lanes), jnp.float32)
    blocks = lanes // block_rows
    totals = held(tiles * blocks + 1, 4, block_rows, lanes)
    targets = held(tiles * blocks + 1, block_rows, feature_rows, dtype=jnp.bfloat16)
    lists = held(list_rows, lanes, dtype=jnp.int32)
    edge = 3 * tiles + 3 * half
    work = 1 << 32

    sibling = swapped(packed, 0)
    beside, aligned, offset = (swapped(packed, 1), swapped(packed, 0, reach), swapped(packed, reach, reach))
    total, target, near_lists, near_weight = call(
        functools.partial(begin, listed, True),
        "first_near",
        [totals, targets, lists, held(near_rows, slots)],
        [(vmem, packed), (vmem, sibling)],
        tools(near_rows, 4),
        work,
    )
    total, far_lists, far_weight, place, speed, sibling, beside = call(
        functools.partial(first_finish, listed),
        "first_far",
        [totals, lists, held(far_rows, slots), held(3 * tiles, slots), held(3 * tiles, slots), held(edge, slots), held(edge, slots)],
        [(vmem, value) for value in (packed, aligned, beside, offset, total, target, near_weight, speed)],
        tools(far_rows, 4) + [sums_scratch],
        work,
        {4: 0},
    )
    sibling = swapped(sibling, 0)
    beside, aligned, offset = (swapped(beside, 1), swapped(place, 0, reach), swapped(place, reach, reach))
    total, target = call(
        functools.partial(begin, listed, False),
        "second_near",
        [totals, targets],
        [(vmem, value) for value in (place, sibling, near_lists, near_weight)],
        tools(near_rows, 3),
        work,
    )
    _, state, sibling, beside, after_first = call(
        functools.partial(second_finish, total_tiles),
        "second_far",
        [
            totals,
            held(6, tiles, slots),
            held(6 * half, slots),
            held(6 * half, slots),
            jax.ShapeDtypeStruct((6, capacity, slots), jnp.float32),
        ],
        [(smem, curve_cuts)]
        + [
            (vmem, value)
            for value in (place, aligned, beside, offset, total, target, near_weight, speed, sibling, far_lists, far_weight)
        ],
        tools(far_rows, 3) + [sums_scratch, pool_scratch],
        work,
        {5: 0},
    )
    (after_second,) = call(
        functools.partial(third_kernel, total_tiles),
        "place",
        [jax.ShapeDtypeStruct((6, capacity, slots), jnp.float32)],
        [(smem, curve_cuts), (vmem, swapped(sibling, 0)), (vmem, state), (vmem, swapped(beside, 1, wrap=False))],
        [pool_scratch],
    )
    return (jnp.transpose(after_first, (1, 0, 2)), jnp.transpose(after_second, (1, 0, 2)))


def solution(mesh):
    in_specs = (P(AXES, None, None), P(AXES), P(AXES, None), P())
    out_specs = (P(AXES, None, None), P(AXES, None, None))
    return jax.shard_map(body, mesh=mesh, in_specs=in_specs, out_specs=out_specs, check_vma=False)
```

```python
import functools

import jax
import jax.numpy as jnp
from jax import lax
from jax.experimental import pallas as pl
from jax.experimental.pallas import tpu as pltpu
from jax.sharding import PartitionSpec as P

AXES = ("gx", "gy")
STEPS = 2

soften = 0.05
time_step = 0.5
reach = 2
chunk = 4
units = 12
feature_rows = 32
far_norm = 1e36
lanes = 128
block_rows = 32
vmem_limit = 16 << 20


def swapped(value, first, wrap=True):
    count = lax.axis_size(AXES)
    pairs = []
    for lower in range(first, count, 2):
        if wrap or lower + 1 < count:
            upper = (lower + 1) % count
            pairs += [(lower, upper), (upper, lower)]
    return lax.ppermute(value, AXES, pairs)


def round_up(value, step):
    return -(-value // step) * step


def device_index():
    return lax.axis_index("gx") * lax.axis_size("gy") + lax.axis_index("gy")


def pieces(value, count):
    parts = []
    rest = value
    for _ in range(count - 1):
        part = rest.astype(jnp.bfloat16).astype(jnp.float32)
        parts.append(part)
        rest = rest - part
    parts.append(rest.astype(jnp.bfloat16).astype(jnp.float32))
    return parts


def pack_kernel(total_tiles, particles_ref, occupancy_ref, neighbours_ref, packed_ref, speed_ref):
    tiles, slots = (particles_ref.shape[0], particles_ref.shape[2])
    listed = neighbours_ref.shape[1]
    for row in range(3):
        packed_ref[row * tiles : (row + 1) * tiles, :] = particles_ref[:, row, :]
        speed_ref[row * tiles : (row + 1) * tiles, :] = particles_ref[:, 3 + row, :]
    tile_ids = lax.broadcasted_iota(jnp.int32, (tiles, listed), 0)
    offsets = neighbours_ref[...] - (device_index() * tiles + tile_ids)
    offsets = jnp.where(offsets < 0, offsets + total_tiles, offsets)
    packed_ref[3 * tiles :, :] = jnp.zeros((tiles, slots), jnp.float32)
    packed_ref[3 * tiles :, :listed] = offsets.astype(jnp.float32)
    for tile in range(tiles):
        live = occupancy_ref[tile].astype(jnp.float32)
        packed_ref[3 * tiles + tile : 3 * tiles + tile + 1, listed : listed + 1] = jnp.full((1, 1), live)


def places_of(index, tiles, offsets):
    place = index + offsets[0]
    for block in range(1, len(offsets)):
        place = jnp.where(index >= block * tiles, index - block * tiles + offsets[block], place)
    return jnp.where(index >= len(offsets) * tiles, -1000.0, place)


def build_lists(aux, own, tiles, listed, offsets):
    rows = aux.shape[0]
    dummy = len(offsets) * tiles
    index = lax.broadcasted_iota(jnp.int32, (rows, lanes), 0).astype(jnp.float32)
    lane = lax.broadcasted_iota(jnp.int32, (rows, lanes), 1).astype(jnp.float32)
    place = places_of(index, tiles, offsets)
    mask = place == lane
    for entry in range(listed):
        mask = mask | (place + aux[:, entry : entry + 1] == lane)
    own_rows = own.shape[0]
    own_index = lax.broadcasted_iota(jnp.int32, (own_rows, lanes), 0).astype(jnp.float32)
    own_lane = lax.broadcasted_iota(jnp.int32, (own_rows, lanes), 1).astype(jnp.float32)
    own_place = places_of(own_lane, tiles, offsets)
    listing = own_index + own[:, 0:1] == own_place
    for entry in range(1, listed):
        listing = listing | (own_index + own[:, entry : entry + 1] == own_place)
    listing = jnp.where(listing, 1.0, 0.0)
    listing = jnp.concatenate([listing, jnp.zeros((lanes - own_rows, lanes), jnp.float32)], axis=0)
    listing = jnp.transpose(listing)[:rows]
    mask = jnp.maximum(jnp.where(mask, 1.0, 0.0), listing)
    mask = jnp.where((lane < tiles) & (index < dummy), mask, 0.0)
    earlier = lax.broadcasted_iota(jnp.int32, (rows, rows), 1) < lax.broadcasted_iota(jnp.int32, (rows, rows), 0)
    rank = jnp.dot(
        jnp.where(earlier, 1.0, 0.0).astype(jnp.bfloat16),
        mask.astype(jnp.bfloat16),
        preferred_element_type=jnp.float32,
    )
    key = jnp.where(mask > 0.5, rank, -1.0)
    counts = jnp.sum(mask, axis=0, keepdims=True)
    lists = []
    for tile in range(tiles):
        hit = key[:, tile : tile + 1] == lane
        row = jnp.sum(jnp.where(hit, index - dummy, 0.0), axis=0, keepdims=True) + dummy
        live = own[tile : tile + 1, listed : listed + 1]
        blocks = jnp.full((1, 1), 1.0)
        for filled in range(block_rows, lanes, block_rows):
            blocks = blocks + jnp.where(live > filled, 1.0, 0.0)
        lists.append(jnp.where(lane[:1] == lanes - 1, blocks, row))
    lists.append(jnp.where(lane[:1] == lanes - 1, 1.0, float(dummy)))
    lists.append(counts)
    return [row.astype(jnp.int32) for row in lists]


def middles(own_place):
    return [jnp.mean(axis[:8], keepdims=True) for axis in own_place]


def feature_of(feature_ref, tile):
    return feature_ref[tile * feature_rows : (tile + 1) * feature_rows, :]


def build_sources(places, middle, weight, feature_ref, moment_ref, source_ref):
    rows = weight.shape[0]
    ones = jnp.ones_like(weight)
    zeros = jnp.zeros_like(weight)
    features = []
    norm = zeros
    for axis in range(3):
        value = weight * (places[axis] - middle[axis])
        norm = norm + value * value
        moment_ref.reshape(rows * 8, lanes)[pl.ds(axis, rows, 8), :] = value
        high, mid, low = pieces(value, 3)
        features += [high, high, mid, mid, high, low]
    features += pieces(jnp.where(weight > 0.5, norm, far_norm), 3) + [ones] * 3
    features += [zeros] * (feature_rows - len(features))
    for row, value in enumerate(features):
        feature_ref[pl.ds(row, rows, feature_rows), :] = value
    for tile in range(rows):
        source_ref[tile] = feature_of(feature_ref, tile).astype(jnp.bfloat16)


def build_targets(own_place, middle, feature_ref, target_ref):
    tiles = own_place[0].shape[0]
    ones = jnp.ones_like(own_place[0])
    zeros = jnp.zeros_like(own_place[0])
    features = []
    norm = zeros
    for axis in range(3):
        value = own_place[axis] - middle[axis]
        norm = norm + value * value
        high, mid, low = [-2.0 * part for part in pieces(value, 3)]
        features += [high, mid, high, mid, low, high]
    features += [ones] * 3 + pieces(norm + soften, 3)
    features += [zeros] * (feature_rows - len(features))
    for row, value in enumerate(features):
        feature_ref[pl.ds(row, tiles, feature_rows), :] = value
    blank = jnp.zeros((lanes - feature_rows, lanes), jnp.float32)
    blocks = lanes // block_rows
    for tile in range(tiles):
        turned = jnp.transpose(jnp.concatenate([feature_of(feature_ref, tile), blank], axis=0))
        turned = turned[:, :feature_rows].astype(jnp.bfloat16)
        for block in range(blocks):
            target_ref[tile * blocks + block] = turned[block * block_rows : (block + 1) * block_rows]
    target_ref[tiles * blocks] = target_ref[0]


def accumulate(tiles, lists_ref, source_ref, target_ref, moment_ref, total_ref):
    blocks = lanes // block_rows
    item_counts = [
        jnp.maximum((lists_ref[tiles + 1, tile] + chunk - 1) // chunk, 1) * lists_ref[tile, lanes - 1] for tile in range(tiles)
    ]
    item_total = functools.reduce(lambda left, right: left + right, item_counts)

    def following(tile, block, part):
        more = (part + 1) * chunk < lists_ref[tiles + 1, tile]
        again = block + 1 < lists_ref[tile, lanes - 1]
        return (
            jnp.where(more | again, tile, jnp.minimum(tile + 1, tiles)),
            jnp.where(more, block, jnp.where(again, block + 1, 0)),
            jnp.where(more, part + 1, 0),
        )

    def sources_of(tile, part):
        return [lists_ref[tile, part * chunk + entry] for entry in range(chunk)]

    def distances(spot, sources):
        target = target_ref[spot]
        features = [source_ref[source] for source in sources]
        return [
            jnp.dot(target, jnp.concatenate(features[first : first + 2], axis=1), preferred_element_type=jnp.float32)
            for first in range(0, chunk, 2)
        ]

    def kernels(spot, places, squares):
        for first in range(0, block_rows, 8):
            strip = slice(first, first + 8)
            sums = [total_ref[spot, row, strip, :] for row in range(4)]
            for entry in range(chunk):
                column = (entry % 2) * lanes
                inverse = lax.rsqrt(squares[entry // 2][strip, column : column + lanes])
                kernel = inverse * inverse * inverse
                for axis in range(3):
                    sums[axis] = sums[axis] + kernel * places[entry][axis]
                sums[3] = sums[3] + kernel
            for row in range(4):
                total_ref[spot, row, strip, :] = sums[row]

    def step(_, carry):
        tile, block, part = carry
        waiting = None
        for _ in range(units):
            sources = sources_of(tile, part)
            places = [
                [jnp.broadcast_to(moment_ref[source, axis : axis + 1, :], (8, lanes)) for axis in range(3)]
                for source in sources
            ]
            spot = tile * blocks + block
            item = (spot, places, distances(spot, sources))
            if waiting is not None:
                kernels(*waiting)
            waiting = item
            tile, block, part = following(tile, block, part)
        kernels(*waiting)
        return (tile, block, part)

    zero = jnp.int32(0)
    lax.fori_loop(0, (item_total + units - 1) // units, step, (zero, zero, zero))


def advance(middle, place_own, speed_own, weight_own, total_ref, sums_ref):
    tiles = weight_own.shape[0]
    blocks = lanes // block_rows
    for tile in range(tiles):
        for row in range(4):
            parts = [total_ref[tile * blocks + block, row] for block in range(blocks)]
            total = jnp.sum(jnp.transpose(jnp.concatenate(parts, axis=0)), axis=0, keepdims=True)
            sums_ref[row, tile : tile + 1, :] = total
    zeroth = sums_ref[3, :tiles, :]
    places, speeds = ([], [])
    for axis in range(3):
        force = sums_ref[axis, :tiles, :] - (place_own[axis] - middle[axis]) * zeroth
        speeds.append(weight_own * (speed_own[axis] + time_step * force / lanes))
        places.append(weight_own * (place_own[axis] + time_step * speeds[axis]))
    return places, speeds


def part_of(ref, tiles, row):
    return ref[row * tiles : (row + 1) * tiles, :]


def fill_planes(planes, tiles, blocks):
    kinds, rows, slots = planes.shape
    filled = len(blocks) * tiles
    planes[:, filled:, :] = jnp.zeros((kinds, rows - filled, slots), jnp.float32)
    for block, ref in enumerate(blocks):
        for kind in range(kinds):
            planes[kind, block * tiles : (block + 1) * tiles, :] = part_of(ref, tiles, kind)


def weights_of(aux, listed):
    slot = lax.broadcasted_iota(jnp.int32, aux.shape, 1).astype(jnp.float32)
    return jnp.where(slot < aux[:, listed : listed + 1], 1.0, 0.0)


def offsets_of(tiles, near_pair):
    device = device_index()
    toward = jnp.where(device % 2 == 0, 1.0, -1.0) * float(tiles)
    if near_pair:
        return [0.0, toward]
    return [-toward, -reach * toward, reach * toward]


def far_blocks(pair, forwarded, first_rows):
    return (pair[:first_rows, :], pair[first_rows:, :], forwarded[:first_rows, :])


def prepare(first, near_pair, listed, own_ref, blocks, lists_ref, weight_ref, tools):
    planes, scalars, copy_sem, feature_ref, moment_ref, source_ref = tools
    tiles = own_ref.shape[0] // planes.shape[0]
    if not first:
        copy = pltpu.make_async_copy(lists_ref, scalars, copy_sem)
        copy.start()
    fill_planes(planes, tiles, blocks)
    if first:
        aux = planes[3]
        own_aux = jnp.concatenate(
            [part_of(own_ref, tiles, 3), jnp.zeros((round_up(tiles, 8) - tiles, lanes), jnp.float32)], axis=0
        )
        for row, value in enumerate(build_lists(aux, own_aux, tiles, listed, offsets_of(tiles, near_pair))):
            lists_ref[row : row + 1, :] = value
        copy = pltpu.make_async_copy(lists_ref, scalars, copy_sem)
        copy.start()
        weight_ref[...] = weights_of(aux, listed)
    middle = middles([part_of(own_ref, tiles, axis) for axis in range(3)])
    build_sources([planes[axis] for axis in range(3)], middle, weight_ref[...], feature_ref, moment_ref, source_ref)
    return middle, copy


def begin(listed, first, *refs):
    if first:
        own_ref, sibling_ref, total_ref, target_ref, lists_ref, weight_ref, *scratch = refs
    else:
        own_ref, sibling_ref, lists_ref, weight_ref, total_ref, target_ref, *scratch = refs
    tools = scratch
    tiles = own_ref.shape[0] // tools[0].shape[0]
    middle, copy = prepare(first, True, listed, own_ref, (own_ref, sibling_ref), lists_ref, weight_ref, tools)
    build_targets([part_of(own_ref, tiles, axis) for axis in range(3)], middle, tools[3], target_ref)
    total_ref[...] = jnp.zeros(total_ref.shape, jnp.float32)
    copy.wait()
    accumulate(tiles, tools[1], tools[5], target_ref, tools[4], total_ref)


def halves(speed, even, half):
    first, last = (speed[:half], speed[half:])
    return jnp.where(even, last, first), jnp.where(even, first, last)


def first_finish(
    listed, own_ref, pair, forwarded, total_in, target_ref, weight_own_ref, speed_ref, *refs
):
    total_ref, lists_ref, weight_ref, place_out, speed_out, sibling_out, beside_out, *scratch = refs
    *tools, sums_ref = scratch
    tiles = own_ref.shape[0] // tools[0].shape[0]
    half = tiles // 2
    middle, copy = prepare(True, False, listed, own_ref, far_blocks(pair, forwarded, own_ref.shape[0]), lists_ref, weight_ref, tools)
    copy.wait()
    accumulate(tiles, tools[1], tools[5], target_ref, tools[4], total_ref)
    places, speeds = advance(
        middle,
        [part_of(own_ref, tiles, axis) for axis in range(3)],
        [part_of(speed_ref, tiles, axis) for axis in range(3)],
        weight_own_ref[:tiles, :],
        total_ref,
        sums_ref,
    )
    even = device_index() % 2 == 0
    for axis in range(3):
        strip = slice(axis * tiles, (axis + 1) * tiles)
        place_out[strip, :] = places[axis]
        speed_out[strip, :] = speeds[axis]
        sibling_out[strip, :] = places[axis]
        beside_out[strip, :] = places[axis]
        strip = slice(3 * tiles + axis * half, 3 * tiles + (axis + 1) * half)
        sibling_out[strip, :], beside_out[strip, :] = halves(speeds[axis], even, half)


def second_finish(
    total_tiles,
    cuts_ref,
    own_ref,
    pair,
    forwarded,
    total_in,
    target_ref,
    weight_own_ref,
    speed_ref,
    sibling_ref,
    lists_ref,
    weight_ref,
    total_ref,
    state_ref,
    sibling_out,
    beside_out,
    out_ref,
    *scratch
):
    *tools, sums_ref, pool_ref = scratch
    tiles = own_ref.shape[0] // 3
    half = tiles // 2
    beside = pair[: 3 * (tiles + half), :]
    blocks = far_blocks(pair, forwarded, beside.shape[0])
    middle, copy = prepare(False, False, None, own_ref, blocks, lists_ref, weight_ref, tools)
    copy.wait()
    accumulate(tiles, tools[1], tools[5], target_ref, tools[4], total_ref)
    place_own = [part_of(own_ref, tiles, axis) for axis in range(3)]
    speed_own = [part_of(speed_ref, tiles, axis) for axis in range(3)]
    places, speeds = advance(middle, place_own, speed_own, weight_own_ref[:tiles, :], total_ref, sums_ref)
    even = device_index() % 2 == 0
    for row, value in enumerate(places + speeds):
        state_ref[row] = value
        strip = slice(row * half, (row + 1) * half)
        sibling_out[strip, :], beside_out[strip, :] = halves(value, even, half)
    lower, upper = ([], [])
    for row in range(6):
        if row < 3:
            sides = [part_of(ref, tiles, row) for ref in (sibling_ref, beside)]
            low_sides, high_sides = ([side[tiles - half :] for side in sides], [side[:half] for side in sides])
        else:
            strip = slice(3 * tiles + (row - 3) * half, 3 * tiles + (row - 2) * half)
            low_sides = high_sides = [ref[strip, :] for ref in (sibling_ref, beside)]
        lower.append(jnp.where(even, low_sides[1], low_sides[0]))
        upper.append(jnp.where(even, high_sides[0], high_sides[1]))
    place_rows(0, total_tiles, cuts_ref, lower, place_own + speed_own, upper, pool_ref, out_ref)


def place_rows(step, total_tiles, cuts_ref, lower, own, upper, pool_ref, out_ref):
    tiles, slots = own[0].shape
    half = tiles // 2
    capacity = out_ref.shape[1]
    device = device_index()
    last = cuts_ref.shape[1] - 1
    first_tile = cuts_ref[step, device]
    next_tile = jnp.where(device == last, total_tiles, cuts_ref[step, jnp.minimum(device + 1, last)])
    owned = next_tile - first_tile
    start = first_tile - (device * tiles - half)
    filled = lax.broadcasted_iota(jnp.int32, (capacity, slots), 0) < owned
    for row in range(6):
        pool_ref[row, :half, :] = lower[row]
        pool_ref[row, half : half + tiles, :] = own[row]
        pool_ref[row, half + tiles : 2 * tiles, :] = upper[row]
    for row in range(6):
        out_ref[row] = jnp.where(filled, pool_ref[row, pl.ds(start, capacity), :], 0.0)


def third_kernel(total_tiles, cuts_ref, sibling_ref, own_ref, beside_ref, out_ref, pool_ref):
    half = own_ref.shape[1] // 2
    even = device_index() % 2 == 0
    lower, upper = ([], [])
    for row in range(6):
        sibling, beside = (part_of(sibling_ref, half, row), part_of(beside_ref, half, row))
        lower.append(jnp.where(even, beside, sibling))
        upper.append(jnp.where(even, sibling, beside))
    place_rows(1, total_tiles, cuts_ref, lower, [own_ref[row] for row in range(6)], upper, pool_ref, out_ref)


def far(value):
    return pltpu.with_memory_space_constraint(value, pltpu.HBM)


def near(value):
    return pltpu.with_memory_space_constraint(value, pltpu.VMEM)


def body(particles, occupancy, neighbours, curve_cuts):
    tiles, _, slots = particles.shape
    listed = neighbours.shape[1]
    total_tiles = tiles * lax.axis_size(AXES)
    half = tiles // 2
    capacity = 2 * tiles
    near_rows = round_up(2 * tiles + 1, 8)
    far_rows = round_up((reach + 1) * tiles + 1, 8)
    list_rows = round_up(tiles + 2, 8)
    vmem = pl.BlockSpec(memory_space=pltpu.VMEM)
    smem = pl.BlockSpec(memory_space=pltpu.SMEM)

    def held(*sizes, dtype=jnp.float32):
        return pltpu.VMEM(sizes, dtype)

    def call(kernel, name, outs, ins, scratch, flops=0, aliases=None):
        held_ins = [far(value) if kind is smem else near(value) for kind, value in ins]
        return pl.pallas_call(
            kernel,
            out_shape=outs,
            in_specs=[kind for kind, _ in ins],
            out_specs=[vmem] * len(outs),
            scratch_shapes=scratch,
            input_output_aliases=aliases or {},
            compiler_params=pltpu.CompilerParams(vmem_limit_bytes=vmem_limit),
            cost_estimate=pl.CostEstimate(flops=flops, bytes_accessed=1 << 20, transcendentals=0),
            name=name,
        )(*held_ins)

    def tools(rows, kinds):
        return [
            pltpu.VMEM((kinds, rows, slots), jnp.float32),
            pltpu.SMEM((list_rows, lanes), jnp.int32),
            pltpu.SemaphoreType.DMA,
            pltpu.VMEM((rows * feature_rows, lanes), jnp.float32),
            pltpu.VMEM((rows, 8, lanes), jnp.float32),
            pltpu.VMEM((rows, feature_rows, lanes), jnp.bfloat16),
        ]

    packed, speed = pl.pallas_call(
        functools.partial(pack_kernel, total_tiles),
        out_shape=(held(4 * tiles, slots), held(3 * tiles, slots)),
        in_specs=[vmem, smem, vmem],
        out_specs=(vmem, vmem),
        compiler_params=pltpu.CompilerParams(vmem_limit_bytes=vmem_limit),
        name="pack",
    )(far(particles), far(occupancy), far(neighbours))
    pool_scratch = pltpu.VMEM((6, round_up(capacity + tiles, 8), slots), jnp.float32)
    sums_scratch = pltpu.VMEM((4, round_up(tiles, 8), lanes), jnp.float32)
    blocks = lanes // block_rows
    totals = held(tiles * blocks + 1, 4, block_rows, lanes)
    targets = held(tiles * blocks + 1, block_rows, feature_rows, dtype=jnp.bfloat16)
    lists = held(list_rows, lanes, dtype=jnp.int32)
    edge = 3 * tiles + 3 * half
    work = 1 << 32

    sibling = swapped(packed, 0)
    pair = swapped(jnp.concatenate([packed, sibling], axis=0), 1)
    total, target, near_lists, near_weight = call(
        functools.partial(begin, listed, True),
        "first_near",
        [totals, targets, lists, held(near_rows, slots)],
        [(vmem, packed), (vmem, sibling)],
        tools(near_rows, 4),
        work,
    )
    pair, near_weight = lax.optimization_barrier((pair, near_weight))
    forwarded = swapped(pair, 0)
    total, far_lists, far_weight, place, speed, sibling, beside = call(
        functools.partial(first_finish, listed),
        "first_far",
        [totals, lists, held(far_rows, slots), held(3 * tiles, slots), held(3 * tiles, slots), held(edge, slots), held(edge, slots)],
        [(vmem, value) for value in (packed, pair, forwarded, total, target, near_weight, speed)],
        tools(far_rows, 4) + [sums_scratch],
        work,
        {3: 0},
    )
    sibling = swapped(sibling, 0)
    pair = swapped(jnp.concatenate([beside, sibling[: 3 * tiles]], axis=0), 1)
    total, target = call(
        functools.partial(begin, listed, False),
        "second_near",
        [totals, targets],
        [(vmem, value) for value in (place, sibling, near_lists, near_weight)],
        tools(near_rows, 3),
        work,
    )
    pair, target = lax.optimization_barrier((pair, target))
    forwarded = swapped(pair, 0)
    _, state, sibling, beside, after_first = call(
        functools.partial(second_finish, total_tiles),
        "second_far",
        [
            totals,
            held(6, tiles, slots),
            held(6 * half, slots),
            held(6 * half, slots),
            jax.ShapeDtypeStruct((6, capacity, slots), jnp.float32),
        ],
        [(smem, curve_cuts)]
        + [
            (vmem, value)
            for value in (place, pair, forwarded, total, target, near_weight, speed, sibling, far_lists, far_weight)
        ],
        tools(far_rows, 3) + [sums_scratch, pool_scratch],
        work,
        {4: 0},
    )
    (after_second,) = call(
        functools.partial(third_kernel, total_tiles),
        "place",
        [jax.ShapeDtypeStruct((6, capacity, slots), jnp.float32)],
        [(smem, curve_cuts), (vmem, swapped(sibling, 0)), (vmem, state), (vmem, swapped(beside, 1, wrap=False))],
        [pool_scratch],
    )
    return (jnp.transpose(after_first, (1, 0, 2)), jnp.transpose(after_second, (1, 0, 2)))


def solution(mesh):
    in_specs = (P(AXES, None, None), P(AXES), P(AXES, None), P())
    out_specs = (P(AXES, None, None), P(AXES, None, None))
    return jax.shard_map(body, mesh=mesh, in_specs=in_specs, out_specs=out_specs, check_vma=False)
```

```python
import functools

import jax
import jax.numpy as jnp
from jax import lax
from jax.experimental import pallas as pl
from jax.experimental.pallas import tpu as pltpu
from jax.sharding import PartitionSpec as P

AXES = ("gx", "gy")
STEPS = 2

soften = 0.05
time_step = 0.5
reach = 2
chunk = 4
units = 8
feature_rows = 32
far_norm = 1e36
lanes = 128
block_rows = 64
vmem_limit = 16 << 20


def swapped(value, first, wrap=True):
    count = lax.axis_size(AXES)
    pairs = []
    for lower in range(first, count, 2):
        if wrap or lower + 1 < count:
            upper = (lower + 1) % count
            pairs += [(lower, upper), (upper, lower)]
    return lax.ppermute(value, AXES, pairs)


def round_up(value, step):
    return -(-value // step) * step


def device_index():
    return lax.axis_index("gx") * lax.axis_size("gy") + lax.axis_index("gy")


def pieces(value, count):
    parts = []
    rest = value
    for _ in range(count - 1):
        part = rest.astype(jnp.bfloat16).astype(jnp.float32)
        parts.append(part)
        rest = rest - part
    parts.append(rest.astype(jnp.bfloat16).astype(jnp.float32))
    return parts


def pack_kernel(total_tiles, particles_ref, occupancy_ref, neighbours_ref, packed_ref, speed_ref):
    tiles, slots = (particles_ref.shape[0], particles_ref.shape[2])
    listed = neighbours_ref.shape[1]
    for row in range(3):
        packed_ref[row * tiles : (row + 1) * tiles, :] = particles_ref[:, row, :]
        speed_ref[row * tiles : (row + 1) * tiles, :] = particles_ref[:, 3 + row, :]
    tile_ids = lax.broadcasted_iota(jnp.int32, (tiles, listed), 0)
    offsets = neighbours_ref[...] - (device_index() * tiles + tile_ids)
    offsets = jnp.where(offsets < 0, offsets + total_tiles, offsets)
    packed_ref[3 * tiles :, :] = jnp.zeros((tiles, slots), jnp.float32)
    packed_ref[3 * tiles :, :listed] = offsets.astype(jnp.float32)
    for tile in range(tiles):
        live = occupancy_ref[tile].astype(jnp.float32)
        packed_ref[3 * tiles + tile : 3 * tiles + tile + 1, listed : listed + 1] = jnp.full((1, 1), live)


def places_of(index, tiles, offsets):
    place = index + offsets[0]
    for block in range(1, len(offsets)):
        place = jnp.where(index >= block * tiles, index - block * tiles + offsets[block], place)
    return jnp.where(index >= len(offsets) * tiles, -1000.0, place)


def build_lists(aux, own, tiles, listed, offsets):
    rows = aux.shape[0]
    dummy = len(offsets) * tiles
    index = lax.broadcasted_iota(jnp.int32, (rows, lanes), 0).astype(jnp.float32)
    lane = lax.broadcasted_iota(jnp.int32, (rows, lanes), 1).astype(jnp.float32)
    place = places_of(index, tiles, offsets)
    mask = place == lane
    for entry in range(listed):
        mask = mask | (place + aux[:, entry : entry + 1] == lane)
    own_rows = own.shape[0]
    own_index = lax.broadcasted_iota(jnp.int32, (own_rows, lanes), 0).astype(jnp.float32)
    own_lane = lax.broadcasted_iota(jnp.int32, (own_rows, lanes), 1).astype(jnp.float32)
    own_place = places_of(own_lane, tiles, offsets)
    listing = own_index + own[:, 0:1] == own_place
    for entry in range(1, listed):
        listing = listing | (own_index + own[:, entry : entry + 1] == own_place)
    listing = jnp.where(listing, 1.0, 0.0)
    listing = jnp.concatenate([listing, jnp.zeros((lanes - own_rows, lanes), jnp.float32)], axis=0)
    listing = jnp.transpose(listing)[:rows]
    mask = jnp.maximum(jnp.where(mask, 1.0, 0.0), listing)
    mask = jnp.where((lane < tiles) & (index < dummy), mask, 0.0)
    earlier = lax.broadcasted_iota(jnp.int32, (rows, rows), 1) < lax.broadcasted_iota(jnp.int32, (rows, rows), 0)
    rank = jnp.dot(
        jnp.where(earlier, 1.0, 0.0).astype(jnp.bfloat16),
        mask.astype(jnp.bfloat16),
        preferred_element_type=jnp.float32,
    )
    key = jnp.where(mask > 0.5, rank, -1.0)
    counts = jnp.sum(mask, axis=0, keepdims=True)
    lists = []
    for tile in range(tiles):
        hit = key[:, tile : tile + 1] == lane
        row = jnp.sum(jnp.where(hit, index - dummy, 0.0), axis=0, keepdims=True) + dummy
        live = own[tile : tile + 1, listed : listed + 1]
        blocks = jnp.full((1, 1), 1.0)
        for filled in range(block_rows, lanes, block_rows):
            blocks = blocks + jnp.where(live > filled, 1.0, 0.0)
        lists.append(jnp.where(lane[:1] == lanes - 1, blocks, row))
    lists.append(jnp.where(lane[:1] == lanes - 1, 1.0, float(dummy)))
    lists.append(counts)
    return [row.astype(jnp.int32) for row in lists]


def middles(own_place):
    return [jnp.mean(axis[:8], keepdims=True) for axis in own_place]


def feature_of(feature_ref, tile):
    return feature_ref[tile * feature_rows : (tile + 1) * feature_rows, :]


def build_sources(places, middle, weight, feature_ref, moment_ref, source_ref):
    rows = weight.shape[0]
    ones = jnp.ones_like(weight)
    zeros = jnp.zeros_like(weight)
    features = []
    norm = zeros
    for axis in range(3):
        value = weight * (places[axis] - middle[axis])
        norm = norm + value * value
        moment_ref.reshape(rows * 8, lanes)[pl.ds(axis, rows, 8), :] = value
        high, mid, low = pieces(value, 3)
        features += [high, high, mid, mid, high, low]
    features += pieces(jnp.where(weight > 0.5, norm, far_norm), 3) + [ones] * 3
    features += [zeros] * (feature_rows - len(features))
    for row, value in enumerate(features):
        feature_ref[pl.ds(row, rows, feature_rows), :] = value
    for tile in range(rows):
        source_ref[tile] = feature_of(feature_ref, tile).astype(jnp.bfloat16)


def build_targets(own_place, middle, feature_ref, target_ref):
    tiles = own_place[0].shape[0]
    ones = jnp.ones_like(own_place[0])
    zeros = jnp.zeros_like(own_place[0])
    features = []
    norm = zeros
    for axis in range(3):
        value = own_place[axis] - middle[axis]
        norm = norm + value * value
        high, mid, low = [-2.0 * part for part in pieces(value, 3)]
        features += [high, mid, high, mid, low, high]
    features += [ones] * 3 + pieces(norm + soften, 3)
    features += [zeros] * (feature_rows - len(features))
    for row, value in enumerate(features):
        feature_ref[pl.ds(row, tiles, feature_rows), :] = value
    blank = jnp.zeros((lanes - feature_rows, lanes), jnp.float32)
    blocks = lanes // block_rows
    for tile in range(tiles):
        turned = jnp.transpose(jnp.concatenate([feature_of(feature_ref, tile), blank], axis=0))
        turned = turned[:, :feature_rows].astype(jnp.bfloat16)
        for block in range(blocks):
            target_ref[tile * blocks + block] = turned[block * block_rows : (block + 1) * block_rows]
    target_ref[tiles * blocks] = target_ref[0]


def accumulate(tiles, lists_ref, source_ref, target_ref, moment_ref, total_ref):
    blocks = lanes // block_rows
    item_counts = [
        jnp.maximum((lists_ref[tiles + 1, tile] + chunk - 1) // chunk, 1) * lists_ref[tile, lanes - 1] for tile in range(tiles)
    ]
    item_total = functools.reduce(lambda left, right: left + right, item_counts)

    def following(tile, block, part):
        more = (part + 1) * chunk < lists_ref[tiles + 1, tile]
        again = block + 1 < lists_ref[tile, lanes - 1]
        return (
            jnp.where(more | again, tile, jnp.minimum(tile + 1, tiles)),
            jnp.where(more, block, jnp.where(again, block + 1, 0)),
            jnp.where(more, part + 1, 0),
        )

    def sources_of(tile, part):
        return [lists_ref[tile, part * chunk + entry] for entry in range(chunk)]

    def distances(spot, sources):
        target = target_ref[spot]
        features = [source_ref[source] for source in sources]
        return [
            jnp.dot(target, jnp.concatenate(features[first : first + 2], axis=1), preferred_element_type=jnp.float32)
            for first in range(0, chunk, 2)
        ]

    def kernels(spot, places, squares):
        for first in range(0, block_rows, 8):
            strip = slice(first, first + 8)
            sums = [total_ref[spot, row, strip, :] for row in range(4)]
            for entry in range(chunk):
                column = (entry % 2) * lanes
                inverse = lax.rsqrt(squares[entry // 2][strip, column : column + lanes])
                kernel = inverse * inverse * inverse
                for axis in range(3):
                    sums[axis] = sums[axis] + kernel * places[entry][axis]
                sums[3] = sums[3] + kernel
            for row in range(4):
                total_ref[spot, row, strip, :] = sums[row]

    def step(_, carry):
        tile, block, part = carry
        waiting = None
        for _ in range(units):
            sources = sources_of(tile, part)
            places = [
                [jnp.broadcast_to(moment_ref[source, axis : axis + 1, :], (8, lanes)) for axis in range(3)]
                for source in sources
            ]
            spot = tile * blocks + block
            item = (spot, places, distances(spot, sources))
            if waiting is not None:
                kernels(*waiting)
            waiting = item
            tile, block, part = following(tile, block, part)
        kernels(*waiting)
        return (tile, block, part)

    zero = jnp.int32(0)
    lax.fori_loop(0, (item_total + units - 1) // units, step, (zero, zero, zero))


def advance(middle, place_own, speed_own, weight_own, total_ref, sums_ref):
    tiles = weight_own.shape[0]
    blocks = lanes // block_rows
    for tile in range(tiles):
        for row in range(4):
            parts = [total_ref[tile * blocks + block, row] for block in range(blocks)]
            total = jnp.sum(jnp.transpose(jnp.concatenate(parts, axis=0)), axis=0, keepdims=True)
            sums_ref[row, tile : tile + 1, :] = total
    zeroth = sums_ref[3, :tiles, :]
    places, speeds = ([], [])
    for axis in range(3):
        force = sums_ref[axis, :tiles, :] - (place_own[axis] - middle[axis]) * zeroth
        speeds.append(weight_own * (speed_own[axis] + time_step * force / lanes))
        places.append(weight_own * (place_own[axis] + time_step * speeds[axis]))
    return places, speeds


def part_of(ref, tiles, row):
    return ref[row * tiles : (row + 1) * tiles, :]


def fill_planes(planes, tiles, blocks):
    kinds, rows, slots = planes.shape
    filled = len(blocks) * tiles
    planes[:, filled:, :] = jnp.zeros((kinds, rows - filled, slots), jnp.float32)
    for block, ref in enumerate(blocks):
        for kind in range(kinds):
            planes[kind, block * tiles : (block + 1) * tiles, :] = part_of(ref, tiles, kind)


def weights_of(aux, listed):
    slot = lax.broadcasted_iota(jnp.int32, aux.shape, 1).astype(jnp.float32)
    return jnp.where(slot < aux[:, listed : listed + 1], 1.0, 0.0)


def offsets_of(tiles, near_pair):
    device = device_index()
    toward = jnp.where(device % 2 == 0, 1.0, -1.0) * float(tiles)
    if near_pair:
        return [0.0, toward]
    return [-toward, -reach * toward, reach * toward]


def far_blocks(pair, forwarded, first_rows):
    return (pair[:first_rows, :], pair[first_rows:, :], forwarded[:first_rows, :])


def prepare(first, near_pair, listed, own_ref, blocks, lists_ref, weight_ref, tools):
    planes, scalars, copy_sem, feature_ref, moment_ref, source_ref = tools
    tiles = own_ref.shape[0] // planes.shape[0]
    if not first:
        copy = pltpu.make_async_copy(lists_ref, scalars, copy_sem)
        copy.start()
    fill_planes(planes, tiles, blocks)
    if first:
        aux = planes[3]
        own_aux = jnp.concatenate(
            [part_of(own_ref, tiles, 3), jnp.zeros((round_up(tiles, 8) - tiles, lanes), jnp.float32)], axis=0
        )
        for row, value in enumerate(build_lists(aux, own_aux, tiles, listed, offsets_of(tiles, near_pair))):
            lists_ref[row : row + 1, :] = value
        copy = pltpu.make_async_copy(lists_ref, scalars, copy_sem)
        copy.start()
        weight_ref[...] = weights_of(aux, listed)
    middle = middles([part_of(own_ref, tiles, axis) for axis in range(3)])
    build_sources([planes[axis] for axis in range(3)], middle, weight_ref[...], feature_ref, moment_ref, source_ref)
    return middle, copy


def begin(listed, first, *refs):
    if first:
        own_ref, sibling_ref, total_ref, target_ref, lists_ref, weight_ref, *scratch = refs
    else:
        own_ref, sibling_ref, lists_ref, weight_ref, total_ref, target_ref, *scratch = refs
    tools = scratch
    tiles = own_ref.shape[0] // tools[0].shape[0]
    middle, copy = prepare(first, True, listed, own_ref, (own_ref, sibling_ref), lists_ref, weight_ref, tools)
    build_targets([part_of(own_ref, tiles, axis) for axis in range(3)], middle, tools[3], target_ref)
    total_ref[...] = jnp.zeros(total_ref.shape, jnp.float32)
    copy.wait()
    accumulate(tiles, tools[1], tools[5], target_ref, tools[4], total_ref)


def halves(speed, even, half):
    first, last = (speed[:half], speed[half:])
    return jnp.where(even, last, first), jnp.where(even, first, last)


def first_finish(
    listed, own_ref, pair, forwarded, total_in, target_ref, weight_own_ref, speed_ref, *refs
):
    total_ref, lists_ref, weight_ref, place_out, speed_out, sibling_out, beside_out, *scratch = refs
    *tools, sums_ref = scratch
    tiles = own_ref.shape[0] // tools[0].shape[0]
    half = tiles // 2
    middle, copy = prepare(True, False, listed, own_ref, far_blocks(pair, forwarded, own_ref.shape[0]), lists_ref, weight_ref, tools)
    copy.wait()
    accumulate(tiles, tools[1], tools[5], target_ref, tools[4], total_ref)
    places, speeds = advance(
        middle,
        [part_of(own_ref, tiles, axis) for axis in range(3)],
        [part_of(speed_ref, tiles, axis) for axis in range(3)],
        weight_own_ref[:tiles, :],
        total_ref,
        sums_ref,
    )
    even = device_index() % 2 == 0
    for axis in range(3):
        strip = slice(axis * tiles, (axis + 1) * tiles)
        place_out[strip, :] = places[axis]
        speed_out[strip, :] = speeds[axis]
        sibling_out[strip, :] = places[axis]
        beside_out[strip, :] = places[axis]
        strip = slice(3 * tiles + axis * half, 3 * tiles + (axis + 1) * half)
        sibling_out[strip, :], beside_out[strip, :] = halves(speeds[axis], even, half)


def second_finish(
    total_tiles,
    cuts_ref,
    own_ref,
    pair,
    forwarded,
    total_in,
    target_ref,
    weight_own_ref,
    speed_ref,
    sibling_ref,
    lists_ref,
    weight_ref,
    total_ref,
    state_ref,
    sibling_out,
    beside_out,
    out_ref,
    *scratch
):
    *tools, sums_ref, pool_ref = scratch
    tiles = own_ref.shape[0] // 3
    half = tiles // 2
    beside = pair[: 3 * (tiles + half), :]
    blocks = far_blocks(pair, forwarded, beside.shape[0])
    middle, copy = prepare(False, False, None, own_ref, blocks, lists_ref, weight_ref, tools)
    copy.wait()
    accumulate(tiles, tools[1], tools[5], target_ref, tools[4], total_ref)
    place_own = [part_of(own_ref, tiles, axis) for axis in range(3)]
    speed_own = [part_of(speed_ref, tiles, axis) for axis in range(3)]
    places, speeds = advance(middle, place_own, speed_own, weight_own_ref[:tiles, :], total_ref, sums_ref)
    even = device_index() % 2 == 0
    for row, value in enumerate(places + speeds):
        state_ref[row] = value
        strip = slice(row * half, (row + 1) * half)
        sibling_out[strip, :], beside_out[strip, :] = halves(value, even, half)
    lower, upper = ([], [])
    for row in range(6):
        if row < 3:
            sides = [part_of(ref, tiles, row) for ref in (sibling_ref, beside)]
            low_sides, high_sides = ([side[tiles - half :] for side in sides], [side[:half] for side in sides])
        else:
            strip = slice(3 * tiles + (row - 3) * half, 3 * tiles + (row - 2) * half)
            low_sides = high_sides = [ref[strip, :] for ref in (sibling_ref, beside)]
        lower.append(jnp.where(even, low_sides[1], low_sides[0]))
        upper.append(jnp.where(even, high_sides[0], high_sides[1]))
    place_rows(0, total_tiles, cuts_ref, lower, place_own + speed_own, upper, pool_ref, out_ref)


def place_rows(step, total_tiles, cuts_ref, lower, own, upper, pool_ref, out_ref):
    tiles, slots = own[0].shape
    half = tiles // 2
    capacity = out_ref.shape[1]
    device = device_index()
    last = cuts_ref.shape[1] - 1
    first_tile = cuts_ref[step, device]
    next_tile = jnp.where(device == last, total_tiles, cuts_ref[step, jnp.minimum(device + 1, last)])
    owned = next_tile - first_tile
    start = first_tile - (device * tiles - half)
    filled = lax.broadcasted_iota(jnp.int32, (capacity, slots), 0) < owned
    for row in range(6):
        pool_ref[row, :half, :] = lower[row]
        pool_ref[row, half : half + tiles, :] = own[row]
        pool_ref[row, half + tiles : 2 * tiles, :] = upper[row]
    for row in range(6):
        out_ref[row] = jnp.where(filled, pool_ref[row, pl.ds(start, capacity), :], 0.0)


def third_kernel(total_tiles, cuts_ref, sibling_ref, own_ref, beside_ref, out_ref, pool_ref):
    half = own_ref.shape[1] // 2
    even = device_index() % 2 == 0
    lower, upper = ([], [])
    for row in range(6):
        sibling, beside = (part_of(sibling_ref, half, row), part_of(beside_ref, half, row))
        lower.append(jnp.where(even, beside, sibling))
        upper.append(jnp.where(even, sibling, beside))
    place_rows(1, total_tiles, cuts_ref, lower, [own_ref[row] for row in range(6)], upper, pool_ref, out_ref)


def far(value):
    return pltpu.with_memory_space_constraint(value, pltpu.HBM)


def near(value):
    return pltpu.with_memory_space_constraint(value, pltpu.VMEM)


def body(particles, occupancy, neighbours, curve_cuts):
    tiles, _, slots = particles.shape
    listed = neighbours.shape[1]
    total_tiles = tiles * lax.axis_size(AXES)
    half = tiles // 2
    capacity = 2 * tiles
    near_rows = round_up(2 * tiles + 1, 8)
    far_rows = round_up((reach + 1) * tiles + 1, 8)
    list_rows = round_up(tiles + 2, 8)
    vmem = pl.BlockSpec(memory_space=pltpu.VMEM)
    smem = pl.BlockSpec(memory_space=pltpu.SMEM)

    def held(*sizes, dtype=jnp.float32):
        return pltpu.VMEM(sizes, dtype)

    def call(kernel, name, outs, ins, scratch, flops=0, aliases=None):
        held_ins = [far(value) if kind is smem else near(value) for kind, value in ins]
        return pl.pallas_call(
            kernel,
            out_shape=outs,
            in_specs=[kind for kind, _ in ins],
            out_specs=[vmem] * len(outs),
            scratch_shapes=scratch,
            input_output_aliases=aliases or {},
            compiler_params=pltpu.CompilerParams(vmem_limit_bytes=vmem_limit),
            cost_estimate=pl.CostEstimate(flops=flops, bytes_accessed=1 << 20, transcendentals=0),
            name=name,
        )(*held_ins)

    def tools(rows, kinds):
        return [
            pltpu.VMEM((kinds, rows, slots), jnp.float32),
            pltpu.SMEM((list_rows, lanes), jnp.int32),
            pltpu.SemaphoreType.DMA,
            pltpu.VMEM((rows * feature_rows, lanes), jnp.float32),
            pltpu.VMEM((rows, 8, lanes), jnp.float32),
            pltpu.VMEM((rows, feature_rows, lanes), jnp.bfloat16),
        ]

    packed, speed = pl.pallas_call(
        functools.partial(pack_kernel, total_tiles),
        out_shape=(held(4 * tiles, slots), held(3 * tiles, slots)),
        in_specs=[vmem, smem, vmem],
        out_specs=(vmem, vmem),
        compiler_params=pltpu.CompilerParams(vmem_limit_bytes=vmem_limit),
        name="pack",
    )(far(particles), far(occupancy), far(neighbours))
    pool_scratch = pltpu.VMEM((6, round_up(capacity + tiles, 8), slots), jnp.float32)
    sums_scratch = pltpu.VMEM((4, round_up(tiles, 8), lanes), jnp.float32)
    blocks = lanes // block_rows
    totals = held(tiles * blocks + 1, 4, block_rows, lanes)
    targets = held(tiles * blocks + 1, block_rows, feature_rows, dtype=jnp.bfloat16)
    lists = held(list_rows, lanes, dtype=jnp.int32)
    edge = 3 * tiles + 3 * half
    work = 1 << 32

    sibling = swapped(packed, 0)
    pair = swapped(jnp.concatenate([packed, sibling], axis=0), 1)
    total, target, near_lists, near_weight = call(
        functools.partial(begin, listed, True),
        "first_near",
        [totals, targets, lists, held(near_rows, slots)],
        [(vmem, packed), (vmem, sibling)],
        tools(near_rows, 4),
        work,
    )
    pair, near_weight = lax.optimization_barrier((pair, near_weight))
    forwarded = swapped(pair, 0)
    total, far_lists, far_weight, place, speed, sibling, beside = call(
        functools.partial(first_finish, listed),
        "first_far",
        [totals, lists, held(far_rows, slots), held(3 * tiles, slots), held(3 * tiles, slots), held(edge, slots), held(edge, slots)],
        [(vmem, value) for value in (packed, pair, forwarded, total, target, near_weight, speed)],
        tools(far_rows, 4) + [sums_scratch],
        work,
        {3: 0},
    )
    sibling = swapped(sibling, 0)
    pair = swapped(jnp.concatenate([beside, sibling[: 3 * tiles]], axis=0), 1)
    total, target = call(
        functools.partial(begin, listed, False),
        "second_near",
        [totals, targets],
        [(vmem, value) for value in (place, sibling, near_lists, near_weight)],
        tools(near_rows, 3),
        work,
    )
    pair, target = lax.optimization_barrier((pair, target))
    forwarded = swapped(pair, 0)
    _, state, sibling, beside, after_first = call(
        functools.partial(second_finish, total_tiles),
        "second_far",
        [
            totals,
            held(6, tiles, slots),
            held(6 * half, slots),
            held(6 * half, slots),
            jax.ShapeDtypeStruct((6, capacity, slots), jnp.float32),
        ],
        [(smem, curve_cuts)]
        + [
            (vmem, value)
            for value in (place, pair, forwarded, total, target, near_weight, speed, sibling, far_lists, far_weight)
        ],
        tools(far_rows, 3) + [sums_scratch, pool_scratch],
        work,
        {4: 0},
    )
    (after_second,) = call(
        functools.partial(third_kernel, total_tiles),
        "place",
        [jax.ShapeDtypeStruct((6, capacity, slots), jnp.float32)],
        [(smem, curve_cuts), (vmem, swapped(sibling, 0)), (vmem, state), (vmem, swapped(beside, 1, wrap=False))],
        [pool_scratch],
    )
    return (jnp.transpose(after_first, (1, 0, 2)), jnp.transpose(after_second, (1, 0, 2)))


def solution(mesh):
    in_specs = (P(AXES, None, None), P(AXES), P(AXES, None), P())
    out_specs = (P(AXES, None, None), P(AXES, None, None))
    return jax.shard_map(body, mesh=mesh, in_specs=in_specs, out_specs=out_specs, check_vma=False)
```

```python
import functools

import jax
import jax.numpy as jnp
from jax import lax
from jax.experimental import pallas as pl
from jax.experimental.pallas import tpu as pltpu
from jax.sharding import PartitionSpec as P

AXES = ("gx", "gy")
STEPS = 2

soften = 0.05
time_step = 0.5
reach = 2
chunk = 4
units = 8
feature_rows = 32
far_norm = 1e36
lanes = 128
block_rows = 64
vmem_limit = 16 << 20


def swapped(value, first, wrap=True):
    count = lax.axis_size(AXES)
    pairs = []
    for lower in range(first, count, 2):
        if wrap or lower + 1 < count:
            upper = (lower + 1) % count
            pairs += [(lower, upper), (upper, lower)]
    return lax.ppermute(value, AXES, pairs)


def round_up(value, step):
    return -(-value // step) * step


def device_index():
    return lax.axis_index("gx") * lax.axis_size("gy") + lax.axis_index("gy")


def pieces(value, count):
    parts = []
    rest = value
    for _ in range(count - 1):
        part = rest.astype(jnp.bfloat16).astype(jnp.float32)
        parts.append(part)
        rest = rest - part
    parts.append(rest.astype(jnp.bfloat16).astype(jnp.float32))
    return parts


def pack_kernel(total_tiles, particles_ref, occupancy_ref, neighbours_ref, packed_ref, speed_ref):
    tiles, slots = (particles_ref.shape[0], particles_ref.shape[2])
    listed = neighbours_ref.shape[1]
    for row in range(3):
        packed_ref[row * tiles : (row + 1) * tiles, :] = particles_ref[:, row, :]
        speed_ref[row * tiles : (row + 1) * tiles, :] = particles_ref[:, 3 + row, :]
    tile_ids = lax.broadcasted_iota(jnp.int32, (tiles, listed), 0)
    offsets = neighbours_ref[...] - (device_index() * tiles + tile_ids)
    offsets = jnp.where(offsets < 0, offsets + total_tiles, offsets)
    packed_ref[3 * tiles :, :] = jnp.zeros((tiles, slots), jnp.float32)
    packed_ref[3 * tiles :, :listed] = offsets.astype(jnp.float32)
    for tile in range(tiles):
        live = occupancy_ref[tile].astype(jnp.float32)
        packed_ref[3 * tiles + tile : 3 * tiles + tile + 1, listed : listed + 1] = jnp.full((1, 1), live)


def places_of(index, tiles, offsets):
    place = index + offsets[0]
    for block in range(1, len(offsets)):
        place = jnp.where(index >= block * tiles, index - block * tiles + offsets[block], place)
    return jnp.where(index >= len(offsets) * tiles, -1000.0, place)


def build_lists(aux, own, tiles, listed, offsets):
    rows = aux.shape[0]
    dummy = len(offsets) * tiles
    index = lax.broadcasted_iota(jnp.int32, (rows, lanes), 0).astype(jnp.float32)
    lane = lax.broadcasted_iota(jnp.int32, (rows, lanes), 1).astype(jnp.float32)
    place = places_of(index, tiles, offsets)
    mask = place == lane
    for entry in range(listed):
        mask = mask | (place + aux[:, entry : entry + 1] == lane)
    own_rows = own.shape[0]
    own_index = lax.broadcasted_iota(jnp.int32, (own_rows, lanes), 0).astype(jnp.float32)
    own_lane = lax.broadcasted_iota(jnp.int32, (own_rows, lanes), 1).astype(jnp.float32)
    own_place = places_of(own_lane, tiles, offsets)
    listing = own_index + own[:, 0:1] == own_place
    for entry in range(1, listed):
        listing = listing | (own_index + own[:, entry : entry + 1] == own_place)
    listing = jnp.where(listing, 1.0, 0.0)
    listing = jnp.concatenate([listing, jnp.zeros((lanes - own_rows, lanes), jnp.float32)], axis=0)
    listing = jnp.transpose(listing)[:rows]
    mask = jnp.maximum(jnp.where(mask, 1.0, 0.0), listing)
    mask = jnp.where((lane < tiles) & (index < dummy), mask, 0.0)
    earlier = lax.broadcasted_iota(jnp.int32, (rows, rows), 1) < lax.broadcasted_iota(jnp.int32, (rows, rows), 0)
    rank = jnp.dot(
        jnp.where(earlier, 1.0, 0.0).astype(jnp.bfloat16),
        mask.astype(jnp.bfloat16),
        preferred_element_type=jnp.float32,
    )
    key = jnp.where(mask > 0.5, rank, -1.0)
    counts = jnp.sum(mask, axis=0, keepdims=True)
    lists = []
    for tile in range(tiles):
        hit = key[:, tile : tile + 1] == lane
        row = jnp.sum(jnp.where(hit, index - dummy, 0.0), axis=0, keepdims=True) + dummy
        live = own[tile : tile + 1, listed : listed + 1]
        blocks = jnp.full((1, 1), 1.0)
        for filled in range(block_rows, lanes, block_rows):
            blocks = blocks + jnp.where(live > filled, 1.0, 0.0)
        lists.append(jnp.where(lane[:1] == lanes - 1, blocks, row))
    lists.append(jnp.where(lane[:1] == lanes - 1, 1.0, float(dummy)))
    lists.append(counts)
    return [row.astype(jnp.int32) for row in lists]


def middles(own_place):
    return [jnp.mean(axis[:8], keepdims=True) for axis in own_place]


def feature_of(feature_ref, tile):
    return feature_ref[tile * feature_rows : (tile + 1) * feature_rows, :]


def build_sources(first, places, middle, weight, feature_ref, moment_ref, source_ref):
    rows = weight.shape[0]
    moment_rows = moment_ref.reshape(moment_ref.shape[0] * 8, lanes)
    ones = jnp.ones_like(weight)
    zeros = jnp.zeros_like(weight)
    features = []
    norm = zeros
    for axis in range(3):
        value = weight * (places[axis] - middle[axis])
        norm = norm + value * value
        moment_rows[pl.ds(first * 8 + axis, rows, 8), :] = value
        high, mid, low = pieces(value, 3)
        features += [high, high, mid, mid, high, low]
    features += pieces(jnp.where(weight > 0.5, norm, far_norm), 3) + [ones] * 3
    features += [zeros] * (feature_rows - len(features))
    for row, value in enumerate(features):
        feature_ref[pl.ds(row, rows, feature_rows), :] = value
    for tile in range(rows):
        source_ref[first + tile] = feature_of(feature_ref, tile).astype(jnp.bfloat16)


def build_targets(own_place, middle, feature_ref, target_ref):
    tiles = own_place[0].shape[0]
    ones = jnp.ones_like(own_place[0])
    zeros = jnp.zeros_like(own_place[0])
    features = []
    norm = zeros
    for axis in range(3):
        value = own_place[axis] - middle[axis]
        norm = norm + value * value
        high, mid, low = [-2.0 * part for part in pieces(value, 3)]
        features += [high, mid, high, mid, low, high]
    features += [ones] * 3 + pieces(norm + soften, 3)
    features += [zeros] * (feature_rows - len(features))
    for row, value in enumerate(features):
        feature_ref[pl.ds(row, tiles, feature_rows), :] = value
    blank = jnp.zeros((lanes - feature_rows, lanes), jnp.float32)
    blocks = lanes // block_rows
    for tile in range(tiles):
        turned = jnp.transpose(jnp.concatenate([feature_of(feature_ref, tile), blank], axis=0))
        turned = turned[:, :feature_rows].astype(jnp.bfloat16)
        for block in range(blocks):
            target_ref[tile * blocks + block] = turned[block * block_rows : (block + 1) * block_rows]
    target_ref[tiles * blocks] = target_ref[0]


def accumulate(tiles, lists_ref, source_ref, target_ref, moment_ref, total_ref):
    blocks = lanes // block_rows
    item_counts = [
        jnp.maximum((lists_ref[tiles + 1, tile] + chunk - 1) // chunk, 1) * lists_ref[tile, lanes - 1] for tile in range(tiles)
    ]
    item_total = functools.reduce(lambda left, right: left + right, item_counts)

    def following(tile, block, part):
        more = (part + 1) * chunk < lists_ref[tiles + 1, tile]
        again = block + 1 < lists_ref[tile, lanes - 1]
        return (
            jnp.where(more | again, tile, jnp.minimum(tile + 1, tiles)),
            jnp.where(more, block, jnp.where(again, block + 1, 0)),
            jnp.where(more, part + 1, 0),
        )

    def sources_of(tile, part):
        return [lists_ref[tile, part * chunk + entry] for entry in range(chunk)]

    def distances(spot, sources):
        target = target_ref[spot]
        features = [source_ref[source] for source in sources]
        return [
            jnp.dot(target, jnp.concatenate(features[first : first + 2], axis=1), preferred_element_type=jnp.float32)
            for first in range(0, chunk, 2)
        ]

    def kernels(spot, places, squares):
        for first in range(0, block_rows, 8):
            strip = slice(first, first + 8)
            sums = [total_ref[spot, row, strip, :] for row in range(4)]
            for entry in range(chunk):
                column = (entry % 2) * lanes
                inverse = lax.rsqrt(squares[entry // 2][strip, column : column + lanes])
                kernel = inverse * inverse * inverse
                for axis in range(3):
                    sums[axis] = sums[axis] + kernel * places[entry][axis]
                sums[3] = sums[3] + kernel
            for row in range(4):
                total_ref[spot, row, strip, :] = sums[row]

    def step(_, carry):
        tile, block, part = carry
        waiting = None
        for _ in range(units):
            sources = sources_of(tile, part)
            places = [
                [jnp.broadcast_to(moment_ref[source, axis : axis + 1, :], (8, lanes)) for axis in range(3)]
                for source in sources
            ]
            spot = tile * blocks + block
            item = (spot, places, distances(spot, sources))
            if waiting is not None:
                kernels(*waiting)
            waiting = item
            tile, block, part = following(tile, block, part)
        kernels(*waiting)
        return (tile, block, part)

    zero = jnp.int32(0)
    lax.fori_loop(0, (item_total + units - 1) // units, step, (zero, zero, zero))


def advance(middle, place_own, speed_own, weight_own, total_ref, sums_ref):
    tiles = weight_own.shape[0]
    blocks = lanes // block_rows
    for tile in range(tiles):
        for row in range(4):
            parts = [total_ref[tile * blocks + block, row] for block in range(blocks)]
            total = jnp.sum(jnp.transpose(jnp.concatenate(parts, axis=0)), axis=0, keepdims=True)
            sums_ref[row, tile : tile + 1, :] = total
    zeroth = sums_ref[3, :tiles, :]
    places, speeds = ([], [])
    for axis in range(3):
        force = sums_ref[axis, :tiles, :] - (place_own[axis] - middle[axis]) * zeroth
        speeds.append(weight_own * (speed_own[axis] + time_step * force / lanes))
        places.append(weight_own * (place_own[axis] + time_step * speeds[axis]))
    return places, speeds


def part_of(ref, tiles, row):
    return ref[row * tiles : (row + 1) * tiles, :]


def fill_planes(planes, tiles, blocks):
    kinds, rows, slots = planes.shape
    filled = len(blocks) * tiles
    planes[:, filled:, :] = jnp.zeros((kinds, rows - filled, slots), jnp.float32)
    for block, ref in enumerate(blocks):
        for kind in range(kinds):
            planes[kind, block * tiles : (block + 1) * tiles, :] = part_of(ref, tiles, kind)


def weights_of(aux, listed):
    slot = lax.broadcasted_iota(jnp.int32, aux.shape, 1).astype(jnp.float32)
    return jnp.where(slot < aux[:, listed : listed + 1], 1.0, 0.0)


def offsets_of(tiles, near_pair):
    device = device_index()
    toward = jnp.where(device % 2 == 0, 1.0, -1.0) * float(tiles)
    if near_pair:
        return [0.0, toward]
    return [-toward, -reach * toward, reach * toward]


def far_blocks(pair, forwarded, first_rows):
    return (pair[:first_rows, :], pair[first_rows:, :], forwarded[:first_rows, :])


def prepare(first, near_pair, listed, own_ref, blocks, lists_ref, weight_ref, tools):
    planes, scalars, copy_sem, feature_ref, moment_ref, source_ref = tools
    first_row = own_ref.shape[0] // planes.shape[0] if near_pair else 0
    tiles = own_ref.shape[0] // planes.shape[0]
    if not first:
        copy = pltpu.make_async_copy(lists_ref, scalars, copy_sem)
        copy.start()
    fill_planes(planes, tiles, blocks)
    if first:
        aux = planes[3]
        own_aux = jnp.concatenate(
            [part_of(own_ref, tiles, 3), jnp.zeros((round_up(tiles, 8) - tiles, lanes), jnp.float32)], axis=0
        )
        for row, value in enumerate(build_lists(aux, own_aux, tiles, listed, offsets_of(tiles, near_pair))):
            lists_ref[row : row + 1, :] = value
        copy = pltpu.make_async_copy(lists_ref, scalars, copy_sem)
        copy.start()
        weight_ref[...] = weights_of(aux, listed)
    middle = middles([part_of(own_ref, tiles, axis) for axis in range(3)])
    places = [planes[axis, first_row:, :] for axis in range(3)]
    build_sources(first_row, places, middle, weight_ref[first_row:, :], feature_ref, moment_ref, source_ref)
    return middle, copy


def alone(listed, first, *refs):
    if first:
        own_ref, total_ref, target_ref, moment_ref, source_ref, feature_ref = refs
        tiles = own_ref.shape[0] // 4
        weight = weights_of(part_of(own_ref, tiles, 3), listed)
    else:
        own_ref, weight_ref, total_ref, target_ref, moment_ref, source_ref, feature_ref = refs
        tiles = own_ref.shape[0] // 3
        weight = weight_ref[:tiles, :]
    own_place = [part_of(own_ref, tiles, axis) for axis in range(3)]
    middle = middles(own_place)
    total_ref[...] = jnp.zeros(total_ref.shape, jnp.float32)
    build_targets(own_place, middle, feature_ref, target_ref)
    build_sources(0, own_place, middle, weight, feature_ref, moment_ref, source_ref)


def begin(listed, first, *refs):
    own_ref, sibling_ref, target_ref, _, _, _, *refs = refs
    if first:
        total_ref, moment_ref, source_ref, lists_ref, weight_ref, *scratch = refs
    else:
        lists_ref, weight_ref, total_ref, moment_ref, source_ref, *scratch = refs
    tools = scratch + [moment_ref, source_ref]
    tiles = own_ref.shape[0] // tools[0].shape[0]
    _, copy = prepare(first, True, listed, own_ref, (own_ref, sibling_ref), lists_ref, weight_ref, tools)
    copy.wait()
    accumulate(tiles, tools[1], tools[5], target_ref, tools[4], total_ref)


def halves(speed, even, half):
    first, last = (speed[:half], speed[half:])
    return jnp.where(even, last, first), jnp.where(even, first, last)


def first_finish(
    listed, own_ref, pair, forwarded, total_in, target_ref, weight_own_ref, speed_ref, *refs
):
    total_ref, lists_ref, weight_ref, place_out, speed_out, sibling_out, beside_out, *scratch = refs
    *tools, sums_ref = scratch
    tiles = own_ref.shape[0] // tools[0].shape[0]
    half = tiles // 2
    middle, copy = prepare(True, False, listed, own_ref, far_blocks(pair, forwarded, own_ref.shape[0]), lists_ref, weight_ref, tools)
    copy.wait()
    accumulate(tiles, tools[1], tools[5], target_ref, tools[4], total_ref)
    places, speeds = advance(
        middle,
        [part_of(own_ref, tiles, axis) for axis in range(3)],
        [part_of(speed_ref, tiles, axis) for axis in range(3)],
        weight_own_ref[:tiles, :],
        total_ref,
        sums_ref,
    )
    even = device_index() % 2 == 0
    for axis in range(3):
        strip = slice(axis * tiles, (axis + 1) * tiles)
        place_out[strip, :] = places[axis]
        speed_out[strip, :] = speeds[axis]
        sibling_out[strip, :] = places[axis]
        beside_out[strip, :] = places[axis]
        strip = slice(3 * tiles + axis * half, 3 * tiles + (axis + 1) * half)
        sibling_out[strip, :], beside_out[strip, :] = halves(speeds[axis], even, half)


def second_finish(
    total_tiles,
    cuts_ref,
    own_ref,
    pair,
    forwarded,
    total_in,
    target_ref,
    weight_own_ref,
    speed_ref,
    sibling_ref,
    lists_ref,
    weight_ref,
    total_ref,
    state_ref,
    sibling_out,
    beside_out,
    out_ref,
    *scratch
):
    *tools, sums_ref, pool_ref = scratch
    tiles = own_ref.shape[0] // 3
    half = tiles // 2
    beside = pair[: 3 * (tiles + half), :]
    blocks = far_blocks(pair, forwarded, beside.shape[0])
    middle, copy = prepare(False, False, None, own_ref, blocks, lists_ref, weight_ref, tools)
    copy.wait()
    accumulate(tiles, tools[1], tools[5], target_ref, tools[4], total_ref)
    place_own = [part_of(own_ref, tiles, axis) for axis in range(3)]
    speed_own = [part_of(speed_ref, tiles, axis) for axis in range(3)]
    places, speeds = advance(middle, place_own, speed_own, weight_own_ref[:tiles, :], total_ref, sums_ref)
    even = device_index() % 2 == 0
    for row, value in enumerate(places + speeds):
        state_ref[row] = value
        strip = slice(row * half, (row + 1) * half)
        sibling_out[strip, :], beside_out[strip, :] = halves(value, even, half)
    lower, upper = ([], [])
    for row in range(6):
        if row < 3:
            sides = [part_of(ref, tiles, row) for ref in (sibling_ref, beside)]
            low_sides, high_sides = ([side[tiles - half :] for side in sides], [side[:half] for side in sides])
        else:
            strip = slice(3 * tiles + (row - 3) * half, 3 * tiles + (row - 2) * half)
            low_sides = high_sides = [ref[strip, :] for ref in (sibling_ref, beside)]
        lower.append(jnp.where(even, low_sides[1], low_sides[0]))
        upper.append(jnp.where(even, high_sides[0], high_sides[1]))
    place_rows(0, total_tiles, cuts_ref, lower, place_own + speed_own, upper, pool_ref, out_ref)


def place_rows(step, total_tiles, cuts_ref, lower, own, upper, pool_ref, out_ref):
    tiles, slots = own[0].shape
    half = tiles // 2
    capacity = out_ref.shape[1]
    device = device_index()
    last = cuts_ref.shape[1] - 1
    first_tile = cuts_ref[step, device]
    next_tile = jnp.where(device == last, total_tiles, cuts_ref[step, jnp.minimum(device + 1, last)])
    owned = next_tile - first_tile
    start = first_tile - (device * tiles - half)
    filled = lax.broadcasted_iota(jnp.int32, (capacity, slots), 0) < owned
    for row in range(6):
        pool_ref[row, :half, :] = lower[row]
        pool_ref[row, half : half + tiles, :] = own[row]
        pool_ref[row, half + tiles : 2 * tiles, :] = upper[row]
    for row in range(6):
        out_ref[row] = jnp.where(filled, pool_ref[row, pl.ds(start, capacity), :], 0.0)


def third_kernel(total_tiles, cuts_ref, sibling_ref, own_ref, beside_ref, out_ref, pool_ref):
    half = own_ref.shape[1] // 2
    even = device_index() % 2 == 0
    lower, upper = ([], [])
    for row in range(6):
        sibling, beside = (part_of(sibling_ref, half, row), part_of(beside_ref, half, row))
        lower.append(jnp.where(even, beside, sibling))
        upper.append(jnp.where(even, sibling, beside))
    place_rows(1, total_tiles, cuts_ref, lower, [own_ref[row] for row in range(6)], upper, pool_ref, out_ref)


def far(value):
    return pltpu.with_memory_space_constraint(value, pltpu.HBM)


def near(value):
    return pltpu.with_memory_space_constraint(value, pltpu.VMEM)


def body(particles, occupancy, neighbours, curve_cuts):
    tiles, _, slots = particles.shape
    listed = neighbours.shape[1]
    total_tiles = tiles * lax.axis_size(AXES)
    half = tiles // 2
    capacity = 2 * tiles
    near_rows = round_up(2 * tiles + 1, 8)
    far_rows = round_up((reach + 1) * tiles + 1, 8)
    list_rows = round_up(tiles + 2, 8)
    vmem = pl.BlockSpec(memory_space=pltpu.VMEM)
    smem = pl.BlockSpec(memory_space=pltpu.SMEM)

    def held(*sizes, dtype=jnp.float32):
        return pltpu.VMEM(sizes, dtype)

    def call(kernel, name, outs, ins, scratch, flops=0, aliases=None):
        held_ins = [far(value) if kind is smem else near(value) for kind, value in ins]
        return pl.pallas_call(
            kernel,
            out_shape=outs,
            in_specs=[kind for kind, _ in ins],
            out_specs=[vmem] * len(outs),
            scratch_shapes=scratch,
            input_output_aliases=aliases or {},
            compiler_params=pltpu.CompilerParams(vmem_limit_bytes=vmem_limit),
            cost_estimate=pl.CostEstimate(flops=flops, bytes_accessed=1 << 20, transcendentals=0),
            name=name,
        )(*held_ins)

    def moments(rows):
        return held(rows, 8, lanes)

    def sources(rows):
        return held(rows, feature_rows, lanes, dtype=jnp.bfloat16)

    def features(rows):
        return pltpu.VMEM((rows * feature_rows, lanes), jnp.float32)

    def tools(rows, kinds):
        return [
            pltpu.VMEM((kinds, rows, slots), jnp.float32),
            pltpu.SMEM((list_rows, lanes), jnp.int32),
            pltpu.SemaphoreType.DMA,
            features(rows),
        ]

    packed, speed = pl.pallas_call(
        functools.partial(pack_kernel, total_tiles),
        out_shape=(held(4 * tiles, slots), held(3 * tiles, slots)),
        in_specs=[vmem, smem, vmem],
        out_specs=(vmem, vmem),
        compiler_params=pltpu.CompilerParams(vmem_limit_bytes=vmem_limit),
        name="pack",
    )(far(particles), far(occupancy), far(neighbours))
    pool_scratch = pltpu.VMEM((6, round_up(capacity + tiles, 8), slots), jnp.float32)
    sums_scratch = pltpu.VMEM((4, round_up(tiles, 8), lanes), jnp.float32)
    blocks = lanes // block_rows
    totals = held(tiles * blocks + 1, 4, block_rows, lanes)
    targets = held(tiles * blocks + 1, block_rows, feature_rows, dtype=jnp.bfloat16)
    lists = held(list_rows, lanes, dtype=jnp.int32)
    edge = 3 * tiles + 3 * half
    work = 1 << 32

    sibling = swapped(packed, 0)
    pair = swapped(jnp.concatenate([packed, sibling], axis=0), 1)
    carried = [totals, moments(near_rows), sources(near_rows)]
    total, target, moment, source = call(
        functools.partial(alone, listed, True),
        "first_alone",
        [totals, targets, *carried[1:]],
        [(vmem, packed)],
        [features(round_up(tiles, 8))],
        1 << 22,
    )
    total, _, _, near_lists, near_weight = call(
        functools.partial(begin, listed, True),
        "first_near",
        carried + [lists, held(near_rows, slots)],
        [(vmem, value) for value in (packed, sibling, target, total, moment, source)],
        tools(near_rows, 4),
        work,
        {3: 0, 4: 1, 5: 2},
    )
    pair, near_weight = lax.optimization_barrier((pair, near_weight))
    forwarded = swapped(pair, 0)
    total, far_lists, far_weight, place, speed, sibling, beside = call(
        functools.partial(first_finish, listed),
        "first_far",
        [totals, lists, held(far_rows, slots), held(3 * tiles, slots), held(3 * tiles, slots), held(edge, slots), held(edge, slots)],
        [(vmem, value) for value in (packed, pair, forwarded, total, target, near_weight, speed)],
        tools(far_rows, 4) + [moments(far_rows), sources(far_rows), sums_scratch],
        work,
        {3: 0},
    )
    sibling = swapped(sibling, 0)
    pair = swapped(jnp.concatenate([beside, sibling[: 3 * tiles]], axis=0), 1)
    total, target, moment, source = call(
        functools.partial(alone, listed, False),
        "second_alone",
        [totals, targets, *carried[1:]],
        [(vmem, place), (vmem, near_weight)],
        [features(round_up(tiles, 8))],
        1 << 22,
    )
    total, _, _ = call(
        functools.partial(begin, listed, False),
        "second_near",
        carried,
        [(vmem, value) for value in (place, sibling, target, total, moment, source, near_lists, near_weight)],
        tools(near_rows, 3),
        work,
        {3: 0, 4: 1, 5: 2},
    )
    pair, total = lax.optimization_barrier((pair, total))
    forwarded = swapped(pair, 0)
    _, state, sibling, beside, after_first = call(
        functools.partial(second_finish, total_tiles),
        "second_far",
        [
            totals,
            held(6, tiles, slots),
            held(6 * half, slots),
            held(6 * half, slots),
            jax.ShapeDtypeStruct((6, capacity, slots), jnp.float32),
        ],
        [(smem, curve_cuts)]
        + [
            (vmem, value)
            for value in (place, pair, forwarded, total, target, near_weight, speed, sibling, far_lists, far_weight)
        ],
        tools(far_rows, 3) + [moments(far_rows), sources(far_rows), sums_scratch, pool_scratch],
        work,
        {4: 0},
    )
    beside = swapped(beside, 1, wrap=False)
    sibling = swapped(sibling, 0)
    (after_second,) = call(
        functools.partial(third_kernel, total_tiles),
        "place",
        [jax.ShapeDtypeStruct((6, capacity, slots), jnp.float32)],
        [(smem, curve_cuts), (vmem, sibling), (vmem, state), (vmem, beside)],
        [pool_scratch],
    )
    return (jnp.transpose(after_first, (1, 0, 2)), jnp.transpose(after_second, (1, 0, 2)))


def solution(mesh):
    in_specs = (P(AXES, None, None), P(AXES), P(AXES, None), P())
    out_specs = (P(AXES, None, None), P(AXES, None, None))
    return jax.shard_map(body, mesh=mesh, in_specs=in_specs, out_specs=out_specs, check_vma=False)
```

```python
import functools

import jax
import jax.numpy as jnp
from jax import lax
from jax.experimental import pallas as pl
from jax.experimental.pallas import tpu as pltpu
from jax.sharding import PartitionSpec as P

AXES = ("gx", "gy")
STEPS = 2

soften = 0.05
time_step = 0.5
reach = 2
chunk = 4
units = 8
feature_rows = 32
far_norm = 1e36
lanes = 128
block_rows = 64
vmem_limit = 16 << 20


def swapped(value, first, wrap=True):
    count = lax.axis_size(AXES)
    pairs = []
    for lower in range(first, count, 2):
        if wrap or lower + 1 < count:
            upper = (lower + 1) % count
            pairs += [(lower, upper), (upper, lower)]
    return lax.ppermute(value, AXES, pairs)


def round_up(value, step):
    return -(-value // step) * step


def device_index():
    return lax.axis_index("gx") * lax.axis_size("gy") + lax.axis_index("gy")


def pieces(value, count):
    parts = []
    rest = value
    for _ in range(count - 1):
        part = rest.astype(jnp.bfloat16).astype(jnp.float32)
        parts.append(part)
        rest = rest - part
    parts.append(rest.astype(jnp.bfloat16).astype(jnp.float32))
    return parts


def pack_kernel(total_tiles, particles_ref, occupancy_ref, neighbours_ref, packed_ref, speed_ref):
    tiles, slots = (particles_ref.shape[0], particles_ref.shape[2])
    listed = neighbours_ref.shape[1]
    for row in range(3):
        packed_ref[row * tiles : (row + 1) * tiles, :] = particles_ref[:, row, :]
        speed_ref[row * tiles : (row + 1) * tiles, :] = particles_ref[:, 3 + row, :]
    tile_ids = lax.broadcasted_iota(jnp.int32, (tiles, listed), 0)
    offsets = neighbours_ref[...] - (device_index() * tiles + tile_ids)
    offsets = jnp.where(offsets < 0, offsets + total_tiles, offsets)
    packed_ref[3 * tiles :, :] = jnp.zeros((tiles, slots), jnp.float32)
    packed_ref[3 * tiles :, :listed] = offsets.astype(jnp.float32)
    for tile in range(tiles):
        live = occupancy_ref[tile].astype(jnp.float32)
        packed_ref[3 * tiles + tile : 3 * tiles + tile + 1, listed : listed + 1] = jnp.full((1, 1), live)


def places_of(index, tiles, offsets):
    place = index + offsets[0]
    for block in range(1, len(offsets)):
        place = jnp.where(index >= block * tiles, index - block * tiles + offsets[block], place)
    return jnp.where(index >= len(offsets) * tiles, -1000.0, place)


def build_lists(aux, own, tiles, listed, offsets):
    rows = aux.shape[0]
    dummy = len(offsets) * tiles
    index = lax.broadcasted_iota(jnp.int32, (rows, lanes), 0).astype(jnp.float32)
    lane = lax.broadcasted_iota(jnp.int32, (rows, lanes), 1).astype(jnp.float32)
    place = places_of(index, tiles, offsets)
    mask = place == lane
    for entry in range(listed):
        mask = mask | (place + aux[:, entry : entry + 1] == lane)
    own_rows = own.shape[0]
    own_index = lax.broadcasted_iota(jnp.int32, (own_rows, lanes), 0).astype(jnp.float32)
    own_lane = lax.broadcasted_iota(jnp.int32, (own_rows, lanes), 1).astype(jnp.float32)
    own_place = places_of(own_lane, tiles, offsets)
    listing = own_index + own[:, 0:1] == own_place
    for entry in range(1, listed):
        listing = listing | (own_index + own[:, entry : entry + 1] == own_place)
    listing = jnp.where(listing, 1.0, 0.0)
    listing = jnp.concatenate([listing, jnp.zeros((lanes - own_rows, lanes), jnp.float32)], axis=0)
    listing = jnp.transpose(listing)[:rows]
    mask = jnp.maximum(jnp.where(mask, 1.0, 0.0), listing)
    mask = jnp.where((lane < tiles) & (index < dummy), mask, 0.0)
    earlier = lax.broadcasted_iota(jnp.int32, (rows, rows), 1) < lax.broadcasted_iota(jnp.int32, (rows, rows), 0)
    rank = jnp.dot(
        jnp.where(earlier, 1.0, 0.0).astype(jnp.bfloat16),
        mask.astype(jnp.bfloat16),
        preferred_element_type=jnp.float32,
    )
    key = jnp.where(mask > 0.5, rank, -1.0)
    counts = jnp.sum(mask, axis=0, keepdims=True)
    lists = []
    for tile in range(tiles):
        hit = key[:, tile : tile + 1] == lane
        row = jnp.sum(jnp.where(hit, index - dummy, 0.0), axis=0, keepdims=True) + dummy
        live = own[tile : tile + 1, listed : listed + 1]
        blocks = jnp.full((1, 1), 1.0)
        for filled in range(block_rows, lanes, block_rows):
            blocks = blocks + jnp.where(live > filled, 1.0, 0.0)
        lists.append(jnp.where(lane[:1] == lanes - 1, blocks, row))
    lists.append(jnp.where(lane[:1] == lanes - 1, 1.0, float(dummy)))
    lists.append(counts)
    return [row.astype(jnp.int32) for row in lists]


def middles(own_place):
    return [jnp.mean(axis[:8], keepdims=True) for axis in own_place]


def feature_of(feature_ref, tile):
    return feature_ref[tile * feature_rows : (tile + 1) * feature_rows, :]


def build_sources(first, places, middle, weight, feature_ref, moment_ref, source_ref):
    rows = weight.shape[0]
    moment_rows = moment_ref.reshape(moment_ref.shape[0] * 8, lanes)
    ones = jnp.ones_like(weight)
    zeros = jnp.zeros_like(weight)
    features = []
    norm = zeros
    for axis in range(3):
        value = weight * (places[axis] - middle[axis])
        norm = norm + value * value
        moment_rows[pl.ds(first * 8 + axis, rows, 8), :] = value
        high, mid, low = pieces(value, 3)
        features += [high, high, mid, mid, high, low]
    features += pieces(jnp.where(weight > 0.5, norm, far_norm), 3) + [ones] * 3
    features += [zeros] * (feature_rows - len(features))
    for row, value in enumerate(features):
        feature_ref[pl.ds(row, rows, feature_rows), :] = value
    for tile in range(rows):
        source_ref[first + tile] = feature_of(feature_ref, tile).astype(jnp.bfloat16)


def build_targets(own_place, middle, feature_ref, target_ref):
    tiles = own_place[0].shape[0]
    ones = jnp.ones_like(own_place[0])
    zeros = jnp.zeros_like(own_place[0])
    features = []
    norm = zeros
    for axis in range(3):
        value = own_place[axis] - middle[axis]
        norm = norm + value * value
        high, mid, low = [-2.0 * part for part in pieces(value, 3)]
        features += [high, mid, high, mid, low, high]
    features += [ones] * 3 + pieces(norm + soften, 3)
    features += [zeros] * (feature_rows - len(features))
    for row, value in enumerate(features):
        feature_ref[pl.ds(row, tiles, feature_rows), :] = value
    blank = jnp.zeros((lanes - feature_rows, lanes), jnp.float32)
    blocks = lanes // block_rows
    for tile in range(tiles):
        turned = jnp.transpose(jnp.concatenate([feature_of(feature_ref, tile), blank], axis=0))
        turned = turned[:, :feature_rows].astype(jnp.bfloat16)
        for block in range(blocks):
            target_ref[tile * blocks + block] = turned[block * block_rows : (block + 1) * block_rows]
    target_ref[tiles * blocks] = target_ref[0]


def accumulate(tiles, lists_ref, source_ref, target_ref, moment_ref, total_ref):
    blocks = lanes // block_rows
    item_counts = [
        jnp.maximum((lists_ref[tiles + 1, tile] + chunk - 1) // chunk, 1) * lists_ref[tile, lanes - 1] for tile in range(tiles)
    ]
    item_total = functools.reduce(lambda left, right: left + right, item_counts)

    def following(tile, block, part):
        more = (part + 1) * chunk < lists_ref[tiles + 1, tile]
        again = block + 1 < lists_ref[tile, lanes - 1]
        return (
            jnp.where(more | again, tile, jnp.minimum(tile + 1, tiles)),
            jnp.where(more, block, jnp.where(again, block + 1, 0)),
            jnp.where(more, part + 1, 0),
        )

    def sources_of(tile, part):
        return [lists_ref[tile, part * chunk + entry] for entry in range(chunk)]

    def distances(spot, sources):
        target = target_ref[spot]
        features = [source_ref[source] for source in sources]
        return [
            jnp.dot(target, jnp.concatenate(features[first : first + 2], axis=1), preferred_element_type=jnp.float32)
            for first in range(0, chunk, 2)
        ]

    def kernels(spot, places, squares):
        for first in range(0, block_rows, 8):
            strip = slice(first, first + 8)
            sums = [total_ref[spot, row, strip, :] for row in range(4)]
            for entry in range(chunk):
                column = (entry % 2) * lanes
                inverse = lax.rsqrt(squares[entry // 2][strip, column : column + lanes])
                kernel = inverse * inverse * inverse
                for axis in range(3):
                    sums[axis] = sums[axis] + kernel * places[entry][axis]
                sums[3] = sums[3] + kernel
            for row in range(4):
                total_ref[spot, row, strip, :] = sums[row]

    def step(_, carry):
        tile, block, part = carry
        waiting = None
        for _ in range(units):
            sources = sources_of(tile, part)
            places = [
                [jnp.broadcast_to(moment_ref[source, axis : axis + 1, :], (8, lanes)) for axis in range(3)]
                for source in sources
            ]
            spot = tile * blocks + block
            item = (spot, places, distances(spot, sources))
            if waiting is not None:
                kernels(*waiting)
            waiting = item
            tile, block, part = following(tile, block, part)
        kernels(*waiting)
        return (tile, block, part)

    zero = jnp.int32(0)
    lax.fori_loop(0, (item_total + units - 1) // units, step, (zero, zero, zero))


def advance(middle, place_own, speed_own, weight_own, total_ref, sums_ref):
    tiles = weight_own.shape[0]
    blocks = lanes // block_rows
    for tile in range(tiles):
        for row in range(4):
            parts = [total_ref[tile * blocks + block, row] for block in range(blocks)]
            total = jnp.sum(jnp.transpose(jnp.concatenate(parts, axis=0)), axis=0, keepdims=True)
            sums_ref[row, tile : tile + 1, :] = total
    zeroth = sums_ref[3, :tiles, :]
    places, speeds = ([], [])
    for axis in range(3):
        force = sums_ref[axis, :tiles, :] - (place_own[axis] - middle[axis]) * zeroth
        speeds.append(weight_own * (speed_own[axis] + time_step * force / lanes))
        places.append(weight_own * (place_own[axis] + time_step * speeds[axis]))
    return places, speeds


def part_of(ref, tiles, row):
    return ref[row * tiles : (row + 1) * tiles, :]


def fill_planes(planes, tiles, blocks):
    kinds, rows, slots = planes.shape
    filled = len(blocks) * tiles
    planes[:, filled:, :] = jnp.zeros((kinds, rows - filled, slots), jnp.float32)
    for block, ref in enumerate(blocks):
        for kind in range(kinds):
            planes[kind, block * tiles : (block + 1) * tiles, :] = part_of(ref, tiles, kind)


def weights_of(aux, listed):
    slot = lax.broadcasted_iota(jnp.int32, aux.shape, 1).astype(jnp.float32)
    return jnp.where(slot < aux[:, listed : listed + 1], 1.0, 0.0)


def offsets_of(tiles, near_pair):
    device = device_index()
    toward = jnp.where(device % 2 == 0, 1.0, -1.0) * float(tiles)
    if near_pair:
        return [0.0, toward]
    return [-toward, -reach * toward, reach * toward]


def far_blocks(pair, forwarded, first_rows):
    return (pair[:first_rows, :], pair[first_rows:, :], forwarded[:first_rows, :])


def prepare(first, near_pair, listed, own_ref, blocks, lists_ref, weight_ref, tools):
    planes, scalars, copy_sem, feature_ref, moment_ref, source_ref = tools
    first_row = own_ref.shape[0] // planes.shape[0] if near_pair else 0
    tiles = own_ref.shape[0] // planes.shape[0]
    if not first:
        copy = pltpu.make_async_copy(lists_ref, scalars, copy_sem)
        copy.start()
    fill_planes(planes, tiles, blocks)
    if first:
        aux = planes[3]
        own_aux = jnp.concatenate(
            [part_of(own_ref, tiles, 3), jnp.zeros((round_up(tiles, 8) - tiles, lanes), jnp.float32)], axis=0
        )
        for row, value in enumerate(build_lists(aux, own_aux, tiles, listed, offsets_of(tiles, near_pair))):
            lists_ref[row : row + 1, :] = value
        copy = pltpu.make_async_copy(lists_ref, scalars, copy_sem)
        copy.start()
        weight_ref[...] = weights_of(aux, listed)
    middle = middles([part_of(own_ref, tiles, axis) for axis in range(3)])
    places = [planes[axis, first_row:, :] for axis in range(3)]
    build_sources(first_row, places, middle, weight_ref[first_row:, :], feature_ref, moment_ref, source_ref)
    return middle, copy


def alone(listed, first, *refs):
    if first:
        own_ref, total_ref, target_ref, moment_ref, source_ref, feature_ref = refs
        tiles = own_ref.shape[0] // 4
        weight = weights_of(part_of(own_ref, tiles, 3), listed)
    else:
        own_ref, weight_ref, total_ref, target_ref, moment_ref, source_ref, feature_ref = refs
        tiles = own_ref.shape[0] // 3
        weight = weight_ref[:tiles, :]
    own_place = [part_of(own_ref, tiles, axis) for axis in range(3)]
    middle = middles(own_place)
    total_ref[...] = jnp.zeros(total_ref.shape, jnp.float32)
    build_targets(own_place, middle, feature_ref, target_ref)
    build_sources(0, own_place, middle, weight, feature_ref, moment_ref, source_ref)


def begin(listed, first, *refs):
    own_ref, sibling_ref, target_ref, _, _, _, *refs = refs
    if first:
        total_ref, moment_ref, source_ref, lists_ref, weight_ref, *scratch = refs
    else:
        lists_ref, weight_ref, total_ref, moment_ref, source_ref, *scratch = refs
    tools = scratch + [moment_ref, source_ref]
    tiles = own_ref.shape[0] // tools[0].shape[0]
    _, copy = prepare(first, True, listed, own_ref, (own_ref, sibling_ref), lists_ref, weight_ref, tools)
    copy.wait()
    accumulate(tiles, tools[1], tools[5], target_ref, tools[4], total_ref)


def halves(speed, even, half):
    first, last = (speed[:half], speed[half:])
    return jnp.where(even, last, first), jnp.where(even, first, last)


def first_finish(
    listed, own_ref, pair, forwarded, total_in, target_ref, weight_own_ref, speed_ref, *refs
):
    total_ref, lists_ref, weight_ref, place_out, speed_out, sibling_out, beside_out, *scratch = refs
    *tools, sums_ref = scratch
    tiles = own_ref.shape[0] // tools[0].shape[0]
    half = tiles // 2
    middle, copy = prepare(True, False, listed, own_ref, far_blocks(pair, forwarded, own_ref.shape[0]), lists_ref, weight_ref, tools)
    copy.wait()
    accumulate(tiles, tools[1], tools[5], target_ref, tools[4], total_ref)
    places, speeds = advance(
        middle,
        [part_of(own_ref, tiles, axis) for axis in range(3)],
        [part_of(speed_ref, tiles, axis) for axis in range(3)],
        weight_own_ref[:tiles, :],
        total_ref,
        sums_ref,
    )
    even = device_index() % 2 == 0
    for axis in range(3):
        strip = slice(axis * tiles, (axis + 1) * tiles)
        place_out[strip, :] = places[axis]
        speed_out[strip, :] = speeds[axis]
        sibling_out[strip, :] = places[axis]
        beside_out[strip, :] = places[axis]
        strip = slice(3 * tiles + axis * half, 3 * tiles + (axis + 1) * half)
        sibling_out[strip, :], beside_out[strip, :] = halves(speeds[axis], even, half)


def second_finish(
    own_ref,
    pair,
    forwarded,
    total_in,
    target_ref,
    weight_own_ref,
    speed_ref,
    lists_ref,
    weight_ref,
    total_ref,
    state_ref,
    sibling_out,
    beside_out,
    *scratch
):
    *tools, sums_ref = scratch
    tiles = own_ref.shape[0] // 3
    half = tiles // 2
    beside = pair[: 3 * (tiles + half), :]
    blocks = far_blocks(pair, forwarded, beside.shape[0])
    middle, copy = prepare(False, False, None, own_ref, blocks, lists_ref, weight_ref, tools)
    copy.wait()
    accumulate(tiles, tools[1], tools[5], target_ref, tools[4], total_ref)
    place_own = [part_of(own_ref, tiles, axis) for axis in range(3)]
    speed_own = [part_of(speed_ref, tiles, axis) for axis in range(3)]
    places, speeds = advance(middle, place_own, speed_own, weight_own_ref[:tiles, :], total_ref, sums_ref)
    even = device_index() % 2 == 0
    for row, value in enumerate(places + speeds):
        state_ref[row] = value
        strip = slice(row * half, (row + 1) * half)
        sibling_out[strip, :], beside_out[strip, :] = halves(value, even, half)


def first_place(total_tiles, cuts_ref, own_ref, speed_ref, sibling_ref, pair, out_ref, pool_ref):
    tiles = own_ref.shape[0] // 3
    half = tiles // 2
    beside = pair[: 3 * (tiles + half), :]
    place_own = [part_of(own_ref, tiles, axis) for axis in range(3)]
    speed_own = [part_of(speed_ref, tiles, axis) for axis in range(3)]
    even = device_index() % 2 == 0
    lower, upper = ([], [])
    for row in range(6):
        if row < 3:
            sides = [part_of(ref, tiles, row) for ref in (sibling_ref, beside)]
            low_sides, high_sides = ([side[tiles - half :] for side in sides], [side[:half] for side in sides])
        else:
            strip = slice(3 * tiles + (row - 3) * half, 3 * tiles + (row - 2) * half)
            low_sides = high_sides = [ref[strip, :] for ref in (sibling_ref, beside)]
        lower.append(jnp.where(even, low_sides[1], low_sides[0]))
        upper.append(jnp.where(even, high_sides[0], high_sides[1]))
    place_rows(0, total_tiles, cuts_ref, lower, place_own + speed_own, upper, pool_ref, out_ref)


def place_rows(step, total_tiles, cuts_ref, lower, own, upper, pool_ref, out_ref):
    tiles, slots = own[0].shape
    half = tiles // 2
    capacity = out_ref.shape[1]
    device = device_index()
    last = cuts_ref.shape[1] - 1
    first_tile = cuts_ref[step, device]
    next_tile = jnp.where(device == last, total_tiles, cuts_ref[step, jnp.minimum(device + 1, last)])
    owned = next_tile - first_tile
    start = first_tile - (device * tiles - half)
    filled = lax.broadcasted_iota(jnp.int32, (capacity, slots), 0) < owned
    for row in range(6):
        pool_ref[row, :half, :] = lower[row]
        pool_ref[row, half : half + tiles, :] = own[row]
        pool_ref[row, half + tiles : 2 * tiles, :] = upper[row]
    for row in range(6):
        out_ref[row] = jnp.where(filled, pool_ref[row, pl.ds(start, capacity), :], 0.0)


def third_kernel(total_tiles, cuts_ref, sibling_ref, own_ref, beside_ref, out_ref, pool_ref):
    half = own_ref.shape[1] // 2
    even = device_index() % 2 == 0
    lower, upper = ([], [])
    for row in range(6):
        sibling, beside = (part_of(sibling_ref, half, row), part_of(beside_ref, half, row))
        lower.append(jnp.where(even, beside, sibling))
        upper.append(jnp.where(even, sibling, beside))
    place_rows(1, total_tiles, cuts_ref, lower, [own_ref[row] for row in range(6)], upper, pool_ref, out_ref)


def far(value):
    return pltpu.with_memory_space_constraint(value, pltpu.HBM)


def near(value):
    return pltpu.with_memory_space_constraint(value, pltpu.VMEM)


def body(particles, occupancy, neighbours, curve_cuts):
    tiles, _, slots = particles.shape
    listed = neighbours.shape[1]
    total_tiles = tiles * lax.axis_size(AXES)
    half = tiles // 2
    capacity = 2 * tiles
    near_rows = round_up(2 * tiles + 1, 8)
    far_rows = round_up((reach + 1) * tiles + 1, 8)
    list_rows = round_up(tiles + 2, 8)
    vmem = pl.BlockSpec(memory_space=pltpu.VMEM)
    smem = pl.BlockSpec(memory_space=pltpu.SMEM)

    def held(*sizes, dtype=jnp.float32):
        return pltpu.VMEM(sizes, dtype)

    def call(kernel, name, outs, ins, scratch, flops=0, aliases=None):
        held_ins = [far(value) if kind is smem else near(value) for kind, value in ins]
        return pl.pallas_call(
            kernel,
            out_shape=outs,
            in_specs=[kind for kind, _ in ins],
            out_specs=[vmem] * len(outs),
            scratch_shapes=scratch,
            input_output_aliases=aliases or {},
            compiler_params=pltpu.CompilerParams(vmem_limit_bytes=vmem_limit),
            cost_estimate=pl.CostEstimate(flops=flops, bytes_accessed=1 << 20, transcendentals=0),
            name=name,
        )(*held_ins)

    def moments(rows):
        return held(rows, 8, lanes)

    def sources(rows):
        return held(rows, feature_rows, lanes, dtype=jnp.bfloat16)

    def features(rows):
        return pltpu.VMEM((rows * feature_rows, lanes), jnp.float32)

    def tools(rows, kinds):
        return [
            pltpu.VMEM((kinds, rows, slots), jnp.float32),
            pltpu.SMEM((list_rows, lanes), jnp.int32),
            pltpu.SemaphoreType.DMA,
            features(rows),
        ]

    packed, speed = pl.pallas_call(
        functools.partial(pack_kernel, total_tiles),
        out_shape=(held(4 * tiles, slots), held(3 * tiles, slots)),
        in_specs=[vmem, smem, vmem],
        out_specs=(vmem, vmem),
        compiler_params=pltpu.CompilerParams(vmem_limit_bytes=vmem_limit),
        name="pack",
    )(far(particles), far(occupancy), far(neighbours))
    pool_scratch = pltpu.VMEM((6, round_up(capacity + tiles, 8), slots), jnp.float32)
    sums_scratch = pltpu.VMEM((4, round_up(tiles, 8), lanes), jnp.float32)
    blocks = lanes // block_rows
    totals = held(tiles * blocks + 1, 4, block_rows, lanes)
    targets = held(tiles * blocks + 1, block_rows, feature_rows, dtype=jnp.bfloat16)
    lists = held(list_rows, lanes, dtype=jnp.int32)
    edge = 3 * tiles + 3 * half
    work = 1 << 32

    sibling = swapped(packed, 0)
    pair = swapped(jnp.concatenate([packed, sibling], axis=0), 1)
    carried = [totals, moments(near_rows), sources(near_rows)]
    total, target, moment, source = call(
        functools.partial(alone, listed, True),
        "first_alone",
        [totals, targets, *carried[1:]],
        [(vmem, packed)],
        [features(round_up(tiles, 8))],
        1 << 22,
    )
    total, _, _, near_lists, near_weight = call(
        functools.partial(begin, listed, True),
        "first_near",
        carried + [lists, held(near_rows, slots)],
        [(vmem, value) for value in (packed, sibling, target, total, moment, source)],
        tools(near_rows, 4),
        work,
        {3: 0, 4: 1, 5: 2},
    )
    pair, near_weight = lax.optimization_barrier((pair, near_weight))
    forwarded = swapped(pair, 0)
    total, far_lists, far_weight, place, speed, sibling, beside = call(
        functools.partial(first_finish, listed),
        "first_far",
        [totals, lists, held(far_rows, slots), held(3 * tiles, slots), held(3 * tiles, slots), held(edge, slots), held(edge, slots)],
        [(vmem, value) for value in (packed, pair, forwarded, total, target, near_weight, speed)],
        tools(far_rows, 4) + [moments(far_rows), sources(far_rows), sums_scratch],
        work,
        {3: 0},
    )
    sibling = swapped(sibling, 0)
    pair = swapped(jnp.concatenate([beside, sibling[: 3 * tiles]], axis=0), 1)
    total, target, moment, source = call(
        functools.partial(alone, listed, False),
        "second_alone",
        [totals, targets, *carried[1:]],
        [(vmem, place), (vmem, near_weight)],
        [features(round_up(tiles, 8))],
        1 << 22,
    )
    total, _, _ = call(
        functools.partial(begin, listed, False),
        "second_near",
        carried,
        [(vmem, value) for value in (place, sibling, target, total, moment, source, near_lists, near_weight)],
        tools(near_rows, 3),
        work,
        {3: 0, 4: 1, 5: 2},
    )
    pair, total = lax.optimization_barrier((pair, total))
    forwarded = swapped(pair, 0)
    (after_first,) = call(
        functools.partial(first_place, total_tiles),
        "first_place",
        [jax.ShapeDtypeStruct((6, capacity, slots), jnp.float32)],
        [(smem, curve_cuts)] + [(vmem, value) for value in (place, speed, sibling, pair)],
        [pool_scratch],
        1 << 22,
    )
    _, state, sibling, beside = call(
        second_finish,
        "second_far",
        [
            totals,
            held(6, tiles, slots),
            held(6 * half, slots),
            held(6 * half, slots),
        ],
        [
            (vmem, value)
            for value in (place, pair, forwarded, total, target, near_weight, speed, far_lists, far_weight)
        ],
        tools(far_rows, 3) + [moments(far_rows), sources(far_rows), sums_scratch],
        work,
        {3: 0},
    )
    beside = swapped(beside, 1, wrap=False)
    sibling = swapped(sibling, 0)
    (after_second,) = call(
        functools.partial(third_kernel, total_tiles),
        "place",
        [jax.ShapeDtypeStruct((6, capacity, slots), jnp.float32)],
        [(smem, curve_cuts), (vmem, sibling), (vmem, state), (vmem, beside)],
        [pool_scratch],
    )
    return (jnp.transpose(after_first, (1, 0, 2)), jnp.transpose(after_second, (1, 0, 2)))


def solution(mesh):
    in_specs = (P(AXES, None, None), P(AXES), P(AXES, None), P())
    out_specs = (P(AXES, None, None), P(AXES, None, None))
    return jax.shard_map(body, mesh=mesh, in_specs=in_specs, out_specs=out_specs, check_vma=False)
```

```python
import functools

import jax
import jax.numpy as jnp
from jax import lax
from jax.experimental import pallas as pl
from jax.experimental.pallas import tpu as pltpu
from jax.sharding import PartitionSpec as P

AXES = ("gx", "gy")
STEPS = 2

soften = 0.05
time_step = 0.5
reach = 2
chunk = 4
units = 8
feature_rows = 32
far_norm = 1e36
lanes = 128
block_rows = 64
vmem_limit = 16 << 20


def swapped(value, first, wrap=True):
    count = lax.axis_size(AXES)
    pairs = []
    for lower in range(first, count, 2):
        if wrap or lower + 1 < count:
            upper = (lower + 1) % count
            pairs += [(lower, upper), (upper, lower)]
    return lax.ppermute(value, AXES, pairs)


def round_up(value, step):
    return -(-value // step) * step


def device_index():
    return lax.axis_index("gx") * lax.axis_size("gy") + lax.axis_index("gy")


def pieces(value, count):
    parts = []
    rest = value
    for _ in range(count - 1):
        part = rest.astype(jnp.bfloat16).astype(jnp.float32)
        parts.append(part)
        rest = rest - part
    parts.append(rest.astype(jnp.bfloat16).astype(jnp.float32))
    return parts


def pack_kernel(total_tiles, particles_ref, occupancy_ref, neighbours_ref, packed_ref, speed_ref):
    tiles, slots = (particles_ref.shape[0], particles_ref.shape[2])
    listed = neighbours_ref.shape[1]
    for row in range(3):
        packed_ref[row * tiles : (row + 1) * tiles, :] = particles_ref[:, row, :]
        speed_ref[row * tiles : (row + 1) * tiles, :] = particles_ref[:, 3 + row, :]
    tile_ids = lax.broadcasted_iota(jnp.int32, (tiles, listed), 0)
    offsets = neighbours_ref[...] - (device_index() * tiles + tile_ids)
    offsets = jnp.where(offsets < 0, offsets + total_tiles, offsets)
    packed_ref[3 * tiles :, :] = jnp.zeros((tiles, slots), jnp.float32)
    packed_ref[3 * tiles :, :listed] = offsets.astype(jnp.float32)
    for tile in range(tiles):
        live = occupancy_ref[tile].astype(jnp.float32)
        packed_ref[3 * tiles + tile : 3 * tiles + tile + 1, listed : listed + 1] = jnp.full((1, 1), live)


def places_of(index, tiles, offsets):
    place = index + offsets[0]
    for block in range(1, len(offsets)):
        place = jnp.where(index >= block * tiles, index - block * tiles + offsets[block], place)
    return jnp.where(index >= len(offsets) * tiles, -1000.0, place)


def build_lists(aux, own, tiles, listed, offsets):
    rows = aux.shape[0]
    dummy = len(offsets) * tiles
    index = lax.broadcasted_iota(jnp.int32, (rows, lanes), 0).astype(jnp.float32)
    lane = lax.broadcasted_iota(jnp.int32, (rows, lanes), 1).astype(jnp.float32)
    place = places_of(index, tiles, offsets)
    mask = place == lane
    for entry in range(listed):
        mask = mask | (place + aux[:, entry : entry + 1] == lane)
    own_rows = own.shape[0]
    own_index = lax.broadcasted_iota(jnp.int32, (own_rows, lanes), 0).astype(jnp.float32)
    own_lane = lax.broadcasted_iota(jnp.int32, (own_rows, lanes), 1).astype(jnp.float32)
    own_place = places_of(own_lane, tiles, offsets)
    listing = own_index + own[:, 0:1] == own_place
    for entry in range(1, listed):
        listing = listing | (own_index + own[:, entry : entry + 1] == own_place)
    listing = jnp.where(listing, 1.0, 0.0)
    listing = jnp.concatenate([listing, jnp.zeros((lanes - own_rows, lanes), jnp.float32)], axis=0)
    listing = jnp.transpose(listing)[:rows]
    mask = jnp.maximum(jnp.where(mask, 1.0, 0.0), listing)
    mask = jnp.where((lane < tiles) & (index < dummy), mask, 0.0)
    earlier = lax.broadcasted_iota(jnp.int32, (rows, rows), 1) < lax.broadcasted_iota(jnp.int32, (rows, rows), 0)
    rank = jnp.dot(
        jnp.where(earlier, 1.0, 0.0).astype(jnp.bfloat16),
        mask.astype(jnp.bfloat16),
        preferred_element_type=jnp.float32,
    )
    key = jnp.where(mask > 0.5, rank, -1.0)
    counts = jnp.sum(mask, axis=0, keepdims=True)
    lists = []
    for tile in range(tiles):
        hit = key[:, tile : tile + 1] == lane
        row = jnp.sum(jnp.where(hit, index - dummy, 0.0), axis=0, keepdims=True) + dummy
        live = own[tile : tile + 1, listed : listed + 1]
        blocks = jnp.full((1, 1), 1.0)
        for filled in range(block_rows, lanes, block_rows):
            blocks = blocks + jnp.where(live > filled, 1.0, 0.0)
        lists.append(jnp.where(lane[:1] == lanes - 1, blocks, row))
    lists.append(jnp.where(lane[:1] == lanes - 1, 1.0, float(dummy)))
    lists.append(counts)
    return [row.astype(jnp.int32) for row in lists]


def middles(own_place):
    return [jnp.mean(axis[:8], keepdims=True) for axis in own_place]


def feature_of(feature_ref, tile):
    return feature_ref[tile * feature_rows : (tile + 1) * feature_rows, :]


def build_sources(first, places, middle, weight, feature_ref, moment_ref, source_ref):
    rows = weight.shape[0]
    moment_rows = moment_ref.reshape(moment_ref.shape[0] * 8, lanes)
    ones = jnp.ones_like(weight)
    zeros = jnp.zeros_like(weight)
    features = []
    norm = zeros
    for axis in range(3):
        value = weight * (places[axis] - middle[axis])
        norm = norm + value * value
        moment_rows[pl.ds(first * 8 + axis, rows, 8), :] = value
        high, mid, low = pieces(value, 3)
        features += [high, high, mid, mid, high, low]
    features += pieces(jnp.where(weight > 0.5, norm, far_norm), 3) + [ones] * 3
    features += [zeros] * (feature_rows - len(features))
    for row, value in enumerate(features):
        feature_ref[pl.ds(row, rows, feature_rows), :] = value
    for tile in range(rows):
        source_ref[first + tile] = feature_of(feature_ref, tile).astype(jnp.bfloat16)


def build_targets(own_place, middle, feature_ref, target_ref):
    tiles = own_place[0].shape[0]
    ones = jnp.ones_like(own_place[0])
    zeros = jnp.zeros_like(own_place[0])
    features = []
    norm = zeros
    for axis in range(3):
        value = own_place[axis] - middle[axis]
        norm = norm + value * value
        high, mid, low = [-2.0 * part for part in pieces(value, 3)]
        features += [high, mid, high, mid, low, high]
    features += [ones] * 3 + pieces(norm + soften, 3)
    features += [zeros] * (feature_rows - len(features))
    for row, value in enumerate(features):
        feature_ref[pl.ds(row, tiles, feature_rows), :] = value
    blank = jnp.zeros((lanes - feature_rows, lanes), jnp.float32)
    blocks = lanes // block_rows
    for tile in range(tiles):
        turned = jnp.transpose(jnp.concatenate([feature_of(feature_ref, tile), blank], axis=0))
        turned = turned[:, :feature_rows].astype(jnp.bfloat16)
        for block in range(blocks):
            target_ref[tile * blocks + block] = turned[block * block_rows : (block + 1) * block_rows]
    target_ref[tiles * blocks] = target_ref[0]


def accumulate(tiles, lists_ref, source_ref, target_ref, moment_ref, total_ref):
    blocks = lanes // block_rows
    item_counts = [
        jnp.maximum((lists_ref[tiles + 1, tile] + chunk - 1) // chunk, 1) * lists_ref[tile, lanes - 1] for tile in range(tiles)
    ]
    item_total = functools.reduce(lambda left, right: left + right, item_counts)

    def following(tile, block, part):
        more = (part + 1) * chunk < lists_ref[tiles + 1, tile]
        again = block + 1 < lists_ref[tile, lanes - 1]
        return (
            jnp.where(more | again, tile, jnp.minimum(tile + 1, tiles)),
            jnp.where(more, block, jnp.where(again, block + 1, 0)),
            jnp.where(more, part + 1, 0),
        )

    def sources_of(tile, part):
        return [lists_ref[tile, part * chunk + entry] for entry in range(chunk)]

    def distances(spot, sources):
        target = target_ref[spot]
        features = [source_ref[source] for source in sources]
        return [
            jnp.dot(target, jnp.concatenate(features[first : first + 2], axis=1), preferred_element_type=jnp.float32)
            for first in range(0, chunk, 2)
        ]

    def kernels(spot, places, squares):
        for first in range(0, block_rows, 8):
            strip = slice(first, first + 8)
            sums = [total_ref[spot, row, strip, :] for row in range(4)]
            for entry in range(chunk):
                column = (entry % 2) * lanes
                inverse = lax.rsqrt(squares[entry // 2][strip, column : column + lanes])
                kernel = inverse * inverse * inverse
                for axis in range(3):
                    sums[axis] = sums[axis] + kernel * places[entry][axis]
                sums[3] = sums[3] + kernel
            for row in range(4):
                total_ref[spot, row, strip, :] = sums[row]

    def step(_, carry):
        tile, block, part = carry
        waiting = None
        for _ in range(units):
            sources = sources_of(tile, part)
            places = [
                [jnp.broadcast_to(moment_ref[source, axis : axis + 1, :], (8, lanes)) for axis in range(3)]
                for source in sources
            ]
            spot = tile * blocks + block
            item = (spot, places, distances(spot, sources))
            if waiting is not None:
                kernels(*waiting)
            waiting = item
            tile, block, part = following(tile, block, part)
        kernels(*waiting)
        return (tile, block, part)

    zero = jnp.int32(0)
    lax.fori_loop(0, (item_total + units - 1) // units, step, (zero, zero, zero))


def advance(middle, place_own, speed_own, weight_own, total_ref, sums_ref):
    tiles = weight_own.shape[0]
    blocks = lanes // block_rows
    for tile in range(tiles):
        for row in range(4):
            parts = [total_ref[tile * blocks + block, row] for block in range(blocks)]
            total = jnp.sum(jnp.transpose(jnp.concatenate(parts, axis=0)), axis=0, keepdims=True)
            sums_ref[row, tile : tile + 1, :] = total
    zeroth = sums_ref[3, :tiles, :]
    places, speeds = ([], [])
    for axis in range(3):
        force = sums_ref[axis, :tiles, :] - (place_own[axis] - middle[axis]) * zeroth
        speeds.append(weight_own * (speed_own[axis] + time_step * force / lanes))
        places.append(weight_own * (place_own[axis] + time_step * speeds[axis]))
    return places, speeds


def part_of(ref, tiles, row):
    return ref[row * tiles : (row + 1) * tiles, :]


def fill_planes(planes, tiles, blocks):
    kinds, rows, slots = planes.shape
    filled = len(blocks) * tiles
    planes[:, filled:, :] = jnp.zeros((kinds, rows - filled, slots), jnp.float32)
    for block, ref in enumerate(blocks):
        for kind in range(kinds):
            planes[kind, block * tiles : (block + 1) * tiles, :] = part_of(ref, tiles, kind)


def weights_of(aux, listed):
    slot = lax.broadcasted_iota(jnp.int32, aux.shape, 1).astype(jnp.float32)
    return jnp.where(slot < aux[:, listed : listed + 1], 1.0, 0.0)


def offsets_of(tiles, near_pair):
    device = device_index()
    toward = jnp.where(device % 2 == 0, 1.0, -1.0) * float(tiles)
    if near_pair:
        return [0.0, toward]
    return [-toward, -reach * toward, reach * toward]


def far_blocks(pair, forwarded, first_rows):
    return (pair[:first_rows, :], pair[first_rows:, :], forwarded[:first_rows, :])


def prepare(first, near_pair, listed, own_ref, blocks, lists_ref, weight_ref, tools):
    planes, scalars, copy_sem, feature_ref, moment_ref, source_ref = tools
    first_row = own_ref.shape[0] // planes.shape[0] * (1 if near_pair else reach)
    tiles = own_ref.shape[0] // planes.shape[0]
    if not first:
        copy = pltpu.make_async_copy(lists_ref, scalars, copy_sem)
        copy.start()
    fill_planes(planes, tiles, blocks)
    if first:
        aux = planes[3]
        own_aux = jnp.concatenate(
            [part_of(own_ref, tiles, 3), jnp.zeros((round_up(tiles, 8) - tiles, lanes), jnp.float32)], axis=0
        )
        for row, value in enumerate(build_lists(aux, own_aux, tiles, listed, offsets_of(tiles, near_pair))):
            lists_ref[row : row + 1, :] = value
        copy = pltpu.make_async_copy(lists_ref, scalars, copy_sem)
        copy.start()
        weight_ref[...] = weights_of(aux, listed)
    middle = middles([part_of(own_ref, tiles, axis) for axis in range(3)])
    places = [planes[axis, first_row:, :] for axis in range(3)]
    build_sources(first_row, places, middle, weight_ref[first_row:, :], feature_ref, moment_ref, source_ref)
    return middle, copy


def alone(listed, first, *refs):
    if first:
        own_ref, total_ref, target_ref, moment_ref, source_ref, feature_ref = refs
        tiles = own_ref.shape[0] // 4
        weight = weights_of(part_of(own_ref, tiles, 3), listed)
    else:
        own_ref, weight_ref, total_ref, target_ref, moment_ref, source_ref, feature_ref = refs
        tiles = own_ref.shape[0] // 3
        weight = weight_ref[:tiles, :]
    own_place = [part_of(own_ref, tiles, axis) for axis in range(3)]
    middle = middles(own_place)
    total_ref[...] = jnp.zeros(total_ref.shape, jnp.float32)
    build_targets(own_place, middle, feature_ref, target_ref)
    build_sources(0, own_place, middle, weight, feature_ref, moment_ref, source_ref)


def ahead(listed, first, *refs):
    own_ref, pair, *refs = refs
    *given, moment_ref, source_ref, feature_ref = refs
    tiles = own_ref.shape[0] // (4 if first else 3)
    first_rows = own_ref.shape[0] if first else 3 * (tiles + tiles // 2)
    middle = middles([part_of(own_ref, tiles, axis) for axis in range(3)])
    for index, block in enumerate((pair[:first_rows, :], pair[first_rows:, :])):
        if first:
            weight = weights_of(part_of(block, tiles, 3), listed)
        else:
            weight = given[0][index * tiles : (index + 1) * tiles, :]
        places = [part_of(block, tiles, axis) for axis in range(3)]
        build_sources(index * tiles, places, middle, weight, feature_ref, moment_ref, source_ref)


def begin(listed, first, *refs):
    own_ref, sibling_ref, target_ref, _, _, _, *refs = refs
    if first:
        total_ref, moment_ref, source_ref, lists_ref, weight_ref, *scratch = refs
    else:
        lists_ref, weight_ref, total_ref, moment_ref, source_ref, *scratch = refs
    tools = scratch + [moment_ref, source_ref]
    tiles = own_ref.shape[0] // tools[0].shape[0]
    _, copy = prepare(first, True, listed, own_ref, (own_ref, sibling_ref), lists_ref, weight_ref, tools)
    copy.wait()
    accumulate(tiles, tools[1], tools[5], target_ref, tools[4], total_ref)


def halves(speed, even, half):
    first, last = (speed[:half], speed[half:])
    return jnp.where(even, last, first), jnp.where(even, first, last)


def first_finish(
    listed, own_ref, pair, forwarded, total_in, target_ref, weight_own_ref, speed_ref, moment_in, source_in, *refs
):
    total_ref, moment_ref, source_ref, lists_ref, weight_ref, place_out, speed_out, *refs = refs
    sibling_out, beside_out, *tools, sums_ref = refs
    tools += [moment_ref, source_ref]
    tiles = own_ref.shape[0] // tools[0].shape[0]
    half = tiles // 2
    middle, copy = prepare(True, False, listed, own_ref, far_blocks(pair, forwarded, own_ref.shape[0]), lists_ref, weight_ref, tools)
    copy.wait()
    accumulate(tiles, tools[1], tools[5], target_ref, tools[4], total_ref)
    places, speeds = advance(
        middle,
        [part_of(own_ref, tiles, axis) for axis in range(3)],
        [part_of(speed_ref, tiles, axis) for axis in range(3)],
        weight_own_ref[:tiles, :],
        total_ref,
        sums_ref,
    )
    even = device_index() % 2 == 0
    for axis in range(3):
        strip = slice(axis * tiles, (axis + 1) * tiles)
        place_out[strip, :] = places[axis]
        speed_out[strip, :] = speeds[axis]
        sibling_out[strip, :] = places[axis]
        beside_out[strip, :] = places[axis]
        strip = slice(3 * tiles + axis * half, 3 * tiles + (axis + 1) * half)
        sibling_out[strip, :], beside_out[strip, :] = halves(speeds[axis], even, half)


def second_finish(
    own_ref,
    pair,
    forwarded,
    total_in,
    target_ref,
    weight_own_ref,
    speed_ref,
    lists_ref,
    weight_ref,
    moment_in,
    source_in,
    total_ref,
    moment_ref,
    source_ref,
    state_ref,
    sibling_out,
    beside_out,
    *scratch
):
    *tools, sums_ref = scratch
    tools += [moment_ref, source_ref]
    tiles = own_ref.shape[0] // 3
    half = tiles // 2
    beside = pair[: 3 * (tiles + half), :]
    blocks = far_blocks(pair, forwarded, beside.shape[0])
    middle, copy = prepare(False, False, None, own_ref, blocks, lists_ref, weight_ref, tools)
    copy.wait()
    accumulate(tiles, tools[1], tools[5], target_ref, tools[4], total_ref)
    place_own = [part_of(own_ref, tiles, axis) for axis in range(3)]
    speed_own = [part_of(speed_ref, tiles, axis) for axis in range(3)]
    places, speeds = advance(middle, place_own, speed_own, weight_own_ref[:tiles, :], total_ref, sums_ref)
    even = device_index() % 2 == 0
    for row, value in enumerate(places + speeds):
        state_ref[row] = value
        strip = slice(row * half, (row + 1) * half)
        sibling_out[strip, :], beside_out[strip, :] = halves(value, even, half)


def first_place(total_tiles, cuts_ref, own_ref, speed_ref, sibling_ref, pair, out_ref, pool_ref):
    tiles = own_ref.shape[0] // 3
    half = tiles // 2
    beside = pair[: 3 * (tiles + half), :]
    place_own = [part_of(own_ref, tiles, axis) for axis in range(3)]
    speed_own = [part_of(speed_ref, tiles, axis) for axis in range(3)]
    even = device_index() % 2 == 0
    lower, upper = ([], [])
    for row in range(6):
        if row < 3:
            sides = [part_of(ref, tiles, row) for ref in (sibling_ref, beside)]
            low_sides, high_sides = ([side[tiles - half :] for side in sides], [side[:half] for side in sides])
        else:
            strip = slice(3 * tiles + (row - 3) * half, 3 * tiles + (row - 2) * half)
            low_sides = high_sides = [ref[strip, :] for ref in (sibling_ref, beside)]
        lower.append(jnp.where(even, low_sides[1], low_sides[0]))
        upper.append(jnp.where(even, high_sides[0], high_sides[1]))
    place_rows(0, total_tiles, cuts_ref, lower, place_own + speed_own, upper, pool_ref, out_ref)


def place_rows(step, total_tiles, cuts_ref, lower, own, upper, pool_ref, out_ref):
    tiles, slots = own[0].shape
    half = tiles // 2
    capacity = out_ref.shape[1]
    device = device_index()
    last = cuts_ref.shape[1] - 1
    first_tile = cuts_ref[step, device]
    next_tile = jnp.where(device == last, total_tiles, cuts_ref[step, jnp.minimum(device + 1, last)])
    owned = next_tile - first_tile
    start = first_tile - (device * tiles - half)
    filled = lax.broadcasted_iota(jnp.int32, (capacity, slots), 0) < owned
    for row in range(6):
        pool_ref[row, :half, :] = lower[row]
        pool_ref[row, half : half + tiles, :] = own[row]
        pool_ref[row, half + tiles : 2 * tiles, :] = upper[row]
    for row in range(6):
        out_ref[row] = jnp.where(filled, pool_ref[row, pl.ds(start, capacity), :], 0.0)


def third_kernel(total_tiles, cuts_ref, sibling_ref, own_ref, beside_ref, out_ref, pool_ref):
    half = own_ref.shape[1] // 2
    even = device_index() % 2 == 0
    lower, upper = ([], [])
    for row in range(6):
        sibling, beside = (part_of(sibling_ref, half, row), part_of(beside_ref, half, row))
        lower.append(jnp.where(even, beside, sibling))
        upper.append(jnp.where(even, sibling, beside))
    place_rows(1, total_tiles, cuts_ref, lower, [own_ref[row] for row in range(6)], upper, pool_ref, out_ref)


def far(value):
    return pltpu.with_memory_space_constraint(value, pltpu.HBM)


def near(value):
    return pltpu.with_memory_space_constraint(value, pltpu.VMEM)


def body(particles, occupancy, neighbours, curve_cuts):
    tiles, _, slots = particles.shape
    listed = neighbours.shape[1]
    total_tiles = tiles * lax.axis_size(AXES)
    half = tiles // 2
    capacity = 2 * tiles
    near_rows = round_up(2 * tiles + 1, 8)
    far_rows = round_up((reach + 1) * tiles + 1, 8)
    list_rows = round_up(tiles + 2, 8)
    vmem = pl.BlockSpec(memory_space=pltpu.VMEM)
    smem = pl.BlockSpec(memory_space=pltpu.SMEM)

    def held(*sizes, dtype=jnp.float32):
        return pltpu.VMEM(sizes, dtype)

    def call(kernel, name, outs, ins, scratch, flops=0, aliases=None):
        held_ins = [far(value) if kind is smem else near(value) for kind, value in ins]
        return pl.pallas_call(
            kernel,
            out_shape=outs,
            in_specs=[kind for kind, _ in ins],
            out_specs=[vmem] * len(outs),
            scratch_shapes=scratch,
            input_output_aliases=aliases or {},
            compiler_params=pltpu.CompilerParams(vmem_limit_bytes=vmem_limit),
            cost_estimate=pl.CostEstimate(flops=flops, bytes_accessed=1 << 20, transcendentals=0),
            name=name,
        )(*held_ins)

    def moments(rows):
        return held(rows, 8, lanes)

    def sources(rows):
        return held(rows, feature_rows, lanes, dtype=jnp.bfloat16)

    def features(rows):
        return pltpu.VMEM((rows * feature_rows, lanes), jnp.float32)

    def tools(rows, kinds):
        return [
            pltpu.VMEM((kinds, rows, slots), jnp.float32),
            pltpu.SMEM((list_rows, lanes), jnp.int32),
            pltpu.SemaphoreType.DMA,
            features(rows),
        ]

    packed, speed = pl.pallas_call(
        functools.partial(pack_kernel, total_tiles),
        out_shape=(held(4 * tiles, slots), held(3 * tiles, slots)),
        in_specs=[vmem, smem, vmem],
        out_specs=(vmem, vmem),
        compiler_params=pltpu.CompilerParams(vmem_limit_bytes=vmem_limit),
        name="pack",
    )(far(particles), far(occupancy), far(neighbours))
    pool_scratch = pltpu.VMEM((6, round_up(capacity + tiles, 8), slots), jnp.float32)
    sums_scratch = pltpu.VMEM((4, round_up(tiles, 8), lanes), jnp.float32)
    blocks = lanes // block_rows
    totals = held(tiles * blocks + 1, 4, block_rows, lanes)
    targets = held(tiles * blocks + 1, block_rows, feature_rows, dtype=jnp.bfloat16)
    lists = held(list_rows, lanes, dtype=jnp.int32)
    edge = 3 * tiles + 3 * half
    work = 1 << 32

    sibling = swapped(packed, 0)
    pair = swapped(jnp.concatenate([packed, sibling], axis=0), 1)
    carried = [totals, moments(near_rows), sources(near_rows)]
    total, target, moment, source = call(
        functools.partial(alone, listed, True),
        "first_alone",
        [totals, targets, *carried[1:]],
        [(vmem, packed)],
        [features(round_up(tiles, 8))],
        1 << 22,
    )
    total, _, _, near_lists, near_weight = call(
        functools.partial(begin, listed, True),
        "first_near",
        carried + [lists, held(near_rows, slots)],
        [(vmem, value) for value in (packed, sibling, target, total, moment, source)],
        tools(near_rows, 4),
        work,
        {3: 0, 4: 1, 5: 2},
    )
    pair, near_weight = lax.optimization_barrier((pair, near_weight))
    forwarded = swapped(pair, 0)
    far_carried = [totals, moments(far_rows), sources(far_rows)]
    moment, source = call(
        functools.partial(ahead, listed, True),
        "first_ahead",
        far_carried[1:],
        [(vmem, packed), (vmem, pair)],
        [features(round_up(tiles, 8))],
        1 << 22,
    )
    total, _, _, far_lists, far_weight, place, speed, sibling, beside = call(
        functools.partial(first_finish, listed),
        "first_far",
        far_carried
        + [lists, held(far_rows, slots), held(3 * tiles, slots), held(3 * tiles, slots), held(edge, slots), held(edge, slots)],
        [(vmem, value) for value in (packed, pair, forwarded, total, target, near_weight, speed, moment, source)],
        tools(far_rows, 4) + [sums_scratch],
        work,
        {3: 0, 7: 1, 8: 2},
    )
    sibling = swapped(sibling, 0)
    pair = swapped(jnp.concatenate([beside, sibling[: 3 * tiles]], axis=0), 1)
    total, target, moment, source = call(
        functools.partial(alone, listed, False),
        "second_alone",
        [totals, targets, *carried[1:]],
        [(vmem, place), (vmem, near_weight)],
        [features(round_up(tiles, 8))],
        1 << 22,
    )
    total, _, _ = call(
        functools.partial(begin, listed, False),
        "second_near",
        carried,
        [(vmem, value) for value in (place, sibling, target, total, moment, source, near_lists, near_weight)],
        tools(near_rows, 3),
        work,
        {3: 0, 4: 1, 5: 2},
    )
    pair, total = lax.optimization_barrier((pair, total))
    forwarded = swapped(pair, 0)
    (after_first,) = call(
        functools.partial(first_place, total_tiles),
        "first_place",
        [jax.ShapeDtypeStruct((6, capacity, slots), jnp.float32)],
        [(smem, curve_cuts)] + [(vmem, value) for value in (place, speed, sibling, pair)],
        [pool_scratch],
        1 << 22,
    )
    moment, source = call(
        functools.partial(ahead, listed, False),
        "second_ahead",
        far_carried[1:],
        [(vmem, place), (vmem, pair), (vmem, far_weight)],
        [features(round_up(tiles, 8))],
        1 << 22,
    )
    _, _, _, state, sibling, beside = call(
        second_finish,
        "second_far",
        far_carried
        + [
            held(6, tiles, slots),
            held(6 * half, slots),
            held(6 * half, slots),
        ],
        [
            (vmem, value)
            for value in (place, pair, forwarded, total, target, near_weight, speed, far_lists, far_weight, moment, source)
        ],
        tools(far_rows, 3) + [sums_scratch],
        work,
        {3: 0, 9: 1, 10: 2},
    )
    beside = swapped(beside, 1, wrap=False)
    sibling = swapped(sibling, 0)
    (after_second,) = call(
        functools.partial(third_kernel, total_tiles),
        "place",
        [jax.ShapeDtypeStruct((6, capacity, slots), jnp.float32)],
        [(smem, curve_cuts), (vmem, sibling), (vmem, state), (vmem, beside)],
        [pool_scratch],
    )
    return (jnp.transpose(after_first, (1, 0, 2)), jnp.transpose(after_second, (1, 0, 2)))


def solution(mesh):
    in_specs = (P(AXES, None, None), P(AXES), P(AXES, None), P())
    out_specs = (P(AXES, None, None), P(AXES, None, None))
    return jax.shard_map(body, mesh=mesh, in_specs=in_specs, out_specs=out_specs, check_vma=False)
```

```python
import functools

import jax
import jax.numpy as jnp
from jax import lax
from jax.experimental import pallas as pl
from jax.experimental.pallas import tpu as pltpu
from jax.sharding import PartitionSpec as P

AXES = ("gx", "gy")
STEPS = 2

soften = 0.05
time_step = 0.5
reach = 2
chunk = 4
units = 12
feature_rows = 32
far_norm = 1e36
lanes = 128
block_rows = 64
vmem_limit = 16 << 20


def swapped(value, first, wrap=True):
    count = lax.axis_size(AXES)
    pairs = []
    for lower in range(first, count, 2):
        if wrap or lower + 1 < count:
            upper = (lower + 1) % count
            pairs += [(lower, upper), (upper, lower)]
    return lax.ppermute(value, AXES, pairs)


def round_up(value, step):
    return -(-value // step) * step


def device_index():
    return lax.axis_index("gx") * lax.axis_size("gy") + lax.axis_index("gy")


def pieces(value, count):
    parts = []
    rest = value
    for _ in range(count - 1):
        part = rest.astype(jnp.bfloat16).astype(jnp.float32)
        parts.append(part)
        rest = rest - part
    parts.append(rest.astype(jnp.bfloat16).astype(jnp.float32))
    return parts


def pack_kernel(total_tiles, particles_ref, occupancy_ref, neighbours_ref, packed_ref, speed_ref):
    tiles, slots = (particles_ref.shape[0], particles_ref.shape[2])
    listed = neighbours_ref.shape[1]
    for row in range(3):
        packed_ref[row * tiles : (row + 1) * tiles, :] = particles_ref[:, row, :]
        speed_ref[row * tiles : (row + 1) * tiles, :] = particles_ref[:, 3 + row, :]
    tile_ids = lax.broadcasted_iota(jnp.int32, (tiles, listed), 0)
    offsets = neighbours_ref[...] - (device_index() * tiles + tile_ids)
    offsets = jnp.where(offsets < 0, offsets + total_tiles, offsets)
    packed_ref[3 * tiles :, :] = jnp.zeros((tiles, slots), jnp.float32)
    packed_ref[3 * tiles :, :listed] = offsets.astype(jnp.float32)
    for tile in range(tiles):
        live = occupancy_ref[tile].astype(jnp.float32)
        packed_ref[3 * tiles + tile : 3 * tiles + tile + 1, listed : listed + 1] = jnp.full((1, 1), live)


def places_of(index, tiles, offsets):
    place = index + offsets[0]
    for block in range(1, len(offsets)):
        place = jnp.where(index >= block * tiles, index - block * tiles + offsets[block], place)
    return jnp.where(index >= len(offsets) * tiles, -1000.0, place)


def build_lists(aux, own, tiles, listed, offsets):
    rows = aux.shape[0]
    dummy = len(offsets) * tiles
    index = lax.broadcasted_iota(jnp.int32, (rows, lanes), 0).astype(jnp.float32)
    lane = lax.broadcasted_iota(jnp.int32, (rows, lanes), 1).astype(jnp.float32)
    place = places_of(index, tiles, offsets)
    mask = place == lane
    for entry in range(listed):
        mask = mask | (place + aux[:, entry : entry + 1] == lane)
    own_rows = own.shape[0]
    own_index = lax.broadcasted_iota(jnp.int32, (own_rows, lanes), 0).astype(jnp.float32)
    own_lane = lax.broadcasted_iota(jnp.int32, (own_rows, lanes), 1).astype(jnp.float32)
    own_place = places_of(own_lane, tiles, offsets)
    listing = own_index + own[:, 0:1] == own_place
    for entry in range(1, listed):
        listing = listing | (own_index + own[:, entry : entry + 1] == own_place)
    listing = jnp.where(listing, 1.0, 0.0)
    listing = jnp.concatenate([listing, jnp.zeros((lanes - own_rows, lanes), jnp.float32)], axis=0)
    listing = jnp.transpose(listing)[:rows]
    mask = jnp.maximum(jnp.where(mask, 1.0, 0.0), listing)
    mask = jnp.where((lane < tiles) & (index < dummy), mask, 0.0)
    earlier = lax.broadcasted_iota(jnp.int32, (rows, rows), 1) < lax.broadcasted_iota(jnp.int32, (rows, rows), 0)
    rank = jnp.dot(
        jnp.where(earlier, 1.0, 0.0).astype(jnp.bfloat16),
        mask.astype(jnp.bfloat16),
        preferred_element_type=jnp.float32,
    )
    key = jnp.where(mask > 0.5, rank, -1.0)
    counts = jnp.sum(mask, axis=0, keepdims=True)
    lists = []
    for tile in range(tiles):
        hit = key[:, tile : tile + 1] == lane
        row = jnp.sum(jnp.where(hit, index - dummy, 0.0), axis=0, keepdims=True) + dummy
        live = own[tile : tile + 1, listed : listed + 1]
        blocks = jnp.full((1, 1), 1.0)
        for filled in range(block_rows, lanes, block_rows):
            blocks = blocks + jnp.where(live > filled, 1.0, 0.0)
        lists.append(jnp.where(lane[:1] == lanes - 1, blocks, row))
    lists.append(jnp.where(lane[:1] == lanes - 1, 1.0, float(dummy)))
    lists.append(counts)
    return [row.astype(jnp.int32) for row in lists]


def middles(own_place):
    return [jnp.mean(axis[:8], keepdims=True) for axis in own_place]


def feature_of(feature_ref, tile):
    return feature_ref[tile * feature_rows : (tile + 1) * feature_rows, :]


def build_sources(first, places, middle, weight, feature_ref, moment_ref, source_ref):
    rows = weight.shape[0]
    moment_rows = moment_ref.reshape(moment_ref.shape[0] * 8, lanes)
    ones = jnp.ones_like(weight)
    zeros = jnp.zeros_like(weight)
    features = []
    norm = zeros
    for axis in range(3):
        value = weight * (places[axis] - middle[axis])
        norm = norm + value * value
        moment_rows[pl.ds(first * 8 + axis, rows, 8), :] = value
        high, mid, low = pieces(value, 3)
        features += [high, high, mid, mid, high, low]
    features += pieces(jnp.where(weight > 0.5, norm, far_norm), 3) + [ones] * 3
    features += [zeros] * (feature_rows - len(features))
    for row, value in enumerate(features):
        feature_ref[pl.ds(row, rows, feature_rows), :] = value
    for tile in range(rows):
        source_ref[first + tile] = feature_of(feature_ref, tile).astype(jnp.bfloat16)


def build_targets(own_place, middle, feature_ref, target_ref):
    tiles = own_place[0].shape[0]
    ones = jnp.ones_like(own_place[0])
    zeros = jnp.zeros_like(own_place[0])
    features = []
    norm = zeros
    for axis in range(3):
        value = own_place[axis] - middle[axis]
        norm = norm + value * value
        high, mid, low = [-2.0 * part for part in pieces(value, 3)]
        features += [high, mid, high, mid, low, high]
    features += [ones] * 3 + pieces(norm + soften, 3)
    features += [zeros] * (feature_rows - len(features))
    for row, value in enumerate(features):
        feature_ref[pl.ds(row, tiles, feature_rows), :] = value
    blank = jnp.zeros((lanes - feature_rows, lanes), jnp.float32)
    blocks = lanes // block_rows
    for tile in range(tiles):
        turned = jnp.transpose(jnp.concatenate([feature_of(feature_ref, tile), blank], axis=0))
        turned = turned[:, :feature_rows].astype(jnp.bfloat16)
        for block in range(blocks):
            target_ref[tile * blocks + block] = turned[block * block_rows : (block + 1) * block_rows]
    target_ref[tiles * blocks] = target_ref[0]


def accumulate(tiles, lists_ref, source_ref, target_ref, moment_ref, total_ref):
    blocks = lanes // block_rows
    item_counts = [
        jnp.maximum((lists_ref[tiles + 1, tile] + chunk - 1) // chunk, 1) * lists_ref[tile, lanes - 1] for tile in range(tiles)
    ]
    item_total = functools.reduce(lambda left, right: left + right, item_counts)

    def following(tile, block, part):
        more = (part + 1) * chunk < lists_ref[tiles + 1, tile]
        again = block + 1 < lists_ref[tile, lanes - 1]
        return (
            jnp.where(more | again, tile, jnp.minimum(tile + 1, tiles)),
            jnp.where(more, block, jnp.where(again, block + 1, 0)),
            jnp.where(more, part + 1, 0),
        )

    def sources_of(tile, part):
        return [lists_ref[tile, part * chunk + entry] for entry in range(chunk)]

    def distances(spot, sources):
        target = target_ref[spot]
        features = [source_ref[source] for source in sources]
        return [
            jnp.dot(target, jnp.concatenate(features[first : first + 2], axis=1), preferred_element_type=jnp.float32)
            for first in range(0, chunk, 2)
        ]

    def kernels(spot, places, squares):
        for first in range(0, block_rows, 8):
            strip = slice(first, first + 8)
            sums = [total_ref[spot, row, strip, :] for row in range(4)]
            for entry in range(chunk):
                column = (entry % 2) * lanes
                inverse = lax.rsqrt(squares[entry // 2][strip, column : column + lanes])
                kernel = inverse * inverse * inverse
                for axis in range(3):
                    sums[axis] = sums[axis] + kernel * places[entry][axis]
                sums[3] = sums[3] + kernel
            for row in range(4):
                total_ref[spot, row, strip, :] = sums[row]

    def step(_, carry):
        tile, block, part = carry
        waiting = None
        for _ in range(units):
            sources = sources_of(tile, part)
            places = [
                [jnp.broadcast_to(moment_ref[source, axis : axis + 1, :], (8, lanes)) for axis in range(3)]
                for source in sources
            ]
            spot = tile * blocks + block
            item = (spot, places, distances(spot, sources))
            if waiting is not None:
                kernels(*waiting)
            waiting = item
            tile, block, part = following(tile, block, part)
        kernels(*waiting)
        return (tile, block, part)

    zero = jnp.int32(0)
    lax.fori_loop(0, (item_total + units - 1) // units, step, (zero, zero, zero))


def advance(middle, place_own, speed_own, weight_own, total_ref, sums_ref):
    tiles = weight_own.shape[0]
    blocks = lanes // block_rows
    for tile in range(tiles):
        for row in range(4):
            parts = [total_ref[tile * blocks + block, row] for block in range(blocks)]
            total = jnp.sum(jnp.transpose(jnp.concatenate(parts, axis=0)), axis=0, keepdims=True)
            sums_ref[row, tile : tile + 1, :] = total
    zeroth = sums_ref[3, :tiles, :]
    places, speeds = ([], [])
    for axis in range(3):
        force = sums_ref[axis, :tiles, :] - (place_own[axis] - middle[axis]) * zeroth
        speeds.append(weight_own * (speed_own[axis] + time_step * force / lanes))
        places.append(weight_own * (place_own[axis] + time_step * speeds[axis]))
    return places, speeds


def part_of(ref, tiles, row):
    return ref[row * tiles : (row + 1) * tiles, :]


def fill_planes(planes, tiles, blocks):
    kinds, rows, slots = planes.shape
    filled = len(blocks) * tiles
    planes[:, filled:, :] = jnp.zeros((kinds, rows - filled, slots), jnp.float32)
    for block, ref in enumerate(blocks):
        for kind in range(kinds):
            planes[kind, block * tiles : (block + 1) * tiles, :] = part_of(ref, tiles, kind)


def weights_of(aux, listed):
    slot = lax.broadcasted_iota(jnp.int32, aux.shape, 1).astype(jnp.float32)
    return jnp.where(slot < aux[:, listed : listed + 1], 1.0, 0.0)


def offsets_of(tiles, near_pair):
    device = device_index()
    toward = jnp.where(device % 2 == 0, 1.0, -1.0) * float(tiles)
    if near_pair:
        return [0.0, toward]
    return [-toward, -reach * toward, reach * toward]


def far_blocks(pair, forwarded, first_rows):
    return (pair[:first_rows, :], pair[first_rows:, :], forwarded[:first_rows, :])


def prepare(first, near_pair, listed, own_ref, blocks, lists_ref, weight_ref, tools):
    planes, scalars, copy_sem, feature_ref, moment_ref, source_ref = tools
    first_row = own_ref.shape[0] // planes.shape[0] * (1 if near_pair else reach)
    tiles = own_ref.shape[0] // planes.shape[0]
    if not first:
        copy = pltpu.make_async_copy(lists_ref, scalars, copy_sem)
        copy.start()
    fill_planes(planes, tiles, blocks)
    if first:
        aux = planes[3]
        own_aux = jnp.concatenate(
            [part_of(own_ref, tiles, 3), jnp.zeros((round_up(tiles, 8) - tiles, lanes), jnp.float32)], axis=0
        )
        for row, value in enumerate(build_lists(aux, own_aux, tiles, listed, offsets_of(tiles, near_pair))):
            lists_ref[row : row + 1, :] = value
        copy = pltpu.make_async_copy(lists_ref, scalars, copy_sem)
        copy.start()
        weight_ref[...] = weights_of(aux, listed)
    middle = middles([part_of(own_ref, tiles, axis) for axis in range(3)])
    places = [planes[axis, first_row:, :] for axis in range(3)]
    build_sources(first_row, places, middle, weight_ref[first_row:, :], feature_ref, moment_ref, source_ref)
    return middle, copy


def alone(listed, first, *refs):
    if first:
        own_ref, total_ref, target_ref, moment_ref, source_ref, feature_ref = refs
        tiles = own_ref.shape[0] // 4
        weight = weights_of(part_of(own_ref, tiles, 3), listed)
    else:
        own_ref, weight_ref, total_ref, target_ref, moment_ref, source_ref, feature_ref = refs
        tiles = own_ref.shape[0] // 3
        weight = weight_ref[:tiles, :]
    own_place = [part_of(own_ref, tiles, axis) for axis in range(3)]
    middle = middles(own_place)
    total_ref[...] = jnp.zeros(total_ref.shape, jnp.float32)
    build_targets(own_place, middle, feature_ref, target_ref)
    build_sources(0, own_place, middle, weight, feature_ref, moment_ref, source_ref)


def ahead(listed, first, *refs):
    own_ref, pair, *refs = refs
    *given, moment_ref, source_ref, feature_ref = refs
    tiles = own_ref.shape[0] // (4 if first else 3)
    first_rows = own_ref.shape[0] if first else 3 * (tiles + tiles // 2)
    middle = middles([part_of(own_ref, tiles, axis) for axis in range(3)])
    for index, block in enumerate((pair[:first_rows, :], pair[first_rows:, :])):
        if first:
            weight = weights_of(part_of(block, tiles, 3), listed)
        else:
            weight = given[0][index * tiles : (index + 1) * tiles, :]
        places = [part_of(block, tiles, axis) for axis in range(3)]
        build_sources(index * tiles, places, middle, weight, feature_ref, moment_ref, source_ref)


def begin(listed, first, *refs):
    own_ref, sibling_ref, target_ref, _, _, _, *refs = refs
    if first:
        total_ref, moment_ref, source_ref, lists_ref, weight_ref, *scratch = refs
    else:
        lists_ref, weight_ref, total_ref, moment_ref, source_ref, *scratch = refs
    tools = scratch + [moment_ref, source_ref]
    tiles = own_ref.shape[0] // tools[0].shape[0]
    _, copy = prepare(first, True, listed, own_ref, (own_ref, sibling_ref), lists_ref, weight_ref, tools)
    copy.wait()
    accumulate(tiles, tools[1], tools[5], target_ref, tools[4], total_ref)


def halves(speed, even, half):
    first, last = (speed[:half], speed[half:])
    return jnp.where(even, last, first), jnp.where(even, first, last)


def first_finish(
    listed, own_ref, pair, forwarded, total_in, target_ref, weight_own_ref, speed_ref, moment_in, source_in, *refs
):
    total_ref, moment_ref, source_ref, lists_ref, weight_ref, place_out, speed_out, *refs = refs
    sibling_out, beside_out, *tools, sums_ref = refs
    tools += [moment_ref, source_ref]
    tiles = own_ref.shape[0] // tools[0].shape[0]
    half = tiles // 2
    middle, copy = prepare(True, False, listed, own_ref, far_blocks(pair, forwarded, own_ref.shape[0]), lists_ref, weight_ref, tools)
    copy.wait()
    accumulate(tiles, tools[1], tools[5], target_ref, tools[4], total_ref)
    places, speeds = advance(
        middle,
        [part_of(own_ref, tiles, axis) for axis in range(3)],
        [part_of(speed_ref, tiles, axis) for axis in range(3)],
        weight_own_ref[:tiles, :],
        total_ref,
        sums_ref,
    )
    even = device_index() % 2 == 0
    for axis in range(3):
        strip = slice(axis * tiles, (axis + 1) * tiles)
        place_out[strip, :] = places[axis]
        speed_out[strip, :] = speeds[axis]
        sibling_out[strip, :] = places[axis]
        beside_out[strip, :] = places[axis]
        strip = slice(3 * tiles + axis * half, 3 * tiles + (axis + 1) * half)
        sibling_out[strip, :], beside_out[strip, :] = halves(speeds[axis], even, half)


def second_finish(
    own_ref,
    pair,
    forwarded,
    total_in,
    target_ref,
    weight_own_ref,
    speed_ref,
    lists_ref,
    weight_ref,
    moment_in,
    source_in,
    total_ref,
    moment_ref,
    source_ref,
    state_ref,
    sibling_out,
    beside_out,
    *scratch
):
    *tools, sums_ref = scratch
    tools += [moment_ref, source_ref]
    tiles = own_ref.shape[0] // 3
    half = tiles // 2
    beside = pair[: 3 * (tiles + half), :]
    blocks = far_blocks(pair, forwarded, beside.shape[0])
    middle, copy = prepare(False, False, None, own_ref, blocks, lists_ref, weight_ref, tools)
    copy.wait()
    accumulate(tiles, tools[1], tools[5], target_ref, tools[4], total_ref)
    place_own = [part_of(own_ref, tiles, axis) for axis in range(3)]
    speed_own = [part_of(speed_ref, tiles, axis) for axis in range(3)]
    places, speeds = advance(middle, place_own, speed_own, weight_own_ref[:tiles, :], total_ref, sums_ref)
    even = device_index() % 2 == 0
    for row, value in enumerate(places + speeds):
        state_ref[row] = value
        strip = slice(row * half, (row + 1) * half)
        sibling_out[strip, :], beside_out[strip, :] = halves(value, even, half)


def first_place(total_tiles, cuts_ref, own_ref, speed_ref, sibling_ref, pair, out_ref, pool_ref):
    tiles = own_ref.shape[0] // 3
    half = tiles // 2
    beside = pair[: 3 * (tiles + half), :]
    place_own = [part_of(own_ref, tiles, axis) for axis in range(3)]
    speed_own = [part_of(speed_ref, tiles, axis) for axis in range(3)]
    even = device_index() % 2 == 0
    lower, upper = ([], [])
    for row in range(6):
        if row < 3:
            sides = [part_of(ref, tiles, row) for ref in (sibling_ref, beside)]
            low_sides, high_sides = ([side[tiles - half :] for side in sides], [side[:half] for side in sides])
        else:
            strip = slice(3 * tiles + (row - 3) * half, 3 * tiles + (row - 2) * half)
            low_sides = high_sides = [ref[strip, :] for ref in (sibling_ref, beside)]
        lower.append(jnp.where(even, low_sides[1], low_sides[0]))
        upper.append(jnp.where(even, high_sides[0], high_sides[1]))
    place_rows(0, total_tiles, cuts_ref, lower, place_own + speed_own, upper, pool_ref, out_ref)


def place_rows(step, total_tiles, cuts_ref, lower, own, upper, pool_ref, out_ref):
    tiles, slots = own[0].shape
    half = tiles // 2
    capacity = out_ref.shape[1]
    device = device_index()
    last = cuts_ref.shape[1] - 1
    first_tile = cuts_ref[step, device]
    next_tile = jnp.where(device == last, total_tiles, cuts_ref[step, jnp.minimum(device + 1, last)])
    owned = next_tile - first_tile
    start = first_tile - (device * tiles - half)
    filled = lax.broadcasted_iota(jnp.int32, (capacity, slots), 0) < owned
    for row in range(6):
        pool_ref[row, :half, :] = lower[row]
        pool_ref[row, half : half + tiles, :] = own[row]
        pool_ref[row, half + tiles : 2 * tiles, :] = upper[row]
    for row in range(6):
        out_ref[row] = jnp.where(filled, pool_ref[row, pl.ds(start, capacity), :], 0.0)


def third_kernel(total_tiles, cuts_ref, sibling_ref, own_ref, beside_ref, out_ref, pool_ref):
    half = own_ref.shape[1] // 2
    even = device_index() % 2 == 0
    lower, upper = ([], [])
    for row in range(6):
        sibling, beside = (part_of(sibling_ref, half, row), part_of(beside_ref, half, row))
        lower.append(jnp.where(even, beside, sibling))
        upper.append(jnp.where(even, sibling, beside))
    place_rows(1, total_tiles, cuts_ref, lower, [own_ref[row] for row in range(6)], upper, pool_ref, out_ref)


def far(value):
    return pltpu.with_memory_space_constraint(value, pltpu.HBM)


def near(value):
    return pltpu.with_memory_space_constraint(value, pltpu.VMEM)


def body(particles, occupancy, neighbours, curve_cuts):
    tiles, _, slots = particles.shape
    listed = neighbours.shape[1]
    total_tiles = tiles * lax.axis_size(AXES)
    half = tiles // 2
    capacity = 2 * tiles
    near_rows = round_up(2 * tiles + 1, 8)
    far_rows = round_up((reach + 1) * tiles + 1, 8)
    list_rows = round_up(tiles + 2, 8)
    vmem = pl.BlockSpec(memory_space=pltpu.VMEM)
    smem = pl.BlockSpec(memory_space=pltpu.SMEM)

    def held(*sizes, dtype=jnp.float32):
        return pltpu.VMEM(sizes, dtype)

    def call(kernel, name, outs, ins, scratch, flops=0, aliases=None):
        held_ins = [far(value) if kind is smem else near(value) for kind, value in ins]
        return pl.pallas_call(
            kernel,
            out_shape=outs,
            in_specs=[kind for kind, _ in ins],
            out_specs=[vmem] * len(outs),
            scratch_shapes=scratch,
            input_output_aliases=aliases or {},
            compiler_params=pltpu.CompilerParams(vmem_limit_bytes=vmem_limit),
            cost_estimate=pl.CostEstimate(flops=flops, bytes_accessed=1 << 20, transcendentals=0),
            name=name,
        )(*held_ins)

    def moments(rows):
        return held(rows, 8, lanes)

    def sources(rows):
        return held(rows, feature_rows, lanes, dtype=jnp.bfloat16)

    def features(rows):
        return pltpu.VMEM((rows * feature_rows, lanes), jnp.float32)

    def tools(rows, kinds):
        return [
            pltpu.VMEM((kinds, rows, slots), jnp.float32),
            pltpu.SMEM((list_rows, lanes), jnp.int32),
            pltpu.SemaphoreType.DMA,
            features(rows),
        ]

    packed, speed = pl.pallas_call(
        functools.partial(pack_kernel, total_tiles),
        out_shape=(held(4 * tiles, slots), held(3 * tiles, slots)),
        in_specs=[vmem, smem, vmem],
        out_specs=(vmem, vmem),
        compiler_params=pltpu.CompilerParams(vmem_limit_bytes=vmem_limit),
        name="pack",
    )(far(particles), far(occupancy), far(neighbours))
    pool_scratch = pltpu.VMEM((6, round_up(capacity + tiles, 8), slots), jnp.float32)
    sums_scratch = pltpu.VMEM((4, round_up(tiles, 8), lanes), jnp.float32)
    blocks = lanes // block_rows
    totals = held(tiles * blocks + 1, 4, block_rows, lanes)
    targets = held(tiles * blocks + 1, block_rows, feature_rows, dtype=jnp.bfloat16)
    lists = held(list_rows, lanes, dtype=jnp.int32)
    edge = 3 * tiles + 3 * half
    work = 1 << 32

    sibling = swapped(packed, 0)
    pair = swapped(jnp.concatenate([packed, sibling], axis=0), 1)
    carried = [totals, moments(near_rows), sources(near_rows)]
    total, target, moment, source = call(
        functools.partial(alone, listed, True),
        "first_alone",
        [totals, targets, *carried[1:]],
        [(vmem, packed)],
        [features(round_up(tiles, 8))],
        1 << 22,
    )
    total, _, _, near_lists, near_weight = call(
        functools.partial(begin, listed, True),
        "first_near",
        carried + [lists, held(near_rows, slots)],
        [(vmem, value) for value in (packed, sibling, target, total, moment, source)],
        tools(near_rows, 4),
        work,
        {3: 0, 4: 1, 5: 2},
    )
    pair, near_weight = lax.optimization_barrier((pair, near_weight))
    forwarded = swapped(pair, 0)
    far_carried = [totals, moments(far_rows), sources(far_rows)]
    moment, source = call(
        functools.partial(ahead, listed, True),
        "first_ahead",
        far_carried[1:],
        [(vmem, packed), (vmem, pair)],
        [features(round_up(tiles, 8))],
        1 << 22,
    )
    total, _, _, far_lists, far_weight, place, speed, sibling, beside = call(
        functools.partial(first_finish, listed),
        "first_far",
        far_carried
        + [lists, held(far_rows, slots), held(3 * tiles, slots), held(3 * tiles, slots), held(edge, slots), held(edge, slots)],
        [(vmem, value) for value in (packed, pair, forwarded, total, target, near_weight, speed, moment, source)],
        tools(far_rows, 4) + [sums_scratch],
        work,
        {3: 0, 7: 1, 8: 2},
    )
    sibling = swapped(sibling, 0)
    pair = swapped(jnp.concatenate([beside, sibling[: 3 * tiles]], axis=0), 1)
    total, target, moment, source = call(
        functools.partial(alone, listed, False),
        "second_alone",
        [totals, targets, *carried[1:]],
        [(vmem, place), (vmem, near_weight)],
        [features(round_up(tiles, 8))],
        1 << 22,
    )
    total, _, _ = call(
        functools.partial(begin, listed, False),
        "second_near",
        carried,
        [(vmem, value) for value in (place, sibling, target, total, moment, source, near_lists, near_weight)],
        tools(near_rows, 3),
        work,
        {3: 0, 4: 1, 5: 2},
    )
    pair, total = lax.optimization_barrier((pair, total))
    forwarded = swapped(pair, 0)
    (after_first,) = call(
        functools.partial(first_place, total_tiles),
        "first_place",
        [jax.ShapeDtypeStruct((6, capacity, slots), jnp.float32)],
        [(smem, curve_cuts)] + [(vmem, value) for value in (place, speed, sibling, pair)],
        [pool_scratch],
        1 << 22,
    )
    moment, source = call(
        functools.partial(ahead, listed, False),
        "second_ahead",
        far_carried[1:],
        [(vmem, place), (vmem, pair), (vmem, far_weight)],
        [features(round_up(tiles, 8))],
        1 << 22,
    )
    _, _, _, state, sibling, beside = call(
        second_finish,
        "second_far",
        far_carried
        + [
            held(6, tiles, slots),
            held(6 * half, slots),
            held(6 * half, slots),
        ],
        [
            (vmem, value)
            for value in (place, pair, forwarded, total, target, near_weight, speed, far_lists, far_weight, moment, source)
        ],
        tools(far_rows, 3) + [sums_scratch],
        work,
        {3: 0, 9: 1, 10: 2},
    )
    beside = swapped(beside, 1, wrap=False)
    sibling = swapped(sibling, 0)
    (after_second,) = call(
        functools.partial(third_kernel, total_tiles),
        "place",
        [jax.ShapeDtypeStruct((6, capacity, slots), jnp.float32)],
        [(smem, curve_cuts), (vmem, sibling), (vmem, state), (vmem, beside)],
        [pool_scratch],
    )
    return (jnp.transpose(after_first, (1, 0, 2)), jnp.transpose(after_second, (1, 0, 2)))


def solution(mesh):
    in_specs = (P(AXES, None, None), P(AXES), P(AXES, None), P())
    out_specs = (P(AXES, None, None), P(AXES, None, None))
    return jax.shard_map(body, mesh=mesh, in_specs=in_specs, out_specs=out_specs, check_vma=False)
```

```python
import functools

import jax
import jax.numpy as jnp
from jax import lax
from jax.experimental import pallas as pl
from jax.experimental.pallas import tpu as pltpu
from jax.sharding import PartitionSpec as P

AXES = ("gx", "gy")
STEPS = 2

soften = 0.05
time_step = 0.5
reach = 2
chunk = 4
units = 16
feature_rows = 32
far_norm = 1e36
lanes = 128
block_rows = 64
vmem_limit = 16 << 20


def swapped(value, first, wrap=True):
    count = lax.axis_size(AXES)
    pairs = []
    for lower in range(first, count, 2):
        if wrap or lower + 1 < count:
            upper = (lower + 1) % count
            pairs += [(lower, upper), (upper, lower)]
    return lax.ppermute(value, AXES, pairs)


def round_up(value, step):
    return -(-value // step) * step


def device_index():
    return lax.axis_index("gx") * lax.axis_size("gy") + lax.axis_index("gy")


def pieces(value, count):
    parts = []
    rest = value
    for _ in range(count - 1):
        part = rest.astype(jnp.bfloat16).astype(jnp.float32)
        parts.append(part)
        rest = rest - part
    parts.append(rest.astype(jnp.bfloat16).astype(jnp.float32))
    return parts


def pack_kernel(total_tiles, particles_ref, occupancy_ref, neighbours_ref, packed_ref, speed_ref):
    tiles, slots = (particles_ref.shape[0], particles_ref.shape[2])
    listed = neighbours_ref.shape[1]
    for row in range(3):
        packed_ref[row * tiles : (row + 1) * tiles, :] = particles_ref[:, row, :]
        speed_ref[row * tiles : (row + 1) * tiles, :] = particles_ref[:, 3 + row, :]
    tile_ids = lax.broadcasted_iota(jnp.int32, (tiles, listed), 0)
    offsets = neighbours_ref[...] - (device_index() * tiles + tile_ids)
    offsets = jnp.where(offsets < 0, offsets + total_tiles, offsets)
    packed_ref[3 * tiles :, :] = jnp.zeros((tiles, slots), jnp.float32)
    packed_ref[3 * tiles :, :listed] = offsets.astype(jnp.float32)
    for tile in range(tiles):
        live = occupancy_ref[tile].astype(jnp.float32)
        packed_ref[3 * tiles + tile : 3 * tiles + tile + 1, listed : listed + 1] = jnp.full((1, 1), live)


def places_of(index, tiles, offsets):
    place = index + offsets[0]
    for block in range(1, len(offsets)):
        place = jnp.where(index >= block * tiles, index - block * tiles + offsets[block], place)
    return jnp.where(index >= len(offsets) * tiles, -1000.0, place)


def build_lists(aux, own, tiles, listed, offsets):
    rows = aux.shape[0]
    dummy = len(offsets) * tiles
    index = lax.broadcasted_iota(jnp.int32, (rows, lanes), 0).astype(jnp.float32)
    lane = lax.broadcasted_iota(jnp.int32, (rows, lanes), 1).astype(jnp.float32)
    place = places_of(index, tiles, offsets)
    mask = place == lane
    for entry in range(listed):
        mask = mask | (place + aux[:, entry : entry + 1] == lane)
    own_rows = own.shape[0]
    own_index = lax.broadcasted_iota(jnp.int32, (own_rows, lanes), 0).astype(jnp.float32)
    own_lane = lax.broadcasted_iota(jnp.int32, (own_rows, lanes), 1).astype(jnp.float32)
    own_place = places_of(own_lane, tiles, offsets)
    listing = own_index + own[:, 0:1] == own_place
    for entry in range(1, listed):
        listing = listing | (own_index + own[:, entry : entry + 1] == own_place)
    listing = jnp.where(listing, 1.0, 0.0)
    listing = jnp.concatenate([listing, jnp.zeros((lanes - own_rows, lanes), jnp.float32)], axis=0)
    listing = jnp.transpose(listing)[:rows]
    mask = jnp.maximum(jnp.where(mask, 1.0, 0.0), listing)
    mask = jnp.where((lane < tiles) & (index < dummy), mask, 0.0)
    earlier = lax.broadcasted_iota(jnp.int32, (rows, rows), 1) < lax.broadcasted_iota(jnp.int32, (rows, rows), 0)
    rank = jnp.dot(
        jnp.where(earlier, 1.0, 0.0).astype(jnp.bfloat16),
        mask.astype(jnp.bfloat16),
        preferred_element_type=jnp.float32,
    )
    key = jnp.where(mask > 0.5, rank, -1.0)
    counts = jnp.sum(mask, axis=0, keepdims=True)
    lists = []
    for tile in range(tiles):
        hit = key[:, tile : tile + 1] == lane
        row = jnp.sum(jnp.where(hit, index - dummy, 0.0), axis=0, keepdims=True) + dummy
        live = own[tile : tile + 1, listed : listed + 1]
        blocks = jnp.full((1, 1), 1.0)
        for filled in range(block_rows, lanes, block_rows):
            blocks = blocks + jnp.where(live > filled, 1.0, 0.0)
        lists.append(jnp.where(lane[:1] == lanes - 1, blocks, row))
    lists.append(jnp.where(lane[:1] == lanes - 1, 1.0, float(dummy)))
    lists.append(counts)
    return [row.astype(jnp.int32) for row in lists]


def middles(own_place):
    return [jnp.mean(axis[:8], keepdims=True) for axis in own_place]


def feature_of(feature_ref, tile):
    return feature_ref[tile * feature_rows : (tile + 1) * feature_rows, :]


def build_sources(first, places, middle, weight, feature_ref, moment_ref, source_ref):
    rows = weight.shape[0]
    moment_rows = moment_ref.reshape(moment_ref.shape[0] * 8, lanes)
    ones = jnp.ones_like(weight)
    zeros = jnp.zeros_like(weight)
    features = []
    norm = zeros
    for axis in range(3):
        value = weight * (places[axis] - middle[axis])
        norm = norm + value * value
        moment_rows[pl.ds(first * 8 + axis, rows, 8), :] = value
        high, mid, low = pieces(value, 3)
        features += [high, high, mid, mid, high, low]
    features += pieces(jnp.where(weight > 0.5, norm, far_norm), 3) + [ones] * 3
    features += [zeros] * (feature_rows - len(features))
    for row, value in enumerate(features):
        feature_ref[pl.ds(row, rows, feature_rows), :] = value
    for tile in range(rows):
        source_ref[first + tile] = feature_of(feature_ref, tile).astype(jnp.bfloat16)


def build_targets(own_place, middle, feature_ref, target_ref):
    tiles = own_place[0].shape[0]
    ones = jnp.ones_like(own_place[0])
    zeros = jnp.zeros_like(own_place[0])
    features = []
    norm = zeros
    for axis in range(3):
        value = own_place[axis] - middle[axis]
        norm = norm + value * value
        high, mid, low = [-2.0 * part for part in pieces(value, 3)]
        features += [high, mid, high, mid, low, high]
    features += [ones] * 3 + pieces(norm + soften, 3)
    features += [zeros] * (feature_rows - len(features))
    for row, value in enumerate(features):
        feature_ref[pl.ds(row, tiles, feature_rows), :] = value
    blank = jnp.zeros((lanes - feature_rows, lanes), jnp.float32)
    blocks = lanes // block_rows
    for tile in range(tiles):
        turned = jnp.transpose(jnp.concatenate([feature_of(feature_ref, tile), blank], axis=0))
        turned = turned[:, :feature_rows].astype(jnp.bfloat16)
        for block in range(blocks):
            target_ref[tile * blocks + block] = turned[block * block_rows : (block + 1) * block_rows]
    target_ref[tiles * blocks] = target_ref[0]


def accumulate(tiles, lists_ref, source_ref, target_ref, moment_ref, total_ref):
    blocks = lanes // block_rows
    item_counts = [
        jnp.maximum((lists_ref[tiles + 1, tile] + chunk - 1) // chunk, 1) * lists_ref[tile, lanes - 1] for tile in range(tiles)
    ]
    item_total = functools.reduce(lambda left, right: left + right, item_counts)

    def following(tile, block, part):
        more = (part + 1) * chunk < lists_ref[tiles + 1, tile]
        again = block + 1 < lists_ref[tile, lanes - 1]
        return (
            jnp.where(more | again, tile, jnp.minimum(tile + 1, tiles)),
            jnp.where(more, block, jnp.where(again, block + 1, 0)),
            jnp.where(more, part + 1, 0),
        )

    def sources_of(tile, part):
        return [lists_ref[tile, part * chunk + entry] for entry in range(chunk)]

    def distances(spot, sources):
        target = target_ref[spot]
        features = [source_ref[source] for source in sources]
        return [
            jnp.dot(target, jnp.concatenate(features[first : first + 2], axis=1), preferred_element_type=jnp.float32)
            for first in range(0, chunk, 2)
        ]

    def kernels(spot, places, squares):
        for first in range(0, block_rows, 8):
            strip = slice(first, first + 8)
            sums = [total_ref[spot, row, strip, :] for row in range(4)]
            for entry in range(chunk):
                column = (entry % 2) * lanes
                inverse = lax.rsqrt(squares[entry // 2][strip, column : column + lanes])
                kernel = inverse * inverse * inverse
                for axis in range(3):
                    sums[axis] = sums[axis] + kernel * places[entry][axis]
                sums[3] = sums[3] + kernel
            for row in range(4):
                total_ref[spot, row, strip, :] = sums[row]

    def step(_, carry):
        tile, block, part = carry
        waiting = None
        for _ in range(units):
            sources = sources_of(tile, part)
            places = [
                [jnp.broadcast_to(moment_ref[source, axis : axis + 1, :], (8, lanes)) for axis in range(3)]
                for source in sources
            ]
            spot = tile * blocks + block
            item = (spot, places, distances(spot, sources))
            if waiting is not None:
                kernels(*waiting)
            waiting = item
            tile, block, part = following(tile, block, part)
        kernels(*waiting)
        return (tile, block, part)

    zero = jnp.int32(0)
    lax.fori_loop(0, (item_total + units - 1) // units, step, (zero, zero, zero))


def advance(middle, place_own, speed_own, weight_own, total_ref, sums_ref):
    tiles = weight_own.shape[0]
    blocks = lanes // block_rows
    for tile in range(tiles):
        for row in range(4):
            parts = [total_ref[tile * blocks + block, row] for block in range(blocks)]
            total = jnp.sum(jnp.transpose(jnp.concatenate(parts, axis=0)), axis=0, keepdims=True)
            sums_ref[row, tile : tile + 1, :] = total
    zeroth = sums_ref[3, :tiles, :]
    places, speeds = ([], [])
    for axis in range(3):
        force = sums_ref[axis, :tiles, :] - (place_own[axis] - middle[axis]) * zeroth
        speeds.append(weight_own * (speed_own[axis] + time_step * force / lanes))
        places.append(weight_own * (place_own[axis] + time_step * speeds[axis]))
    return places, speeds


def part_of(ref, tiles, row):
    return ref[row * tiles : (row + 1) * tiles, :]


def fill_planes(planes, tiles, blocks):
    kinds, rows, slots = planes.shape
    filled = len(blocks) * tiles
    planes[:, filled:, :] = jnp.zeros((kinds, rows - filled, slots), jnp.float32)
    for block, ref in enumerate(blocks):
        for kind in range(kinds):
            planes[kind, block * tiles : (block + 1) * tiles, :] = part_of(ref, tiles, kind)


def weights_of(aux, listed):
    slot = lax.broadcasted_iota(jnp.int32, aux.shape, 1).astype(jnp.float32)
    return jnp.where(slot < aux[:, listed : listed + 1], 1.0, 0.0)


def offsets_of(tiles, near_pair):
    device = device_index()
    toward = jnp.where(device % 2 == 0, 1.0, -1.0) * float(tiles)
    if near_pair:
        return [0.0, toward]
    return [-toward, -reach * toward, reach * toward]


def far_blocks(pair, forwarded, first_rows):
    return (pair[:first_rows, :], pair[first_rows:, :], forwarded[:first_rows, :])


def prepare(first, near_pair, listed, own_ref, blocks, lists_ref, weight_ref, tools):
    planes, scalars, copy_sem, feature_ref, moment_ref, source_ref = tools
    first_row = own_ref.shape[0] // planes.shape[0] * (1 if near_pair else reach)
    tiles = own_ref.shape[0] // planes.shape[0]
    if not first:
        copy = pltpu.make_async_copy(lists_ref, scalars, copy_sem)
        copy.start()
    fill_planes(planes, tiles, blocks)
    if first:
        aux = planes[3]
        own_aux = jnp.concatenate(
            [part_of(own_ref, tiles, 3), jnp.zeros((round_up(tiles, 8) - tiles, lanes), jnp.float32)], axis=0
        )
        for row, value in enumerate(build_lists(aux, own_aux, tiles, listed, offsets_of(tiles, near_pair))):
            lists_ref[row : row + 1, :] = value
        copy = pltpu.make_async_copy(lists_ref, scalars, copy_sem)
        copy.start()
        weight_ref[...] = weights_of(aux, listed)
    middle = middles([part_of(own_ref, tiles, axis) for axis in range(3)])
    places = [planes[axis, first_row:, :] for axis in range(3)]
    build_sources(first_row, places, middle, weight_ref[first_row:, :], feature_ref, moment_ref, source_ref)
    return middle, copy


def alone(listed, first, *refs):
    if first:
        own_ref, total_ref, target_ref, moment_ref, source_ref, feature_ref = refs
        tiles = own_ref.shape[0] // 4
        weight = weights_of(part_of(own_ref, tiles, 3), listed)
    else:
        own_ref, weight_ref, total_ref, target_ref, moment_ref, source_ref, feature_ref = refs
        tiles = own_ref.shape[0] // 3
        weight = weight_ref[:tiles, :]
    own_place = [part_of(own_ref, tiles, axis) for axis in range(3)]
    middle = middles(own_place)
    total_ref[...] = jnp.zeros(total_ref.shape, jnp.float32)
    build_targets(own_place, middle, feature_ref, target_ref)
    build_sources(0, own_place, middle, weight, feature_ref, moment_ref, source_ref)


def ahead(listed, first, *refs):
    own_ref, pair, *refs = refs
    *given, moment_ref, source_ref, feature_ref = refs
    tiles = own_ref.shape[0] // (4 if first else 3)
    first_rows = own_ref.shape[0] if first else 3 * (tiles + tiles // 2)
    middle = middles([part_of(own_ref, tiles, axis) for axis in range(3)])
    for index, block in enumerate((pair[:first_rows, :], pair[first_rows:, :])):
        if first:
            weight = weights_of(part_of(block, tiles, 3), listed)
        else:
            weight = given[0][index * tiles : (index + 1) * tiles, :]
        places = [part_of(block, tiles, axis) for axis in range(3)]
        build_sources(index * tiles, places, middle, weight, feature_ref, moment_ref, source_ref)


def begin(listed, first, *refs):
    own_ref, sibling_ref, target_ref, _, _, _, *refs = refs
    if first:
        total_ref, moment_ref, source_ref, lists_ref, weight_ref, *scratch = refs
    else:
        lists_ref, weight_ref, total_ref, moment_ref, source_ref, *scratch = refs
    tools = scratch + [moment_ref, source_ref]
    tiles = own_ref.shape[0] // tools[0].shape[0]
    _, copy = prepare(first, True, listed, own_ref, (own_ref, sibling_ref), lists_ref, weight_ref, tools)
    copy.wait()
    accumulate(tiles, tools[1], tools[5], target_ref, tools[4], total_ref)


def halves(speed, even, half):
    first, last = (speed[:half], speed[half:])
    return jnp.where(even, last, first), jnp.where(even, first, last)


def first_finish(
    listed, own_ref, pair, forwarded, total_in, target_ref, weight_own_ref, speed_ref, moment_in, source_in, *refs
):
    total_ref, moment_ref, source_ref, lists_ref, weight_ref, place_out, speed_out, *refs = refs
    sibling_out, beside_out, *tools, sums_ref = refs
    tools += [moment_ref, source_ref]
    tiles = own_ref.shape[0] // tools[0].shape[0]
    half = tiles // 2
    middle, copy = prepare(True, False, listed, own_ref, far_blocks(pair, forwarded, own_ref.shape[0]), lists_ref, weight_ref, tools)
    copy.wait()
    accumulate(tiles, tools[1], tools[5], target_ref, tools[4], total_ref)
    places, speeds = advance(
        middle,
        [part_of(own_ref, tiles, axis) for axis in range(3)],
        [part_of(speed_ref, tiles, axis) for axis in range(3)],
        weight_own_ref[:tiles, :],
        total_ref,
        sums_ref,
    )
    even = device_index() % 2 == 0
    for axis in range(3):
        strip = slice(axis * tiles, (axis + 1) * tiles)
        place_out[strip, :] = places[axis]
        speed_out[strip, :] = speeds[axis]
        sibling_out[strip, :] = places[axis]
        beside_out[strip, :] = places[axis]
        strip = slice(3 * tiles + axis * half, 3 * tiles + (axis + 1) * half)
        sibling_out[strip, :], beside_out[strip, :] = halves(speeds[axis], even, half)


def second_finish(
    own_ref,
    pair,
    forwarded,
    total_in,
    target_ref,
    weight_own_ref,
    speed_ref,
    lists_ref,
    weight_ref,
    moment_in,
    source_in,
    total_ref,
    moment_ref,
    source_ref,
    state_ref,
    sibling_out,
    beside_out,
    *scratch
):
    *tools, sums_ref = scratch
    tools += [moment_ref, source_ref]
    tiles = own_ref.shape[0] // 3
    half = tiles // 2
    beside = pair[: 3 * (tiles + half), :]
    blocks = far_blocks(pair, forwarded, beside.shape[0])
    middle, copy = prepare(False, False, None, own_ref, blocks, lists_ref, weight_ref, tools)
    copy.wait()
    accumulate(tiles, tools[1], tools[5], target_ref, tools[4], total_ref)
    place_own = [part_of(own_ref, tiles, axis) for axis in range(3)]
    speed_own = [part_of(speed_ref, tiles, axis) for axis in range(3)]
    places, speeds = advance(middle, place_own, speed_own, weight_own_ref[:tiles, :], total_ref, sums_ref)
    even = device_index() % 2 == 0
    for row, value in enumerate(places + speeds):
        state_ref[row] = value
        strip = slice(row * half, (row + 1) * half)
        sibling_out[strip, :], beside_out[strip, :] = halves(value, even, half)


def first_place(total_tiles, cuts_ref, own_ref, speed_ref, sibling_ref, pair, out_ref, pool_ref):
    tiles = own_ref.shape[0] // 3
    half = tiles // 2
    beside = pair[: 3 * (tiles + half), :]
    place_own = [part_of(own_ref, tiles, axis) for axis in range(3)]
    speed_own = [part_of(speed_ref, tiles, axis) for axis in range(3)]
    even = device_index() % 2 == 0
    lower, upper = ([], [])
    for row in range(6):
        if row < 3:
            sides = [part_of(ref, tiles, row) for ref in (sibling_ref, beside)]
            low_sides, high_sides = ([side[tiles - half :] for side in sides], [side[:half] for side in sides])
        else:
            strip = slice(3 * tiles + (row - 3) * half, 3 * tiles + (row - 2) * half)
            low_sides = high_sides = [ref[strip, :] for ref in (sibling_ref, beside)]
        lower.append(jnp.where(even, low_sides[1], low_sides[0]))
        upper.append(jnp.where(even, high_sides[0], high_sides[1]))
    place_rows(0, total_tiles, cuts_ref, lower, place_own + speed_own, upper, pool_ref, out_ref)


def place_rows(step, total_tiles, cuts_ref, lower, own, upper, pool_ref, out_ref):
    tiles, slots = own[0].shape
    half = tiles // 2
    capacity = out_ref.shape[1]
    device = device_index()
    last = cuts_ref.shape[1] - 1
    first_tile = cuts_ref[step, device]
    next_tile = jnp.where(device == last, total_tiles, cuts_ref[step, jnp.minimum(device + 1, last)])
    owned = next_tile - first_tile
    start = first_tile - (device * tiles - half)
    filled = lax.broadcasted_iota(jnp.int32, (capacity, slots), 0) < owned
    for row in range(6):
        pool_ref[row, :half, :] = lower[row]
        pool_ref[row, half : half + tiles, :] = own[row]
        pool_ref[row, half + tiles : 2 * tiles, :] = upper[row]
    for row in range(6):
        out_ref[row] = jnp.where(filled, pool_ref[row, pl.ds(start, capacity), :], 0.0)


def third_kernel(total_tiles, cuts_ref, sibling_ref, own_ref, beside_ref, out_ref, pool_ref):
    half = own_ref.shape[1] // 2
    even = device_index() % 2 == 0
    lower, upper = ([], [])
    for row in range(6):
        sibling, beside = (part_of(sibling_ref, half, row), part_of(beside_ref, half, row))
        lower.append(jnp.where(even, beside, sibling))
        upper.append(jnp.where(even, sibling, beside))
    place_rows(1, total_tiles, cuts_ref, lower, [own_ref[row] for row in range(6)], upper, pool_ref, out_ref)


def far(value):
    return pltpu.with_memory_space_constraint(value, pltpu.HBM)


def near(value):
    return pltpu.with_memory_space_constraint(value, pltpu.VMEM)


def body(particles, occupancy, neighbours, curve_cuts):
    tiles, _, slots = particles.shape
    listed = neighbours.shape[1]
    total_tiles = tiles * lax.axis_size(AXES)
    half = tiles // 2
    capacity = 2 * tiles
    near_rows = round_up(2 * tiles + 1, 8)
    far_rows = round_up((reach + 1) * tiles + 1, 8)
    list_rows = round_up(tiles + 2, 8)
    vmem = pl.BlockSpec(memory_space=pltpu.VMEM)
    smem = pl.BlockSpec(memory_space=pltpu.SMEM)

    def held(*sizes, dtype=jnp.float32):
        return pltpu.VMEM(sizes, dtype)

    def call(kernel, name, outs, ins, scratch, flops=0, aliases=None):
        held_ins = [far(value) if kind is smem else near(value) for kind, value in ins]
        return pl.pallas_call(
            kernel,
            out_shape=outs,
            in_specs=[kind for kind, _ in ins],
            out_specs=[vmem] * len(outs),
            scratch_shapes=scratch,
            input_output_aliases=aliases or {},
            compiler_params=pltpu.CompilerParams(vmem_limit_bytes=vmem_limit),
            cost_estimate=pl.CostEstimate(flops=flops, bytes_accessed=1 << 20, transcendentals=0),
            name=name,
        )(*held_ins)

    def moments(rows):
        return held(rows, 8, lanes)

    def sources(rows):
        return held(rows, feature_rows, lanes, dtype=jnp.bfloat16)

    def features(rows):
        return pltpu.VMEM((rows * feature_rows, lanes), jnp.float32)

    def tools(rows, kinds):
        return [
            pltpu.VMEM((kinds, rows, slots), jnp.float32),
            pltpu.SMEM((list_rows, lanes), jnp.int32),
            pltpu.SemaphoreType.DMA,
            features(rows),
        ]

    packed, speed = pl.pallas_call(
        functools.partial(pack_kernel, total_tiles),
        out_shape=(held(4 * tiles, slots), held(3 * tiles, slots)),
        in_specs=[vmem, smem, vmem],
        out_specs=(vmem, vmem),
        compiler_params=pltpu.CompilerParams(vmem_limit_bytes=vmem_limit),
        name="pack",
    )(far(particles), far(occupancy), far(neighbours))
    pool_scratch = pltpu.VMEM((6, round_up(capacity + tiles, 8), slots), jnp.float32)
    sums_scratch = pltpu.VMEM((4, round_up(tiles, 8), lanes), jnp.float32)
    blocks = lanes // block_rows
    totals = held(tiles * blocks + 1, 4, block_rows, lanes)
    targets = held(tiles * blocks + 1, block_rows, feature_rows, dtype=jnp.bfloat16)
    lists = held(list_rows, lanes, dtype=jnp.int32)
    edge = 3 * tiles + 3 * half
    work = 1 << 32

    sibling = swapped(packed, 0)
    pair = swapped(jnp.concatenate([packed, sibling], axis=0), 1)
    carried = [totals, moments(near_rows), sources(near_rows)]
    total, target, moment, source = call(
        functools.partial(alone, listed, True),
        "first_alone",
        [totals, targets, *carried[1:]],
        [(vmem, packed)],
        [features(round_up(tiles, 8))],
        1 << 22,
    )
    total, _, _, near_lists, near_weight = call(
        functools.partial(begin, listed, True),
        "first_near",
        carried + [lists, held(near_rows, slots)],
        [(vmem, value) for value in (packed, sibling, target, total, moment, source)],
        tools(near_rows, 4),
        work,
        {3: 0, 4: 1, 5: 2},
    )
    pair, near_weight = lax.optimization_barrier((pair, near_weight))
    forwarded = swapped(pair, 0)
    far_carried = [totals, moments(far_rows), sources(far_rows)]
    moment, source = call(
        functools.partial(ahead, listed, True),
        "first_ahead",
        far_carried[1:],
        [(vmem, packed), (vmem, pair)],
        [features(round_up(tiles, 8))],
        1 << 22,
    )
    total, _, _, far_lists, far_weight, place, speed, sibling, beside = call(
        functools.partial(first_finish, listed),
        "first_far",
        far_carried
        + [lists, held(far_rows, slots), held(3 * tiles, slots), held(3 * tiles, slots), held(edge, slots), held(edge, slots)],
        [(vmem, value) for value in (packed, pair, forwarded, total, target, near_weight, speed, moment, source)],
        tools(far_rows, 4) + [sums_scratch],
        work,
        {3: 0, 7: 1, 8: 2},
    )
    sibling = swapped(sibling, 0)
    pair = swapped(jnp.concatenate([beside, sibling[: 3 * tiles]], axis=0), 1)
    total, target, moment, source = call(
        functools.partial(alone, listed, False),
        "second_alone",
        [totals, targets, *carried[1:]],
        [(vmem, place), (vmem, near_weight)],
        [features(round_up(tiles, 8))],
        1 << 22,
    )
    total, _, _ = call(
        functools.partial(begin, listed, False),
        "second_near",
        carried,
        [(vmem, value) for value in (place, sibling, target, total, moment, source, near_lists, near_weight)],
        tools(near_rows, 3),
        work,
        {3: 0, 4: 1, 5: 2},
    )
    pair, total = lax.optimization_barrier((pair, total))
    forwarded = swapped(pair, 0)
    (after_first,) = call(
        functools.partial(first_place, total_tiles),
        "first_place",
        [jax.ShapeDtypeStruct((6, capacity, slots), jnp.float32)],
        [(smem, curve_cuts)] + [(vmem, value) for value in (place, speed, sibling, pair)],
        [pool_scratch],
        1 << 22,
    )
    moment, source = call(
        functools.partial(ahead, listed, False),
        "second_ahead",
        far_carried[1:],
        [(vmem, place), (vmem, pair), (vmem, far_weight)],
        [features(round_up(tiles, 8))],
        1 << 22,
    )
    _, _, _, state, sibling, beside = call(
        second_finish,
        "second_far",
        far_carried
        + [
            held(6, tiles, slots),
            held(6 * half, slots),
            held(6 * half, slots),
        ],
        [
            (vmem, value)
            for value in (place, pair, forwarded, total, target, near_weight, speed, far_lists, far_weight, moment, source)
        ],
        tools(far_rows, 3) + [sums_scratch],
        work,
        {3: 0, 9: 1, 10: 2},
    )
    beside = swapped(beside, 1, wrap=False)
    sibling = swapped(sibling, 0)
    (after_second,) = call(
        functools.partial(third_kernel, total_tiles),
        "place",
        [jax.ShapeDtypeStruct((6, capacity, slots), jnp.float32)],
        [(smem, curve_cuts), (vmem, sibling), (vmem, state), (vmem, beside)],
        [pool_scratch],
    )
    return (jnp.transpose(after_first, (1, 0, 2)), jnp.transpose(after_second, (1, 0, 2)))


def solution(mesh):
    in_specs = (P(AXES, None, None), P(AXES), P(AXES, None), P())
    out_specs = (P(AXES, None, None), P(AXES, None, None))
    return jax.shard_map(body, mesh=mesh, in_specs=in_specs, out_specs=out_specs, check_vma=False)
```

```python
import functools

import jax
import jax.numpy as jnp
from jax import lax
from jax.experimental import pallas as pl
from jax.experimental.pallas import tpu as pltpu
from jax.sharding import PartitionSpec as P

AXES = ("gx", "gy")
STEPS = 2

soften = 0.05
time_step = 0.5
reach = 2
chunk = 4
units = 12
feature_rows = 32
far_norm = 1e36
lanes = 128
block_rows = 64
vmem_limit = 16 << 20


def swapped(value, first, wrap=True):
    count = lax.axis_size(AXES)
    pairs = []
    for lower in range(first, count, 2):
        if wrap or lower + 1 < count:
            upper = (lower + 1) % count
            pairs += [(lower, upper), (upper, lower)]
    return lax.ppermute(value, AXES, pairs)


def round_up(value, step):
    return -(-value // step) * step


def device_index():
    return lax.axis_index("gx") * lax.axis_size("gy") + lax.axis_index("gy")


def pieces(value, count):
    parts = []
    rest = value
    for _ in range(count - 1):
        part = rest.astype(jnp.bfloat16).astype(jnp.float32)
        parts.append(part)
        rest = rest - part
    parts.append(rest.astype(jnp.bfloat16).astype(jnp.float32))
    return parts


def pack_kernel(total_tiles, particles_ref, occupancy_ref, neighbours_ref, packed_ref, speed_ref):
    tiles, slots = (particles_ref.shape[0], particles_ref.shape[2])
    listed = neighbours_ref.shape[1]
    for row in range(3):
        packed_ref[row * tiles : (row + 1) * tiles, :] = particles_ref[:, row, :]
        speed_ref[row * tiles : (row + 1) * tiles, :] = particles_ref[:, 3 + row, :]
    tile_ids = lax.broadcasted_iota(jnp.int32, (tiles, listed), 0)
    offsets = neighbours_ref[...] - (device_index() * tiles + tile_ids)
    offsets = jnp.where(offsets < 0, offsets + total_tiles, offsets)
    packed_ref[3 * tiles :, :] = jnp.zeros((tiles, slots), jnp.float32)
    packed_ref[3 * tiles :, :listed] = offsets.astype(jnp.float32)
    for tile in range(tiles):
        live = occupancy_ref[tile].astype(jnp.float32)
        packed_ref[3 * tiles + tile : 3 * tiles + tile + 1, listed : listed + 1] = jnp.full((1, 1), live)


def places_of(index, tiles, offsets):
    place = index + offsets[0]
    for block in range(1, len(offsets)):
        place = jnp.where(index >= block * tiles, index - block * tiles + offsets[block], place)
    return jnp.where(index >= len(offsets) * tiles, -1000.0, place)


def build_lists(aux, own, tiles, listed, offsets):
    rows = aux.shape[0]
    dummy = len(offsets) * tiles
    index = lax.broadcasted_iota(jnp.int32, (rows, lanes), 0).astype(jnp.float32)
    lane = lax.broadcasted_iota(jnp.int32, (rows, lanes), 1).astype(jnp.float32)
    place = places_of(index, tiles, offsets)
    mask = place == lane
    for entry in range(listed):
        mask = mask | (place + aux[:, entry : entry + 1] == lane)
    own_rows = own.shape[0]
    own_index = lax.broadcasted_iota(jnp.int32, (own_rows, lanes), 0).astype(jnp.float32)
    own_lane = lax.broadcasted_iota(jnp.int32, (own_rows, lanes), 1).astype(jnp.float32)
    own_place = places_of(own_lane, tiles, offsets)
    listing = own_index + own[:, 0:1] == own_place
    for entry in range(1, listed):
        listing = listing | (own_index + own[:, entry : entry + 1] == own_place)
    listing = jnp.where(listing, 1.0, 0.0)
    listing = jnp.concatenate([listing, jnp.zeros((lanes - own_rows, lanes), jnp.float32)], axis=0)
    listing = jnp.transpose(listing)[:rows]
    mask = jnp.maximum(jnp.where(mask, 1.0, 0.0), listing)
    mask = jnp.where((lane < tiles) & (index < dummy), mask, 0.0)
    earlier = lax.broadcasted_iota(jnp.int32, (rows, rows), 1) < lax.broadcasted_iota(jnp.int32, (rows, rows), 0)
    rank = jnp.dot(
        jnp.where(earlier, 1.0, 0.0).astype(jnp.bfloat16),
        mask.astype(jnp.bfloat16),
        preferred_element_type=jnp.float32,
    )
    key = jnp.where(mask > 0.5, rank, -1.0)
    counts = jnp.sum(mask, axis=0, keepdims=True)
    lists = []
    for tile in range(tiles):
        hit = key[:, tile : tile + 1] == lane
        row = jnp.sum(jnp.where(hit, index - dummy, 0.0), axis=0, keepdims=True) + dummy
        live = own[tile : tile + 1, listed : listed + 1]
        blocks = jnp.full((1, 1), 1.0)
        for filled in range(block_rows, lanes, block_rows):
            blocks = blocks + jnp.where(live > filled, 1.0, 0.0)
        lists.append(jnp.where(lane[:1] == lanes - 1, blocks, row))
    lists.append(jnp.where(lane[:1] == lanes - 1, 1.0, float(dummy)))
    lists.append(counts)
    return [row.astype(jnp.int32) for row in lists]


def middles(own_place):
    return [jnp.mean(axis[:8], keepdims=True) for axis in own_place]


def feature_of(feature_ref, tile):
    return feature_ref[tile * feature_rows : (tile + 1) * feature_rows, :]


def build_sources(first, places, middle, weight, feature_ref, moment_ref, source_ref):
    rows = weight.shape[0]
    moment_rows = moment_ref.reshape(moment_ref.shape[0] * 8, lanes)
    ones = jnp.ones_like(weight)
    zeros = jnp.zeros_like(weight)
    features = []
    norm = zeros
    for axis in range(3):
        value = weight * (places[axis] - middle[axis])
        norm = norm + value * value
        moment_rows[pl.ds(first * 8 + axis, rows, 8), :] = value
        high, mid, low = pieces(value, 3)
        features += [high, high, mid, mid, high, low]
    features += pieces(jnp.where(weight > 0.5, norm, far_norm), 3) + [ones] * 3
    features += [zeros] * (feature_rows - len(features))
    for row, value in enumerate(features):
        feature_ref[pl.ds(row, rows, feature_rows), :] = value
    for tile in range(rows):
        source_ref[first + tile] = feature_of(feature_ref, tile).astype(jnp.bfloat16)


def build_targets(own_place, middle, feature_ref, target_ref):
    tiles = own_place[0].shape[0]
    ones = jnp.ones_like(own_place[0])
    zeros = jnp.zeros_like(own_place[0])
    features = []
    norm = zeros
    for axis in range(3):
        value = own_place[axis] - middle[axis]
        norm = norm + value * value
        high, mid, low = [-2.0 * part for part in pieces(value, 3)]
        features += [high, mid, high, mid, low, high]
    features += [ones] * 3 + pieces(norm + soften, 3)
    features += [zeros] * (feature_rows - len(features))
    for row, value in enumerate(features):
        feature_ref[pl.ds(row, tiles, feature_rows), :] = value
    blank = jnp.zeros((lanes - feature_rows, lanes), jnp.float32)
    blocks = lanes // block_rows
    for tile in range(tiles):
        turned = jnp.transpose(jnp.concatenate([feature_of(feature_ref, tile), blank], axis=0))
        turned = turned[:, :feature_rows].astype(jnp.bfloat16)
        for block in range(blocks):
            target_ref[tile * blocks + block] = turned[block * block_rows : (block + 1) * block_rows]
    target_ref[tiles * blocks] = target_ref[0]


def accumulate(tiles, lists_ref, source_ref, target_ref, moment_ref, total_ref):
    blocks = lanes // block_rows
    item_counts = [
        jnp.maximum((lists_ref[tiles + 1, tile] + chunk - 1) // chunk, 1) * lists_ref[tile, lanes - 1] for tile in range(tiles)
    ]
    item_total = functools.reduce(lambda left, right: left + right, item_counts)

    def following(tile, block, part):
        more = (part + 1) * chunk < lists_ref[tiles + 1, tile]
        again = block + 1 < lists_ref[tile, lanes - 1]
        return (
            jnp.where(more | again, tile, jnp.minimum(tile + 1, tiles)),
            jnp.where(more, block, jnp.where(again, block + 1, 0)),
            jnp.where(more, part + 1, 0),
        )

    def sources_of(tile, part):
        return [lists_ref[tile, part * chunk + entry] for entry in range(chunk)]

    def distances(spot, sources):
        target = target_ref[spot]
        features = [source_ref[source] for source in sources]
        return [
            jnp.dot(target, jnp.concatenate(features[first : first + 2], axis=1), preferred_element_type=jnp.float32)
            for first in range(0, chunk, 2)
        ]

    def kernels(spot, places, squares):
        for first in range(0, block_rows, 8):
            strip = slice(first, first + 8)
            sums = [total_ref[spot, row, strip, :] for row in range(4)]
            for entry in range(chunk):
                column = (entry % 2) * lanes
                inverse = lax.rsqrt(squares[entry // 2][strip, column : column + lanes])
                kernel = inverse * inverse * inverse
                for axis in range(3):
                    sums[axis] = sums[axis] + kernel * places[entry][axis]
                sums[3] = sums[3] + kernel
            for row in range(4):
                total_ref[spot, row, strip, :] = sums[row]

    def step(count, _, carry):
        tile, block, part = carry
        waiting = None
        for _ in range(count):
            sources = sources_of(tile, part)
            places = [
                [jnp.broadcast_to(moment_ref[source, axis : axis + 1, :], (8, lanes)) for axis in range(3)]
                for source in sources
            ]
            spot = tile * blocks + block
            item = (spot, places, distances(spot, sources))
            if waiting is not None:
                kernels(*waiting)
            waiting = item
            tile, block, part = following(tile, block, part)
        kernels(*waiting)
        return (tile, block, part)

    zero = jnp.int32(0)
    whole = item_total // units
    few = units // 2
    carry = lax.fori_loop(0, whole, functools.partial(step, units), (zero, zero, zero))
    lax.fori_loop(0, (item_total - whole * units + few - 1) // few, functools.partial(step, few), carry)


def advance(middle, place_own, speed_own, weight_own, total_ref, sums_ref):
    tiles = weight_own.shape[0]
    blocks = lanes // block_rows
    for tile in range(tiles):
        for row in range(4):
            parts = [total_ref[tile * blocks + block, row] for block in range(blocks)]
            total = jnp.sum(jnp.transpose(jnp.concatenate(parts, axis=0)), axis=0, keepdims=True)
            sums_ref[row, tile : tile + 1, :] = total
    zeroth = sums_ref[3, :tiles, :]
    places, speeds = ([], [])
    for axis in range(3):
        force = sums_ref[axis, :tiles, :] - (place_own[axis] - middle[axis]) * zeroth
        speeds.append(weight_own * (speed_own[axis] + time_step * force / lanes))
        places.append(weight_own * (place_own[axis] + time_step * speeds[axis]))
    return places, speeds


def part_of(ref, tiles, row):
    return ref[row * tiles : (row + 1) * tiles, :]


def fill_planes(planes, tiles, blocks):
    kinds, rows, slots = planes.shape
    filled = len(blocks) * tiles
    planes[:, filled:, :] = jnp.zeros((kinds, rows - filled, slots), jnp.float32)
    for block, ref in enumerate(blocks):
        for kind in range(kinds):
            planes[kind, block * tiles : (block + 1) * tiles, :] = part_of(ref, tiles, kind)


def weights_of(aux, listed):
    slot = lax.broadcasted_iota(jnp.int32, aux.shape, 1).astype(jnp.float32)
    return jnp.where(slot < aux[:, listed : listed + 1], 1.0, 0.0)


def offsets_of(tiles, near_pair):
    device = device_index()
    toward = jnp.where(device % 2 == 0, 1.0, -1.0) * float(tiles)
    if near_pair:
        return [0.0, toward]
    return [-toward, -reach * toward, reach * toward]


def far_blocks(pair, forwarded, first_rows):
    return (pair[:first_rows, :], pair[first_rows:, :], forwarded[:first_rows, :])


def prepare(first, near_pair, listed, own_ref, blocks, lists_ref, weight_ref, tools):
    planes, scalars, copy_sem, feature_ref, moment_ref, source_ref = tools
    first_row = own_ref.shape[0] // planes.shape[0] * (1 if near_pair else reach)
    tiles = own_ref.shape[0] // planes.shape[0]
    if not first:
        copy = pltpu.make_async_copy(lists_ref, scalars, copy_sem)
        copy.start()
    fill_planes(planes, tiles, blocks)
    if first:
        aux = planes[3]
        own_aux = jnp.concatenate(
            [part_of(own_ref, tiles, 3), jnp.zeros((round_up(tiles, 8) - tiles, lanes), jnp.float32)], axis=0
        )
        for row, value in enumerate(build_lists(aux, own_aux, tiles, listed, offsets_of(tiles, near_pair))):
            lists_ref[row : row + 1, :] = value
        copy = pltpu.make_async_copy(lists_ref, scalars, copy_sem)
        copy.start()
        weight_ref[...] = weights_of(aux, listed)
    middle = middles([part_of(own_ref, tiles, axis) for axis in range(3)])
    places = [planes[axis, first_row:, :] for axis in range(3)]
    build_sources(first_row, places, middle, weight_ref[first_row:, :], feature_ref, moment_ref, source_ref)
    return middle, copy


def alone(listed, first, *refs):
    if first:
        own_ref, total_ref, target_ref, moment_ref, source_ref, feature_ref = refs
        tiles = own_ref.shape[0] // 4
        weight = weights_of(part_of(own_ref, tiles, 3), listed)
    else:
        own_ref, weight_ref, total_ref, target_ref, moment_ref, source_ref, feature_ref = refs
        tiles = own_ref.shape[0] // 3
        weight = weight_ref[:tiles, :]
    own_place = [part_of(own_ref, tiles, axis) for axis in range(3)]
    middle = middles(own_place)
    total_ref[...] = jnp.zeros(total_ref.shape, jnp.float32)
    build_targets(own_place, middle, feature_ref, target_ref)
    build_sources(0, own_place, middle, weight, feature_ref, moment_ref, source_ref)


def ahead(listed, first, *refs):
    own_ref, pair, *refs = refs
    *given, moment_ref, source_ref, feature_ref = refs
    tiles = own_ref.shape[0] // (4 if first else 3)
    first_rows = own_ref.shape[0] if first else 3 * (tiles + tiles // 2)
    middle = middles([part_of(own_ref, tiles, axis) for axis in range(3)])
    for index, block in enumerate((pair[:first_rows, :], pair[first_rows:, :])):
        if first:
            weight = weights_of(part_of(block, tiles, 3), listed)
        else:
            weight = given[0][index * tiles : (index + 1) * tiles, :]
        places = [part_of(block, tiles, axis) for axis in range(3)]
        build_sources(index * tiles, places, middle, weight, feature_ref, moment_ref, source_ref)


def begin(listed, first, *refs):
    own_ref, sibling_ref, target_ref, _, _, _, *refs = refs
    if first:
        total_ref, moment_ref, source_ref, lists_ref, weight_ref, *scratch = refs
    else:
        lists_ref, weight_ref, total_ref, moment_ref, source_ref, *scratch = refs
    tools = scratch + [moment_ref, source_ref]
    tiles = own_ref.shape[0] // tools[0].shape[0]
    _, copy = prepare(first, True, listed, own_ref, (own_ref, sibling_ref), lists_ref, weight_ref, tools)
    copy.wait()
    accumulate(tiles, tools[1], tools[5], target_ref, tools[4], total_ref)


def halves(speed, even, half):
    first, last = (speed[:half], speed[half:])
    return jnp.where(even, last, first), jnp.where(even, first, last)


def first_finish(
    listed, own_ref, pair, forwarded, total_in, target_ref, weight_own_ref, speed_ref, moment_in, source_in, *refs
):
    total_ref, moment_ref, source_ref, lists_ref, weight_ref, place_out, speed_out, *refs = refs
    sibling_out, beside_out, *tools, sums_ref = refs
    tools += [moment_ref, source_ref]
    tiles = own_ref.shape[0] // tools[0].shape[0]
    half = tiles // 2
    middle, copy = prepare(True, False, listed, own_ref, far_blocks(pair, forwarded, own_ref.shape[0]), lists_ref, weight_ref, tools)
    copy.wait()
    accumulate(tiles, tools[1], tools[5], target_ref, tools[4], total_ref)
    places, speeds = advance(
        middle,
        [part_of(own_ref, tiles, axis) for axis in range(3)],
        [part_of(speed_ref, tiles, axis) for axis in range(3)],
        weight_own_ref[:tiles, :],
        total_ref,
        sums_ref,
    )
    even = device_index() % 2 == 0
    for axis in range(3):
        strip = slice(axis * tiles, (axis + 1) * tiles)
        place_out[strip, :] = places[axis]
        speed_out[strip, :] = speeds[axis]
        sibling_out[strip, :] = places[axis]
        beside_out[strip, :] = places[axis]
        strip = slice(3 * tiles + axis * half, 3 * tiles + (axis + 1) * half)
        sibling_out[strip, :], beside_out[strip, :] = halves(speeds[axis], even, half)


def second_finish(
    own_ref,
    pair,
    forwarded,
    total_in,
    target_ref,
    weight_own_ref,
    speed_ref,
    lists_ref,
    weight_ref,
    moment_in,
    source_in,
    total_ref,
    moment_ref,
    source_ref,
    state_ref,
    sibling_out,
    beside_out,
    *scratch
):
    *tools, sums_ref = scratch
    tools += [moment_ref, source_ref]
    tiles = own_ref.shape[0] // 3
    half = tiles // 2
    beside = pair[: 3 * (tiles + half), :]
    blocks = far_blocks(pair, forwarded, beside.shape[0])
    middle, copy = prepare(False, False, None, own_ref, blocks, lists_ref, weight_ref, tools)
    copy.wait()
    accumulate(tiles, tools[1], tools[5], target_ref, tools[4], total_ref)
    place_own = [part_of(own_ref, tiles, axis) for axis in range(3)]
    speed_own = [part_of(speed_ref, tiles, axis) for axis in range(3)]
    places, speeds = advance(middle, place_own, speed_own, weight_own_ref[:tiles, :], total_ref, sums_ref)
    even = device_index() % 2 == 0
    for row, value in enumerate(places + speeds):
        state_ref[row] = value
        strip = slice(row * half, (row + 1) * half)
        sibling_out[strip, :], beside_out[strip, :] = halves(value, even, half)


def first_place(total_tiles, cuts_ref, own_ref, speed_ref, sibling_ref, pair, out_ref, pool_ref):
    tiles = own_ref.shape[0] // 3
    half = tiles // 2
    beside = pair[: 3 * (tiles + half), :]
    place_own = [part_of(own_ref, tiles, axis) for axis in range(3)]
    speed_own = [part_of(speed_ref, tiles, axis) for axis in range(3)]
    even = device_index() % 2 == 0
    lower, upper = ([], [])
    for row in range(6):
        if row < 3:
            sides = [part_of(ref, tiles, row) for ref in (sibling_ref, beside)]
            low_sides, high_sides = ([side[tiles - half :] for side in sides], [side[:half] for side in sides])
        else:
            strip = slice(3 * tiles + (row - 3) * half, 3 * tiles + (row - 2) * half)
            low_sides = high_sides = [ref[strip, :] for ref in (sibling_ref, beside)]
        lower.append(jnp.where(even, low_sides[1], low_sides[0]))
        upper.append(jnp.where(even, high_sides[0], high_sides[1]))
    place_rows(0, total_tiles, cuts_ref, lower, place_own + speed_own, upper, pool_ref, out_ref)


def place_rows(step, total_tiles, cuts_ref, lower, own, upper, pool_ref, out_ref):
    tiles, slots = own[0].shape
    half = tiles // 2
    capacity = out_ref.shape[1]
    device = device_index()
    last = cuts_ref.shape[1] - 1
    first_tile = cuts_ref[step, device]
    next_tile = jnp.where(device == last, total_tiles, cuts_ref[step, jnp.minimum(device + 1, last)])
    owned = next_tile - first_tile
    start = first_tile - (device * tiles - half)
    filled = lax.broadcasted_iota(jnp.int32, (capacity, slots), 0) < owned
    for row in range(6):
        pool_ref[row, :half, :] = lower[row]
        pool_ref[row, half : half + tiles, :] = own[row]
        pool_ref[row, half + tiles : 2 * tiles, :] = upper[row]
    for row in range(6):
        out_ref[row] = jnp.where(filled, pool_ref[row, pl.ds(start, capacity), :], 0.0)


def third_kernel(total_tiles, cuts_ref, sibling_ref, own_ref, beside_ref, out_ref, pool_ref):
    half = own_ref.shape[1] // 2
    even = device_index() % 2 == 0
    lower, upper = ([], [])
    for row in range(6):
        sibling, beside = (part_of(sibling_ref, half, row), part_of(beside_ref, half, row))
        lower.append(jnp.where(even, beside, sibling))
        upper.append(jnp.where(even, sibling, beside))
    place_rows(1, total_tiles, cuts_ref, lower, [own_ref[row] for row in range(6)], upper, pool_ref, out_ref)


def far(value):
    return pltpu.with_memory_space_constraint(value, pltpu.HBM)


def near(value):
    return pltpu.with_memory_space_constraint(value, pltpu.VMEM)


def body(particles, occupancy, neighbours, curve_cuts):
    tiles, _, slots = particles.shape
    listed = neighbours.shape[1]
    total_tiles = tiles * lax.axis_size(AXES)
    half = tiles // 2
    capacity = 2 * tiles
    near_rows = round_up(2 * tiles + 1, 8)
    far_rows = round_up((reach + 1) * tiles + 1, 8)
    list_rows = round_up(tiles + 2, 8)
    vmem = pl.BlockSpec(memory_space=pltpu.VMEM)
    smem = pl.BlockSpec(memory_space=pltpu.SMEM)

    def held(*sizes, dtype=jnp.float32):
        return pltpu.VMEM(sizes, dtype)

    def call(kernel, name, outs, ins, scratch, flops=0, aliases=None):
        held_ins = [far(value) if kind is smem else near(value) for kind, value in ins]
        return pl.pallas_call(
            kernel,
            out_shape=outs,
            in_specs=[kind for kind, _ in ins],
            out_specs=[vmem] * len(outs),
            scratch_shapes=scratch,
            input_output_aliases=aliases or {},
            compiler_params=pltpu.CompilerParams(vmem_limit_bytes=vmem_limit),
            cost_estimate=pl.CostEstimate(flops=flops, bytes_accessed=1 << 20, transcendentals=0),
            name=name,
        )(*held_ins)

    def moments(rows):
        return held(rows, 8, lanes)

    def sources(rows):
        return held(rows, feature_rows, lanes, dtype=jnp.bfloat16)

    def features(rows):
        return pltpu.VMEM((rows * feature_rows, lanes), jnp.float32)

    def tools(rows, kinds):
        return [
            pltpu.VMEM((kinds, rows, slots), jnp.float32),
            pltpu.SMEM((list_rows, lanes), jnp.int32),
            pltpu.SemaphoreType.DMA,
            features(rows),
        ]

    packed, speed = pl.pallas_call(
        functools.partial(pack_kernel, total_tiles),
        out_shape=(held(4 * tiles, slots), held(3 * tiles, slots)),
        in_specs=[vmem, smem, vmem],
        out_specs=(vmem, vmem),
        compiler_params=pltpu.CompilerParams(vmem_limit_bytes=vmem_limit),
        name="pack",
    )(far(particles), far(occupancy), far(neighbours))
    pool_scratch = pltpu.VMEM((6, round_up(capacity + tiles, 8), slots), jnp.float32)
    sums_scratch = pltpu.VMEM((4, round_up(tiles, 8), lanes), jnp.float32)
    blocks = lanes // block_rows
    totals = held(tiles * blocks + 1, 4, block_rows, lanes)
    targets = held(tiles * blocks + 1, block_rows, feature_rows, dtype=jnp.bfloat16)
    lists = held(list_rows, lanes, dtype=jnp.int32)
    edge = 3 * tiles + 3 * half
    work = 1 << 32

    sibling = swapped(packed, 0)
    pair = swapped(jnp.concatenate([packed, sibling], axis=0), 1)
    carried = [totals, moments(near_rows), sources(near_rows)]
    total, target, moment, source = call(
        functools.partial(alone, listed, True),
        "first_alone",
        [totals, targets, *carried[1:]],
        [(vmem, packed)],
        [features(round_up(tiles, 8))],
        1 << 22,
    )
    total, _, _, near_lists, near_weight = call(
        functools.partial(begin, listed, True),
        "first_near",
        carried + [lists, held(near_rows, slots)],
        [(vmem, value) for value in (packed, sibling, target, total, moment, source)],
        tools(near_rows, 4),
        work,
        {3: 0, 4: 1, 5: 2},
    )
    pair, near_weight = lax.optimization_barrier((pair, near_weight))
    forwarded = swapped(pair, 0)
    far_carried = [totals, moments(far_rows), sources(far_rows)]
    moment, source = call(
        functools.partial(ahead, listed, True),
        "first_ahead",
        far_carried[1:],
        [(vmem, packed), (vmem, pair)],
        [features(round_up(tiles, 8))],
        1 << 22,
    )
    total, _, _, far_lists, far_weight, place, speed, sibling, beside = call(
        functools.partial(first_finish, listed),
        "first_far",
        far_carried
        + [lists, held(far_rows, slots), held(3 * tiles, slots), held(3 * tiles, slots), held(edge, slots), held(edge, slots)],
        [(vmem, value) for value in (packed, pair, forwarded, total, target, near_weight, speed, moment, source)],
        tools(far_rows, 4) + [sums_scratch],
        work,
        {3: 0, 7: 1, 8: 2},
    )
    sibling = swapped(sibling, 0)
    pair = swapped(jnp.concatenate([beside, sibling[: 3 * tiles]], axis=0), 1)
    total, target, moment, source = call(
        functools.partial(alone, listed, False),
        "second_alone",
        [totals, targets, *carried[1:]],
        [(vmem, place), (vmem, near_weight)],
        [features(round_up(tiles, 8))],
        1 << 22,
    )
    total, _, _ = call(
        functools.partial(begin, listed, False),
        "second_near",
        carried,
        [(vmem, value) for value in (place, sibling, target, total, moment, source, near_lists, near_weight)],
        tools(near_rows, 3),
        work,
        {3: 0, 4: 1, 5: 2},
    )
    pair, total = lax.optimization_barrier((pair, total))
    forwarded = swapped(pair, 0)
    (after_first,) = call(
        functools.partial(first_place, total_tiles),
        "first_place",
        [jax.ShapeDtypeStruct((6, capacity, slots), jnp.float32)],
        [(smem, curve_cuts)] + [(vmem, value) for value in (place, speed, sibling, pair)],
        [pool_scratch],
        1 << 22,
    )
    moment, source = call(
        functools.partial(ahead, listed, False),
        "second_ahead",
        far_carried[1:],
        [(vmem, place), (vmem, pair), (vmem, far_weight)],
        [features(round_up(tiles, 8))],
        1 << 22,
    )
    _, _, _, state, sibling, beside = call(
        second_finish,
        "second_far",
        far_carried
        + [
            held(6, tiles, slots),
            held(6 * half, slots),
            held(6 * half, slots),
        ],
        [
            (vmem, value)
            for value in (place, pair, forwarded, total, target, near_weight, speed, far_lists, far_weight, moment, source)
        ],
        tools(far_rows, 3) + [sums_scratch],
        work,
        {3: 0, 9: 1, 10: 2},
    )
    beside = swapped(beside, 1, wrap=False)
    sibling = swapped(sibling, 0)
    (after_second,) = call(
        functools.partial(third_kernel, total_tiles),
        "place",
        [jax.ShapeDtypeStruct((6, capacity, slots), jnp.float32)],
        [(smem, curve_cuts), (vmem, sibling), (vmem, state), (vmem, beside)],
        [pool_scratch],
    )
    return (jnp.transpose(after_first, (1, 0, 2)), jnp.transpose(after_second, (1, 0, 2)))


def solution(mesh):
    in_specs = (P(AXES, None, None), P(AXES), P(AXES, None), P())
    out_specs = (P(AXES, None, None), P(AXES, None, None))
    return jax.shard_map(body, mesh=mesh, in_specs=in_specs, out_specs=out_specs, check_vma=False)
```
